32 devices in a mesh: gx: 8 (over z, y), gz: 4 (over x, core).
Axes of the slice: x: 2, y: 2, z: 4, core: 2. Of those that a mesh axis runs over, the one named last changes fastest.
Arguments:
- pressure: float32 [64, 128, 256], P('gz', 'gx'), may hold values from -6 to 6
- saturation: float32 [64, 128, 256], P('gz', 'gx'), may hold values from 0.05 to 0.8
- sat_history: float32 [64, 128, 256], P('gz', 'gx'), may hold values from 0.05 to 0.85, as said below
- storage: float32 [64, 128, 256], P('gz', 'gx'), may hold values from 0.3 to 3
- step_volume: float32 [64, 128, 256], P('gz', 'gx'), may hold values from 0.005 to 0.05
- transmiss: float32 [3, 64, 128, 256], P(None, 'gz', 'gx'), may hold values from 0.1 to 2
- perf_cell: int32 [256, 16], P('gx'), may hold values from 0 to 262143, as said below
- perf_index: float32 [256, 16], P('gx'), may hold values from 0.2 to 2
- control: int32 [256], P('gx'), may hold values from 0 to 1
- target: float32 [256], P('gx'), may hold values from 0.5 to 3
Outputs:
- new_pressure: float32 [64, 128, 256], P('gz', 'gx')
- residual: float32 [64, 128, 256], P('gz', 'gx')
- new_saturation: float32 [64, 128, 256], P('gz', 'gx')
- new_history: float32 [64, 128, 256], P('gz', 'gx')
- bottom_hole: float32 [256], P('gx')
The draws below stay inside these ranges and needn't reach their ends.
Inputs may be any that keep to these rules, and one draw needn't show every extreme that they name: `perf_cell`: each perforation number names a cell of its own well's row of tiles, counted as layer * 16 * 256 + first lateral index within the row * 256 + second lateral index; a well's perforations lie in 16 consecutive layers, one a layer, top first, and from one to the next each lateral index moves by at most one cell. sat_history is at least the cell's saturation.
All inputs are finite; a program needn't handle non-finite values.
Results may differ from the reference program's by a relative error of at most 0.0003.
Values sent between devices are 32-bit elements; how exact they have to be, the bound alone decides.
No kernel may reach another device: no remote copies, remote signals or barrier semaphores. Data moves between devices by JAX's collectives and lax.ppermute only.
A program may use at most 64 MiB of HBM per device.

```python
import math
import jax
import jax.numpy as jnp
from jax import lax

CX = 16
NY = 256
WELL_ROW = 32
NPERF = 16
SWEEPS = 4
NZ = 64
NX = 128
NWELL = 256


def joint_saturation(key):
    base = jax.random.fold_in(key, 11)
    first, second, third = jax.random.split(base, 3)
    shape = (NZ, NX, NY)
    sat = jax.random.uniform(first, shape, jnp.float32, 0.05, 0.8)
    increment = jax.random.uniform(second, shape, jnp.float32, 0.0, 0.4)
    keep = jax.random.uniform(third, shape, jnp.float32) < 0.3
    history = jnp.minimum(sat + jnp.where(keep, 0.0, increment), 0.85)
    return (sat, history)


def draw_saturation(key, part):
    return joint_saturation(key)[0]


def draw_sat_history(key, part):
    return joint_saturation(key)[1]


def draw_perf_cell(key, part):
    base = jax.random.fold_in(key, 23)
    keys = jax.random.split(base, 5)
    top = jax.random.randint(keys[0], (NWELL, 1), 0, NZ - NPERF + 1)
    lateral_head = jax.random.randint(keys[1], (NWELL, 1), 0, CX)
    column_head = jax.random.randint(keys[2], (NWELL, 1), 0, NY)
    first_col = jnp.arange(NPERF, dtype=jnp.int32)[None, :] == 0
    lateral_step = jnp.where(first_col, 0, jax.random.randint(keys[3], (NWELL, NPERF), -1, 2))
    column_step = jnp.where(first_col, 0, jax.random.randint(keys[4], (NWELL, NPERF), -1, 2))
    lateral = jnp.clip(lateral_head + jnp.cumsum(lateral_step, axis=1), 0, CX - 1)
    column = jnp.clip(column_head + jnp.cumsum(column_step, axis=1), 0, NY - 1)
    layer = top + jnp.arange(NPERF, dtype=jnp.int32)[None, :]
    return (layer * (CX * NY) + lateral * NY + column).astype(jnp.int32)


def set_ends(values, stream_key, low, high):
    longest = values.shape.index(max(values.shape))
    spots = []
    for shift in (0, 1):
        where = [jax.random.randint(jax.random.fold_in(stream_key, axis), (), 0, length) for axis, length in enumerate(values.shape)]
        where[longest] = (where[longest] + shift) % values.shape[longest]
        spots.append(tuple(where))
    return values.at[spots[0]].set(low).at[spots[1]].set(high)


def levels(own_key, shape, pieces, least, high):
    def one(dim, parts):
        heights = jax.random.uniform(jax.random.fold_in(jax.random.fold_in(own_key, 6), dim), (parts,), jnp.float32, least / len(pieces), high / len(pieces))
        return jnp.repeat(jnp.exp(heights), shape[dim] // parts).reshape((-1,) + (1,) * (len(shape) - dim - 1))

    level = one(*pieces[0])
    for cut in pieces[1:]:
        level = level * one(*cut)
    return level


def scatter_about(key, extent, scale, bound, cuts=(), kind=jnp.bfloat16):
    factor_of = levels(key, extent, cuts, -0.22, 0.18) if cuts else 1.0
    array = jax.random.normal(key, extent, jnp.float32) * scale * factor_of
    return jnp.minimum(jnp.maximum(array, -bound), bound).astype(kind)


def setup_inputs(seed: int = 0) -> dict:
    splits = jax.random.split(jax.random.key(seed), 11)
    return {
        "pressure": scatter_about(splits[0], (NZ, NX, NY), 1.0, 6.0, ((0, 4), (1, 8)), jnp.float32),
        "saturation": draw_saturation(jax.random.fold_in(splits[10], 71), 0),
        "sat_history": draw_sat_history(jax.random.fold_in(splits[10], 71), 0),
        "storage": jnp.clip(jnp.exp(math.log(3.0) - 2.3025851 * jax.random.uniform(splits[3], (NZ, NX, NY), jnp.float32) ** levels(splits[3], (NZ, NX, NY), ((0, 4), (1, 8)), -0.2, 0.2)), 0.3, 3.0),
        "step_volume": jnp.clip(jnp.exp(math.log(0.05) - 2.3025851 * jax.random.uniform(splits[4], (NZ, NX, NY), jnp.float32) ** levels(splits[4], (NZ, NX, NY), ((0, 4), (1, 8)), -0.2, 0.2)), 0.005, 0.05),
        "transmiss": jnp.clip(jnp.exp(math.log(2.0) - 2.9957323 * jax.random.uniform(splits[5], (3, NZ, NX, NY), jnp.float32) ** levels(splits[5], (3, NZ, NX, NY), ((1, 4), (2, 8)), -0.2, 0.2)), 0.1, 2.0),
        "perf_cell": draw_perf_cell(jax.random.fold_in(splits[10], 71), 0),
        "perf_index": jnp.clip(jnp.exp(math.log(2.0) - 2.3025851 * jax.random.uniform(splits[7], (NWELL, NPERF), jnp.float32) ** levels(splits[7], (NWELL, NPERF), ((0, 8),), -0.2, 0.2)), 0.2, 2.0),
        "control": set_ends(jax.random.randint(splits[8], (NWELL,), 0, 2), jax.random.fold_in(splits[8], 1), 0, 1).astype(jnp.int32),
        "target": jnp.clip(0.5 + 2.5 * jax.random.uniform(splits[9], (NWELL,), jnp.float32) ** levels(splits[9], (NWELL,), ((0, 8),), -0.2, 0.2), 0.5, 3.0),
    }


def mobility(sat, history):
    trapped = history / (1.0 + 1.5 * history)
    excess = jnp.maximum(sat - trapped, 0.0)
    free_gas = 0.5 * (excess + jnp.sqrt(excess * excess + excess / 0.375))
    relperm = jnp.where(sat < history, free_gas * free_gas, sat * sat)
    gas = relperm / 0.5
    total = (1.0 - sat) * (1.0 - sat) + gas
    return (total, gas / total)

def next_cell(field, axis):
    size = field.shape[axis]
    tail = jnp.zeros_like(lax.slice_in_dim(field, 0, 1, axis=axis))
    return jnp.concatenate([lax.slice_in_dim(field, 1, size, axis=axis), tail], axis=axis)

def prev_cell(field, axis):
    size = field.shape[axis]
    head = jnp.zeros_like(lax.slice_in_dim(field, 0, 1, axis=axis))
    return jnp.concatenate([head, lax.slice_in_dim(field, 0, size - 1, axis=axis)], axis=axis)

def face_terms(transmiss, total):
    terms = []
    for axis in range(3):
        faces = transmiss[axis]
        index = lax.broadcasted_iota(jnp.int32, faces.shape, axis)
        plus_t = jnp.where(index < faces.shape[axis] - 1, faces, 0.0)
        minus_t = prev_cell(faces, axis)
        plus = plus_t * 0.5 * (total + next_cell(total, axis))
        minus = minus_t * 0.5 * (total + prev_cell(total, axis))
        terms.append((plus, minus))
    return terms

def operate(field, storage, terms):
    result = storage * field
    for axis in range(3):
        plus, minus = terms[axis]
        result = result + plus * (field - next_cell(field, axis)) + minus * (field - prev_cell(field, axis))
    return result

def reference(pressure, saturation, sat_history, storage, step_volume, transmiss, perf_cell, perf_index, control, target):
    total, frac = mobility(saturation, sat_history)
    terms = face_terms(transmiss, total)
    diag = storage
    for axis in range(3):
        diag = diag + terms[axis][0] + terms[axis][1]
    row_id = (jnp.arange(NWELL, dtype=jnp.int32) // WELL_ROW)[:, None]
    layer = perf_cell // (CX * NY)
    rest = perf_cell % (CX * NY)
    lateral = row_id * CX + rest // NY
    column = rest % NY
    weight = perf_index * total[layer, lateral, column]
    cell_p = pressure[layer, lateral, column]
    sum_p = lax.optimization_barrier(jnp.sum(weight * cell_p, axis=1))
    sum_w = lax.optimization_barrier(jnp.sum(weight, axis=1))
    bottom_hole = jnp.where(control == 0, (target + sum_p) / sum_w, target)
    rate = weight * (bottom_hole[:, None] - cell_p)
    source = jnp.zeros(pressure.shape, jnp.float32).at[layer, lateral, column].add(rate)
    rhs = storage * pressure + source
    field = pressure
    for sweep in range(SWEEPS):
        field = field + (rhs - operate(field, storage, terms)) / diag
    residual = rhs - operate(field, storage, terms)
    out = jnp.zeros_like(field)
    for axis in range(3):
        plus, minus = terms[axis]
        flow_up = plus * (field - next_cell(field, axis))
        out = out + flow_up * jnp.where(flow_up > 0, frac, next_cell(frac, axis))
        flow_down = minus * (field - prev_cell(field, axis))
        out = out + flow_down * jnp.where(flow_down > 0, frac, prev_cell(frac, axis))
    gas_source = jnp.maximum(source, 0.0) + jnp.minimum(source, 0.0) * frac
    new_saturation = saturation + step_volume * (gas_source - out)
    new_history = jnp.maximum(sat_history, new_saturation)
    return (field, residual, new_saturation, new_history, bottom_hole)
```

```python
import functools

import jax
import jax.numpy as jnp
from jax import lax
from jax.experimental import pallas as pl
from jax.experimental.pallas import tpu as pltpu
from jax.sharding import PartitionSpec as P

SWEEPS = 4
H = SWEEPS + 1
LANES = 128

Z_LAYERS = 3 * H + 3 * (H - 1) + 1

T1, TOT, P0, DIAG, RHS1, RHS2, F0, F2 = range(8)
RHS3, F1, FRAC, G2, G3, F0_2, F2_2, DIAG_2 = range(8)


def mobility(sat, history):
    trapped = history / (1.0 + 1.5 * history)
    excess = jnp.maximum(sat - trapped, 0.0)
    free_gas = 0.5 * (excess + jnp.sqrt(excess * excess + excess / 0.375))
    relperm = jnp.where(sat < history, free_gas * free_gas, sat * sat)
    gas = relperm / 0.5
    total = (1.0 - sat) * (1.0 - sat) + gas
    return (total, gas / total)


def roll(x, shift, axis):
    return pltpu.roll(x, shift % x.shape[axis], axis)


def split(x):
    high = x.astype(jnp.bfloat16)
    return (high, (x - high.astype(jnp.float32)).astype(jnp.bfloat16))


def one_hots(cell, first_layer, layers, rows, columns):
    count = cell.shape[1]
    layer = cell // (rows * columns)
    rest = cell - layer * (rows * columns)
    row = rest // columns
    column = rest - row * columns
    place = (layer - first_layer) * rows + row
    at_place = lax.broadcasted_iota(jnp.int32, (layers * rows, count), 0) == place
    at_column = lax.broadcasted_iota(jnp.int32, (columns, count), 0) == column
    return (at_place, at_column)


def gather(field, at_place, at_column):
    high, low = split(field)
    hot = at_column.astype(jnp.bfloat16)
    by_column = jnp.dot(high, hot, preferred_element_type=jnp.float32) + jnp.dot(
        low, hot, preferred_element_type=jnp.float32
    )
    return jnp.sum(jnp.where(at_place, by_column, 0.0), axis=0, keepdims=True)


def prepare_kernel(
    sat, hist, pressure, storage, trans, cell, wells, total, frac, up, down, sums, *, gz, group
):
    layers, rows, columns = pressure.shape

    def layer_step(l, carry):
        t, f = mobility(sat[l], hist[l])
        total[l] = t
        frac[l] = f
        return carry

    lax.fori_loop(0, layers, layer_step, 0, unroll=2)
    for message, edge in ((up, lambda n: pl.ds(layers - n, n)), (down, lambda n: pl.ds(0, n))):
        at = 0
        for source, count in (
            (pressure, H),
            (total, H),
            (trans.at[0], H),
            (storage, H - 1),
            (trans.at[1], H - 1),
            (trans.at[2], H - 1),
            (frac, 1),
        ):
            message[pl.ds(at, count)] = source[edge(count)]
            at += count
    at_place, at_column = one_hots(
        cell[...], lax.axis_index(gz) * layers, layers, rows, columns
    )
    flat = (layers * rows, columns)
    weight = wells[0:1, :] * gather(total[...].reshape(flat), at_place, at_column)
    cell_p = gather(pressure[...].reshape(flat), at_place, at_column)
    for i, value in enumerate((weight * cell_p, weight)):
        part = value[:, 0:LANES]
        for lane in range(LANES, value.shape[1], LANES):
            part = part + value[:, lane : lane + LANES]
        shift = LANES // 2
        while shift >= group:
            part = part + roll(part, shift, 1)
            shift //= 2
        sums[i : i + 1, :] = part


def build_kernel(
    pressure,
    total,
    frac,
    storage,
    trans,
    low,
    high,
    sums,
    cell,
    wells,
    p0e,
    tote,
    rhse,
    diage,
    f0e,
    f1e,
    f2e,
    source,
    up,
    down,
    bottom,
    stor,
    t0,
    t1,
    t2,
    p1,
    rhs1u,
    rhs1d,
    rhs2u,
    rhs2d,
    g2u,
    g2d,
    g3u,
    g3d,
    *,
    gx,
    gz,
):
    layers, rows, columns = pressure.shape
    ext = layers + 2 * H
    at = 0
    for target, own, count in (
        (p0e, pressure, H),
        (tote, total, H),
        (t0, trans.at[0], H),
        (stor, storage, H - 1),
        (t1, trans.at[1], H - 1),
        (t2, trans.at[2], H - 1),
    ):
        target[pl.ds(H - count, count)] = low[pl.ds(at, count)]
        target[pl.ds(H, layers)] = own[...]
        target[pl.ds(H + layers, count)] = high[pl.ds(at, count)]
        at += count
    top_z = lax.axis_index(gz) == lax.axis_size(gz) - 1
    top_x = lax.axis_index(gx) == lax.axis_size(gx) - 1
    t0[H + layers - 1] = jnp.where(top_z, 0.0, t0[H + layers - 1])

    inner = ext - 2
    at_place, at_column = one_hots(
        cell[...], lax.axis_index(gz) * layers - (H - 1), inner, rows, columns
    )
    flat = (inner * rows, columns)
    weight = wells[0:1, :] * gather(tote[1 : ext - 1].reshape(flat), at_place, at_column)
    cell_p = gather(p0e[1 : ext - 1].reshape(flat), at_place, at_column)
    count = weight.shape[1]
    repeat = lambda x: jnp.concatenate([x] * (count // LANES), axis=1)
    goal = wells[1:2, :]
    hole = jnp.where(
        wells[2:3, :] == 0.0, (goal + repeat(sums[0:1, :])) / repeat(sums[1:2, :]), goal
    )
    bottom[...] = hole[:, 0:LANES]
    rate = weight * (hole - cell_p)
    hot = at_place.astype(jnp.bfloat16)
    spread = jnp.zeros(flat, jnp.float32)
    for piece in split(jnp.where(at_column, rate, 0.0)):
        spread = spread + lax.dot_general(
            hot, piece, (((1,), (1,)), ((), ())), preferred_element_type=jnp.float32
        )
    spread = spread.reshape(inner, rows, columns)
    rhse[1 : ext - 1] = spread
    source[...] = spread[H - 1 : H - 1 + layers]

    row = lax.broadcasted_iota(jnp.int32, (rows, columns), 0)
    column = lax.broadcasted_iota(jnp.int32, (rows, columns), 1)
    last_row = row == rows - 1
    last_column = column == columns - 1
    f0e[0] = t0[0] * 0.5 * (tote[0] + tote[1])

    def face_step(e, below):
        tot = tote[e]
        above = t0[e] * 0.5 * (tot + tote[e + 1])
        f0e[e] = above
        along = jnp.where(last_row, 0.0, t1[e]) * 0.5 * (tot + roll(tot, -1, 0))
        f1e[e] = jnp.where(last_row, jnp.where(top_x, 0.0, t1[e]), along)
        across = jnp.where(last_column, 0.0, t2[e]) * 0.5 * (tot + roll(tot, -1, 1))
        f2e[e] = across
        store = stor[e]
        diag = store + above + below + along + roll(along, 1, 0) + across + roll(across, 1, 1)
        diage[e] = diag
        p = p0e[e]
        rhs = store * p + rhse[e]
        rhse[e] = rhs
        lower = roll(along * p, 1, 0)
        upper = along * roll(p, -1, 0)
        rhs1u[e] = rhs + lower
        rhs1d[e] = rhs + upper
        new = rhs + lower + upper + above * p0e[e + 1] + below * p0e[e - 1]
        new = new + across * roll(p, -1, 1) + roll(across * p, 1, 1)
        p1[e] = jnp.where(diag > 0.0, new / diag, 0.0)
        return above

    lax.fori_loop(1, ext - 1, face_step, f0e[0])

    def second_step(e, carry):
        along = jnp.where(last_row, 0.0, f1e[e])
        across = f2e[e]
        p = p1[e]
        rhs = rhse[e]
        diag = diage[e]
        lower = roll(along * p, 1, 0)
        upper = along * roll(p, -1, 0)
        rhs2u[e] = rhs + lower
        rhs2d[e] = rhs + upper
        part = rhs + f0e[e] * p1[e + 1] + f0e[e - 1] * p1[e - 1]
        part = part + across * roll(p, -1, 1) + roll(across * p, 1, 1)
        g2u[e] = part + lower
        g2d[e] = part + upper
        p2 = jnp.where(diag > 0.0, (part + lower + upper) / diag, 0.0)
        g3u[e] = rhs + roll(along * p2, 1, 0)
        g3d[e] = rhs + along * roll(p2, -1, 0)
        return carry

    rhs2u[1] = rhse[1]
    rhs2d[1] = rhse[1]
    rhs2u[ext - 2] = rhse[ext - 2]
    rhs2d[ext - 2] = rhse[ext - 2]
    lax.fori_loop(2, ext - 2, second_step, 0)

    wide = ext - 2
    narrow = layers + 2

    for message, d1, d2, r1, r2, g2, g3, inside in (
        (up, rows - 1, rows - 2, rhs1u, rhs2u, g2u, g3u, rows - 2),
        (down, 0, 1, rhs1d, rhs2d, g2d, g3d, 0),
    ):
        for slot, ref in (
            (T1, t1),
            (TOT, tote),
            (P0, p0e),
            (DIAG, diage),
            (RHS1, r1),
            (RHS2, r2),
            (F0, f0e),
            (F2, f2e),
        ):
            message[0:wide, slot : slot + 1, :] = ref[1 : 1 + wide, d1 : d1 + 1, :]
        for slot, ref, index in (
            (RHS3, rhse, d1),
            (F1, f1e, inside),
            (G2, g2, d2),
            (G3, g3, d2),
            (F0_2, f0e, d2),
            (F2_2, f2e, d2),
            (DIAG_2, diage, d2),
        ):
            message[wide : wide + narrow, slot : slot + 1, :] = ref[
                H - 1 : H - 1 + narrow, index : index + 1, :
            ]
        for l in (0, narrow - 1):
            message[wide + l, FRAC : FRAC + 1] = jnp.zeros((1, columns), jnp.float32)
        message[wide + 1 : wide + 1 + layers, FRAC : FRAC + 1, :] = frac[:, d1 : d1 + 1, :]


def finish_kernel(
    sat,
    hist,
    volume,
    storage,
    frac,
    source,
    p0e,
    tote,
    rhse,
    diage,
    f0e,
    f1e,
    f2e,
    zlow,
    zhigh,
    xlow,
    xhigh,
    new_p,
    residual,
    new_sat,
    new_hist,
    pa,
    pb,
    f1,
    rdiag,
    sf0,
    sf1,
    sf2,
    stot,
    sdiag,
    sp0,
    srhs1,
    srhs2,
    srhs3,
    sfrac,
    fracs,
):
    layers, rows, columns = sat.shape
    ext = layers + 2 * H
    wide = ext - 2
    narrow = layers + 2

    def fill(seam, entries):
        seam[...] = jnp.zeros(seam.shape, jnp.float32)
        for side, slot, place, is_wide in entries:
            first, number, offset = (1, wide, 0) if is_wide else (H - 1, narrow, wide)
            seam[first : first + number, place : place + 1, :] = side[
                offset : offset + number, slot : slot + 1, :
            ]

    def pair(slot):
        return [(xhigh, slot, 0, True), (xlow, slot, 7, True)]

    def inner(slot):
        return [(xhigh, slot, 1, False), (xlow, slot, 6, False)]

    fill(sf0, pair(F0) + inner(F0_2))
    fill(sf2, pair(F2) + inner(F2_2))
    fill(stot, pair(TOT))
    fill(sdiag, pair(DIAG) + inner(DIAG_2))
    fill(sp0, pair(P0))
    fill(srhs1, pair(RHS1))
    fill(srhs2, pair(RHS2) + inner(G2))
    fill(
        srhs3,
        [(xhigh, RHS3, 0, False), (xlow, RHS3, 7, False)] + inner(G3),
    )
    fill(sfrac, [(xhigh, FRAC, 0, False), (xlow, FRAC, 7, False)])
    fill(sf1, [(xhigh, F1, 0, False), (xlow, F1, 6, False), (xlow, T1, 7, True)])

    full = rows + 8
    row = lax.broadcasted_iota(jnp.int32, (full, columns), 0)
    edge = (row == rows - 1) | (row == full - 1)
    beyond = (row == rows + 1) | (row == full - 2)
    join = lambda a, b: jnp.concatenate([a, b], axis=0)

    pa[0] = join(p0e[0], sp0[0])
    pa[ext - 1] = join(p0e[ext - 1], sp0[ext - 1])

    def face_step(e, carry):
        tot = join(tote[e], stot[e])
        mixed = join(f1e[e], sf1[e])
        border = jnp.where(edge, mixed * 0.5 * (tot + roll(tot, -1, 0)), 0.0)
        f1[e] = jnp.where(edge, border, mixed)
        diag = join(diage[e], sdiag[e]) + border + roll(border, 1, 0)
        rdiag[e] = jnp.where(diag > 0.0, 1.0 / diag, 0.0)
        pa[e] = join(p0e[e], sp0[e])
        return carry

    lax.fori_loop(1, ext - 1, face_step, 0)

    def sweep(number, old, new, srhs):
        def step(e, below):
            p = old[e]
            above = old[e + 1]
            face = join(f0e[e], sf0[e])
            x = f1[e]
            y = join(f2e[e], sf2[e])
            total = join(rhse[e], srhs[e]) + below + face * above
            total = total + x * roll(p, -1, 0) + roll(x * p, 1, 0)
            total = total + y * roll(p, -1, 1) + roll(y * p, 1, 1)
            value = total * rdiag[e]
            if number == 1:
                value = jnp.where(beyond, 0.0, value)
            new[e] = value
            return face * p

        first = join(f0e[number - 1], sf0[number - 1]) * old[number - 1]
        lax.fori_loop(number, ext - number, step, first)

    fields = (pa, pb)
    for number in range(1, SWEEPS + 1):
        sweep(
            number,
            fields[(number - 1) % 2],
            fields[number % 2],
            {1: srhs1, 2: srhs2}.get(number, srhs3),
        )
    field = fields[SWEEPS % 2]

    fracs[0] = zlow[Z_LAYERS - 1]
    fracs[pl.ds(1, layers)] = frac[...]
    fracs[layers + 1] = zhigh[Z_LAYERS - 1]

    def flow(face, p, p_next, f, f_next):
        water = face * (p - p_next)
        return (water, water * jnp.where(water > 0, f, f_next))

    def last_step(l, carry):
        below_w, below_g = carry
        e = l + H
        p = field[e]
        f = join(fracs[l + 1], sfrac[e])
        own_p = p[:rows]
        own_f = f[:rows]
        above_w, above_g = flow(f0e[e], own_p, field[e + 1][:rows], own_f, fracs[l + 2])
        xw, xg = flow(f1[e], p, roll(p, -1, 0), f, roll(f, -1, 0))
        yw, yg = flow(f2e[e], own_p, roll(own_p, -1, 1), own_f, roll(own_f, -1, 1))
        water = above_w - below_w + (xw - roll(xw, 1, 0))[:rows] + yw - roll(yw, 1, 1)
        out = above_g - below_g + (xg - roll(xg, 1, 0))[:rows] + yg - roll(yg, 1, 1)
        new_p[l] = own_p
        residual[l] = rhse[e] - storage[l] * own_p - water
        src = source[l]
        gas = jnp.maximum(src, 0.0) + jnp.minimum(src, 0.0) * own_f
        s = sat[l] + volume[l] * (gas - out)
        new_sat[l] = s
        new_hist[l] = jnp.maximum(hist[l], s)
        return (above_w, above_g)

    first = flow(f0e[H - 1], field[H - 1][:rows], field[H][:rows], fracs[0], fracs[1])
    lax.fori_loop(0, layers, last_step, first)


def shift(block, axis, up):
    count = lax.axis_size(axis)
    pairs = [(i, i + 1) if up else (i + 1, i) for i in range(count - 1)]
    return lax.ppermute(block, axis, pairs)


VMEM = pl.BlockSpec(memory_space=pltpu.VMEM)


def call(kernel, outs, scratch, *args):
    f32 = jnp.float32
    return pl.pallas_call(
        kernel,
        out_shape=[jax.ShapeDtypeStruct(s, f32) for s in outs],
        in_specs=[VMEM] * len(args),
        out_specs=[VMEM] * len(outs),
        scratch_shapes=[pltpu.VMEM(s, f32) for s in scratch],
        compiler_params=pltpu.CompilerParams(vmem_limit_bytes=40 * 1024 * 1024),
    )(*args)


def body(
    pressure,
    saturation,
    sat_history,
    storage,
    step_volume,
    transmiss,
    perf_cell,
    perf_index,
    control,
    target,
):
    layers, rows, columns = pressure.shape
    ext = layers + 2 * H
    wells, perfs = perf_cell.shape
    block = (layers, rows, columns)
    ext_block = (ext, rows, columns)
    z_message = (Z_LAYERS, rows, columns)
    x_message = (ext - 2 + layers + 2, 8, columns)
    seam = (ext, 8, columns)
    cell = perf_cell.T.reshape(1, wells * perfs)
    per_perf = jnp.stack(
        [
            perf_index.T.reshape(-1),
            jnp.tile(target, perfs),
            jnp.tile(control, perfs).astype(jnp.float32),
        ]
    )
    total, frac, z_up, z_down, part = call(
        functools.partial(prepare_kernel, gz="gz", group=wells),
        [block, block, z_message, z_message, (2, LANES)],
        [],
        saturation,
        sat_history,
        pressure,
        storage,
        transmiss,
        cell,
        per_perf,
    )
    z_low = shift(z_up, "gz", True)
    z_high = shift(z_down, "gz", False)
    sums = lax.psum(part, "gz")
    p0e, tote, rhse, diage, f0e, f1e, f2e, source, x_up, x_down, bottom = call(
        functools.partial(build_kernel, gx="gx", gz="gz"),
        [ext_block] * 7 + [block, x_message, x_message, (1, LANES)],
        [ext_block] * 13,
        pressure,
        total,
        frac,
        storage,
        transmiss,
        z_low,
        z_high,
        sums,
        cell,
        per_perf,
    )
    x_low = shift(x_up, "gx", True)
    x_high = shift(x_down, "gx", False)
    field, residual, new_sat, new_hist = call(
        finish_kernel,
        [block] * 4,
        [(ext, rows + 8, columns)] * 4 + [seam] * 10 + [(layers + 2, rows, columns)],
        saturation,
        sat_history,
        step_volume,
        storage,
        frac,
        source,
        p0e,
        tote,
        rhse,
        diage,
        f0e,
        f1e,
        f2e,
        z_low,
        z_high,
        x_low,
        x_high,
    )
    return (field, residual, new_sat, new_hist, bottom[0, :wells])


def solution(mesh):
    return jax.shard_map(
        body,
        mesh=mesh,
        in_specs=(
            P("gz", "gx", None),
            P("gz", "gx", None),
            P("gz", "gx", None),
            P("gz", "gx", None),
            P("gz", "gx", None),
            P(None, "gz", "gx", None),
            P("gx", None),
            P("gx", None),
            P("gx"),
            P("gx"),
        ),
        out_specs=(
            P("gz", "gx", None),
            P("gz", "gx", None),
            P("gz", "gx", None),
            P("gz", "gx", None),
            P("gx"),
        ),
        check_vma=False,
    )
```

```python
import functools

import jax
import jax.numpy as jnp
from jax import lax
from jax.experimental import pallas as pl
from jax.experimental.pallas import tpu as pltpu
from jax.sharding import PartitionSpec as P

SWEEPS = 4
H = SWEEPS + 1
LANES = 128

FRAC_LAYER = 3 * H + 3 * (H - 1)
SUM_LAYER = FRAC_LAYER + 1
Z_LAYERS = SUM_LAYER + 1

T1, TOT, P0, DIAG, RHS1, RHS2, F0, F2 = range(8)
RHS3, F1, FRAC, G2, G3, F0_2, F2_2, DIAG_2 = range(8)


def mobility(sat, history):
    trapped = history / (1.0 + 1.5 * history)
    excess = jnp.maximum(sat - trapped, 0.0)
    free_gas = 0.5 * (excess + jnp.sqrt(excess * excess + excess / 0.375))
    relperm = jnp.where(sat < history, free_gas * free_gas, sat * sat)
    gas = relperm / 0.5
    total = (1.0 - sat) * (1.0 - sat) + gas
    return (total, gas / total)


def roll(x, shift, axis):
    return pltpu.roll(x, shift % x.shape[axis], axis)


def loop(first, last, step, carry, unroll=4):
    groups = (last - first) // unroll

    def group(g, carry):
        for i in range(unroll):
            carry = step(first + g * unroll + i, carry)
        return carry

    carry = lax.fori_loop(0, groups, group, carry)
    for index in range(first + groups * unroll, last):
        carry = step(index, carry)
    return carry


def split(x):
    high = x.astype(jnp.bfloat16)
    return (high, (x - high.astype(jnp.float32)).astype(jnp.bfloat16))


def one_hots(cell, first_layer, layers, rows, columns):
    count = cell.shape[1]
    layer = cell // (rows * columns)
    rest = cell - layer * (rows * columns)
    row = rest // columns
    column = rest - row * columns
    place = (layer - first_layer) * rows + row
    at_place = lax.broadcasted_iota(jnp.int32, (layers * rows, count), 0) == place
    at_column = lax.broadcasted_iota(jnp.int32, (columns, count), 0) == column
    return (at_place, at_column)


def gather(field, at_place, at_column):
    high, low = split(field)
    hot = at_column.astype(jnp.bfloat16)
    by_column = jnp.dot(high, hot, preferred_element_type=jnp.float32) + jnp.dot(
        low, hot, preferred_element_type=jnp.float32
    )
    return jnp.sum(jnp.where(at_place, by_column, 0.0), axis=0, keepdims=True)


def flatten(block, spread):
    perfs, wells = block.shape
    spread[...] = jnp.zeros(spread.shape, jnp.float32)
    spread[:, 0:wells] = block
    wide = spread[...]
    shift = wells
    while shift < LANES:
        wide = wide + roll(wide, shift, 1)
        shift *= 2
    each = LANES // wells
    entry = lax.broadcasted_iota(jnp.int32, (perfs, LANES), 0)
    group = lax.broadcasted_iota(jnp.int32, (perfs, LANES), 1) // wells
    tiles = [
        jnp.sum(jnp.where(entry == first + group, wide, 0.0), axis=0, keepdims=True)
        for first in range(0, perfs, each)
    ]
    return jnp.concatenate(tiles, axis=1)


def prepare_kernel(
    sat,
    hist,
    pressure,
    storage,
    trans,
    cell_in,
    index_in,
    control_in,
    target_in,
    p0e,
    tote,
    stor,
    t0,
    t1,
    t2,
    frac,
    up,
    down,
    sums,
    cell,
    wells,
    sat_v,
    hist_v,
    cell_v,
    index_v,
    control_v,
    target_v,
    spread,
    sems,
    *,
    gz,
):
    layers, rows, columns = pressure.shape
    ext = layers + 2 * H
    own = pl.ds(H, layers)
    copies = [
        pltpu.make_async_copy(a, b, sems.at[i])
        for i, (a, b) in enumerate(
            (
                (sat, sat_v),
                (hist, hist_v),
                (cell_in, cell_v),
                (index_in, index_v),
                (control_in, control_v),
                (target_in, target_v),
                (pressure, p0e.at[own]),
                (trans.at[0], t0.at[own]),
                (storage, stor.at[own]),
                (trans.at[1], t1.at[own]),
                (trans.at[2], t2.at[own]),
            )
        )
    ]
    for copy in copies:
        copy.start()
    for copy in copies[:2]:
        copy.wait()

    def layer_step(l, carry):
        t, f = mobility(sat_v[l], hist_v[l])
        tote[l + H] = t
        frac[l] = f
        return carry

    loop(0, layers, layer_step, 0)
    for copy in copies[2:7]:
        copy.wait()
    perfs, group = cell_v.shape
    cell[...] = flatten(cell_v[...].astype(jnp.float32), spread).astype(jnp.int32)
    wells[0:1, :] = flatten(index_v[...], spread)
    wells[1:2, :] = flatten(jnp.broadcast_to(target_v[...], (perfs, group)), spread)
    wells[2:3, :] = flatten(
        jnp.broadcast_to(control_v[...].astype(jnp.float32), (perfs, group)), spread
    )
    at_place, at_column = one_hots(
        cell[...], lax.axis_index(gz) * layers, layers, rows, columns
    )
    flat = (layers * rows, columns)
    weight = wells[0:1, :] * gather(tote[own].reshape(flat), at_place, at_column)
    cell_p = gather(p0e[own].reshape(flat), at_place, at_column)
    for i, value in enumerate((weight * cell_p, weight)):
        part = value[:, 0:LANES]
        for lane in range(LANES, value.shape[1], LANES):
            part = part + value[:, lane : lane + LANES]
        shift = LANES // 2
        while shift >= group:
            part = part + roll(part, shift, 1)
            shift //= 2
        sums[i : i + 1, :] = part
    for copy in copies[7:]:
        copy.wait()
    for message, edge in (
        (up, lambda n: pl.ds(H + layers - n, n)),
        (down, lambda n: pl.ds(H, n)),
    ):
        at = 0
        for ref, count in (
            (p0e, H),
            (tote, H),
            (t0, H),
            (stor, H - 1),
            (t1, H - 1),
            (t2, H - 1),
        ):
            message[pl.ds(at, count)] = ref[edge(count)]
            at += count
        message[at] = frac[layers - 1] if message is up else frac[0]
        message[at + 1] = jnp.zeros((rows, columns), jnp.float32)
        message[at + 1, 0:2, 0:LANES] = sums[...]


def build_kernel(
    p0_in,
    tot_in,
    stor_in,
    t0_in,
    t1_in,
    t2_in,
    frac,
    low,
    high,
    own_sums,
    *rest,
    gx,
    gz,
    far,
):
    fars = rest[:far]
    (
        cell,
        wells,
        p0e,
        tote,
        stor,
        t0,
        t1,
        t2,
        rhse,
        diage,
        f0e,
        f1e,
        f2e,
        source,
        up,
        down,
        p1,
        rhs1u,
        rhs1d,
        rhs2u,
        rhs2d,
        g2u,
        g2d,
        g3u,
        g3d,
    ) = rest[far:]
    layers, rows, columns = frac.shape
    ext = layers + 2 * H
    at = 0
    for target, count in ((p0e, H), (tote, H), (t0, H), (stor, H - 1), (t1, H - 1), (t2, H - 1)):
        target[pl.ds(H - count, count)] = low[pl.ds(at, count)]
        target[pl.ds(H + layers, count)] = high[pl.ds(at, count)]
        at += count
    sums = own_sums[...] + low[SUM_LAYER, 0:2, 0:LANES] + high[SUM_LAYER, 0:2, 0:LANES]
    for ref in fars:
        sums = sums + ref[...]
    top_z = lax.axis_index(gz) == lax.axis_size(gz) - 1
    top_x = lax.axis_index(gx) == lax.axis_size(gx) - 1
    t0[H + layers - 1] = jnp.where(top_z, 0.0, t0[H + layers - 1])

    inner = ext - 2
    at_place, at_column = one_hots(
        cell[...], lax.axis_index(gz) * layers - (H - 1), inner, rows, columns
    )
    flat = (inner * rows, columns)
    weight = wells[0:1, :] * gather(tote[1 : ext - 1].reshape(flat), at_place, at_column)
    cell_p = gather(p0e[1 : ext - 1].reshape(flat), at_place, at_column)
    count = weight.shape[1]
    repeat = lambda x: jnp.concatenate([x] * (count // LANES), axis=1)
    goal = wells[1:2, :]
    sum_w = repeat(sums[1:2, :])
    sum_w = jnp.where(sum_w > 0.0, sum_w, 1.0)
    hole = jnp.where(wells[2:3, :] == 0.0, (goal + repeat(sums[0:1, :])) / sum_w, goal)
    rate = weight * (hole - cell_p)
    hot = at_place.astype(jnp.bfloat16)
    spread = jnp.zeros(flat, jnp.float32)
    for piece in split(jnp.where(at_column, rate, 0.0)):
        spread = spread + lax.dot_general(
            hot, piece, (((1,), (1,)), ((), ())), preferred_element_type=jnp.float32
        )
    spread = spread.reshape(inner, rows, columns)
    rhse[1 : ext - 1] = spread
    source[...] = spread[H - 1 : H - 1 + layers]

    row = lax.broadcasted_iota(jnp.int32, (rows, columns), 0)
    column = lax.broadcasted_iota(jnp.int32, (rows, columns), 1)
    last_row = row == rows - 1
    last_column = column == columns - 1
    f0e[0] = t0[0] * 0.5 * (tote[0] + tote[1])

    def face_step(e, below):
        tot = tote[e]
        above = t0[e] * 0.5 * (tot + tote[e + 1])
        f0e[e] = above
        along = jnp.where(last_row, 0.0, t1[e]) * 0.5 * (tot + roll(tot, -1, 0))
        f1e[e] = jnp.where(last_row, jnp.where(top_x, 0.0, t1[e]), along)
        across = jnp.where(last_column, 0.0, t2[e]) * 0.5 * (tot + roll(tot, -1, 1))
        f2e[e] = across
        store = stor[e]
        diag = store + above + below + along + roll(along, 1, 0) + across + roll(across, 1, 1)
        diage[e] = diag
        p = p0e[e]
        rhs = store * p + rhse[e]
        rhse[e] = rhs
        lower = roll(along * p, 1, 0)
        upper = along * roll(p, -1, 0)
        rhs1u[e] = rhs + lower
        rhs1d[e] = rhs + upper
        new = rhs + lower + upper + above * p0e[e + 1] + below * p0e[e - 1]
        new = new + across * roll(p, -1, 1) + roll(across * p, 1, 1)
        p1[e] = jnp.where(diag > 0.0, new / diag, 0.0)
        return above

    loop(1, ext - 1, face_step, f0e[0])

    def second_step(e, carry):
        along = jnp.where(last_row, 0.0, f1e[e])
        across = f2e[e]
        p = p1[e]
        rhs = rhse[e]
        diag = diage[e]
        lower = roll(along * p, 1, 0)
        upper = along * roll(p, -1, 0)
        rhs2u[e] = rhs + lower
        rhs2d[e] = rhs + upper
        part = rhs + f0e[e] * p1[e + 1] + f0e[e - 1] * p1[e - 1]
        part = part + across * roll(p, -1, 1) + roll(across * p, 1, 1)
        g2u[e] = part + lower
        g2d[e] = part + upper
        p2 = jnp.where(diag > 0.0, (part + lower + upper) / diag, 0.0)
        g3u[e] = rhs + roll(along * p2, 1, 0)
        g3d[e] = rhs + along * roll(p2, -1, 0)
        return carry

    rhs2u[1] = rhse[1]
    rhs2d[1] = rhse[1]
    rhs2u[ext - 2] = rhse[ext - 2]
    rhs2d[ext - 2] = rhse[ext - 2]
    loop(2, ext - 2, second_step, 0)

    wide = ext - 2
    narrow = layers + 2

    for message, d1, d2, r1, r2, g2, g3, inside in (
        (up, rows - 1, rows - 2, rhs1u, rhs2u, g2u, g3u, rows - 2),
        (down, 0, 1, rhs1d, rhs2d, g2d, g3d, 0),
    ):
        for slot, ref in (
            (T1, t1),
            (TOT, tote),
            (P0, p0e),
            (DIAG, diage),
            (RHS1, r1),
            (RHS2, r2),
            (F0, f0e),
            (F2, f2e),
        ):
            message[0:wide, slot : slot + 1, :] = ref[1 : 1 + wide, d1 : d1 + 1, :]
        for slot, ref, index in (
            (RHS3, rhse, d1),
            (F1, f1e, inside),
            (G2, g2, d2),
            (G3, g3, d2),
            (F0_2, f0e, d2),
            (F2_2, f2e, d2),
            (DIAG_2, diage, d2),
        ):
            message[wide : wide + narrow, slot : slot + 1, :] = ref[
                H - 1 : H - 1 + narrow, index : index + 1, :
            ]
        for l in (0, narrow - 1):
            message[wide + l, FRAC : FRAC + 1] = jnp.zeros((1, columns), jnp.float32)
        message[wide + 1 : wide + 1 + layers, FRAC : FRAC + 1, :] = frac[:, d1 : d1 + 1, :]


def finish_kernel(
    sat,
    hist,
    volume,
    storage,
    frac,
    source,
    p0e,
    tote,
    rhse,
    diage,
    f0e,
    f1e,
    f2e,
    zlow,
    zhigh,
    xlow,
    xhigh,
    new_p,
    residual,
    new_sat,
    new_hist,
    pa,
    pb,
    f1,
    rdiag,
    sf0,
    sf1,
    sf2,
    stot,
    sdiag,
    sp0,
    srhs1,
    srhs2,
    srhs3,
    sfrac,
    fracs,
):
    layers, rows, columns = sat.shape
    ext = layers + 2 * H
    wide = ext - 2
    narrow = layers + 2

    def fill(seam, entries):
        seam[...] = jnp.zeros(seam.shape, jnp.float32)
        for side, slot, place, is_wide in entries:
            first, number, offset = (1, wide, 0) if is_wide else (H - 1, narrow, wide)
            seam[first : first + number, place : place + 1, :] = side[
                offset : offset + number, slot : slot + 1, :
            ]

    def pair(slot):
        return [(xhigh, slot, 0, True), (xlow, slot, 7, True)]

    def inner(slot):
        return [(xhigh, slot, 1, False), (xlow, slot, 6, False)]

    fill(sf0, pair(F0) + inner(F0_2))
    fill(sf2, pair(F2) + inner(F2_2))
    fill(stot, pair(TOT))
    fill(sdiag, pair(DIAG) + inner(DIAG_2))
    fill(sp0, pair(P0))
    fill(srhs1, pair(RHS1))
    fill(srhs2, pair(RHS2) + inner(G2))
    fill(
        srhs3,
        [(xhigh, RHS3, 0, False), (xlow, RHS3, 7, False)] + inner(G3),
    )
    fill(sfrac, [(xhigh, FRAC, 0, False), (xlow, FRAC, 7, False)])
    fill(sf1, [(xhigh, F1, 0, False), (xlow, F1, 6, False), (xlow, T1, 7, True)])

    full = rows + 8
    row = lax.broadcasted_iota(jnp.int32, (full, columns), 0)
    edge = (row == rows - 1) | (row == full - 1)
    beyond = (row == rows + 1) | (row == full - 2)
    join = lambda a, b: jnp.concatenate([a, b], axis=0)

    pa[0] = join(p0e[0], sp0[0])
    pa[ext - 1] = join(p0e[ext - 1], sp0[ext - 1])

    def face_step(e, carry):
        tot = join(tote[e], stot[e])
        mixed = join(f1e[e], sf1[e])
        border = jnp.where(edge, mixed * 0.5 * (tot + roll(tot, -1, 0)), 0.0)
        f1[e] = jnp.where(edge, border, mixed)
        diag = join(diage[e], sdiag[e]) + border + roll(border, 1, 0)
        rdiag[e] = jnp.where(diag > 0.0, 1.0 / diag, 0.0)
        pa[e] = join(p0e[e], sp0[e])
        return carry

    loop(1, ext - 1, face_step, 0)

    def sweep(number, old, new, srhs):
        def step(e, below):
            p = old[e]
            above = old[e + 1]
            face = join(f0e[e], sf0[e])
            x = f1[e]
            y = join(f2e[e], sf2[e])
            total = join(rhse[e], srhs[e]) + below + face * above
            total = total + x * roll(p, -1, 0) + roll(x * p, 1, 0)
            total = total + y * roll(p, -1, 1) + roll(y * p, 1, 1)
            value = total * rdiag[e]
            if number == 1:
                value = jnp.where(beyond, 0.0, value)
            new[e] = value
            return face * p

        first = join(f0e[number - 1], sf0[number - 1]) * old[number - 1]
        loop(number, ext - number, step, first)

    fields = (pa, pb)
    for number in range(1, SWEEPS + 1):
        sweep(
            number,
            fields[(number - 1) % 2],
            fields[number % 2],
            {1: srhs1, 2: srhs2}.get(number, srhs3),
        )
    field = fields[SWEEPS % 2]

    fracs[0] = zlow[FRAC_LAYER]
    fracs[pl.ds(1, layers)] = frac[...]
    fracs[layers + 1] = zhigh[FRAC_LAYER]

    def flow(face, p, p_next, f, f_next):
        water = face * (p - p_next)
        return (water, water * jnp.where(water > 0, f, f_next))

    def last_step(l, carry):
        below_w, below_g = carry
        e = l + H
        p = field[e]
        f = join(fracs[l + 1], sfrac[e])
        own_p = p[:rows]
        own_f = f[:rows]
        above_w, above_g = flow(f0e[e], own_p, field[e + 1][:rows], own_f, fracs[l + 2])
        xw, xg = flow(f1[e], p, roll(p, -1, 0), f, roll(f, -1, 0))
        yw, yg = flow(f2e[e], own_p, roll(own_p, -1, 1), own_f, roll(own_f, -1, 1))
        water = above_w - below_w + (xw - roll(xw, 1, 0))[:rows] + yw - roll(yw, 1, 1)
        out = above_g - below_g + (xg - roll(xg, 1, 0))[:rows] + yg - roll(yg, 1, 1)
        new_p[l] = own_p
        residual[l] = rhse[e] - storage[l] * own_p - water
        src = source[l]
        gas = jnp.maximum(src, 0.0) + jnp.minimum(src, 0.0) * own_f
        s = sat[l] + volume[l] * (gas - out)
        new_sat[l] = s
        new_hist[l] = jnp.maximum(hist[l], s)
        return (above_w, above_g)

    first = flow(f0e[H - 1], field[H - 1][:rows], field[H][:rows], fracs[0], fracs[1])
    loop(0, layers, last_step, first)


def shift(block, axis, up):
    count = lax.axis_size(axis)
    pairs = [(i, i + 1) if up else (i + 1, i) for i in range(count - 1)]
    return lax.ppermute(block, axis, pairs)


VMEM = pl.BlockSpec(memory_space=pltpu.VMEM)
HBM = pl.BlockSpec(memory_space=pltpu.HBM)


def call(kernel, outs, scratch, *args, space=VMEM, sems=0, aliases={}):
    as_struct = lambda s: s if hasattr(s, "dtype") else jax.ShapeDtypeStruct(s, jnp.float32)
    as_scratch = lambda s: pltpu.VMEM(as_struct(s).shape, as_struct(s).dtype)
    return pl.pallas_call(
        kernel,
        out_shape=[as_struct(s) for s in outs],
        in_specs=[space] * len(args),
        out_specs=[VMEM] * len(outs),
        scratch_shapes=[as_scratch(s) for s in scratch]
        + ([pltpu.SemaphoreType.DMA((sems,))] if sems else []),
        input_output_aliases=aliases,
        compiler_params=pltpu.CompilerParams(vmem_limit_bytes=40 * 1024 * 1024),
    )(*args)


def body(
    pressure,
    saturation,
    sat_history,
    storage,
    step_volume,
    transmiss,
    perf_cell,
    perf_index,
    control,
    target,
):
    layers, rows, columns = pressure.shape
    ext = layers + 2 * H
    wells, perfs = perf_cell.shape
    block = (layers, rows, columns)
    ext_block = (ext, rows, columns)
    z_message = (Z_LAYERS, rows, columns)
    x_message = (ext - 2 + layers + 2, 8, columns)
    seam = (ext, 8, columns)
    ints = lambda *shape: jax.ShapeDtypeStruct(shape, jnp.int32)
    *fields, frac, z_up, z_down, part, cell, per_perf = call(
        functools.partial(prepare_kernel, gz="gz"),
        [ext_block] * 6
        + [block, z_message, z_message, (2, LANES), ints(1, wells * perfs), (3, wells * perfs)],
        [
            block,
            block,
            ints(perfs, wells),
            (perfs, wells),
            ints(1, wells),
            (1, wells),
            (perfs, LANES),
        ],
        saturation,
        sat_history,
        pressure,
        storage,
        transmiss,
        perf_cell.T,
        perf_index.T,
        control.reshape(1, wells),
        target.reshape(1, wells),
        space=HBM,
        sems=11,
    )
    z_low = shift(z_up, "gz", True)
    z_high = shift(z_down, "gz", False)
    count = lax.axis_size("gz")
    far = [
        lax.ppermute(part, "gz", [(i, (i + step) % count) for i in range(count)])
        for step in sorted({2 % count, -2 % count} - {0, 1, count - 1})
    ]
    p0e, tote, _, _, _, _, rhse, diage, f0e, f1e, f2e, source, x_up, x_down = call(
        functools.partial(build_kernel, gx="gx", gz="gz", far=len(far)),
        [ext_block] * 11 + [block, x_message, x_message],
        [ext_block] * 9,
        *fields,
        frac,
        z_low,
        z_high,
        part,
        *far,
        cell,
        per_perf,
        aliases={i: i for i in range(6)},
    )
    x_low = shift(x_up, "gx", True)
    x_high = shift(x_down, "gx", False)
    part, x_up = lax.optimization_barrier((part, x_up))
    sum_p, sum_w = lax.psum(part, "gz")[:, :wells]
    bottom_hole = jnp.where(control == 0, (target + sum_p) / sum_w, target)
    field, residual, new_sat, new_hist = call(
        finish_kernel,
        [block] * 4,
        [(ext, rows + 8, columns)] * 4 + [seam] * 10 + [(layers + 2, rows, columns)],
        saturation,
        sat_history,
        step_volume,
        storage,
        frac,
        source,
        p0e,
        tote,
        rhse,
        diage,
        f0e,
        f1e,
        f2e,
        z_low,
        z_high,
        x_low,
        x_high,
    )
    return (field, residual, new_sat, new_hist, bottom_hole)


def solution(mesh):
    return jax.shard_map(
        body,
        mesh=mesh,
        in_specs=(
            P("gz", "gx", None),
            P("gz", "gx", None),
            P("gz", "gx", None),
            P("gz", "gx", None),
            P("gz", "gx", None),
            P(None, "gz", "gx", None),
            P("gx", None),
            P("gx", None),
            P("gx"),
            P("gx"),
        ),
        out_specs=(
            P("gz", "gx", None),
            P("gz", "gx", None),
            P("gz", "gx", None),
            P("gz", "gx", None),
            P("gx"),
        ),
        check_vma=False,
    )
```

```python
import functools

import jax
import jax.numpy as jnp
from jax import lax
from jax.experimental import pallas as pl
from jax.experimental.pallas import tpu as pltpu
from jax.sharding import PartitionSpec as P

SWEEPS = 4
H = SWEEPS + 1
LANES = 128

FRAC_LAYER = 3 * H + 3 * (H - 1)
SUM_LAYER = FRAC_LAYER + 1
Z_LAYERS = SUM_LAYER + 1

T1, TOT, P0, DIAG, RHS1, RHS2, F0, F2 = range(8)
RHS3, F1, FRAC, G2, G3, F0_2, F2_2, DIAG_2 = range(8)


def mobility(sat, history):
    trapped = history / (1.0 + 1.5 * history)
    excess = jnp.maximum(sat - trapped, 0.0)
    free_gas = 0.5 * (excess + jnp.sqrt(excess * excess + excess / 0.375))
    relperm = jnp.where(sat < history, free_gas * free_gas, sat * sat)
    gas = relperm / 0.5
    total = (1.0 - sat) * (1.0 - sat) + gas
    return (total, gas / total)


def roll(x, shift, axis):
    return pltpu.roll(x, shift % x.shape[axis], axis)


def loop(first, last, step, carry, unroll=4):
    groups = (last - first) // unroll

    def group(g, carry):
        for i in range(unroll):
            carry = step(first + g * unroll + i, carry)
        return carry

    carry = lax.fori_loop(0, groups, group, carry)
    for index in range(first + groups * unroll, last):
        carry = step(index, carry)
    return carry


def split(x):
    high = x.astype(jnp.bfloat16)
    return (high, (x - high.astype(jnp.float32)).astype(jnp.bfloat16))


def one_hots(cell, first_layer, layers, rows, columns):
    count = cell.shape[1]
    layer = cell // (rows * columns)
    rest = cell - layer * (rows * columns)
    row = rest // columns
    column = rest - row * columns
    place = (layer - first_layer) * rows + row
    at_place = lax.broadcasted_iota(jnp.int32, (layers * rows, count), 0) == place
    at_column = lax.broadcasted_iota(jnp.int32, (columns, count), 0) == column
    return (at_place, at_column)


def gather(field, at_place, at_column):
    high, low = split(field)
    hot = at_column.astype(jnp.bfloat16)
    by_column = jnp.dot(high, hot, preferred_element_type=jnp.float32) + jnp.dot(
        low, hot, preferred_element_type=jnp.float32
    )
    return jnp.sum(jnp.where(at_place, by_column, 0.0), axis=0, keepdims=True)


def flatten(block, spread):
    perfs, wells = block.shape
    spread[...] = jnp.zeros(spread.shape, jnp.float32)
    spread[:, 0:wells] = block
    wide = spread[...]
    shift = wells
    while shift < LANES:
        wide = wide + roll(wide, shift, 1)
        shift *= 2
    each = LANES // wells
    entry = lax.broadcasted_iota(jnp.int32, (perfs, LANES), 0)
    group = lax.broadcasted_iota(jnp.int32, (perfs, LANES), 1) // wells
    tiles = [
        jnp.sum(jnp.where(entry == first + group, wide, 0.0), axis=0, keepdims=True)
        for first in range(0, perfs, each)
    ]
    return jnp.concatenate(tiles, axis=1)


def prepare_kernel(
    sat,
    hist,
    pressure,
    storage,
    trans,
    cell_in,
    index_in,
    control_in,
    target_in,
    p0e,
    tote,
    stor,
    t0,
    t1,
    t2,
    frac,
    near,
    cross,
    sums,
    cell,
    wells,
    sat_v,
    hist_v,
    cell_v,
    index_v,
    control_v,
    target_v,
    spread,
    sems,
    *,
    gz,
):
    layers, rows, columns = pressure.shape
    ext = layers + 2 * H
    own = pl.ds(H, layers)
    copies = [
        pltpu.make_async_copy(a, b, sems.at[i])
        for i, (a, b) in enumerate(
            (
                (sat, sat_v),
                (hist, hist_v),
                (cell_in, cell_v),
                (index_in, index_v),
                (control_in, control_v),
                (target_in, target_v),
                (pressure, p0e.at[own]),
                (trans.at[0], t0.at[own]),
                (storage, stor.at[own]),
                (trans.at[1], t1.at[own]),
                (trans.at[2], t2.at[own]),
            )
        )
    ]
    for copy in copies:
        copy.start()
    for copy in copies[:2]:
        copy.wait()

    def layer_step(l, carry):
        t, f = mobility(sat_v[l], hist_v[l])
        tote[l + H] = t
        frac[l] = f
        return carry

    loop(0, layers, layer_step, 0)
    for copy in copies[2:7]:
        copy.wait()
    perfs, group = cell_v.shape
    cell[...] = flatten(cell_v[...].astype(jnp.float32), spread).astype(jnp.int32)
    wells[0:1, :] = flatten(index_v[...], spread)
    wells[1:2, :] = flatten(jnp.broadcast_to(target_v[...], (perfs, group)), spread)
    wells[2:3, :] = flatten(
        jnp.broadcast_to(control_v[...].astype(jnp.float32), (perfs, group)), spread
    )
    at_place, at_column = one_hots(
        cell[...], lax.axis_index(gz) * layers, layers, rows, columns
    )
    flat = (layers * rows, columns)
    weight = wells[0:1, :] * gather(tote[own].reshape(flat), at_place, at_column)
    cell_p = gather(p0e[own].reshape(flat), at_place, at_column)
    for i, value in enumerate((weight * cell_p, weight)):
        part = value[:, 0:LANES]
        for lane in range(LANES, value.shape[1], LANES):
            part = part + value[:, lane : lane + LANES]
        shift = LANES // 2
        while shift >= group:
            part = part + roll(part, shift, 1)
            shift //= 2
        sums[i : i + 1, :] = part
    for copy in copies[7:]:
        copy.wait()
    even = lax.axis_index(gz) % 2 == 0
    for message, is_top in ((near, even), (cross, jnp.logical_not(even))):
        at = 0
        for ref, count in (
            (p0e, H),
            (tote, H),
            (t0, H),
            (stor, H - 1),
            (t1, H - 1),
            (t2, H - 1),
        ):
            edge = jnp.where(is_top, H + layers - count, H)
            message[pl.ds(at, count)] = ref[pl.ds(edge, count)]
            at += count
        message[at] = frac[jnp.where(is_top, layers - 1, 0)]
        message[at + 1] = jnp.zeros((rows, columns), jnp.float32)
        message[at + 1, 0:2, 0:LANES] = sums[...]


def build_kernel(
    p0_in,
    tot_in,
    stor_in,
    t0_in,
    t1_in,
    t2_in,
    frac,
    near,
    cross,
    own_sums,
    *rest,
    gx,
    gz,
    far,
):
    fars = rest[:far]
    (
        cell,
        wells,
        p0e,
        tote,
        stor,
        t0,
        t1,
        t2,
        rhse,
        diage,
        f0e,
        f1e,
        f2e,
        source,
        fracs,
        up,
        down,
        p1,
        rhs1u,
        rhs1d,
        rhs2u,
        rhs2d,
        g2u,
        g2d,
        g3u,
        g3d,
    ) = rest[far:]
    layers, rows, columns = frac.shape
    ext = layers + 2 * H
    even = lax.axis_index(gz) % 2 == 0
    at = 0
    for target, count in ((p0e, H), (tote, H), (t0, H), (stor, H - 1), (t1, H - 1), (t2, H - 1)):
        one, two = (near[pl.ds(at, count)], cross[pl.ds(at, count)])
        target[pl.ds(H - count, count)] = jnp.where(even, two, one)
        target[pl.ds(H + layers, count)] = jnp.where(even, one, two)
        at += count
    fracs[0] = jnp.where(even, cross[at], near[at])
    fracs[pl.ds(1, layers)] = frac[...]
    fracs[layers + 1] = jnp.where(even, near[at], cross[at])
    sums = own_sums[...] + near[SUM_LAYER, 0:2, 0:LANES] + cross[SUM_LAYER, 0:2, 0:LANES]
    for ref in fars:
        sums = sums + ref[...]
    top_z = lax.axis_index(gz) == lax.axis_size(gz) - 1
    top_x = lax.axis_index(gx) == lax.axis_size(gx) - 1
    t0[H + layers - 1] = jnp.where(top_z, 0.0, t0[H + layers - 1])

    inner = ext - 2
    at_place, at_column = one_hots(
        cell[...], lax.axis_index(gz) * layers - (H - 1), inner, rows, columns
    )
    flat = (inner * rows, columns)
    weight = wells[0:1, :] * gather(tote[1 : ext - 1].reshape(flat), at_place, at_column)
    cell_p = gather(p0e[1 : ext - 1].reshape(flat), at_place, at_column)
    count = weight.shape[1]
    repeat = lambda x: jnp.concatenate([x] * (count // LANES), axis=1)
    goal = wells[1:2, :]
    sum_w = repeat(sums[1:2, :])
    sum_w = jnp.where(sum_w > 0.0, sum_w, 1.0)
    hole = jnp.where(wells[2:3, :] == 0.0, (goal + repeat(sums[0:1, :])) / sum_w, goal)
    rate = weight * (hole - cell_p)
    hot = at_place.astype(jnp.bfloat16)
    spread = jnp.zeros(flat, jnp.float32)
    for piece in split(jnp.where(at_column, rate, 0.0)):
        spread = spread + lax.dot_general(
            hot, piece, (((1,), (1,)), ((), ())), preferred_element_type=jnp.float32
        )
    spread = spread.reshape(inner, rows, columns)
    rhse[1 : ext - 1] = spread
    source[...] = spread[H - 1 : H - 1 + layers]

    row = lax.broadcasted_iota(jnp.int32, (rows, columns), 0)
    column = lax.broadcasted_iota(jnp.int32, (rows, columns), 1)
    last_row = row == rows - 1
    last_column = column == columns - 1
    f0e[0] = t0[0] * 0.5 * (tote[0] + tote[1])

    def face_step(e, below):
        tot = tote[e]
        above = t0[e] * 0.5 * (tot + tote[e + 1])
        f0e[e] = above
        along = jnp.where(last_row, 0.0, t1[e]) * 0.5 * (tot + roll(tot, -1, 0))
        f1e[e] = jnp.where(last_row, jnp.where(top_x, 0.0, t1[e]), along)
        across = jnp.where(last_column, 0.0, t2[e]) * 0.5 * (tot + roll(tot, -1, 1))
        f2e[e] = across
        store = stor[e]
        diag = store + above + below + along + roll(along, 1, 0) + across + roll(across, 1, 1)
        diage[e] = diag
        p = p0e[e]
        rhs = store * p + rhse[e]
        rhse[e] = rhs
        lower = roll(along * p, 1, 0)
        upper = along * roll(p, -1, 0)
        rhs1u[e] = rhs + lower
        rhs1d[e] = rhs + upper
        new = rhs + lower + upper + above * p0e[e + 1] + below * p0e[e - 1]
        new = new + across * roll(p, -1, 1) + roll(across * p, 1, 1)
        p1[e] = jnp.where(diag > 0.0, new / diag, 0.0)
        return above

    loop(1, ext - 1, face_step, f0e[0])

    def second_step(e, carry):
        along = jnp.where(last_row, 0.0, f1e[e])
        across = f2e[e]
        p = p1[e]
        rhs = rhse[e]
        diag = diage[e]
        lower = roll(along * p, 1, 0)
        upper = along * roll(p, -1, 0)
        rhs2u[e] = rhs + lower
        rhs2d[e] = rhs + upper
        part = rhs + f0e[e] * p1[e + 1] + f0e[e - 1] * p1[e - 1]
        part = part + across * roll(p, -1, 1) + roll(across * p, 1, 1)
        g2u[e] = part + lower
        g2d[e] = part + upper
        p2 = jnp.where(diag > 0.0, (part + lower + upper) / diag, 0.0)
        g3u[e] = rhs + roll(along * p2, 1, 0)
        g3d[e] = rhs + along * roll(p2, -1, 0)
        return carry

    rhs2u[1] = rhse[1]
    rhs2d[1] = rhse[1]
    rhs2u[ext - 2] = rhse[ext - 2]
    rhs2d[ext - 2] = rhse[ext - 2]
    loop(2, ext - 2, second_step, 0)

    wide = ext - 2
    narrow = layers + 2

    for message, d1, d2, r1, r2, g2, g3, inside in (
        (up, rows - 1, rows - 2, rhs1u, rhs2u, g2u, g3u, rows - 2),
        (down, 0, 1, rhs1d, rhs2d, g2d, g3d, 0),
    ):
        for slot, ref in (
            (T1, t1),
            (TOT, tote),
            (P0, p0e),
            (DIAG, diage),
            (RHS1, r1),
            (RHS2, r2),
            (F0, f0e),
            (F2, f2e),
        ):
            message[0:wide, slot : slot + 1, :] = ref[1 : 1 + wide, d1 : d1 + 1, :]
        for slot, ref, index in (
            (RHS3, rhse, d1),
            (F1, f1e, inside),
            (G2, g2, d2),
            (G3, g3, d2),
            (F0_2, f0e, d2),
            (F2_2, f2e, d2),
            (DIAG_2, diage, d2),
        ):
            message[wide : wide + narrow, slot : slot + 1, :] = ref[
                H - 1 : H - 1 + narrow, index : index + 1, :
            ]
        for l in (0, narrow - 1):
            message[wide + l, FRAC : FRAC + 1] = jnp.zeros((1, columns), jnp.float32)
        message[wide + 1 : wide + 1 + layers, FRAC : FRAC + 1, :] = frac[:, d1 : d1 + 1, :]


def finish_kernel(
    sat,
    hist,
    volume,
    storage,
    fracs,
    source,
    p0e,
    tote,
    rhse,
    diage,
    f0e,
    f1e,
    f2e,
    xlow,
    xhigh,
    new_p,
    residual,
    new_sat,
    new_hist,
    pa,
    pb,
    f1,
    rdiag,
    sf0,
    sf1,
    sf2,
    stot,
    sdiag,
    sp0,
    srhs1,
    srhs2,
    srhs3,
    sfrac,
):
    layers, rows, columns = sat.shape
    ext = layers + 2 * H
    wide = ext - 2
    narrow = layers + 2

    def fill(seam, entries):
        seam[...] = jnp.zeros(seam.shape, jnp.float32)
        for side, slot, place, is_wide in entries:
            first, number, offset = (1, wide, 0) if is_wide else (H - 1, narrow, wide)
            seam[first : first + number, place : place + 1, :] = side[
                offset : offset + number, slot : slot + 1, :
            ]

    def pair(slot):
        return [(xhigh, slot, 0, True), (xlow, slot, 7, True)]

    def inner(slot):
        return [(xhigh, slot, 1, False), (xlow, slot, 6, False)]

    fill(sf0, pair(F0) + inner(F0_2))
    fill(sf2, pair(F2) + inner(F2_2))
    fill(stot, pair(TOT))
    fill(sdiag, pair(DIAG) + inner(DIAG_2))
    fill(sp0, pair(P0))
    fill(srhs1, pair(RHS1))
    fill(srhs2, pair(RHS2) + inner(G2))
    fill(
        srhs3,
        [(xhigh, RHS3, 0, False), (xlow, RHS3, 7, False)] + inner(G3),
    )
    fill(sfrac, [(xhigh, FRAC, 0, False), (xlow, FRAC, 7, False)])
    fill(sf1, [(xhigh, F1, 0, False), (xlow, F1, 6, False), (xlow, T1, 7, True)])

    full = rows + 8
    row = lax.broadcasted_iota(jnp.int32, (full, columns), 0)
    edge = (row == rows - 1) | (row == full - 1)
    beyond = (row == rows + 1) | (row == full - 2)
    join = lambda a, b: jnp.concatenate([a, b], axis=0)

    pa[0] = join(p0e[0], sp0[0])
    pa[ext - 1] = join(p0e[ext - 1], sp0[ext - 1])

    def face_step(e, carry):
        tot = join(tote[e], stot[e])
        mixed = join(f1e[e], sf1[e])
        border = jnp.where(edge, mixed * 0.5 * (tot + roll(tot, -1, 0)), 0.0)
        f1[e] = jnp.where(edge, border, mixed)
        diag = join(diage[e], sdiag[e]) + border + roll(border, 1, 0)
        rdiag[e] = jnp.where(diag > 0.0, 1.0 / diag, 0.0)
        pa[e] = join(p0e[e], sp0[e])
        return carry

    loop(1, ext - 1, face_step, 0)

    def sweep(number, old, new, srhs):
        def step(e, below):
            p = old[e]
            above = old[e + 1]
            face = join(f0e[e], sf0[e])
            x = f1[e]
            y = join(f2e[e], sf2[e])
            total = join(rhse[e], srhs[e]) + below + face * above
            total = total + x * roll(p, -1, 0) + roll(x * p, 1, 0)
            total = total + y * roll(p, -1, 1) + roll(y * p, 1, 1)
            value = total * rdiag[e]
            if number == 1:
                value = jnp.where(beyond, 0.0, value)
            new[e] = value
            return face * p

        first = join(f0e[number - 1], sf0[number - 1]) * old[number - 1]
        loop(number, ext - number, step, first)

    fields = (pa, pb)
    for number in range(1, SWEEPS + 1):
        sweep(
            number,
            fields[(number - 1) % 2],
            fields[number % 2],
            {1: srhs1, 2: srhs2}.get(number, srhs3),
        )
    field = fields[SWEEPS % 2]

    def flow(face, p, p_next, f, f_next):
        water = face * (p - p_next)
        return (water, water * jnp.where(water > 0, f, f_next))

    def last_step(l, carry):
        below_w, below_g = carry
        e = l + H
        p = field[e]
        f = join(fracs[l + 1], sfrac[e])
        own_p = p[:rows]
        own_f = f[:rows]
        above_w, above_g = flow(f0e[e], own_p, field[e + 1][:rows], own_f, fracs[l + 2])
        xw, xg = flow(f1[e], p, roll(p, -1, 0), f, roll(f, -1, 0))
        yw, yg = flow(f2e[e], own_p, roll(own_p, -1, 1), own_f, roll(own_f, -1, 1))
        water = above_w - below_w + (xw - roll(xw, 1, 0))[:rows] + yw - roll(yw, 1, 1)
        out = above_g - below_g + (xg - roll(xg, 1, 0))[:rows] + yg - roll(yg, 1, 1)
        new_p[l] = own_p
        residual[l] = rhse[e] - storage[l] * own_p - water
        src = source[l]
        gas = jnp.maximum(src, 0.0) + jnp.minimum(src, 0.0) * own_f
        s = sat[l] + volume[l] * (gas - out)
        new_sat[l] = s
        new_hist[l] = jnp.maximum(hist[l], s)
        return (above_w, above_g)

    first = flow(f0e[H - 1], field[H - 1][:rows], field[H][:rows], fracs[0], fracs[1])
    loop(0, layers, last_step, first)


def shift(block, axis, up):
    count = lax.axis_size(axis)
    pairs = [(i, i + 1) if up else (i + 1, i) for i in range(count - 1)]
    return lax.ppermute(block, axis, pairs)


def swap(block, axis, first):
    pairs = [(i, i + 1) for i in range(first, lax.axis_size(axis) - 1, 2)]
    return lax.ppermute(block, axis, pairs + [(b, a) for a, b in pairs])


def pin(*shape, dtype=jnp.float32):
    return pltpu.VMEM(shape, dtype)


VMEM = pl.BlockSpec(memory_space=pltpu.VMEM)
HBM = pl.BlockSpec(memory_space=pltpu.HBM)


def call(kernel, outs, scratch, *args, space=VMEM, sems=0, aliases={}):
    as_struct = lambda s: s if hasattr(s, "dtype") else jax.ShapeDtypeStruct(s, jnp.float32)
    as_scratch = lambda s: pltpu.VMEM(as_struct(s).shape, as_struct(s).dtype)
    return pl.pallas_call(
        kernel,
        out_shape=[as_struct(s) for s in outs],
        in_specs=[space] * len(args),
        out_specs=[VMEM] * len(outs),
        scratch_shapes=[as_scratch(s) for s in scratch]
        + ([pltpu.SemaphoreType.DMA((sems,))] if sems else []),
        input_output_aliases=aliases,
        compiler_params=pltpu.CompilerParams(vmem_limit_bytes=24 * 1024 * 1024),
    )(*(pltpu.with_memory_space_constraint(a, pltpu.HBM) if space is HBM else a for a in args))


def body(
    pressure,
    saturation,
    sat_history,
    storage,
    step_volume,
    transmiss,
    perf_cell,
    perf_index,
    control,
    target,
):
    layers, rows, columns = pressure.shape
    ext = layers + 2 * H
    wells, perfs = perf_cell.shape
    block = (layers, rows, columns)
    pinned = pin(*block)
    ext_block = pin(ext, rows, columns)
    z_message = (Z_LAYERS, rows, columns)
    x_message = (ext - 2 + layers + 2, 8, columns)
    inner_block = pin(layers + 2, rows, columns)
    seam = (ext, 8, columns)
    ints = lambda *shape: jax.ShapeDtypeStruct(shape, jnp.int32)
    *fields, frac, z_near, z_cross, part, cell, per_perf = call(
        functools.partial(prepare_kernel, gz="gz"),
        [ext_block] * 6
        + [
            pinned,
            z_message,
            z_message,
            (2, LANES),
            pin(1, wells * perfs, dtype=jnp.int32),
            pin(3, wells * perfs),
        ],
        [
            block,
            block,
            ints(perfs, wells),
            (perfs, wells),
            ints(1, wells),
            (1, wells),
            (perfs, LANES),
        ],
        saturation,
        sat_history,
        pressure,
        storage,
        transmiss,
        perf_cell.T,
        perf_index.T,
        control.reshape(1, wells),
        target.reshape(1, wells),
        space=HBM,
        sems=11,
    )
    z_cross = swap(z_cross, "gz", 1)
    z_near = swap(z_near, "gz", 0)
    count = lax.axis_size("gz")
    far = [
        lax.ppermute(part, "gz", [(i, (i + step) % count) for i in range(count)])
        for step in sorted({2 % count, -2 % count} - {0, 1, count - 1})
    ]
    p0e, tote, _, _, _, _, rhse, diage, f0e, f1e, f2e, source, fracs, x_up, x_down = call(
        functools.partial(build_kernel, gx="gx", gz="gz", far=len(far)),
        [ext_block] * 11 + [pinned, inner_block, x_message, x_message],
        [ext_block] * 9,
        *fields,
        frac,
        z_near,
        z_cross,
        part,
        *far,
        cell,
        per_perf,
        aliases={i: i for i in range(6)},
    )
    x_low = shift(x_up, "gx", True)
    x_high = shift(x_down, "gx", False)
    part, x_up = lax.optimization_barrier((part, x_up))
    sum_p, sum_w = lax.psum(part, "gz")[:, :wells]
    bottom_hole = jnp.where(control == 0, (target + sum_p) / sum_w, target)
    field, residual, new_sat, new_hist = call(
        finish_kernel,
        [block] * 4,
        [(ext, rows + 8, columns)] * 4 + [seam] * 10,
        saturation,
        sat_history,
        step_volume,
        storage,
        fracs,
        source,
        p0e,
        tote,
        rhse,
        diage,
        f0e,
        f1e,
        f2e,
        x_low,
        x_high,
    )
    return (field, residual, new_sat, new_hist, bottom_hole)


def solution(mesh):
    return jax.shard_map(
        body,
        mesh=mesh,
        in_specs=(
            P("gz", "gx", None),
            P("gz", "gx", None),
            P("gz", "gx", None),
            P("gz", "gx", None),
            P("gz", "gx", None),
            P(None, "gz", "gx", None),
            P("gx", None),
            P("gx", None),
            P("gx"),
            P("gx"),
        ),
        out_specs=(
            P("gz", "gx", None),
            P("gz", "gx", None),
            P("gz", "gx", None),
            P("gz", "gx", None),
            P("gx"),
        ),
        check_vma=False,
    )
```

```python
import functools

import jax
import jax.numpy as jnp
from jax import lax
from jax.experimental import pallas as pl
from jax.experimental.pallas import tpu as pltpu
from jax.sharding import PartitionSpec as P

SWEEPS = 4
H = SWEEPS + 1
LANES = 128

Z_PIECES = (
    (("p0", H), ("tot", H), ("t0", H)),
    (("stor", H - 1), ("t1", H - 1), ("t2", H - 1), ("frac", 1), ("sums", 1)),
)


def z_layers(piece):
    return sum(count for _, count in piece)


def early_parts(layers):
    own = (H, layers)
    inner = (H, layers - 1)
    return (
        ("t1", *own),
        ("tot", *own),
        ("p0", *own),
        ("dp", *own),
        ("f0", *inner),
        ("f2", *own),
        ("f1", *own),
        ("frac", *own),
        ("f0_d2", *inner),
        ("f2_d2", *own),
        ("dp_d2", *own),
    )


def late_parts(layers):
    top = H + layers
    both = lambda name, n: ((name, H - n, n), (name, top, n))
    faces = lambda name, n: ((name, H - n, n), (name, top - 1, n))
    return (
        ("rhs1", 2, layers + 6),
        ("rhs2", 3, layers + 4),
        ("rhs3", 4, layers + 2),
        ("g2", 4, layers + 2),
        ("g3", H, layers),
        *both("t1", H - 1),
        *both("tot", H - 1),
        *both("p0", H - 1),
        *both("dp", H - 2),
        *faces("f0", H - 1),
        *both("f2", H - 2),
        *both("f1", 1),
        *faces("f0_d2", 2),
        *both("dp_d2", 1),
    )


def tiles(parts):
    return -(-sum(count for _, _, count in parts) // 8)


SEAMS = ("f0", "f1", "f2", "tot", "dp", "p0", "frac", "rhs1", "rhs2", "rhs3")
PLACES = {
    "t1": ("f1", None, 7),
    "f1": ("f1", 0, 6),
    "tot": ("tot", 0, 7),
    "p0": ("p0", 0, 7),
    "dp": ("dp", 0, 7),
    "dp_d2": ("dp", 1, 6),
    "f0": ("f0", 0, 7),
    "f0_d2": ("f0", 1, 6),
    "f2": ("f2", 0, 7),
    "f2_d2": ("f2", 1, 6),
    "frac": ("frac", 0, 7),
    "rhs1": ("rhs1", 0, 7),
    "rhs2": ("rhs2", 0, 7),
    "g2": ("rhs2", 1, 6),
    "rhs3": ("rhs3", 0, 7),
    "g3": ("rhs3", 1, 6),
}


def pack(message, parts, refs, rows):
    at = 0
    for name, first, count in parts:
        for e in range(first, first + count):
            message[at // 8, at % 8 : at % 8 + 1, :] = refs[name][e, rows[name] : rows[name] + 1, :]
            at += 1


def pack_both(near, cross, parts, up, down, rows, gx):
    last = rows - 1
    outer = {name: 0 if PLACES[name][2] == 7 else 1 for name in PLACES}
    up_rows = {name: last - outer[name] for name in PLACES} | {"f1": last - 1}
    down_rows = dict(outer) | {"f1": 0}
    even = lax.axis_index(gx) % 2 == 0

    @pl.when(even)
    def _():
        pack(near, parts, up, up_rows)
        pack(cross, parts, down, down_rows)

    @pl.when(jnp.logical_not(even))
    def _():
        pack(cross, parts, up, up_rows)
        pack(near, parts, down, down_rows)


def unpack(message, parts, seams, side):
    at = 0
    for name, first, count in parts:
        seam, *places = PLACES[name]
        place = places[side]
        for e in range(first, first + count):
            if place is not None:
                seams[seam][e, place : place + 1, :] = message[at // 8, at % 8 : at % 8 + 1, :]
            at += 1


def unpack_both(near, cross, parts, seams, gx):
    even = lax.axis_index(gx) % 2 == 0

    @pl.when(even)
    def _():
        unpack(near, parts, seams, 0)
        unpack(cross, parts, seams, 1)

    @pl.when(jnp.logical_not(even))
    def _():
        unpack(cross, parts, seams, 0)
        unpack(near, parts, seams, 1)


def mobility(sat, history):
    trapped = history / (1.0 + 1.5 * history)
    excess = jnp.maximum(sat - trapped, 0.0)
    free_gas = 0.5 * (excess + jnp.sqrt(excess * excess + excess / 0.375))
    relperm = jnp.where(sat < history, free_gas * free_gas, sat * sat)
    gas = relperm / 0.5
    total = (1.0 - sat) * (1.0 - sat) + gas
    return (total, gas / total)


def roll(x, shift, axis):
    return pltpu.roll(x, shift % x.shape[axis], axis)


def loop(first, last, step, carry, unroll=4):
    groups = (last - first) // unroll

    def group(g, carry):
        for i in range(unroll):
            carry = step(first + g * unroll + i, carry)
        return carry

    carry = lax.fori_loop(0, groups, group, carry)
    for index in range(first + groups * unroll, last):
        carry = step(index, carry)
    return carry


def split(x):
    high = x.astype(jnp.bfloat16)
    return (high, (x - high.astype(jnp.float32)).astype(jnp.bfloat16))


def one_hots(cell, first_layer, layers, rows, columns):
    count = cell.shape[1]
    layer = cell // (rows * columns)
    rest = cell - layer * (rows * columns)
    row = rest // columns
    column = rest - row * columns
    place = (layer - first_layer) * rows + row
    at_place = lax.broadcasted_iota(jnp.int32, (layers * rows, count), 0) == place
    at_column = lax.broadcasted_iota(jnp.int32, (columns, count), 0) == column
    return (at_place, at_column)


def gather(field, at_place, at_column):
    high, low = split(field)
    hot = at_column.astype(jnp.bfloat16)
    by_column = jnp.dot(high, hot, preferred_element_type=jnp.float32) + jnp.dot(
        low, hot, preferred_element_type=jnp.float32
    )
    return jnp.sum(jnp.where(at_place, by_column, 0.0), axis=0, keepdims=True)


def flatten(block, spread):
    perfs, wells = block.shape
    spread[...] = jnp.zeros(spread.shape, jnp.float32)
    spread[:, 0:wells] = block
    wide = spread[...]
    shift = wells
    while shift < LANES:
        wide = wide + roll(wide, shift, 1)
        shift *= 2
    each = LANES // wells
    entry = lax.broadcasted_iota(jnp.int32, (perfs, LANES), 0)
    group = lax.broadcasted_iota(jnp.int32, (perfs, LANES), 1) // wells
    tiles = [
        jnp.sum(jnp.where(entry == first + group, wide, 0.0), axis=0, keepdims=True)
        for first in range(0, perfs, each)
    ]
    return jnp.concatenate(tiles, axis=1)


def prepare_kernel(
    sat,
    hist,
    pressure,
    storage,
    trans,
    cell_in,
    index_in,
    control_in,
    target_in,
    p0e,
    tote,
    frace,
    stor,
    t0,
    t1,
    t2,
    near_a,
    near_b,
    cross_a,
    cross_b,
    sums,
    cell,
    wells,
    sat_v,
    hist_v,
    cell_v,
    index_v,
    control_v,
    target_v,
    spread,
    sems,
    *,
    gz,
):
    layers, rows, columns = pressure.shape
    ext = layers + 2 * H
    own = pl.ds(H, layers)
    copies = [
        pltpu.make_async_copy(a, b, sems.at[i])
        for i, (a, b) in enumerate(
            (
                (sat, sat_v),
                (hist, hist_v),
                (cell_in, cell_v),
                (index_in, index_v),
                (control_in, control_v),
                (target_in, target_v),
                (pressure, p0e.at[own]),
                (trans.at[0], t0.at[own]),
                (storage, stor.at[own]),
                (trans.at[1], t1.at[own]),
                (trans.at[2], t2.at[own]),
            )
        )
    ]
    for copy in copies:
        copy.start()
    for copy in copies[:2]:
        copy.wait()

    def layer_step(l, carry):
        t, f = mobility(sat_v[l], hist_v[l])
        tote[l + H] = t
        frace[l + H] = f
        return carry

    loop(0, layers, layer_step, 0)
    for copy in copies[2:7]:
        copy.wait()
    perfs, group = cell_v.shape
    cell[...] = flatten(cell_v[...].astype(jnp.float32), spread).astype(jnp.int32)
    wells[0:1, :] = flatten(index_v[...], spread)
    wells[1:2, :] = flatten(jnp.broadcast_to(target_v[...], (perfs, group)), spread)
    wells[2:3, :] = flatten(
        jnp.broadcast_to(control_v[...].astype(jnp.float32), (perfs, group)), spread
    )
    at_place, at_column = one_hots(
        cell[...], lax.axis_index(gz) * layers, layers, rows, columns
    )
    flat = (layers * rows, columns)
    weight = wells[0:1, :] * gather(tote[own].reshape(flat), at_place, at_column)
    cell_p = gather(p0e[own].reshape(flat), at_place, at_column)
    for i, value in enumerate((weight * cell_p, weight)):
        part = value[:, 0:LANES]
        for lane in range(LANES, value.shape[1], LANES):
            part = part + value[:, lane : lane + LANES]
        shift = LANES // 2
        while shift >= group:
            part = part + roll(part, shift, 1)
            shift //= 2
        sums[i : i + 1, :] = part
    for copy in copies[7:]:
        copy.wait()
    even = lax.axis_index(gz) % 2 == 0
    refs = {"p0": p0e, "tot": tote, "t0": t0, "stor": stor, "t1": t1, "t2": t2, "frac": frace}
    for messages, is_top in (
        ((near_a, near_b), even),
        ((cross_a, cross_b), jnp.logical_not(even)),
    ):
        for message, piece in zip(messages, Z_PIECES):
            at = 0
            for name, count in piece:
                if name == "sums":
                    message[at] = jnp.zeros((rows, columns), jnp.float32)
                    message[at, 0:2, 0:LANES] = sums[...]
                else:
                    edge = jnp.where(is_top, H + layers - count, H)
                    message[pl.ds(at, count)] = refs[name][pl.ds(edge, count)]
                at += count


def masks(rows, columns):
    row = lax.broadcasted_iota(jnp.int32, (rows, columns), 0)
    column = lax.broadcasted_iota(jnp.int32, (rows, columns), 1)
    return (row == rows - 1, column == columns - 1)


def lateral_faces(tot, t1, t2, store, last_row, last_column, top_x):
    along = jnp.where(last_row, 0.0, t1) * 0.5 * (tot + roll(tot, -1, 0))
    across = jnp.where(last_column, 0.0, t2) * 0.5 * (tot + roll(tot, -1, 1))
    part = store + along + roll(along, 1, 0) + across + roll(across, 1, 1)
    return (jnp.where(last_row, jnp.where(top_x, 0.0, t1), along), across, part)


def is_last(axis):
    return lax.axis_index(axis) == lax.axis_size(axis) - 1


def faces_kernel(
    p0e, tote, frace, stor, t0, t1, t2, f0e, f1e, f2e, dpe, near, cross, *, layers, gx
):
    _, rows, columns = p0e.shape
    last_row, last_column = masks(rows, columns)
    top_x = is_last(gx)

    def step(e, carry):
        tot = tote[e]
        f0e[e] = t0[e] * 0.5 * (tot + tote[e + 1])
        f1e[e], f2e[e], dpe[e] = lateral_faces(
            tot, t1[e], t2[e], stor[e], last_row, last_column, top_x
        )
        return carry

    loop(H, H + layers, step, 0)
    refs = {"t1": f1e, "tot": tote, "p0": p0e, "dp": dpe, "f0": f0e, "f2": f2e, "f1": f1e}
    refs |= {"frac": frace, "f0_d2": f0e, "f2_d2": f2e, "dp_d2": dpe}
    pack_both(near, cross, early_parts(layers), refs, refs, rows, gx)


def seam_kernel(near, cross, *seams, layers, gx):
    for seam in seams:
        seam[...] = jnp.zeros(seam.shape, jnp.float32)
    unpack_both(near, cross, early_parts(layers), dict(zip(SEAMS, seams)), gx)


def build_kernel(*refs, layers, gx, gz, far):
    near = refs[9:11]
    cross = refs[11:13]
    own_t0, own_sums = refs[8], refs[13]
    fars = refs[14 : 14 + far]
    cell, wells = refs[14 + far : 16 + far]
    (
        p0e,
        tote,
        frace,
        stor,
        f0e,
        f1e,
        f2e,
        dpe,
        rhse,
        source,
        x_near,
        x_cross,
        diage,
        p1,
        rhs1u,
        rhs1d,
        rhs2u,
        rhs2d,
        g2u,
        g2d,
        g3u,
        g3d,
    ) = refs[16 + far :]
    ext, rows, columns = p0e.shape
    even = lax.axis_index(gz) % 2 == 0
    top_z = is_last(gz)
    top_x = is_last(gx)
    last_row, last_column = masks(rows, columns)
    where = {}
    for number, piece in enumerate(Z_PIECES):
        at = 0
        for name, count in piece:
            where[name] = (number, at, count)
            at += count

    def halo(name, e):
        number, at, count = where[name]
        low = e < H
        at = at + e - (H - count if low else H + layers)
        one, two = (near[number][at], cross[number][at])
        return jnp.where(even, two, one) if low else jnp.where(even, one, two)

    for name, target in (("p0", p0e), ("tot", tote), ("frac", frace), ("stor", stor)):
        count = where[name][2]
        for e in (*range(H - count, H), *range(H + layers, H + layers + count)):
            target[e] = halo(name, e)
    f0e[H + layers - 1] = jnp.where(top_z, 0.0, own_t0[H + layers - 1]) * 0.5 * (
        tote[H + layers - 1] + tote[H + layers]
    )
    for e in (*range(0, H), *range(H + layers, ext - 1)):
        f0e[e] = halo("t0", e) * 0.5 * (tote[e] + tote[e + 1])
    for e in (*range(1, H), *range(H + layers, ext - 1)):
        f1e[e], f2e[e], dpe[e] = lateral_faces(
            tote[e], halo("t1", e), halo("t2", e), stor[e], last_row, last_column, top_x
        )
    number, at, _ = where["sums"]
    sums = own_sums[...] + near[number][at, 0:2, 0:LANES] + cross[number][at, 0:2, 0:LANES]
    for ref in fars:
        sums = sums + ref[...]

    inner = ext - 2
    at_place, at_column = one_hots(
        cell[...], lax.axis_index(gz) * layers - (H - 1), inner, rows, columns
    )
    flat = (inner * rows, columns)
    weight = wells[0:1, :] * gather(tote[1 : ext - 1].reshape(flat), at_place, at_column)
    cell_p = gather(p0e[1 : ext - 1].reshape(flat), at_place, at_column)
    count = weight.shape[1]
    repeat = lambda x: jnp.concatenate([x] * (count // LANES), axis=1)
    goal = wells[1:2, :]
    sum_w = repeat(sums[1:2, :])
    sum_w = jnp.where(sum_w > 0.0, sum_w, 1.0)
    hole = jnp.where(wells[2:3, :] == 0.0, (goal + repeat(sums[0:1, :])) / sum_w, goal)
    rate = weight * (hole - cell_p)
    hot = at_place.astype(jnp.bfloat16)
    spread = jnp.zeros(flat, jnp.float32)
    for piece in split(jnp.where(at_column, rate, 0.0)):
        spread = spread + lax.dot_general(
            hot, piece, (((1,), (1,)), ((), ())), preferred_element_type=jnp.float32
        )
    spread = spread.reshape(inner, rows, columns)
    rhse[1 : ext - 1] = spread
    source[...] = spread[H - 1 : H - 1 + layers]

    def first_step(e, below):
        above = f0e[e]
        along = jnp.where(last_row, 0.0, f1e[e])
        across = f2e[e]
        diag = dpe[e] + above + below
        diage[e] = diag
        p = p0e[e]
        rhs = stor[e] * p + rhse[e]
        rhse[e] = rhs
        lower = roll(along * p, 1, 0)
        upper = along * roll(p, -1, 0)
        rhs1u[e] = rhs + lower
        rhs1d[e] = rhs + upper
        new = rhs + lower + upper + above * p0e[e + 1] + below * p0e[e - 1]
        new = new + across * roll(p, -1, 1) + roll(across * p, 1, 1)
        p1[e] = jnp.where(diag > 0.0, new / diag, 0.0)
        return above

    loop(1, ext - 1, first_step, f0e[0])

    def second_step(e, carry):
        along = jnp.where(last_row, 0.0, f1e[e])
        across = f2e[e]
        p = p1[e]
        rhs = rhse[e]
        diag = diage[e]
        lower = roll(along * p, 1, 0)
        upper = along * roll(p, -1, 0)
        rhs2u[e] = rhs + lower
        rhs2d[e] = rhs + upper
        part = rhs + f0e[e] * p1[e + 1] + f0e[e - 1] * p1[e - 1]
        part = part + across * roll(p, -1, 1) + roll(across * p, 1, 1)
        g2u[e] = part + lower
        g2d[e] = part + upper
        p2 = jnp.where(diag > 0.0, (part + lower + upper) / diag, 0.0)
        g3u[e] = rhs + roll(along * p2, 1, 0)
        g3d[e] = rhs + along * roll(p2, -1, 0)
        return carry

    loop(2, ext - 2, second_step, 0)

    shared = {"t1": f1e, "tot": tote, "p0": p0e, "dp": dpe, "f0": f0e, "f2": f2e, "f1": f1e}
    shared |= {"f0_d2": f0e, "dp_d2": dpe, "rhs3": rhse}
    up = shared | {"rhs1": rhs1u, "rhs2": rhs2u, "g2": g2u, "g3": g3u}
    down = shared | {"rhs1": rhs1d, "rhs2": rhs2d, "g2": g2d, "g3": g3d}
    pack_both(x_near, x_cross, late_parts(layers), up, down, rows, gx)


def finish_kernel(*refs, gx):
    sat, hist, volume, storage, source = refs[:5]
    p0e, tote, frace, f0e, f1e, f2e, dpe, rhse, near, cross = refs[5:15]
    refs = refs[15 + len(SEAMS) :]
    new_p, residual, new_sat, new_hist = refs[:4]
    seams = dict(zip(SEAMS, refs[4:]))
    pa, pb, f1, rdiag = refs[4 + len(SEAMS) :]
    layers, rows, columns = sat.shape
    ext = layers + 2 * H
    unpack_both(near, cross, late_parts(layers), seams, gx)
    sf0, sf1, sf2, stot, sdp, sp0, sfrac = (seams[name] for name in SEAMS[:7])

    full = rows + 8
    row = lax.broadcasted_iota(jnp.int32, (full, columns), 0)
    edge = (row == rows - 1) | (row == full - 1)
    beyond = (row == rows + 1) | (row == full - 2)
    join = lambda a, b: jnp.concatenate([a, b], axis=0)

    pa[0] = join(p0e[0], sp0[0])
    pa[ext - 1] = join(p0e[ext - 1], sp0[ext - 1])

    def face_step(e, below):
        tot = join(tote[e], stot[e])
        mixed = join(f1e[e], sf1[e])
        border = jnp.where(edge, mixed * 0.5 * (tot + roll(tot, -1, 0)), 0.0)
        f1[e] = jnp.where(edge, border, mixed)
        above = join(f0e[e], sf0[e])
        diag = join(dpe[e], sdp[e]) + above + below + border + roll(border, 1, 0)
        rdiag[e] = jnp.where(diag > 0.0, 1.0 / diag, 0.0)
        pa[e] = join(p0e[e], sp0[e])
        return above

    loop(1, ext - 1, face_step, join(f0e[0], sf0[0]))

    def sweep(number, old, new, srhs):
        def step(e, below):
            p = old[e]
            above = old[e + 1]
            face = join(f0e[e], sf0[e])
            x = f1[e]
            y = join(f2e[e], sf2[e])
            total = join(rhse[e], srhs[e]) + below + face * above
            total = total + x * roll(p, -1, 0) + roll(x * p, 1, 0)
            total = total + y * roll(p, -1, 1) + roll(y * p, 1, 1)
            value = total * rdiag[e]
            if number == 1:
                value = jnp.where(beyond, 0.0, value)
            new[e] = value
            return face * p

        first = join(f0e[number - 1], sf0[number - 1]) * old[number - 1]
        loop(number, ext - number, step, first)

    fields = (pa, pb)
    for number in range(1, SWEEPS + 1):
        sweep(
            number,
            fields[(number - 1) % 2],
            fields[number % 2],
            seams[f"rhs{min(number, 3)}"],
        )
    field = fields[SWEEPS % 2]

    def flow(face, p, p_next, f, f_next):
        water = face * (p - p_next)
        return (water, water * jnp.where(water > 0, f, f_next))

    def last_step(l, carry):
        below_w, below_g = carry
        e = l + H
        p = field[e]
        f = join(frace[e], sfrac[e])
        own_p = p[:rows]
        own_f = f[:rows]
        above_w, above_g = flow(f0e[e], own_p, field[e + 1][:rows], own_f, frace[e + 1])
        xw, xg = flow(f1[e], p, roll(p, -1, 0), f, roll(f, -1, 0))
        yw, yg = flow(f2e[e], own_p, roll(own_p, -1, 1), own_f, roll(own_f, -1, 1))
        water = above_w - below_w + (xw - roll(xw, 1, 0))[:rows] + yw - roll(yw, 1, 1)
        out = above_g - below_g + (xg - roll(xg, 1, 0))[:rows] + yg - roll(yg, 1, 1)
        new_p[l] = own_p
        residual[l] = rhse[e] - storage[l] * own_p - water
        src = source[l]
        gas = jnp.maximum(src, 0.0) + jnp.minimum(src, 0.0) * own_f
        s = sat[l] + volume[l] * (gas - out)
        new_sat[l] = s
        new_hist[l] = jnp.maximum(hist[l], s)
        return (above_w, above_g)

    first = flow(f0e[H - 1], field[H - 1][:rows], field[H][:rows], frace[H - 1], frace[H])
    loop(0, layers, last_step, first)


def swap(block, axis, first):
    pairs = [(i, i + 1) for i in range(first, lax.axis_size(axis) - 1, 2)]
    return lax.ppermute(block, axis, pairs + [(b, a) for a, b in pairs])


def total_over(part, axis):
    count = lax.axis_size(axis)
    step = 1
    while step < count:
        part = part + lax.ppermute(part, axis, [(i, i ^ step) for i in range(count)])
        step *= 2
    return part


def pin(*shape, dtype=jnp.float32):
    return pltpu.VMEM(shape, dtype)


VMEM = pl.BlockSpec(memory_space=pltpu.VMEM)
HBM = pl.BlockSpec(memory_space=pltpu.HBM)


def call(kernel, outs, scratch, *args, space=VMEM, sems=0, aliases={}):
    as_struct = lambda s: s if hasattr(s, "dtype") else jax.ShapeDtypeStruct(s, jnp.float32)
    as_scratch = lambda s: pltpu.VMEM(as_struct(s).shape, as_struct(s).dtype)
    return pl.pallas_call(
        kernel,
        out_shape=[as_struct(s) for s in outs],
        in_specs=[space] * len(args),
        out_specs=[VMEM] * len(outs),
        scratch_shapes=[as_scratch(s) for s in scratch]
        + ([pltpu.SemaphoreType.DMA((sems,))] if sems else []),
        input_output_aliases=aliases,
        compiler_params=pltpu.CompilerParams(vmem_limit_bytes=24 * 1024 * 1024),
    )(*(pltpu.with_memory_space_constraint(a, pltpu.HBM) if space is HBM else a for a in args))


def body(
    pressure,
    saturation,
    sat_history,
    storage,
    step_volume,
    transmiss,
    perf_cell,
    perf_index,
    control,
    target,
):
    layers, rows, columns = pressure.shape
    ext = layers + 2 * H
    wells, perfs = perf_cell.shape
    block = (layers, rows, columns)
    pinned = pin(*block)
    ext_block = pin(ext, rows, columns)
    z_messages = [(z_layers(piece), rows, columns) for piece in Z_PIECES]
    early, late = ((tiles(f(layers)), 8, columns) for f in (early_parts, late_parts))
    seams = [pin(ext, 8, columns)] * len(SEAMS)
    *fields, near_a, near_b, cross_a, cross_b, part, cell, per_perf = call(
        functools.partial(prepare_kernel, gz="gz"),
        [ext_block] * 7
        + z_messages * 2
        + [(2, LANES), pin(1, wells * perfs, dtype=jnp.int32), pin(3, wells * perfs)],
        [
            block,
            block,
            jax.ShapeDtypeStruct((perfs, wells), jnp.int32),
            (perfs, wells),
            jax.ShapeDtypeStruct((1, wells), jnp.int32),
            (1, wells),
            (perfs, LANES),
        ],
        saturation,
        sat_history,
        pressure,
        storage,
        transmiss,
        perf_cell.T,
        perf_index.T,
        control.reshape(1, wells),
        target.reshape(1, wells),
        space=HBM,
        sems=11,
    )
    cross_a = swap(cross_a, "gz", 1)
    cross_b = swap(cross_b, "gz", 1)
    near_a = swap(near_a, "gz", 0)
    near_b = swap(near_b, "gz", 0)
    count = lax.axis_size("gz")
    far = [
        lax.ppermute(part, "gz", [(i, (i + step) % count) for i in range(count)])
        for step in sorted({2 % count, -2 % count} - {0, 1, count - 1})
    ]
    p0e, tote, frace, stor, t0, t1, t2 = fields
    f0e, f1e, f2e, dpe, early_near, early_cross = call(
        functools.partial(faces_kernel, layers=layers, gx="gx"),
        [ext_block] * 4 + [early, early],
        [],
        *fields,
    )
    early_cross = swap(early_cross, "gx", 1)
    early_near = swap(early_near, "gx", 0)
    p0e, tote, frace, _, f0e, f1e, f2e, dpe, rhse, source, late_near, late_cross = call(
        functools.partial(build_kernel, layers=layers, gx="gx", gz="gz", far=len(far)),
        [ext_block] * 9 + [pinned, late, late],
        [ext_block] * 10,
        p0e,
        tote,
        frace,
        stor,
        f0e,
        f1e,
        f2e,
        dpe,
        t0,
        near_a,
        near_b,
        cross_a,
        cross_b,
        part,
        *far,
        cell,
        per_perf,
        aliases={i: i for i in range(8)},
    )
    late_cross = swap(late_cross, "gx", 1)
    late_near = swap(late_near, "gx", 0)
    early_near, early_cross, part, rhse = lax.optimization_barrier(
        (early_near, early_cross, part, rhse)
    )
    filled = call(
        functools.partial(seam_kernel, layers=layers, gx="gx"), seams, [], early_near, early_cross
    )
    sum_p, sum_w = total_over(part, "gz")[:, :wells]
    bottom_hole = jnp.where(control == 0, (target + sum_p) / sum_w, target)
    field, residual, new_sat, new_hist, *_ = call(
        functools.partial(finish_kernel, gx="gx"),
        [block] * 4 + seams,
        [(ext, rows + 8, columns)] * 4,
        saturation,
        sat_history,
        step_volume,
        storage,
        source,
        p0e,
        tote,
        frace,
        f0e,
        f1e,
        f2e,
        dpe,
        rhse,
        late_near,
        late_cross,
        *filled,
        aliases={15 + i: 4 + i for i in range(len(SEAMS))},
    )
    return (field, residual, new_sat, new_hist, bottom_hole)


def solution(mesh):
    return jax.shard_map(
        body,
        mesh=mesh,
        in_specs=(
            P("gz", "gx", None),
            P("gz", "gx", None),
            P("gz", "gx", None),
            P("gz", "gx", None),
            P("gz", "gx", None),
            P(None, "gz", "gx", None),
            P("gx", None),
            P("gx", None),
            P("gx"),
            P("gx"),
        ),
        out_specs=(
            P("gz", "gx", None),
            P("gz", "gx", None),
            P("gz", "gx", None),
            P("gz", "gx", None),
            P("gx"),
        ),
        check_vma=False,
    )
```

```python
import functools

import jax
import jax.numpy as jnp
from jax import lax
from jax.experimental import pallas as pl
from jax.experimental.pallas import tpu as pltpu
from jax.sharding import PartitionSpec as P

SWEEPS = 4
H = SWEEPS + 1
LANES = 128

Z_PIECES = (
    (
        ("p0", H),
        ("tot", H),
        ("t0", H),
        ("stor", H - 1),
        ("t1", H - 1),
        ("t2", H - 1),
        ("frac", 1),
        ("sums", 1),
    ),
)


def z_layers(piece):
    return sum(count for _, count in piece)


def early_parts(layers):
    own = (H, layers)
    inner = (H, layers - 1)
    return (
        ("t1", *own),
        ("tot", *own),
        ("p0", *own),
        ("dp", *own),
        ("f0", *inner),
        ("f2", *own),
        ("f1", *own),
        ("frac", *own),
        ("f0_d2", *inner),
        ("f2_d2", *own),
        ("dp_d2", *own),
    )


def late_parts(layers):
    top = H + layers
    both = lambda name, n: ((name, H - n, n), (name, top, n))
    faces = lambda name, n: ((name, H - n, n), (name, top - 1, n))
    return (
        ("rhs1", 2, layers + 6),
        ("rhs2", 3, layers + 4),
        ("rhs3", 4, layers + 2),
        ("g2", 4, layers + 2),
        ("g3", H, layers),
        *both("t1", H - 1),
        *both("tot", H - 1),
        *both("p0", H - 1),
        *both("dp", H - 2),
        *faces("f0", H - 1),
        *both("f2", H - 2),
        *both("f1", 1),
        *faces("f0_d2", 2),
        *both("dp_d2", 1),
    )


def tiles(parts):
    return -(-sum(count for _, _, count in parts) // 8)


SEAMS = ("f0", "f1", "f2", "tot", "dp", "p0", "frac", "rhs1", "rhs2", "rhs3")
PLACES = {
    "t1": ("f1", None, 7),
    "f1": ("f1", 0, 6),
    "tot": ("tot", 0, 7),
    "p0": ("p0", 0, 7),
    "dp": ("dp", 0, 7),
    "dp_d2": ("dp", 1, 6),
    "f0": ("f0", 0, 7),
    "f0_d2": ("f0", 1, 6),
    "f2": ("f2", 0, 7),
    "f2_d2": ("f2", 1, 6),
    "frac": ("frac", 0, 7),
    "rhs1": ("rhs1", 0, 7),
    "rhs2": ("rhs2", 0, 7),
    "g2": ("rhs2", 1, 6),
    "rhs3": ("rhs3", 0, 7),
    "g3": ("rhs3", 1, 6),
}


def pack(message, parts, refs, rows):
    at = 0
    for name, first, count in parts:
        for e in range(first, first + count):
            message[at // 8, at % 8 : at % 8 + 1, :] = refs[name][e, rows[name] : rows[name] + 1, :]
            at += 1


def pack_both(near, cross, parts, up, down, rows, gx):
    last = rows - 1
    outer = {name: 0 if PLACES[name][2] == 7 else 1 for name in PLACES}
    up_rows = {name: last - outer[name] for name in PLACES} | {"f1": last - 1}
    down_rows = dict(outer) | {"f1": 0}
    even = lax.axis_index(gx) % 2 == 0

    @pl.when(even)
    def _():
        pack(near, parts, up, up_rows)
        pack(cross, parts, down, down_rows)

    @pl.when(jnp.logical_not(even))
    def _():
        pack(cross, parts, up, up_rows)
        pack(near, parts, down, down_rows)


def unpack(message, parts, seams, side):
    at = 0
    for name, first, count in parts:
        seam, *places = PLACES[name]
        place = places[side]
        for e in range(first, first + count):
            if place is not None:
                seams[seam][e, place : place + 1, :] = message[at // 8, at % 8 : at % 8 + 1, :]
            at += 1


def unpack_both(near, cross, parts, seams, gx):
    even = lax.axis_index(gx) % 2 == 0

    @pl.when(even)
    def _():
        unpack(near, parts, seams, 0)
        unpack(cross, parts, seams, 1)

    @pl.when(jnp.logical_not(even))
    def _():
        unpack(cross, parts, seams, 0)
        unpack(near, parts, seams, 1)


def mobility(sat, history):
    trapped = history / (1.0 + 1.5 * history)
    excess = jnp.maximum(sat - trapped, 0.0)
    free_gas = 0.5 * (excess + jnp.sqrt(excess * excess + excess / 0.375))
    relperm = jnp.where(sat < history, free_gas * free_gas, sat * sat)
    gas = relperm / 0.5
    total = (1.0 - sat) * (1.0 - sat) + gas
    return (total, gas / total)


def roll(x, shift, axis):
    return pltpu.roll(x, shift % x.shape[axis], axis)


def loop(first, last, step, carry, unroll=4):
    groups = (last - first) // unroll

    def group(g, carry):
        for i in range(unroll):
            carry = step(first + g * unroll + i, carry)
        return carry

    carry = lax.fori_loop(0, groups, group, carry)
    for index in range(first + groups * unroll, last):
        carry = step(index, carry)
    return carry


def split(x):
    high = x.astype(jnp.bfloat16)
    return (high, (x - high.astype(jnp.float32)).astype(jnp.bfloat16))


def one_hots(cell, first_layer, layers, rows, columns):
    count = cell.shape[1]
    layer = cell // (rows * columns)
    rest = cell - layer * (rows * columns)
    row = rest // columns
    column = rest - row * columns
    place = (layer - first_layer) * rows + row
    at_place = lax.broadcasted_iota(jnp.int32, (layers * rows, count), 0) == place
    at_column = lax.broadcasted_iota(jnp.int32, (columns, count), 0) == column
    return (at_place, at_column)


def gather(field, at_place, at_column):
    high, low = split(field)
    hot = at_column.astype(jnp.bfloat16)
    by_column = jnp.dot(high, hot, preferred_element_type=jnp.float32) + jnp.dot(
        low, hot, preferred_element_type=jnp.float32
    )
    return jnp.sum(jnp.where(at_place, by_column, 0.0), axis=0, keepdims=True)


def flatten(block, spread):
    perfs, wells = block.shape
    spread[...] = jnp.zeros(spread.shape, jnp.float32)
    spread[:, 0:wells] = block
    wide = spread[...]
    shift = wells
    while shift < LANES:
        wide = wide + roll(wide, shift, 1)
        shift *= 2
    each = LANES // wells
    entry = lax.broadcasted_iota(jnp.int32, (perfs, LANES), 0)
    group = lax.broadcasted_iota(jnp.int32, (perfs, LANES), 1) // wells
    tiles = [
        jnp.sum(jnp.where(entry == first + group, wide, 0.0), axis=0, keepdims=True)
        for first in range(0, perfs, each)
    ]
    return jnp.concatenate(tiles, axis=1)


def prepare_kernel(
    sat,
    hist,
    pressure,
    storage,
    trans,
    cell_in,
    index_in,
    control_in,
    target_in,
    p0e,
    tote,
    frace,
    stor,
    t0,
    t1,
    t2,
    near,
    cross,
    sums,
    cell,
    wells,
    sat_v,
    hist_v,
    cell_v,
    index_v,
    control_v,
    target_v,
    spread,
    sems,
    *,
    gz,
):
    layers, rows, columns = pressure.shape
    ext = layers + 2 * H
    own = pl.ds(H, layers)
    copies = [
        pltpu.make_async_copy(a, b, sems.at[i])
        for i, (a, b) in enumerate(
            (
                (sat, sat_v),
                (hist, hist_v),
                (cell_in, cell_v),
                (index_in, index_v),
                (control_in, control_v),
                (target_in, target_v),
                (pressure, p0e.at[own]),
                (trans.at[0], t0.at[own]),
                (storage, stor.at[own]),
                (trans.at[1], t1.at[own]),
                (trans.at[2], t2.at[own]),
            )
        )
    ]
    for copy in copies:
        copy.start()
    for copy in copies[:2]:
        copy.wait()

    def layer_step(l, carry):
        t, f = mobility(sat_v[l], hist_v[l])
        tote[l + H] = t
        frace[l + H] = f
        return carry

    loop(0, layers, layer_step, 0)
    for copy in copies[2:7]:
        copy.wait()
    perfs, group = cell_v.shape
    cell[...] = flatten(cell_v[...].astype(jnp.float32), spread).astype(jnp.int32)
    wells[0:1, :] = flatten(index_v[...], spread)
    wells[1:2, :] = flatten(jnp.broadcast_to(target_v[...], (perfs, group)), spread)
    wells[2:3, :] = flatten(
        jnp.broadcast_to(control_v[...].astype(jnp.float32), (perfs, group)), spread
    )
    at_place, at_column = one_hots(
        cell[...], lax.axis_index(gz) * layers, layers, rows, columns
    )
    flat = (layers * rows, columns)
    weight = wells[0:1, :] * gather(tote[own].reshape(flat), at_place, at_column)
    cell_p = gather(p0e[own].reshape(flat), at_place, at_column)
    for i, value in enumerate((weight * cell_p, weight)):
        part = value[:, 0:LANES]
        for lane in range(LANES, value.shape[1], LANES):
            part = part + value[:, lane : lane + LANES]
        shift = LANES // 2
        while shift >= group:
            part = part + roll(part, shift, 1)
            shift //= 2
        sums[i : i + 1, :] = part
    for copy in copies[7:]:
        copy.wait()
    even = lax.axis_index(gz) % 2 == 0
    refs = {"p0": p0e, "tot": tote, "t0": t0, "stor": stor, "t1": t1, "t2": t2, "frac": frace}
    for messages, is_top in (
        ((near,), even),
        ((cross,), jnp.logical_not(even)),
    ):
        for message, piece in zip(messages, Z_PIECES):
            at = 0
            for name, count in piece:
                if name == "sums":
                    message[at] = jnp.zeros((rows, columns), jnp.float32)
                    message[at, 0:2, 0:LANES] = sums[...]
                else:
                    edge = jnp.where(is_top, H + layers - count, H)
                    message[pl.ds(at, count)] = refs[name][pl.ds(edge, count)]
                at += count


def masks(rows, columns):
    row = lax.broadcasted_iota(jnp.int32, (rows, columns), 0)
    column = lax.broadcasted_iota(jnp.int32, (rows, columns), 1)
    return (row == rows - 1, column == columns - 1)


def lateral_faces(tot, t1, t2, store, last_row, last_column, top_x):
    along = jnp.where(last_row, 0.0, t1) * 0.5 * (tot + roll(tot, -1, 0))
    across = jnp.where(last_column, 0.0, t2) * 0.5 * (tot + roll(tot, -1, 1))
    part = store + along + roll(along, 1, 0) + across + roll(across, 1, 1)
    return (jnp.where(last_row, jnp.where(top_x, 0.0, t1), along), across, part)


def is_last(axis):
    return lax.axis_index(axis) == lax.axis_size(axis) - 1


def faces_kernel(
    p0e, tote, frace, stor, t0, t1, t2, part, f0e, f1e, f2e, dpe, near, cross, sums, *, layers, gx
):
    _, rows, columns = p0e.shape
    last_row, last_column = masks(rows, columns)
    top_x = is_last(gx)

    def step(e, carry):
        tot = tote[e]
        f0e[e] = t0[e] * 0.5 * (tot + tote[e + 1])
        f1e[e], f2e[e], dpe[e] = lateral_faces(
            tot, t1[e], t2[e], stor[e], last_row, last_column, top_x
        )
        return carry

    loop(H, H + layers, step, 0)
    refs = {"t1": f1e, "tot": tote, "p0": p0e, "dp": dpe, "f0": f0e, "f2": f2e, "f1": f1e}
    sums[...] = part[...]
    refs |= {"frac": frace, "f0_d2": f0e, "f2_d2": f2e, "dp_d2": dpe}
    pack_both(near, cross, early_parts(layers), refs, refs, rows, gx)


def seam_kernel(near, cross, *seams, layers, gx):
    for seam in seams:
        seam[...] = jnp.zeros(seam.shape, jnp.float32)
    unpack_both(near, cross, early_parts(layers), dict(zip(SEAMS, seams)), gx)


def build_kernel(*refs, layers, gx, gz, far):
    own_t0 = refs[8]
    cross, near = refs[9:10], refs[10:11]
    own_sums, *fars = refs[11 : 12 + far]
    cell, wells = refs[12 + far : 14 + far]
    (
        p0e,
        tote,
        frace,
        stor,
        f0e,
        f1e,
        f2e,
        dpe,
        rhse,
        source,
        x_near,
        x_cross,
        bottom,
        diage,
        p1,
        rhs1u,
        rhs1d,
        rhs2u,
        rhs2d,
        g2u,
        g2d,
        g3u,
        g3d,
    ) = refs[14 + far :]
    ext, rows, columns = p0e.shape
    even = lax.axis_index(gz) % 2 == 0
    top_z = is_last(gz)
    top_x = is_last(gx)
    last_row, last_column = masks(rows, columns)
    where = {}
    for number, piece in enumerate(Z_PIECES):
        at = 0
        for name, count in piece:
            where[name] = (number, at, count)
            at += count

    def halo(name, e):
        number, at, count = where[name]
        low = e < H
        at = at + e - (H - count if low else H + layers)
        one, two = (near[number][at], cross[number][at])
        return jnp.where(even, two, one) if low else jnp.where(even, one, two)

    for name, target in (("p0", p0e), ("tot", tote), ("frac", frace), ("stor", stor)):
        count = where[name][2]
        for e in (*range(H - count, H), *range(H + layers, H + layers + count)):
            target[e] = halo(name, e)
    f0e[H + layers - 1] = jnp.where(top_z, 0.0, own_t0[H + layers - 1]) * 0.5 * (
        tote[H + layers - 1] + tote[H + layers]
    )
    for e in (*range(0, H), *range(H + layers, ext - 1)):
        f0e[e] = halo("t0", e) * 0.5 * (tote[e] + tote[e + 1])
    for e in (*range(1, H), *range(H + layers, ext - 1)):
        f1e[e], f2e[e], dpe[e] = lateral_faces(
            tote[e], halo("t1", e), halo("t2", e), stor[e], last_row, last_column, top_x
        )
    number, at, _ = where["sums"]
    sums = own_sums[...] + near[number][at, 0:2, 0:LANES] + cross[number][at, 0:2, 0:LANES]
    for ref in fars:
        sums = sums + ref[...]

    inner = ext - 2
    at_place, at_column = one_hots(
        cell[...], lax.axis_index(gz) * layers - (H - 1), inner, rows, columns
    )
    flat = (inner * rows, columns)
    weight = wells[0:1, :] * gather(tote[1 : ext - 1].reshape(flat), at_place, at_column)
    cell_p = gather(p0e[1 : ext - 1].reshape(flat), at_place, at_column)
    count = weight.shape[1]
    repeat = lambda x: jnp.concatenate([x] * (count // LANES), axis=1)
    goal = wells[1:2, :]
    hole = jnp.where(
        wells[2:3, :] == 0.0, (goal + repeat(sums[0:1, :])) / repeat(sums[1:2, :]), goal
    )
    bottom[...] = hole[:, 0:LANES]
    rate = weight * (hole - cell_p)
    hot = at_place.astype(jnp.bfloat16)
    spread = jnp.zeros(flat, jnp.float32)
    for piece in split(jnp.where(at_column, rate, 0.0)):
        spread = spread + lax.dot_general(
            hot, piece, (((1,), (1,)), ((), ())), preferred_element_type=jnp.float32
        )
    spread = spread.reshape(inner, rows, columns)
    rhse[1 : ext - 1] = spread
    source[...] = spread[H - 1 : H - 1 + layers]

    def first_step(e, below):
        above = f0e[e]
        along = jnp.where(last_row, 0.0, f1e[e])
        across = f2e[e]
        diag = dpe[e] + above + below
        diage[e] = diag
        p = p0e[e]
        rhs = stor[e] * p + rhse[e]
        rhse[e] = rhs
        lower = roll(along * p, 1, 0)
        upper = along * roll(p, -1, 0)
        rhs1u[e] = rhs + lower
        rhs1d[e] = rhs + upper
        new = rhs + lower + upper + above * p0e[e + 1] + below * p0e[e - 1]
        new = new + across * roll(p, -1, 1) + roll(across * p, 1, 1)
        p1[e] = jnp.where(diag > 0.0, new / diag, 0.0)
        return above

    loop(1, ext - 1, first_step, f0e[0])

    def second_step(e, carry):
        along = jnp.where(last_row, 0.0, f1e[e])
        across = f2e[e]
        p = p1[e]
        rhs = rhse[e]
        diag = diage[e]
        lower = roll(along * p, 1, 0)
        upper = along * roll(p, -1, 0)
        rhs2u[e] = rhs + lower
        rhs2d[e] = rhs + upper
        part = rhs + f0e[e] * p1[e + 1] + f0e[e - 1] * p1[e - 1]
        part = part + across * roll(p, -1, 1) + roll(across * p, 1, 1)
        g2u[e] = part + lower
        g2d[e] = part + upper
        p2 = jnp.where(diag > 0.0, (part + lower + upper) / diag, 0.0)
        g3u[e] = rhs + roll(along * p2, 1, 0)
        g3d[e] = rhs + along * roll(p2, -1, 0)
        return carry

    loop(2, ext - 2, second_step, 0)

    shared = {"t1": f1e, "tot": tote, "p0": p0e, "dp": dpe, "f0": f0e, "f2": f2e, "f1": f1e}
    shared |= {"f0_d2": f0e, "dp_d2": dpe, "rhs3": rhse}
    up = shared | {"rhs1": rhs1u, "rhs2": rhs2u, "g2": g2u, "g3": g3u}
    down = shared | {"rhs1": rhs1d, "rhs2": rhs2d, "g2": g2d, "g3": g3d}
    pack_both(x_near, x_cross, late_parts(layers), up, down, rows, gx)


def finish_kernel(*refs, gx):
    sat, hist, volume, storage, source = refs[:5]
    p0e, tote, frace, f0e, f1e, f2e, dpe, rhse, near, cross = refs[5:15]
    refs = refs[15 + len(SEAMS) :]
    new_p, residual, new_sat, new_hist = refs[:4]
    seams = dict(zip(SEAMS, refs[4:]))
    pa, pb, f1, rdiag = refs[4 + len(SEAMS) :]
    layers, rows, columns = sat.shape
    ext = layers + 2 * H
    unpack_both(near, cross, late_parts(layers), seams, gx)
    sf0, sf1, sf2, stot, sdp, sp0, sfrac = (seams[name] for name in SEAMS[:7])

    full = rows + 8
    row = lax.broadcasted_iota(jnp.int32, (full, columns), 0)
    edge = (row == rows - 1) | (row == full - 1)
    beyond = (row == rows + 1) | (row == full - 2)
    join = lambda a, b: jnp.concatenate([a, b], axis=0)

    pa[0] = join(p0e[0], sp0[0])
    pa[ext - 1] = join(p0e[ext - 1], sp0[ext - 1])

    def face_step(e, below):
        tot = join(tote[e], stot[e])
        mixed = join(f1e[e], sf1[e])
        border = jnp.where(edge, mixed * 0.5 * (tot + roll(tot, -1, 0)), 0.0)
        f1[e] = jnp.where(edge, border, mixed)
        above = join(f0e[e], sf0[e])
        diag = join(dpe[e], sdp[e]) + above + below + border + roll(border, 1, 0)
        rdiag[e] = jnp.where(diag > 0.0, 1.0 / diag, 0.0)
        pa[e] = join(p0e[e], sp0[e])
        return above

    loop(1, ext - 1, face_step, join(f0e[0], sf0[0]))

    def sweep(number, old, new, srhs):
        def step(e, below):
            p = old[e]
            above = old[e + 1]
            face = join(f0e[e], sf0[e])
            x = f1[e]
            y = join(f2e[e], sf2[e])
            total = join(rhse[e], srhs[e]) + below + face * above
            total = total + x * roll(p, -1, 0) + roll(x * p, 1, 0)
            total = total + y * roll(p, -1, 1) + roll(y * p, 1, 1)
            value = total * rdiag[e]
            if number == 1:
                value = jnp.where(beyond, 0.0, value)
            new[e] = value
            return face * p

        first = join(f0e[number - 1], sf0[number - 1]) * old[number - 1]
        loop(number, ext - number, step, first)

    fields = (pa, pb)
    for number in range(1, SWEEPS + 1):
        sweep(
            number,
            fields[(number - 1) % 2],
            fields[number % 2],
            seams[f"rhs{min(number, 3)}"],
        )
    field = fields[SWEEPS % 2]

    def flow(face, p, p_next, f, f_next):
        water = face * (p - p_next)
        return (water, water * jnp.where(water > 0, f, f_next))

    def last_step(l, carry):
        below_w, below_g = carry
        e = l + H
        p = field[e]
        f = join(frace[e], sfrac[e])
        own_p = p[:rows]
        own_f = f[:rows]
        above_w, above_g = flow(f0e[e], own_p, field[e + 1][:rows], own_f, frace[e + 1])
        xw, xg = flow(f1[e], p, roll(p, -1, 0), f, roll(f, -1, 0))
        yw, yg = flow(f2e[e], own_p, roll(own_p, -1, 1), own_f, roll(own_f, -1, 1))
        water = above_w - below_w + (xw - roll(xw, 1, 0))[:rows] + yw - roll(yw, 1, 1)
        out = above_g - below_g + (xg - roll(xg, 1, 0))[:rows] + yg - roll(yg, 1, 1)
        new_p[l] = own_p
        residual[l] = rhse[e] - storage[l] * own_p - water
        src = source[l]
        gas = jnp.maximum(src, 0.0) + jnp.minimum(src, 0.0) * own_f
        s = sat[l] + volume[l] * (gas - out)
        new_sat[l] = s
        new_hist[l] = jnp.maximum(hist[l], s)
        return (above_w, above_g)

    first = flow(f0e[H - 1], field[H - 1][:rows], field[H][:rows], frace[H - 1], frace[H])
    loop(0, layers, last_step, first)


def swap(block, axis, first):
    pairs = [(i, i + 1) for i in range(first, lax.axis_size(axis) - 1, 2)]
    return lax.ppermute(block, axis, pairs + [(b, a) for a, b in pairs])


def from_distant(part, axis):
    count = lax.axis_size(axis)
    parts = []
    for step in range(2, 1 << (count - 1).bit_length()):
        pairs = [(i, i ^ step) for i in range(count)]
        pairs = [(a, b) for a, b in pairs if abs(a - b) > 1 and b < count]
        parts.append(lax.ppermute(part, axis, pairs))
    return parts


def pin(*shape, dtype=jnp.float32):
    return pltpu.VMEM(shape, dtype)


VMEM = pl.BlockSpec(memory_space=pltpu.VMEM)
HBM = pl.BlockSpec(memory_space=pltpu.HBM)


def call(kernel, outs, scratch, *args, space=VMEM, sems=0, aliases={}):
    as_struct = lambda s: s if hasattr(s, "dtype") else jax.ShapeDtypeStruct(s, jnp.float32)
    as_scratch = lambda s: pltpu.VMEM(as_struct(s).shape, as_struct(s).dtype)
    return pl.pallas_call(
        kernel,
        out_shape=[as_struct(s) for s in outs],
        in_specs=[space] * len(args),
        out_specs=[VMEM] * len(outs),
        scratch_shapes=[as_scratch(s) for s in scratch]
        + ([pltpu.SemaphoreType.DMA((sems,))] if sems else []),
        input_output_aliases=aliases,
        compiler_params=pltpu.CompilerParams(vmem_limit_bytes=24 * 1024 * 1024),
    )(*(pltpu.with_memory_space_constraint(a, pltpu.HBM) if space is HBM else a for a in args))


def body(
    pressure,
    saturation,
    sat_history,
    storage,
    step_volume,
    transmiss,
    perf_cell,
    perf_index,
    control,
    target,
):
    layers, rows, columns = pressure.shape
    ext = layers + 2 * H
    wells, perfs = perf_cell.shape
    block = (layers, rows, columns)
    pinned = pin(*block)
    ext_block = pin(ext, rows, columns)
    z_messages = [(z_layers(piece), rows, columns) for piece in Z_PIECES]
    early, late = ((tiles(f(layers)), 8, columns) for f in (early_parts, late_parts))
    seams = [pin(ext, 8, columns)] * len(SEAMS)
    *fields, near, cross, part, cell, per_perf = call(
        functools.partial(prepare_kernel, gz="gz"),
        [ext_block] * 7
        + z_messages * 2
        + [(2, LANES), pin(1, wells * perfs, dtype=jnp.int32), pin(3, wells * perfs)],
        [
            block,
            block,
            jax.ShapeDtypeStruct((perfs, wells), jnp.int32),
            (perfs, wells),
            jax.ShapeDtypeStruct((1, wells), jnp.int32),
            (1, wells),
            (perfs, LANES),
        ],
        saturation,
        sat_history,
        pressure,
        storage,
        transmiss,
        perf_cell.T,
        perf_index.T,
        control.reshape(1, wells),
        target.reshape(1, wells),
        space=HBM,
        sems=11,
    )
    cross = swap(cross, "gz", 1)
    near = swap(near, "gz", 0)
    p0e, tote, frace, stor, t0, t1, t2 = fields
    f0e, f1e, f2e, dpe, early_near, early_cross, part = call(
        functools.partial(faces_kernel, layers=layers, gx="gx"),
        [ext_block] * 4 + [early, early, (2, LANES)],
        [],
        *fields,
        part,
    )
    early_cross = swap(early_cross, "gx", 1)
    early_near = swap(early_near, "gx", 0)
    far = from_distant(part, "gz")
    p0e, tote, frace, _, f0e, f1e, f2e, dpe, rhse, source, late_near, late_cross, hole = call(
        functools.partial(build_kernel, layers=layers, gx="gx", gz="gz", far=len(far)),
        [ext_block] * 9 + [pinned, late, late, (1, LANES)],
        [ext_block] * 10,
        p0e,
        tote,
        frace,
        stor,
        f0e,
        f1e,
        f2e,
        dpe,
        t0,
        cross,
        near,
        part,
        *far,
        cell,
        per_perf,
        aliases={i: i for i in range(8)},
    )
    late_cross = swap(late_cross, "gx", 1)
    late_near = swap(late_near, "gx", 0)
    early_near, early_cross, rhse = lax.optimization_barrier((early_near, early_cross, rhse))
    filled = call(
        functools.partial(seam_kernel, layers=layers, gx="gx"), seams, [], early_near, early_cross
    )
    field, residual, new_sat, new_hist, *_ = call(
        functools.partial(finish_kernel, gx="gx"),
        [block] * 4 + seams,
        [(ext, rows + 8, columns)] * 4,
        saturation,
        sat_history,
        step_volume,
        storage,
        source,
        p0e,
        tote,
        frace,
        f0e,
        f1e,
        f2e,
        dpe,
        rhse,
        late_near,
        late_cross,
        *filled,
        aliases={15 + i: 4 + i for i in range(len(SEAMS))},
    )
    return (field, residual, new_sat, new_hist, hole[0, :wells])


def solution(mesh):
    return jax.shard_map(
        body,
        mesh=mesh,
        in_specs=(
            P("gz", "gx", None),
            P("gz", "gx", None),
            P("gz", "gx", None),
            P("gz", "gx", None),
            P("gz", "gx", None),
            P(None, "gz", "gx", None),
            P("gx", None),
            P("gx", None),
            P("gx"),
            P("gx"),
        ),
        out_specs=(
            P("gz", "gx", None),
            P("gz", "gx", None),
            P("gz", "gx", None),
            P("gz", "gx", None),
            P("gx"),
        ),
        check_vma=False,
    )
```

```python
import functools

import jax
import jax.numpy as jnp
from jax import lax
from jax.experimental import pallas as pl
from jax.experimental.pallas import tpu as pltpu
from jax.sharding import PartitionSpec as P

SWEEPS = 4
H = SWEEPS + 1
LANES = 128

Z_PARTS = (
    ("p0", H),
    ("tot", H),
    ("t0", H),
    ("stor", H - 1),
    ("t1", H - 1),
    ("t2", H - 1),
    ("frac", 1),
    ("sums", 1),
)


def early_parts(layers):
    own = (H, layers)
    inner = (H, layers - 1)
    return (
        ("t1", *own),
        ("tot", *own),
        ("p0", *own),
        ("dp", *own),
        ("f0", *inner),
        ("f2", *own),
        ("f1", *own),
        ("frac", *own),
        ("f0_d2", *inner),
        ("f2_d2", *own),
        ("dp_d2", *own),
    )


def late_parts(layers):
    top = H + layers
    both = lambda name, n: ((name, H - n, n), (name, top, n))
    faces = lambda name, n: ((name, H - n, n), (name, top - 1, n))
    return (
        ("rhs1", 2, layers + 6),
        ("rhs2", 3, layers + 4),
        ("rhs3", 4, layers + 2),
        ("g2", 4, layers + 2),
        ("g3", H, layers),
        *both("t1", H - 1),
        *both("tot", H - 1),
        *both("p0", H - 1),
        *both("dp", H - 2),
        *faces("f0", H - 1),
        *both("f2", H - 2),
        *both("f1", 1),
        *faces("f0_d2", 2),
        *both("dp_d2", 1),
    )


def tiles(parts):
    return -(-sum(count for _, _, count in parts) // 8)


SEAMS = ("f0", "f1", "f2", "tot", "dp", "p0", "frac", "rhs1", "rhs2", "rhs3")
PLACES = {
    "t1": ("f1", None, 7),
    "f1": ("f1", 0, 6),
    "tot": ("tot", 0, 7),
    "p0": ("p0", 0, 7),
    "dp": ("dp", 0, 7),
    "dp_d2": ("dp", 1, 6),
    "f0": ("f0", 0, 7),
    "f0_d2": ("f0", 1, 6),
    "f2": ("f2", 0, 7),
    "f2_d2": ("f2", 1, 6),
    "frac": ("frac", 0, 7),
    "rhs1": ("rhs1", 0, 7),
    "rhs2": ("rhs2", 0, 7),
    "g2": ("rhs2", 1, 6),
    "rhs3": ("rhs3", 0, 7),
    "g3": ("rhs3", 1, 6),
}


def pack(message, parts, refs, rows):
    at = 0
    for name, first, count in parts:
        for e in range(first, first + count):
            message[at // 8, at % 8 : at % 8 + 1, :] = refs[name][e, rows[name] : rows[name] + 1, :]
            at += 1


def pack_both(near, cross, parts, up, down, rows, gx):
    last = rows - 1
    outer = {name: 0 if PLACES[name][2] == 7 else 1 for name in PLACES}
    up_rows = {name: last - outer[name] for name in PLACES} | {"f1": last - 1}
    down_rows = dict(outer) | {"f1": 0}
    even = lax.axis_index(gx) % 2 == 0

    @pl.when(even)
    def _():
        pack(near, parts, up, up_rows)
        pack(cross, parts, down, down_rows)

    @pl.when(jnp.logical_not(even))
    def _():
        pack(cross, parts, up, up_rows)
        pack(near, parts, down, down_rows)


def unpack(message, parts, seams, side):
    at = 0
    for name, first, count in parts:
        seam, *places = PLACES[name]
        place = places[side]
        for e in range(first, first + count):
            if place is not None:
                seams[seam][e, place : place + 1, :] = message[at // 8, at % 8 : at % 8 + 1, :]
            at += 1


def unpack_both(near, cross, parts, seams, gx):
    even = lax.axis_index(gx) % 2 == 0

    @pl.when(even)
    def _():
        unpack(near, parts, seams, 0)
        unpack(cross, parts, seams, 1)

    @pl.when(jnp.logical_not(even))
    def _():
        unpack(cross, parts, seams, 0)
        unpack(near, parts, seams, 1)


def mobility(sat, history):
    trapped = history / (1.0 + 1.5 * history)
    excess = jnp.maximum(sat - trapped, 0.0)
    free_gas = 0.5 * (excess + jnp.sqrt(excess * excess + excess / 0.375))
    relperm = jnp.where(sat < history, free_gas * free_gas, sat * sat)
    gas = relperm / 0.5
    total = (1.0 - sat) * (1.0 - sat) + gas
    return (total, gas / total)


def roll(x, shift, axis):
    return pltpu.roll(x, shift % x.shape[axis], axis)


def loop(first, last, step, carry, unroll=4):
    groups = (last - first) // unroll

    def group(g, carry):
        for i in range(unroll):
            carry = step(first + g * unroll + i, carry)
        return carry

    carry = lax.fori_loop(0, groups, group, carry)
    for index in range(first + groups * unroll, last):
        carry = step(index, carry)
    return carry


def split(x):
    high = x.astype(jnp.bfloat16)
    return (high, (x - high.astype(jnp.float32)).astype(jnp.bfloat16))


def one_hots(cell, first_layer, layers, rows, columns):
    count = cell.shape[1]
    layer = cell // (rows * columns)
    rest = cell - layer * (rows * columns)
    row = rest // columns
    column = rest - row * columns
    place = (layer - first_layer) * rows + row
    at_place = lax.broadcasted_iota(jnp.int32, (layers * rows, count), 0) == place
    at_column = lax.broadcasted_iota(jnp.int32, (columns, count), 0) == column
    return (at_place, at_column)


def gather(field, at_place, at_column):
    high, low = split(field)
    hot = at_column.astype(jnp.bfloat16)
    by_column = jnp.dot(high, hot, preferred_element_type=jnp.float32) + jnp.dot(
        low, hot, preferred_element_type=jnp.float32
    )
    return jnp.sum(jnp.where(at_place, by_column, 0.0), axis=0, keepdims=True)


def flatten(block, spread):
    perfs, wells = block.shape
    spread[...] = jnp.zeros(spread.shape, jnp.float32)
    spread[:, 0:wells] = block
    wide = spread[...]
    shift = wells
    while shift < LANES:
        wide = wide + roll(wide, shift, 1)
        shift *= 2
    each = LANES // wells
    entry = lax.broadcasted_iota(jnp.int32, (perfs, LANES), 0)
    group = lax.broadcasted_iota(jnp.int32, (perfs, LANES), 1) // wells
    tiles = [
        jnp.sum(jnp.where(entry == first + group, wide, 0.0), axis=0, keepdims=True)
        for first in range(0, perfs, each)
    ]
    return jnp.concatenate(tiles, axis=1)


def prepare_kernel(
    sat,
    hist,
    pressure,
    storage,
    trans,
    cell_in,
    index_in,
    control_in,
    target_in,
    p0e,
    tote,
    frace,
    stor,
    t0,
    t1,
    t2,
    near,
    cross,
    sums,
    cell,
    wells,
    sat_v,
    hist_v,
    cell_v,
    index_v,
    control_v,
    target_v,
    spread,
    sems,
    *,
    gz,
):
    layers, rows, columns = pressure.shape
    ext = layers + 2 * H
    own = pl.ds(H, layers)
    copies = [
        pltpu.make_async_copy(a, b, sems.at[i])
        for i, (a, b) in enumerate(
            (
                (sat, sat_v),
                (hist, hist_v),
                (cell_in, cell_v),
                (index_in, index_v),
                (control_in, control_v),
                (target_in, target_v),
                (pressure, p0e.at[own]),
                (trans.at[0], t0.at[own]),
                (storage, stor.at[own]),
                (trans.at[1], t1.at[own]),
                (trans.at[2], t2.at[own]),
            )
        )
    ]
    for copy in copies:
        copy.start()
    for copy in copies[:2]:
        copy.wait()

    def layer_step(l, carry):
        t, f = mobility(sat_v[l], hist_v[l])
        tote[l + H] = t
        frace[l + H] = f
        return carry

    loop(0, layers, layer_step, 0)
    for copy in copies[2:7]:
        copy.wait()
    perfs, group = cell_v.shape
    cell[...] = flatten(cell_v[...].astype(jnp.float32), spread).astype(jnp.int32)
    wells[0:1, :] = flatten(index_v[...], spread)
    wells[1:2, :] = flatten(jnp.broadcast_to(target_v[...], (perfs, group)), spread)
    wells[2:3, :] = flatten(
        jnp.broadcast_to(control_v[...].astype(jnp.float32), (perfs, group)), spread
    )
    at_place, at_column = one_hots(
        cell[...], lax.axis_index(gz) * layers, layers, rows, columns
    )
    flat = (layers * rows, columns)
    weight = wells[0:1, :] * gather(tote[own].reshape(flat), at_place, at_column)
    cell_p = gather(p0e[own].reshape(flat), at_place, at_column)
    for i, value in enumerate((weight * cell_p, weight)):
        part = value[:, 0:LANES]
        for lane in range(LANES, value.shape[1], LANES):
            part = part + value[:, lane : lane + LANES]
        shift = LANES // 2
        while shift >= group:
            part = part + roll(part, shift, 1)
            shift //= 2
        sums[i : i + 1, :] = part
    for copy in copies[7:]:
        copy.wait()
    even = lax.axis_index(gz) % 2 == 0
    refs = {"p0": p0e, "tot": tote, "t0": t0, "stor": stor, "t1": t1, "t2": t2, "frac": frace}
    for message, is_top in ((near, even), (cross, jnp.logical_not(even))):
        at = 0
        for name, count in Z_PARTS:
            if name == "sums":
                message[at] = jnp.zeros((rows, columns), jnp.float32)
                message[at, 0:2, 0:LANES] = sums[...]
            else:
                edge = jnp.where(is_top, H + layers - count, H)
                message[pl.ds(at, count)] = refs[name][pl.ds(edge, count)]
            at += count


def masks(rows, columns):
    row = lax.broadcasted_iota(jnp.int32, (rows, columns), 0)
    column = lax.broadcasted_iota(jnp.int32, (rows, columns), 1)
    return (row == rows - 1, column == columns - 1)


def lateral_faces(tot, t1, t2, store, last_row, last_column, top_x):
    along = jnp.where(last_row, 0.0, t1) * 0.5 * (tot + roll(tot, -1, 0))
    across = jnp.where(last_column, 0.0, t2) * 0.5 * (tot + roll(tot, -1, 1))
    part = store + along + roll(along, 1, 0) + across + roll(across, 1, 1)
    return (jnp.where(last_row, jnp.where(top_x, 0.0, t1), along), across, part)


def is_last(axis):
    return lax.axis_index(axis) == lax.axis_size(axis) - 1


def faces_kernel(
    p0e, tote, frace, stor, t0, t1, t2, part, f0e, f1e, f2e, dpe, near, cross, sums, *, layers, gx
):
    _, rows, columns = p0e.shape
    last_row, last_column = masks(rows, columns)
    top_x = is_last(gx)

    def step(e, carry):
        tot = tote[e]
        f0e[e] = t0[e] * 0.5 * (tot + tote[e + 1])
        f1e[e], f2e[e], dpe[e] = lateral_faces(
            tot, t1[e], t2[e], stor[e], last_row, last_column, top_x
        )
        return carry

    loop(H, H + layers, step, 0)
    refs = {"t1": f1e, "tot": tote, "p0": p0e, "dp": dpe, "f0": f0e, "f2": f2e, "f1": f1e}
    sums[...] = part[...]
    refs |= {"frac": frace, "f0_d2": f0e, "f2_d2": f2e, "dp_d2": dpe}
    pack_both(near, cross, early_parts(layers), refs, refs, rows, gx)


def well_holes(sums, wells):
    repeat = lambda x: jnp.concatenate([x] * (wells.shape[1] // LANES), axis=1)
    sum_w = repeat(sums[1:2, :])
    sum_w = jnp.where(sum_w > 0.0, sum_w, 1.0)
    goal = wells[1:2, :]
    return jnp.where(wells[2:3, :] == 0.0, (goal + repeat(sums[0:1, :])) / sum_w, goal)


def seam_kernel(near, cross, *seams, layers, gx):
    for seam in seams:
        seam[...] = jnp.zeros(seam.shape, jnp.float32)
    unpack_both(near, cross, early_parts(layers), dict(zip(SEAMS, seams)), gx)


def halo_kernel(*refs, layers, gx, gz):
    own_t0, cross, near, own_sums, cell, wells = refs[8:14]
    p0e, tote, frace, stor, f0e, f1e, f2e, dpe, sums, perfs, hot = refs[14:]
    ext, rows, columns = p0e.shape
    even = lax.axis_index(gz) % 2 == 0
    top_z = is_last(gz)
    top_x = is_last(gx)
    last_row, last_column = masks(rows, columns)
    where = {}
    at = 0
    for name, count in Z_PARTS:
        where[name] = (at, count)
        at += count

    def halo(name, e):
        at, count = where[name]
        low = e < H
        at = at + e - (H - count if low else H + layers)
        one, two = (near[at], cross[at])
        return jnp.where(even, two, one) if low else jnp.where(even, one, two)

    for name, target in (("p0", p0e), ("tot", tote), ("frac", frace), ("stor", stor)):
        count = where[name][1]
        for e in (*range(H - count, H), *range(H + layers, H + layers + count)):
            target[e] = halo(name, e)
    f0e[H + layers - 1] = jnp.where(top_z, 0.0, own_t0[H + layers - 1]) * 0.5 * (
        tote[H + layers - 1] + tote[H + layers]
    )
    for e in (*range(0, H), *range(H + layers, ext - 1)):
        f0e[e] = halo("t0", e) * 0.5 * (tote[e] + tote[e + 1])
    for e in (*range(1, H), *range(H + layers, ext - 1)):
        f1e[e], f2e[e], dpe[e] = lateral_faces(
            tote[e], halo("t1", e), halo("t2", e), stor[e], last_row, last_column, top_x
        )
    at = where["sums"][0]
    sums[...] = own_sums[...] + near[at, 0:2, 0:LANES] + cross[at, 0:2, 0:LANES]
    inner = ext - 2
    at_place, at_column = one_hots(
        cell[...], lax.axis_index(gz) * layers - (H - 1), inner, rows, columns
    )
    flat = (inner * rows, columns)
    perfs[0:1, :] = wells[0:1, :] * gather(tote[1 : ext - 1].reshape(flat), at_place, at_column)
    perfs[1:2, :] = gather(p0e[1 : ext - 1].reshape(flat), at_place, at_column)
    hot[...] = at_place.astype(jnp.bfloat16)


def build_kernel(*refs, layers, gx, far):
    p0e, stor, f0e, f1e, f2e, dpe, tote, near_sums, perfs, hot, cell, wells = refs[:12]
    fars = refs[12 : 12 + far]
    (
        rhse,
        source,
        x_near,
        x_cross,
        own_sums,
        all_sums,
        diage,
        p1,
        rhs1u,
        rhs1d,
        rhs2u,
        rhs2d,
        g2u,
        g2d,
        g3u,
        g3d,
    ) = refs[13 + far :]
    ext, rows, columns = p0e.shape
    last_row, _ = masks(rows, columns)
    own_sums[...] = refs[12 + far][...]
    sums = near_sums[...]
    for ref in fars:
        sums = sums + ref[...]
    all_sums[...] = sums
    rate = perfs[0:1, :] * (well_holes(sums, wells[...]) - perfs[1:2, :])
    column = cell[...] % columns
    at_column = lax.broadcasted_iota(jnp.int32, (columns, cell.shape[1]), 0) == column
    inner = ext - 2
    spread = jnp.zeros((inner * rows, columns), jnp.float32)
    for piece in split(jnp.where(at_column, rate, 0.0)):
        spread = spread + lax.dot_general(
            hot[...], piece, (((1,), (1,)), ((), ())), preferred_element_type=jnp.float32
        )
    spread = spread.reshape(inner, rows, columns)
    rhse[1 : ext - 1] = spread
    source[...] = spread[H - 1 : H - 1 + layers]

    def first_step(e, below):
        above = f0e[e]
        along = jnp.where(last_row, 0.0, f1e[e])
        across = f2e[e]
        diag = dpe[e] + above + below
        diage[e] = diag
        p = p0e[e]
        rhs = stor[e] * p + rhse[e]
        rhse[e] = rhs
        lower = roll(along * p, 1, 0)
        upper = along * roll(p, -1, 0)
        rhs1u[e] = rhs + lower
        rhs1d[e] = rhs + upper
        new = rhs + lower + upper + above * p0e[e + 1] + below * p0e[e - 1]
        new = new + across * roll(p, -1, 1) + roll(across * p, 1, 1)
        p1[e] = jnp.where(diag > 0.0, new / diag, 0.0)
        return above

    loop(1, ext - 1, first_step, f0e[0])

    def second_step(e, carry):
        along = jnp.where(last_row, 0.0, f1e[e])
        across = f2e[e]
        p = p1[e]
        rhs = rhse[e]
        diag = diage[e]
        lower = roll(along * p, 1, 0)
        upper = along * roll(p, -1, 0)
        rhs2u[e] = rhs + lower
        rhs2d[e] = rhs + upper
        part = rhs + f0e[e] * p1[e + 1] + f0e[e - 1] * p1[e - 1]
        part = part + across * roll(p, -1, 1) + roll(across * p, 1, 1)
        g2u[e] = part + lower
        g2d[e] = part + upper
        p2 = jnp.where(diag > 0.0, (part + lower + upper) / diag, 0.0)
        g3u[e] = rhs + roll(along * p2, 1, 0)
        g3d[e] = rhs + along * roll(p2, -1, 0)
        return carry

    loop(2, ext - 2, second_step, 0)

    shared = {"t1": f1e, "tot": tote, "p0": p0e, "dp": dpe, "f0": f0e, "f2": f2e, "f1": f1e}
    shared |= {"f0_d2": f0e, "dp_d2": dpe, "rhs3": rhse}
    up = shared | {"rhs1": rhs1u, "rhs2": rhs2u, "g2": g2u, "g3": g3u}
    down = shared | {"rhs1": rhs1d, "rhs2": rhs2d, "g2": g2d, "g3": g3d}
    pack_both(x_near, x_cross, late_parts(layers), up, down, rows, gx)


def finish_kernel(*refs, gx):
    sat, hist, volume, storage, source = refs[:5]
    p0e, tote, frace, f0e, f1e, f2e, dpe, rhse, near, cross = refs[5:15]
    sums, wells, *ends = refs[15 + len(SEAMS) : -(9 + len(SEAMS))]
    refs = refs[-(9 + len(SEAMS)) :]
    new_p, residual, new_sat, new_hist, bottom = refs[:5]
    seams = dict(zip(SEAMS, refs[5:]))
    pa, pb, f1, rdiag = refs[5 + len(SEAMS) :]
    total = sums[...]
    for ref in ends:
        total = total + ref[...]
    bottom[...] = well_holes(total, wells[...])[:, 0 : bottom.shape[1]]
    layers, rows, columns = sat.shape
    ext = layers + 2 * H
    unpack_both(near, cross, late_parts(layers), seams, gx)
    sf0, sf1, sf2, stot, sdp, sp0, sfrac = (seams[name] for name in SEAMS[:7])

    full = rows + 8
    row = lax.broadcasted_iota(jnp.int32, (full, columns), 0)
    edge = (row == rows - 1) | (row == full - 1)
    beyond = (row == rows + 1) | (row == full - 2)
    join = lambda a, b: jnp.concatenate([a, b], axis=0)

    pa[0] = join(p0e[0], sp0[0])
    pa[ext - 1] = join(p0e[ext - 1], sp0[ext - 1])

    def face_step(e, below):
        tot = join(tote[e], stot[e])
        mixed = join(f1e[e], sf1[e])
        border = jnp.where(edge, mixed * 0.5 * (tot + roll(tot, -1, 0)), 0.0)
        f1[e] = jnp.where(edge, border, mixed)
        above = join(f0e[e], sf0[e])
        diag = join(dpe[e], sdp[e]) + above + below + border + roll(border, 1, 0)
        rdiag[e] = jnp.where(diag > 0.0, 1.0 / diag, 0.0)
        pa[e] = join(p0e[e], sp0[e])
        return above

    loop(1, ext - 1, face_step, join(f0e[0], sf0[0]))

    def sweep(number, old, new, srhs):
        def step(e, below):
            p = old[e]
            above = old[e + 1]
            face = join(f0e[e], sf0[e])
            x = f1[e]
            y = join(f2e[e], sf2[e])
            total = join(rhse[e], srhs[e]) + below + face * above
            total = total + x * roll(p, -1, 0) + roll(x * p, 1, 0)
            total = total + y * roll(p, -1, 1) + roll(y * p, 1, 1)
            value = total * rdiag[e]
            if number == 1:
                value = jnp.where(beyond, 0.0, value)
            new[e] = value
            return face * p

        first = join(f0e[number - 1], sf0[number - 1]) * old[number - 1]
        loop(number, ext - number, step, first)

    fields = (pa, pb)
    for number in range(1, SWEEPS + 1):
        sweep(
            number,
            fields[(number - 1) % 2],
            fields[number % 2],
            seams[f"rhs{min(number, 3)}"],
        )
    field = fields[SWEEPS % 2]

    def flow(face, p, p_next, f, f_next):
        water = face * (p - p_next)
        return (water, water * jnp.where(water > 0, f, f_next))

    def last_step(l, carry):
        below_w, below_g = carry
        e = l + H
        p = field[e]
        f = join(frace[e], sfrac[e])
        own_p = p[:rows]
        own_f = f[:rows]
        above_w, above_g = flow(f0e[e], own_p, field[e + 1][:rows], own_f, frace[e + 1])
        xw, xg = flow(f1[e], p, roll(p, -1, 0), f, roll(f, -1, 0))
        yw, yg = flow(f2e[e], own_p, roll(own_p, -1, 1), own_f, roll(own_f, -1, 1))
        water = above_w - below_w + (xw - roll(xw, 1, 0))[:rows] + yw - roll(yw, 1, 1)
        out = above_g - below_g + (xg - roll(xg, 1, 0))[:rows] + yg - roll(yg, 1, 1)
        new_p[l] = own_p
        residual[l] = rhse[e] - storage[l] * own_p - water
        src = source[l]
        gas = jnp.maximum(src, 0.0) + jnp.minimum(src, 0.0) * own_f
        s = sat[l] + volume[l] * (gas - out)
        new_sat[l] = s
        new_hist[l] = jnp.maximum(hist[l], s)
        return (above_w, above_g)

    first = flow(f0e[H - 1], field[H - 1][:rows], field[H][:rows], frace[H - 1], frace[H])
    loop(0, layers, last_step, first)


def swap(block, axis, first):
    pairs = [(i, i + 1) for i in range(first, lax.axis_size(axis) - 1, 2)]
    return lax.ppermute(block, axis, pairs + [(b, a) for a, b in pairs])


def from_blocks(part, axis, step):
    count = lax.axis_size(axis)
    up = [(i, i + step) for i in range(count - step)]
    down = [(b, a) for a, b in up]
    if 2 * step >= count:
        return [lax.ppermute(part, axis, up + down)] if up else []
    return [lax.ppermute(part, axis, up), lax.ppermute(part, axis, down)]


def pin(*shape, dtype=jnp.float32):
    return pltpu.VMEM(shape, dtype)


VMEM = pl.BlockSpec(memory_space=pltpu.VMEM)
HBM = pl.BlockSpec(memory_space=pltpu.HBM)


def call(kernel, outs, scratch, *args, space=VMEM, sems=0, aliases={}):
    as_struct = lambda s: s if hasattr(s, "dtype") else jax.ShapeDtypeStruct(s, jnp.float32)
    as_scratch = lambda s: pltpu.VMEM(as_struct(s).shape, as_struct(s).dtype)
    return pl.pallas_call(
        kernel,
        out_shape=[as_struct(s) for s in outs],
        in_specs=[space] * len(args),
        out_specs=[VMEM] * len(outs),
        scratch_shapes=[as_scratch(s) for s in scratch]
        + ([pltpu.SemaphoreType.DMA((sems,))] if sems else []),
        input_output_aliases=aliases,
        compiler_params=pltpu.CompilerParams(vmem_limit_bytes=24 * 1024 * 1024),
    )(*(pltpu.with_memory_space_constraint(a, pltpu.HBM) if space is HBM else a for a in args))


def body(
    pressure,
    saturation,
    sat_history,
    storage,
    step_volume,
    transmiss,
    perf_cell,
    perf_index,
    control,
    target,
):
    layers, rows, columns = pressure.shape
    ext = layers + 2 * H
    wells, perfs = perf_cell.shape
    block = (layers, rows, columns)
    pinned = pin(*block)
    ext_block = pin(ext, rows, columns)
    z_message = (sum(count for _, count in Z_PARTS), rows, columns)
    entries = wells * perfs
    early, late = ((tiles(f(layers)), 8, columns) for f in (early_parts, late_parts))
    seams = [pin(ext, 8, columns)] * len(SEAMS)
    *fields, near, cross, part, cell, per_perf = call(
        functools.partial(prepare_kernel, gz="gz"),
        [ext_block] * 7
        + [z_message] * 2
        + [(2, LANES), pin(1, entries, dtype=jnp.int32), pin(3, entries)],
        [
            block,
            block,
            jax.ShapeDtypeStruct((perfs, wells), jnp.int32),
            (perfs, wells),
            jax.ShapeDtypeStruct((1, wells), jnp.int32),
            (1, wells),
            (perfs, LANES),
        ],
        saturation,
        sat_history,
        pressure,
        storage,
        transmiss,
        perf_cell.T,
        perf_index.T,
        control.reshape(1, wells),
        target.reshape(1, wells),
        space=HBM,
        sems=11,
    )
    cross = swap(cross, "gz", 1)
    near = swap(near, "gz", 0)
    p0e, tote, frace, stor, t0, t1, t2 = fields
    f0e, f1e, f2e, dpe, early_near, early_cross, part = call(
        functools.partial(faces_kernel, layers=layers, gx="gx"),
        [ext_block] * 4 + [early, early, (2, LANES)],
        [],
        *fields,
        part,
    )
    early_cross = swap(early_cross, "gx", 1)
    early_near = swap(early_near, "gx", 0)
    far = from_blocks(part, "gz", 2)
    p0e, tote, frace, stor, f0e, f1e, f2e, dpe, sums, perf_values, hot = call(
        functools.partial(halo_kernel, layers=layers, gx="gx", gz="gz"),
        [ext_block] * 8
        + [
            pin(2, LANES),
            pin(2, entries),
            pin((ext - 2) * rows, entries, dtype=jnp.bfloat16),
        ],
        [],
        p0e,
        tote,
        frace,
        stor,
        f0e,
        f1e,
        f2e,
        dpe,
        t0,
        cross,
        near,
        part,
        cell,
        per_perf,
        aliases={i: i for i in range(8)},
    )
    rhse, source, late_near, late_cross, part, sums = call(
        functools.partial(build_kernel, layers=layers, gx="gx", far=len(far)),
        [ext_block, pinned, late, late, (2, LANES), pin(2, LANES)],
        [ext_block] * 10,
        p0e,
        stor,
        f0e,
        f1e,
        f2e,
        dpe,
        tote,
        sums,
        perf_values,
        hot,
        cell,
        per_perf,
        *far,
        part,
    )
    late_cross = swap(late_cross, "gx", 1)
    late_near = swap(late_near, "gx", 0)
    early_near, early_cross, rhse, part = lax.optimization_barrier(
        (early_near, early_cross, rhse, part)
    )
    ends = [x for step in range(3, lax.axis_size("gz")) for x in from_blocks(part, "gz", step)]
    filled = call(
        functools.partial(seam_kernel, layers=layers, gx="gx"), seams, [], early_near, early_cross
    )
    field, residual, new_sat, new_hist, hole, *_ = call(
        functools.partial(finish_kernel, gx="gx"),
        [block] * 4 + [(1, wells)] + seams,
        [(ext, rows + 8, columns)] * 4,
        saturation,
        sat_history,
        step_volume,
        storage,
        source,
        p0e,
        tote,
        frace,
        f0e,
        f1e,
        f2e,
        dpe,
        rhse,
        late_near,
        late_cross,
        *filled,
        sums,
        per_perf,
        *ends,
        aliases={15 + i: 5 + i for i in range(len(SEAMS))},
    )
    return (field, residual, new_sat, new_hist, hole.reshape(wells))


def solution(mesh):
    return jax.shard_map(
        body,
        mesh=mesh,
        in_specs=(
            P("gz", "gx", None),
            P("gz", "gx", None),
            P("gz", "gx", None),
            P("gz", "gx", None),
            P("gz", "gx", None),
            P(None, "gz", "gx", None),
            P("gx", None),
            P("gx", None),
            P("gx"),
            P("gx"),
        ),
        out_specs=(
            P("gz", "gx", None),
            P("gz", "gx", None),
            P("gz", "gx", None),
            P("gz", "gx", None),
            P("gx"),
        ),
        check_vma=False,
    )
```

```python
import functools

import jax
import jax.numpy as jnp
from jax import lax
from jax.experimental import pallas as pl
from jax.experimental.pallas import tpu as pltpu
from jax.sharding import PartitionSpec as P

SWEEPS = 4
H = SWEEPS + 1
LANES = 128

Z_PARTS = (
    ("p0", H),
    ("tot", H),
    ("t0", H),
    ("stor", H - 1),
    ("t1", H - 1),
    ("t2", H - 1),
    ("frac", 1),
    ("sums", 1),
)


def early_parts(layers):
    own = (H, layers)
    inner = (H, layers - 1)
    return (
        ("t1", *own),
        ("tot", *own),
        ("p0", *own),
        ("dp", *own),
        ("f0", *inner),
        ("f2", *own),
        ("f1", *own),
        ("frac", *own),
        ("p0_d2", *own),
        ("f0_d2", *inner),
        ("f2_d2", *own),
        ("dp_d2", *own),
    )


def late_parts(layers):
    top = H + layers
    both = lambda name, n: ((name, H - n, n), (name, top, n))
    faces = lambda name, n: ((name, H - n, n), (name, top - 1, n))
    return (
        ("rhs", 2, layers + 6),
        ("p1_d2", 3, layers + 4),
        ("g2", 4, layers + 2),
        ("g3", H, layers),
        *both("t1", H - 1),
        *both("tot", H - 1),
        *both("p0", H - 1),
        *both("dp", H - 2),
        *faces("f0", H - 1),
        *both("f2", H - 2),
        *both("f1", H - 2),
        *both("p0_d2", H - 2),
        *faces("f0_d2", 2),
        *both("f2_d2", 1),
        *both("dp_d2", 1),
    )


def tiles(parts):
    return -(-sum(count for _, _, count in parts) // 8)


SEAMS = ("f0", "f1", "f2", "tot", "dp", "p0", "frac", "p1", "rhs2", "rhs3")
PLACES = {
    "t1": ("f1", None, 7),
    "f1": ("f1", 0, 6),
    "tot": ("tot", 0, 7),
    "p0": ("p0", 0, 7),
    "dp": ("dp", 0, 7),
    "dp_d2": ("dp", 1, 6),
    "f0": ("f0", 0, 7),
    "f0_d2": ("f0", 1, 6),
    "f2": ("f2", 0, 7),
    "f2_d2": ("f2", 1, 6),
    "frac": ("frac", 0, 7),
    "p0_d2": ("p0", 1, 6),
    "p1_d2": ("p1", 1, 6),
    "rhs": ("rhs2", 0, 7),
    "g2": ("rhs2", 1, 6),
    "g3": ("rhs3", 1, 6),
}


def pack(message, parts, refs, rows):
    at = 0
    for name, first, count in parts:
        for e in range(first, first + count):
            message[at // 8, at % 8 : at % 8 + 1, :] = refs[name][e, rows[name] : rows[name] + 1, :]
            at += 1


def pack_both(near, cross, parts, up, down, rows, gx):
    last = rows - 1
    outer = {name: 0 if PLACES[name][2] == 7 else 1 for name in PLACES}
    up_rows = {name: last - outer[name] for name in PLACES} | {"f1": last - 1}
    down_rows = dict(outer) | {"f1": 0}
    even = lax.axis_index(gx) % 2 == 0

    @pl.when(even)
    def _():
        pack(near, parts, up, up_rows)
        pack(cross, parts, down, down_rows)

    @pl.when(jnp.logical_not(even))
    def _():
        pack(cross, parts, up, up_rows)
        pack(near, parts, down, down_rows)


def unpack(message, parts, seams, side):
    at = 0
    for name, first, count in parts:
        seam, *places = PLACES[name]
        place = places[side]
        for e in range(first, first + count):
            if place is not None:
                seams[seam][e, place : place + 1, :] = message[at // 8, at % 8 : at % 8 + 1, :]
            at += 1


def unpack_both(near, cross, parts, seams, gx):
    even = lax.axis_index(gx) % 2 == 0

    @pl.when(even)
    def _():
        unpack(near, parts, seams, 0)
        unpack(cross, parts, seams, 1)

    @pl.when(jnp.logical_not(even))
    def _():
        unpack(cross, parts, seams, 0)
        unpack(near, parts, seams, 1)


def mobility(sat, history):
    trapped = history / (1.0 + 1.5 * history)
    excess = jnp.maximum(sat - trapped, 0.0)
    free_gas = 0.5 * (excess + jnp.sqrt(excess * excess + excess / 0.375))
    relperm = jnp.where(sat < history, free_gas * free_gas, sat * sat)
    gas = relperm / 0.5
    total = (1.0 - sat) * (1.0 - sat) + gas
    return (total, gas / total)


def roll(x, shift, axis):
    return pltpu.roll(x, shift % x.shape[axis], axis)


def loop(first, last, step, carry, unroll=4):
    groups = (last - first) // unroll

    def group(g, carry):
        for i in range(unroll):
            carry = step(first + g * unroll + i, carry)
        return carry

    carry = lax.fori_loop(0, groups, group, carry)
    for index in range(first + groups * unroll, last):
        carry = step(index, carry)
    return carry


def split(x):
    high = x.astype(jnp.bfloat16)
    return (high, (x - high.astype(jnp.float32)).astype(jnp.bfloat16))


def one_hots(cell, first_layer, layers, rows, columns):
    count = cell.shape[1]
    layer = cell // (rows * columns)
    rest = cell - layer * (rows * columns)
    row = rest // columns
    column = rest - row * columns
    place = (layer - first_layer) * rows + row
    at_place = lax.broadcasted_iota(jnp.int32, (layers * rows, count), 0) == place
    at_column = lax.broadcasted_iota(jnp.int32, (columns, count), 0) == column
    return (at_place, at_column)


def gather(field, at_place, at_column):
    high, low = split(field)
    hot = at_column.astype(jnp.bfloat16)
    by_column = jnp.dot(high, hot, preferred_element_type=jnp.float32) + jnp.dot(
        low, hot, preferred_element_type=jnp.float32
    )
    return jnp.sum(jnp.where(at_place, by_column, 0.0), axis=0, keepdims=True)


def flatten(block, spread):
    perfs, wells = block.shape
    spread[...] = jnp.zeros(spread.shape, jnp.float32)
    spread[:, 0:wells] = block
    wide = spread[...]
    shift = wells
    while shift < LANES:
        wide = wide + roll(wide, shift, 1)
        shift *= 2
    each = LANES // wells
    entry = lax.broadcasted_iota(jnp.int32, (perfs, LANES), 0)
    group = lax.broadcasted_iota(jnp.int32, (perfs, LANES), 1) // wells
    tiles = [
        jnp.sum(jnp.where(entry == first + group, wide, 0.0), axis=0, keepdims=True)
        for first in range(0, perfs, each)
    ]
    return jnp.concatenate(tiles, axis=1)


def prepare_kernel(
    sat,
    hist,
    pressure,
    storage,
    trans,
    cell_in,
    index_in,
    control_in,
    target_in,
    p0e,
    tote,
    frace,
    stor,
    t0,
    t1,
    t2,
    near,
    cross,
    sums,
    cell,
    wells,
    sat_v,
    hist_v,
    cell_v,
    index_v,
    control_v,
    target_v,
    spread,
    sems,
    *,
    gz,
):
    layers, rows, columns = pressure.shape
    ext = layers + 2 * H
    own = pl.ds(H, layers)
    copies = [
        pltpu.make_async_copy(a, b, sems.at[i])
        for i, (a, b) in enumerate(
            (
                (sat, sat_v),
                (hist, hist_v),
                (cell_in, cell_v),
                (index_in, index_v),
                (control_in, control_v),
                (target_in, target_v),
                (pressure, p0e.at[own]),
                (trans.at[0], t0.at[own]),
                (storage, stor.at[own]),
                (trans.at[1], t1.at[own]),
                (trans.at[2], t2.at[own]),
            )
        )
    ]
    for copy in copies:
        copy.start()
    for copy in copies[:2]:
        copy.wait()

    def layer_step(l, carry):
        t, f = mobility(sat_v[l], hist_v[l])
        tote[l + H] = t
        frace[l + H] = f
        return carry

    loop(0, layers, layer_step, 0)
    for copy in copies[2:7]:
        copy.wait()
    perfs, group = cell_v.shape
    cell[...] = flatten(cell_v[...].astype(jnp.float32), spread).astype(jnp.int32)
    wells[0:1, :] = flatten(index_v[...], spread)
    wells[1:2, :] = flatten(jnp.broadcast_to(target_v[...], (perfs, group)), spread)
    wells[2:3, :] = flatten(
        jnp.broadcast_to(control_v[...].astype(jnp.float32), (perfs, group)), spread
    )
    at_place, at_column = one_hots(
        cell[...], lax.axis_index(gz) * layers, layers, rows, columns
    )
    flat = (layers * rows, columns)
    weight = wells[0:1, :] * gather(tote[own].reshape(flat), at_place, at_column)
    cell_p = gather(p0e[own].reshape(flat), at_place, at_column)
    for i, value in enumerate((weight * cell_p, weight)):
        part = value[:, 0:LANES]
        for lane in range(LANES, value.shape[1], LANES):
            part = part + value[:, lane : lane + LANES]
        shift = LANES // 2
        while shift >= group:
            part = part + roll(part, shift, 1)
            shift //= 2
        sums[i : i + 1, :] = part
    for copy in copies[7:]:
        copy.wait()
    even = lax.axis_index(gz) % 2 == 0
    refs = {"p0": p0e, "tot": tote, "t0": t0, "stor": stor, "t1": t1, "t2": t2, "frac": frace}
    for message, is_top in ((near, even), (cross, jnp.logical_not(even))):
        at = 0
        for name, count in Z_PARTS:
            if name == "sums":
                message[at] = jnp.zeros((rows, columns), jnp.float32)
                message[at, 0:2, 0:LANES] = sums[...]
            else:
                edge = jnp.where(is_top, H + layers - count, H)
                message[pl.ds(at, count)] = refs[name][pl.ds(edge, count)]
            at += count


def masks(rows, columns):
    row = lax.broadcasted_iota(jnp.int32, (rows, columns), 0)
    column = lax.broadcasted_iota(jnp.int32, (rows, columns), 1)
    return (row == rows - 1, column == columns - 1)


def lateral_faces(tot, t1, t2, store, last_row, last_column, top_x):
    along = jnp.where(last_row, 0.0, t1) * 0.5 * (tot + roll(tot, -1, 0))
    across = jnp.where(last_column, 0.0, t2) * 0.5 * (tot + roll(tot, -1, 1))
    part = store + along + roll(along, 1, 0) + across + roll(across, 1, 1)
    return (jnp.where(last_row, jnp.where(top_x, 0.0, t1), along), across, part)


def is_last(axis):
    return lax.axis_index(axis) == lax.axis_size(axis) - 1


def faces_kernel(
    p0e, tote, frace, stor, t0, t1, t2, f0e, f1e, f2e, dpe, near, cross, *, layers, gx
):
    _, rows, columns = p0e.shape
    last_row, last_column = masks(rows, columns)
    top_x = is_last(gx)

    def step(e, carry):
        tot = tote[e]
        f0e[e] = t0[e] * 0.5 * (tot + tote[e + 1])
        f1e[e], f2e[e], dpe[e] = lateral_faces(
            tot, t1[e], t2[e], stor[e], last_row, last_column, top_x
        )
        return carry

    loop(H, H + layers, step, 0)
    refs = {"t1": f1e, "tot": tote, "p0": p0e, "dp": dpe, "f0": f0e, "f2": f2e, "f1": f1e}
    refs |= {"frac": frace, "p0_d2": p0e, "f0_d2": f0e, "f2_d2": f2e, "dp_d2": dpe}
    pack_both(near, cross, early_parts(layers), refs, refs, rows, gx)


def well_holes(sums, wells):
    repeat = lambda x: jnp.concatenate([x] * (wells.shape[1] // LANES), axis=1)
    sum_w = repeat(sums[1:2, :])
    sum_w = jnp.where(sum_w > 0.0, sum_w, 1.0)
    goal = wells[1:2, :]
    return jnp.where(wells[2:3, :] == 0.0, (goal + repeat(sums[0:1, :])) / sum_w, goal)


def seam_kernel(cross, near, *seams, layers, gx):
    for seam in seams:
        seam[...] = jnp.zeros(seam.shape, jnp.float32)
    unpack_both(near, cross, early_parts(layers), dict(zip(SEAMS, seams)), gx)


def halo_kernel(*refs, layers, gx, gz):
    own_t0, near, cross, own_sums, cell, wells = refs[8:14]
    p0e, tote, frace, stor, f0e, f1e, f2e, dpe, sums, perfs, hot = refs[14:]
    ext, rows, columns = p0e.shape
    even = lax.axis_index(gz) % 2 == 0
    top_z = is_last(gz)
    top_x = is_last(gx)
    last_row, last_column = masks(rows, columns)
    where = {}
    at = 0
    for name, count in Z_PARTS:
        where[name] = (at, count)
        at += count

    def halo(name, e):
        at, count = where[name]
        low = e < H
        at = at + e - (H - count if low else H + layers)
        one, two = (near[at], cross[at])
        return jnp.where(even, two, one) if low else jnp.where(even, one, two)

    for name, target in (("p0", p0e), ("tot", tote), ("frac", frace), ("stor", stor)):
        count = where[name][1]
        for e in (*range(H - count, H), *range(H + layers, H + layers + count)):
            target[e] = halo(name, e)
    f0e[H + layers - 1] = jnp.where(top_z, 0.0, own_t0[H + layers - 1]) * 0.5 * (
        tote[H + layers - 1] + tote[H + layers]
    )
    for e in (*range(0, H), *range(H + layers, ext - 1)):
        f0e[e] = halo("t0", e) * 0.5 * (tote[e] + tote[e + 1])
    for e in (*range(1, H), *range(H + layers, ext - 1)):
        f1e[e], f2e[e], dpe[e] = lateral_faces(
            tote[e], halo("t1", e), halo("t2", e), stor[e], last_row, last_column, top_x
        )
    at = where["sums"][0]
    sums[...] = own_sums[...] + near[at, 0:2, 0:LANES] + cross[at, 0:2, 0:LANES]
    inner = ext - 2
    at_place, at_column = one_hots(
        cell[...], lax.axis_index(gz) * layers - (H - 1), inner, rows, columns
    )
    flat = (inner * rows, columns)
    perfs[0:1, :] = wells[0:1, :] * gather(tote[1 : ext - 1].reshape(flat), at_place, at_column)
    perfs[1:2, :] = gather(p0e[1 : ext - 1].reshape(flat), at_place, at_column)
    hot[...] = at_place.astype(jnp.bfloat16)


def build_kernel(*refs, layers, gx, far):
    p0e, stor, f0e, f1e, f2e, dpe, tote, near_sums, perfs, hot, cell, wells = refs[:12]
    fars = refs[12 : 12 + far]
    rhse, source, x_near, x_cross, bottom, diage, p1, g2u, g2d, g3u, g3d = refs[12 + far :]
    ext, rows, columns = p0e.shape
    last_row, _ = masks(rows, columns)
    sums = near_sums[...]
    for ref in fars:
        sums = sums + ref[...]
    hole = well_holes(sums, wells[...])
    bottom[...] = hole[:, 0 : bottom.shape[1]]
    rate = perfs[0:1, :] * (hole - perfs[1:2, :])
    column = cell[...] % columns
    at_column = lax.broadcasted_iota(jnp.int32, (columns, cell.shape[1]), 0) == column
    inner = ext - 2
    spread = jnp.zeros((inner * rows, columns), jnp.float32)
    for piece in split(jnp.where(at_column, rate, 0.0)):
        spread = spread + lax.dot_general(
            hot[...], piece, (((1,), (1,)), ((), ())), preferred_element_type=jnp.float32
        )
    spread = spread.reshape(inner, rows, columns)
    rhse[1 : ext - 1] = spread
    source[...] = spread[H - 1 : H - 1 + layers]

    def first_step(e, below):
        above = f0e[e]
        along = jnp.where(last_row, 0.0, f1e[e])
        across = f2e[e]
        diag = dpe[e] + above + below
        diage[e] = diag
        p = p0e[e]
        rhs = stor[e] * p + rhse[e]
        rhse[e] = rhs
        new = rhs + above * p0e[e + 1] + below * p0e[e - 1]
        new = new + along * roll(p, -1, 0) + roll(along * p, 1, 0)
        new = new + across * roll(p, -1, 1) + roll(across * p, 1, 1)
        p1[e] = jnp.where(diag > 0.0, new / diag, 0.0)
        return above

    loop(1, ext - 1, first_step, f0e[0])

    def second_step(e, carry):
        along = jnp.where(last_row, 0.0, f1e[e])
        across = f2e[e]
        p = p1[e]
        rhs = rhse[e]
        diag = diage[e]
        lower = roll(along * p, 1, 0)
        upper = along * roll(p, -1, 0)
        g2u[e] = rhs + lower
        g2d[e] = rhs + upper
        new = rhs + lower + upper + f0e[e] * p1[e + 1] + f0e[e - 1] * p1[e - 1]
        new = new + across * roll(p, -1, 1) + roll(across * p, 1, 1)
        p2 = jnp.where(diag > 0.0, new / diag, 0.0)
        g3u[e] = rhs + roll(along * p2, 1, 0)
        g3d[e] = rhs + along * roll(p2, -1, 0)
        return carry

    loop(H - 1, ext - H + 1, second_step, 0)

    shared = {"t1": f1e, "tot": tote, "p0": p0e, "dp": dpe, "f0": f0e, "f2": f2e, "f1": f1e}
    shared |= {"p0_d2": p0e, "f0_d2": f0e, "f2_d2": f2e, "dp_d2": dpe, "rhs": rhse, "p1_d2": p1}
    up = shared | {"g2": g2u, "g3": g3u}
    down = shared | {"g2": g2d, "g3": g3d}
    pack_both(x_near, x_cross, late_parts(layers), up, down, rows, gx)


def finish_kernel(*refs, gx):
    sat, hist, volume, storage, source = refs[:5]
    p0e, tote, frace, f0e, f1e, f2e, dpe, rhse, cross, near = refs[5:15]
    refs = refs[15 + len(SEAMS) :]
    new_p, residual, new_sat, new_hist = refs[:4]
    seams = dict(zip(SEAMS, refs[4:]))
    pa, pb, f1, rdiag = refs[4 + len(SEAMS) :]
    layers, rows, columns = sat.shape
    ext = layers + 2 * H
    unpack_both(near, cross, late_parts(layers), seams, gx)
    sf0, sf1, sf2, stot, sdp, sp0, sfrac = (seams[name] for name in SEAMS[:7])

    full = rows + 8
    row = lax.broadcasted_iota(jnp.int32, (full, columns), 0)
    edge = (row == rows - 1) | (row == full - 1)
    beyond = (row == rows + 1) | (row == full - 2)
    join = lambda a, b: jnp.concatenate([a, b], axis=0)
    blank = jnp.zeros((rows, columns), jnp.float32)

    pa[0] = join(p0e[0], sp0[0])
    pa[ext - 1] = join(p0e[ext - 1], sp0[ext - 1])

    def face_step(e, below):
        tot = join(tote[e], stot[e])
        mixed = join(f1e[e], sf1[e])
        border = jnp.where(edge, mixed * 0.5 * (tot + roll(tot, -1, 0)), 0.0)
        f1[e] = jnp.where(edge, border, mixed)
        above = join(f0e[e], sf0[e])
        diag = join(dpe[e], sdp[e]) + above + below + border + roll(border, 1, 0)
        rdiag[e] = jnp.where(diag > 0.0, 1.0 / diag, 0.0)
        pa[e] = join(p0e[e], sp0[e])
        return above

    loop(1, ext - 1, face_step, join(f0e[0], sf0[0]))

    def sweep(number, old, new):
        def step(e, below):
            p = old[e]
            above = old[e + 1]
            face = join(f0e[e], sf0[e])
            x = f1[e]
            y = join(f2e[e], sf2[e])
            side = seams["rhs2"][e]
            if number == 3:
                side = jnp.where(beyond[rows:], seams["rhs3"][e], side)
            total = join(rhse[e], side) + below + face * above
            total = total + x * roll(p, -1, 0) + roll(x * p, 1, 0)
            total = total + y * roll(p, -1, 1) + roll(y * p, 1, 1)
            value = total * rdiag[e]
            if number == 1:
                value = jnp.where(beyond, join(blank, seams["p1"][e]), value)
            new[e] = value
            return face * p

        first = join(f0e[number - 1], sf0[number - 1]) * old[number - 1]
        loop(number, ext - number, step, first)

    fields = (pa, pb)
    for number in range(1, SWEEPS + 1):
        sweep(number, fields[(number - 1) % 2], fields[number % 2])
    field = fields[SWEEPS % 2]

    def flow(face, p, p_next, f, f_next):
        water = face * (p - p_next)
        return (water, water * jnp.where(water > 0, f, f_next))

    def last_step(l, carry):
        below_w, below_g = carry
        e = l + H
        p = field[e]
        f = join(frace[e], sfrac[e])
        own_p = p[:rows]
        own_f = f[:rows]
        above_w, above_g = flow(f0e[e], own_p, field[e + 1][:rows], own_f, frace[e + 1])
        xw, xg = flow(f1[e], p, roll(p, -1, 0), f, roll(f, -1, 0))
        yw, yg = flow(f2e[e], own_p, roll(own_p, -1, 1), own_f, roll(own_f, -1, 1))
        water = above_w - below_w + (xw - roll(xw, 1, 0))[:rows] + yw - roll(yw, 1, 1)
        out = above_g - below_g + (xg - roll(xg, 1, 0))[:rows] + yg - roll(yg, 1, 1)
        new_p[l] = own_p
        residual[l] = rhse[e] - storage[l] * own_p - water
        src = source[l]
        gas = jnp.maximum(src, 0.0) + jnp.minimum(src, 0.0) * own_f
        s = sat[l] + volume[l] * (gas - out)
        new_sat[l] = s
        new_hist[l] = jnp.maximum(hist[l], s)
        return (above_w, above_g)

    first = flow(f0e[H - 1], field[H - 1][:rows], field[H][:rows], frace[H - 1], frace[H])
    loop(0, layers, last_step, first)


def swap(block, axis, first):
    pairs = [(i, i + 1) for i in range(first, lax.axis_size(axis) - 1, 2)]
    return lax.ppermute(block, axis, pairs + [(b, a) for a, b in pairs])


def from_blocks(part, axis, step):
    count = lax.axis_size(axis)
    up = [(i, i + step) for i in range(count - step)]
    down = [(b, a) for a, b in up]
    if 2 * step >= count:
        return [lax.ppermute(part, axis, up + down)] if up else []
    return [lax.ppermute(part, axis, up), lax.ppermute(part, axis, down)]


def pin(*shape, dtype=jnp.float32):
    return pltpu.VMEM(shape, dtype)


VMEM = pl.BlockSpec(memory_space=pltpu.VMEM)
HBM = pl.BlockSpec(memory_space=pltpu.HBM)


def call(kernel, outs, scratch, *args, space=VMEM, sems=0, aliases={}):
    as_struct = lambda s: s if hasattr(s, "dtype") else jax.ShapeDtypeStruct(s, jnp.float32)
    as_scratch = lambda s: pltpu.VMEM(as_struct(s).shape, as_struct(s).dtype)
    return pl.pallas_call(
        kernel,
        out_shape=[as_struct(s) for s in outs],
        in_specs=[space] * len(args),
        out_specs=[VMEM] * len(outs),
        scratch_shapes=[as_scratch(s) for s in scratch]
        + ([pltpu.SemaphoreType.DMA((sems,))] if sems else []),
        input_output_aliases=aliases,
        compiler_params=pltpu.CompilerParams(vmem_limit_bytes=24 * 1024 * 1024),
    )(*(pltpu.with_memory_space_constraint(a, pltpu.HBM) if space is HBM else a for a in args))


def body(
    pressure,
    saturation,
    sat_history,
    storage,
    step_volume,
    transmiss,
    perf_cell,
    perf_index,
    control,
    target,
):
    layers, rows, columns = pressure.shape
    ext = layers + 2 * H
    wells, perfs = perf_cell.shape
    block = (layers, rows, columns)
    pinned = pin(*block)
    ext_block = pin(ext, rows, columns)
    z_message = (sum(count for _, count in Z_PARTS), rows, columns)
    entries = wells * perfs
    early, late = ((tiles(f(layers)), 8, columns) for f in (early_parts, late_parts))
    seams = [pin(ext, 8, columns)] * len(SEAMS)
    *fields, near, cross, part, cell, per_perf = call(
        functools.partial(prepare_kernel, gz="gz"),
        [ext_block] * 7
        + [z_message] * 2
        + [(2, LANES), pin(1, entries, dtype=jnp.int32), pin(3, entries)],
        [
            block,
            block,
            jax.ShapeDtypeStruct((perfs, wells), jnp.int32),
            (perfs, wells),
            jax.ShapeDtypeStruct((1, wells), jnp.int32),
            (1, wells),
            (perfs, LANES),
        ],
        saturation,
        sat_history,
        pressure,
        storage,
        transmiss,
        perf_cell.T,
        perf_index.T,
        control.reshape(1, wells),
        target.reshape(1, wells),
        space=HBM,
        sems=11,
    )
    cross = swap(cross, "gz", 1)
    near = swap(near, "gz", 0)
    p0e, tote, frace, stor, t0, t1, t2 = fields
    f0e, f1e, f2e, dpe, early_near, early_cross = call(
        functools.partial(faces_kernel, layers=layers, gx="gx"),
        [ext_block] * 4 + [early, early],
        [],
        *fields,
    )
    early_cross = swap(early_cross, "gx", 1)
    early_near = swap(early_near, "gx", 0)
    far = [x for step in reversed(range(2, lax.axis_size("gz"))) for x in from_blocks(part, "gz", step)]
    p0e, tote, frace, stor, f0e, f1e, f2e, dpe, sums, perf_values, hot = call(
        functools.partial(halo_kernel, layers=layers, gx="gx", gz="gz"),
        [ext_block] * 8
        + [
            pin(2, LANES),
            pin(2, entries),
            pin((ext - 2) * rows, entries, dtype=jnp.bfloat16),
        ],
        [],
        p0e,
        tote,
        frace,
        stor,
        f0e,
        f1e,
        f2e,
        dpe,
        t0,
        near,
        cross,
        part,
        cell,
        per_perf,
        aliases={i: i for i in range(8)},
    )
    rhse, source, late_near, late_cross, hole = call(
        functools.partial(build_kernel, layers=layers, gx="gx", far=len(far)),
        [ext_block, pinned, late, late, (1, wells)],
        [ext_block] * 6,
        p0e,
        stor,
        f0e,
        f1e,
        f2e,
        dpe,
        tote,
        sums,
        perf_values,
        hot,
        cell,
        per_perf,
        *far,
    )
    late_cross = swap(late_cross, "gx", 1)
    late_near = swap(late_near, "gx", 0)
    early_cross, early_near, rhse = lax.optimization_barrier((early_cross, early_near, rhse))
    filled = call(
        functools.partial(seam_kernel, layers=layers, gx="gx"), seams, [], early_cross, early_near
    )
    field, residual, new_sat, new_hist, *_ = call(
        functools.partial(finish_kernel, gx="gx"),
        [block] * 4 + seams,
        [(ext, rows + 8, columns)] * 4,
        saturation,
        sat_history,
        step_volume,
        storage,
        source,
        p0e,
        tote,
        frace,
        f0e,
        f1e,
        f2e,
        dpe,
        rhse,
        late_cross,
        late_near,
        *filled,
        aliases={15 + i: 4 + i for i in range(len(SEAMS))},
    )
    return (field, residual, new_sat, new_hist, hole.reshape(wells))


def solution(mesh):
    return jax.shard_map(
        body,
        mesh=mesh,
        in_specs=(
            P("gz", "gx", None),
            P("gz", "gx", None),
            P("gz", "gx", None),
            P("gz", "gx", None),
            P("gz", "gx", None),
            P(None, "gz", "gx", None),
            P("gx", None),
            P("gx", None),
            P("gx"),
            P("gx"),
        ),
        out_specs=(
            P("gz", "gx", None),
            P("gz", "gx", None),
            P("gz", "gx", None),
            P("gz", "gx", None),
            P("gx"),
        ),
        check_vma=False,
    )
```

```python
import functools

import jax
import jax.numpy as jnp
from jax import lax
from jax.experimental import pallas as pl
from jax.experimental.pallas import tpu as pltpu
from jax.sharding import PartitionSpec as P

SWEEPS = 4
H = SWEEPS + 1
LANES = 128

Z_PARTS = (
    ("p0", H),
    ("tot", H),
    ("t0", H),
    ("stor", H - 1),
    ("t1", H - 1),
    ("t2", H - 1),
    ("frac", 1),
    ("sums", 1),
)


def early_parts(layers):
    own = (H, layers)
    inner = (H, layers - 1)
    return (
        ("t1", *own),
        ("tot", *own),
        ("p0", *own),
        ("dp", *own),
        ("f0", *inner),
        ("f2", *own),
        ("f1", *own),
        ("frac", *own),
        ("p0_d2", *own),
        ("f0_d2", *inner),
        ("f2_d2", *own),
        ("dp_d2", *own),
    )


def late_parts(layers):
    top = H + layers
    both = lambda name, n: ((name, H - n, n), (name, top, n))
    faces = lambda name, n: ((name, H - n, n), (name, top - 1, n))
    return (
        ("rhs", 2, layers + 6),
        ("p1_d2", 3, layers + 4),
        ("g2", 4, layers + 2),
        ("g3", H, layers),
        *both("t1", H - 1),
        *both("tot", H - 1),
        *both("p0", H - 1),
        *both("dp", H - 2),
        *faces("f0", H - 1),
        *both("f2", H - 2),
        *both("f1", H - 2),
        *both("p0_d2", H - 2),
        *faces("f0_d2", 2),
        *both("f2_d2", 1),
        *both("dp_d2", 1),
    )


def tiles(parts):
    return -(-sum(count for _, _, count in parts) // 8)


SEAMS = ("f0", "f1", "f2", "tot", "dp", "p0", "frac", "p1", "rhs2", "rhs3")
PLACES = {
    "t1": ("f1", None, 7),
    "f1": ("f1", 0, 6),
    "tot": ("tot", 0, 7),
    "p0": ("p0", 0, 7),
    "dp": ("dp", 0, 7),
    "dp_d2": ("dp", 1, 6),
    "f0": ("f0", 0, 7),
    "f0_d2": ("f0", 1, 6),
    "f2": ("f2", 0, 7),
    "f2_d2": ("f2", 1, 6),
    "frac": ("frac", 0, 7),
    "p0_d2": ("p0", 1, 6),
    "p1_d2": ("p1", 1, 6),
    "rhs": ("rhs2", 0, 7),
    "g2": ("rhs2", 1, 6),
    "g3": ("rhs3", 1, 6),
}


def pack(message, parts, refs, rows):
    at = 0
    for name, first, count in parts:
        for e in range(first, first + count):
            message[at // 8, at % 8 : at % 8 + 1, :] = refs[name][e, rows[name] : rows[name] + 1, :]
            at += 1


def pack_both(near, cross, parts, up, down, rows, gx):
    last = rows - 1
    outer = {name: 0 if PLACES[name][2] == 7 else 1 for name in PLACES}
    up_rows = {name: last - outer[name] for name in PLACES} | {"f1": last - 1}
    down_rows = dict(outer) | {"f1": 0}
    even = lax.axis_index(gx) % 2 == 0

    @pl.when(even)
    def _():
        pack(near, parts, up, up_rows)
        pack(cross, parts, down, down_rows)

    @pl.when(jnp.logical_not(even))
    def _():
        pack(cross, parts, up, up_rows)
        pack(near, parts, down, down_rows)


def unpack(message, parts, seams, side):
    at = 0
    for name, first, count in parts:
        seam, *places = PLACES[name]
        place = places[side]
        for e in range(first, first + count):
            if place is not None:
                seams[seam][e, place : place + 1, :] = message[at // 8, at % 8 : at % 8 + 1, :]
            at += 1


def unpack_both(near, cross, parts, seams, gx):
    even = lax.axis_index(gx) % 2 == 0

    @pl.when(even)
    def _():
        unpack(near, parts, seams, 0)
        unpack(cross, parts, seams, 1)

    @pl.when(jnp.logical_not(even))
    def _():
        unpack(cross, parts, seams, 0)
        unpack(near, parts, seams, 1)


def mobility(sat, history):
    trapped = history / (1.0 + 1.5 * history)
    excess = jnp.maximum(sat - trapped, 0.0)
    free_gas = 0.5 * (excess + jnp.sqrt(excess * excess + excess / 0.375))
    relperm = jnp.where(sat < history, free_gas * free_gas, sat * sat)
    gas = relperm / 0.5
    total = (1.0 - sat) * (1.0 - sat) + gas
    return (total, gas / total)


def roll(x, shift, axis):
    return pltpu.roll(x, shift % x.shape[axis], axis)


def loop(first, last, step, carry, unroll=4):
    groups = (last - first) // unroll

    def group(g, carry):
        for i in range(unroll):
            carry = step(first + g * unroll + i, carry)
        return carry

    carry = lax.fori_loop(0, groups, group, carry)
    for index in range(first + groups * unroll, last):
        carry = step(index, carry)
    return carry


def split(x):
    high = x.astype(jnp.bfloat16)
    return (high, (x - high.astype(jnp.float32)).astype(jnp.bfloat16))


def one_hots(cell, first_layer, layers, rows, columns):
    count = cell.shape[1]
    layer = cell // (rows * columns)
    rest = cell - layer * (rows * columns)
    row = rest // columns
    column = rest - row * columns
    place = (layer - first_layer) * rows + row
    at_place = lax.broadcasted_iota(jnp.int32, (layers * rows, count), 0) == place
    at_column = lax.broadcasted_iota(jnp.int32, (columns, count), 0) == column
    return (at_place, at_column)


def gather(field, at_place, at_column):
    high, low = split(field)
    hot = at_column.astype(jnp.bfloat16)
    by_column = jnp.dot(high, hot, preferred_element_type=jnp.float32) + jnp.dot(
        low, hot, preferred_element_type=jnp.float32
    )
    return jnp.sum(jnp.where(at_place, by_column, 0.0), axis=0, keepdims=True)


def flatten(block, spread):
    perfs, wells = block.shape
    spread[...] = jnp.zeros(spread.shape, jnp.float32)
    spread[:, 0:wells] = block
    wide = spread[...]
    shift = wells
    while shift < LANES:
        wide = wide + roll(wide, shift, 1)
        shift *= 2
    each = LANES // wells
    entry = lax.broadcasted_iota(jnp.int32, (perfs, LANES), 0)
    group = lax.broadcasted_iota(jnp.int32, (perfs, LANES), 1) // wells
    tiles = [
        jnp.sum(jnp.where(entry == first + group, wide, 0.0), axis=0, keepdims=True)
        for first in range(0, perfs, each)
    ]
    return jnp.concatenate(tiles, axis=1)


def prepare_kernel(
    sat,
    hist,
    pressure,
    storage,
    trans,
    cell_in,
    index_in,
    control_in,
    target_in,
    p0e,
    tote,
    frace,
    stor,
    t0,
    t1,
    t2,
    near,
    cross,
    sums,
    cell,
    wells,
    sat_v,
    hist_v,
    cell_v,
    index_v,
    control_v,
    target_v,
    spread,
    sems,
    *,
    gz,
):
    layers, rows, columns = pressure.shape
    ext = layers + 2 * H
    own = pl.ds(H, layers)
    copies = [
        pltpu.make_async_copy(a, b, sems.at[i])
        for i, (a, b) in enumerate(
            (
                (sat, sat_v),
                (hist, hist_v),
                (cell_in, cell_v),
                (index_in, index_v),
                (control_in, control_v),
                (target_in, target_v),
                (pressure, p0e.at[own]),
                (trans.at[0], t0.at[own]),
                (storage, stor.at[own]),
                (trans.at[1], t1.at[own]),
                (trans.at[2], t2.at[own]),
            )
        )
    ]
    for copy in copies:
        copy.start()
    for copy in copies[:2]:
        copy.wait()

    def layer_step(l, carry):
        t, f = mobility(sat_v[l], hist_v[l])
        tote[l + H] = t
        frace[l + H] = f
        return carry

    loop(0, layers, layer_step, 0)
    for copy in copies[2:7]:
        copy.wait()
    perfs, group = cell_v.shape
    cell[...] = flatten(cell_v[...].astype(jnp.float32), spread).astype(jnp.int32)
    wells[0:1, :] = flatten(index_v[...], spread)
    wells[1:2, :] = flatten(jnp.broadcast_to(target_v[...], (perfs, group)), spread)
    wells[2:3, :] = flatten(
        jnp.broadcast_to(control_v[...].astype(jnp.float32), (perfs, group)), spread
    )
    at_place, at_column = one_hots(
        cell[...], lax.axis_index(gz) * layers, layers, rows, columns
    )
    flat = (layers * rows, columns)
    weight = wells[0:1, :] * gather(tote[own].reshape(flat), at_place, at_column)
    cell_p = gather(p0e[own].reshape(flat), at_place, at_column)
    for i, value in enumerate((weight * cell_p, weight)):
        part = value[:, 0:LANES]
        for lane in range(LANES, value.shape[1], LANES):
            part = part + value[:, lane : lane + LANES]
        shift = LANES // 2
        while shift >= group:
            part = part + roll(part, shift, 1)
            shift //= 2
        sums[i : i + 1, :] = part
    for copy in copies[7:]:
        copy.wait()
    even = lax.axis_index(gz) % 2 == 0
    refs = {"p0": p0e, "tot": tote, "t0": t0, "stor": stor, "t1": t1, "t2": t2, "frac": frace}
    for message, is_top in ((near, even), (cross, jnp.logical_not(even))):
        at = 0
        for name, count in Z_PARTS:
            if name == "sums" and message is cross:
                continue
            if name == "sums":
                message[at] = jnp.zeros((rows, columns), jnp.float32)
                message[at, 0:2, 0:LANES] = sums[...]
            else:
                edge = jnp.where(is_top, H + layers - count, H)
                message[pl.ds(at, count)] = refs[name][pl.ds(edge, count)]
            at += count


def masks(rows, columns):
    row = lax.broadcasted_iota(jnp.int32, (rows, columns), 0)
    column = lax.broadcasted_iota(jnp.int32, (rows, columns), 1)
    return (row == rows - 1, column == columns - 1)


def lateral_faces(tot, t1, t2, store, last_row, last_column, top_x):
    along = jnp.where(last_row, 0.0, t1) * 0.5 * (tot + roll(tot, -1, 0))
    across = jnp.where(last_column, 0.0, t2) * 0.5 * (tot + roll(tot, -1, 1))
    part = store + along + roll(along, 1, 0) + across + roll(across, 1, 1)
    return (jnp.where(last_row, jnp.where(top_x, 0.0, t1), along), across, part)


def is_last(axis):
    return lax.axis_index(axis) == lax.axis_size(axis) - 1


def faces_kernel(
    p0e, tote, frace, stor, t0, t1, t2, part, f0e, f1e, f2e, dpe, near, cross, sums, *, layers, gx
):
    _, rows, columns = p0e.shape
    last_row, last_column = masks(rows, columns)
    top_x = is_last(gx)

    def step(e, carry):
        tot = tote[e]
        f0e[e] = t0[e] * 0.5 * (tot + tote[e + 1])
        f1e[e], f2e[e], dpe[e] = lateral_faces(
            tot, t1[e], t2[e], stor[e], last_row, last_column, top_x
        )
        return carry

    loop(H, H + layers, step, 0)
    refs = {"t1": f1e, "tot": tote, "p0": p0e, "dp": dpe, "f0": f0e, "f2": f2e, "f1": f1e}
    sums[...] = part[...]
    refs |= {"frac": frace, "p0_d2": p0e, "f0_d2": f0e, "f2_d2": f2e, "dp_d2": dpe}
    pack_both(near, cross, early_parts(layers), refs, refs, rows, gx)


def well_holes(sums, wells):
    repeat = lambda x: jnp.concatenate([x] * (wells.shape[1] // LANES), axis=1)
    goal = wells[1:2, :]
    return jnp.where(
        wells[2:3, :] == 0.0, (goal + repeat(sums[0:1, :])) / repeat(sums[1:2, :]), goal
    )


def seam_kernel(near, cross, *seams, layers, gx):
    for seam in seams:
        seam[...] = jnp.zeros(seam.shape, jnp.float32)
    unpack_both(near, cross, early_parts(layers), dict(zip(SEAMS, seams)), gx)


def halo_kernel(*refs, layers, gx, gz):
    own_t0, cross, near, cell, wells = refs[8:13]
    p0e, tote, frace, stor, f0e, f1e, f2e, dpe, perfs, hot = refs[13:]
    ext, rows, columns = p0e.shape
    even = lax.axis_index(gz) % 2 == 0
    top_z = is_last(gz)
    top_x = is_last(gx)
    last_row, last_column = masks(rows, columns)
    where = {}
    at = 0
    for name, count in Z_PARTS:
        where[name] = (at, count)
        at += count

    def halo(name, e):
        at, count = where[name]
        low = e < H
        at = at + e - (H - count if low else H + layers)
        one, two = (near[at], cross[at])
        return jnp.where(even, two, one) if low else jnp.where(even, one, two)

    for name, target in (("p0", p0e), ("tot", tote), ("frac", frace), ("stor", stor)):
        count = where[name][1]
        for e in (*range(H - count, H), *range(H + layers, H + layers + count)):
            target[e] = halo(name, e)
    f0e[H + layers - 1] = jnp.where(top_z, 0.0, own_t0[H + layers - 1]) * 0.5 * (
        tote[H + layers - 1] + tote[H + layers]
    )
    for e in (*range(0, H), *range(H + layers, ext - 1)):
        f0e[e] = halo("t0", e) * 0.5 * (tote[e] + tote[e + 1])
    for e in (*range(1, H), *range(H + layers, ext - 1)):
        f1e[e], f2e[e], dpe[e] = lateral_faces(
            tote[e], halo("t1", e), halo("t2", e), stor[e], last_row, last_column, top_x
        )
    inner = ext - 2
    at_place, at_column = one_hots(
        cell[...], lax.axis_index(gz) * layers - (H - 1), inner, rows, columns
    )
    flat = (inner * rows, columns)
    perfs[0:1, :] = wells[0:1, :] * gather(tote[1 : ext - 1].reshape(flat), at_place, at_column)
    perfs[1:2, :] = gather(p0e[1 : ext - 1].reshape(flat), at_place, at_column)
    hot[...] = at_place.astype(jnp.bfloat16)


def build_kernel(*refs, layers, gx):
    p0e, stor, f0e, f1e, f2e, dpe, tote, sums, perfs, hot, cell, wells = refs[:12]
    rhse, source, x_near, x_cross, bottom, diage, p1, g2u, g2d, g3u, g3d = refs[12:]
    ext, rows, columns = p0e.shape
    last_row, _ = masks(rows, columns)
    hole = well_holes(sums[...], wells[...])
    bottom[...] = hole[:, 0:LANES]
    rate = perfs[0:1, :] * (hole - perfs[1:2, :])
    column = cell[...] % columns
    at_column = lax.broadcasted_iota(jnp.int32, (columns, cell.shape[1]), 0) == column
    inner = ext - 2
    spread = jnp.zeros((inner * rows, columns), jnp.float32)
    for piece in split(jnp.where(at_column, rate, 0.0)):
        spread = spread + lax.dot_general(
            hot[...], piece, (((1,), (1,)), ((), ())), preferred_element_type=jnp.float32
        )
    spread = spread.reshape(inner, rows, columns)
    rhse[1 : ext - 1] = spread
    source[...] = spread[H - 1 : H - 1 + layers]

    def first_step(e, below):
        above = f0e[e]
        along = jnp.where(last_row, 0.0, f1e[e])
        across = f2e[e]
        diag = dpe[e] + above + below
        diage[e] = diag
        p = p0e[e]
        rhs = stor[e] * p + rhse[e]
        rhse[e] = rhs
        new = rhs + above * p0e[e + 1] + below * p0e[e - 1]
        new = new + along * roll(p, -1, 0) + roll(along * p, 1, 0)
        new = new + across * roll(p, -1, 1) + roll(across * p, 1, 1)
        p1[e] = jnp.where(diag > 0.0, new / diag, 0.0)
        return above

    loop(1, ext - 1, first_step, f0e[0])

    def second_step(e, carry):
        along = jnp.where(last_row, 0.0, f1e[e])
        across = f2e[e]
        p = p1[e]
        rhs = rhse[e]
        diag = diage[e]
        lower = roll(along * p, 1, 0)
        upper = along * roll(p, -1, 0)
        g2u[e] = rhs + lower
        g2d[e] = rhs + upper
        new = rhs + lower + upper + f0e[e] * p1[e + 1] + f0e[e - 1] * p1[e - 1]
        new = new + across * roll(p, -1, 1) + roll(across * p, 1, 1)
        p2 = jnp.where(diag > 0.0, new / diag, 0.0)
        g3u[e] = rhs + roll(along * p2, 1, 0)
        g3d[e] = rhs + along * roll(p2, -1, 0)
        return carry

    loop(H - 1, ext - H + 1, second_step, 0)

    shared = {"t1": f1e, "tot": tote, "p0": p0e, "dp": dpe, "f0": f0e, "f2": f2e, "f1": f1e}
    shared |= {"p0_d2": p0e, "f0_d2": f0e, "f2_d2": f2e, "dp_d2": dpe, "rhs": rhse, "p1_d2": p1}
    up = shared | {"g2": g2u, "g3": g3u}
    down = shared | {"g2": g2d, "g3": g3d}
    pack_both(x_near, x_cross, late_parts(layers), up, down, rows, gx)


def finish_kernel(*refs, gx):
    sat, hist, volume, storage, source = refs[:5]
    p0e, tote, frace, f0e, f1e, f2e, dpe, rhse, near, cross = refs[5:15]
    hole = refs[15 + len(SEAMS)]
    refs = refs[16 + len(SEAMS) :]
    new_p, residual, new_sat, new_hist, bottom = refs[:5]
    seams = dict(zip(SEAMS, refs[5:]))
    pa, pb, f1, rdiag = refs[5 + len(SEAMS) :]
    bottom[...] = hole[:, 0 : bottom.shape[1]]
    layers, rows, columns = sat.shape
    ext = layers + 2 * H
    unpack_both(near, cross, late_parts(layers), seams, gx)
    sf0, sf1, sf2, stot, sdp, sp0, sfrac = (seams[name] for name in SEAMS[:7])

    full = rows + 8
    row = lax.broadcasted_iota(jnp.int32, (full, columns), 0)
    edge = (row == rows - 1) | (row == full - 1)
    beyond = (row == rows + 1) | (row == full - 2)
    join = lambda a, b: jnp.concatenate([a, b], axis=0)
    blank = jnp.zeros((rows, columns), jnp.float32)

    pa[0] = join(p0e[0], sp0[0])
    pa[ext - 1] = join(p0e[ext - 1], sp0[ext - 1])

    def face_step(e, below):
        tot = join(tote[e], stot[e])
        mixed = join(f1e[e], sf1[e])
        border = jnp.where(edge, mixed * 0.5 * (tot + roll(tot, -1, 0)), 0.0)
        f1[e] = jnp.where(edge, border, mixed)
        above = join(f0e[e], sf0[e])
        diag = join(dpe[e], sdp[e]) + above + below + border + roll(border, 1, 0)
        rdiag[e] = jnp.where(diag > 0.0, 1.0 / diag, 0.0)
        pa[e] = join(p0e[e], sp0[e])
        return above

    loop(1, ext - 1, face_step, join(f0e[0], sf0[0]))

    def sweep(number, old, new):
        def step(e, below):
            p = old[e]
            above = old[e + 1]
            face = join(f0e[e], sf0[e])
            x = f1[e]
            y = join(f2e[e], sf2[e])
            side = seams["rhs2"][e]
            if number == 3:
                side = jnp.where(beyond[rows:], seams["rhs3"][e], side)
            total = join(rhse[e], side) + below + face * above
            total = total + x * roll(p, -1, 0) + roll(x * p, 1, 0)
            total = total + y * roll(p, -1, 1) + roll(y * p, 1, 1)
            value = total * rdiag[e]
            if number == 1:
                value = jnp.where(beyond, join(blank, seams["p1"][e]), value)
            new[e] = value
            return face * p

        first = join(f0e[number - 1], sf0[number - 1]) * old[number - 1]
        loop(number, ext - number, step, first)

    fields = (pa, pb)
    for number in range(1, SWEEPS + 1):
        sweep(number, fields[(number - 1) % 2], fields[number % 2])
    field = fields[SWEEPS % 2]

    def flow(face, p, p_next, f, f_next):
        water = face * (p - p_next)
        return (water, water * jnp.where(water > 0, f, f_next))

    def last_step(l, carry):
        below_w, below_g = carry
        e = l + H
        p = field[e]
        f = join(frace[e], sfrac[e])
        own_p = p[:rows]
        own_f = f[:rows]
        above_w, above_g = flow(f0e[e], own_p, field[e + 1][:rows], own_f, frace[e + 1])
        xw, xg = flow(f1[e], p, roll(p, -1, 0), f, roll(f, -1, 0))
        yw, yg = flow(f2e[e], own_p, roll(own_p, -1, 1), own_f, roll(own_f, -1, 1))
        water = above_w - below_w + (xw - roll(xw, 1, 0))[:rows] + yw - roll(yw, 1, 1)
        out = above_g - below_g + (xg - roll(xg, 1, 0))[:rows] + yg - roll(yg, 1, 1)
        new_p[l] = own_p
        residual[l] = rhse[e] - storage[l] * own_p - water
        src = source[l]
        gas = jnp.maximum(src, 0.0) + jnp.minimum(src, 0.0) * own_f
        s = sat[l] + volume[l] * (gas - out)
        new_sat[l] = s
        new_hist[l] = jnp.maximum(hist[l], s)
        return (above_w, above_g)

    first = flow(f0e[H - 1], field[H - 1][:rows], field[H][:rows], frace[H - 1], frace[H])
    loop(0, layers, last_step, first)


def swap(block, axis, first):
    pairs = [(i, i + 1) for i in range(first, lax.axis_size(axis) - 1, 2)]
    return lax.ppermute(block, axis, pairs + [(b, a) for a, b in pairs])


def pin(*shape, dtype=jnp.float32):
    return pltpu.VMEM(shape, dtype)


VMEM = pl.BlockSpec(memory_space=pltpu.VMEM)
HBM = pl.BlockSpec(memory_space=pltpu.HBM)


def call(kernel, outs, scratch, *args, space=VMEM, sems=0, aliases={}):
    as_struct = lambda s: s if hasattr(s, "dtype") else jax.ShapeDtypeStruct(s, jnp.float32)
    as_scratch = lambda s: pltpu.VMEM(as_struct(s).shape, as_struct(s).dtype)
    return pl.pallas_call(
        kernel,
        out_shape=[as_struct(s) for s in outs],
        in_specs=[space] * len(args),
        out_specs=[VMEM] * len(outs),
        scratch_shapes=[as_scratch(s) for s in scratch]
        + ([pltpu.SemaphoreType.DMA((sems,))] if sems else []),
        input_output_aliases=aliases,
        compiler_params=pltpu.CompilerParams(vmem_limit_bytes=24 * 1024 * 1024),
    )(*(pltpu.with_memory_space_constraint(a, pltpu.HBM) if space is HBM else a for a in args))


def body(
    pressure,
    saturation,
    sat_history,
    storage,
    step_volume,
    transmiss,
    perf_cell,
    perf_index,
    control,
    target,
):
    layers, rows, columns = pressure.shape
    ext = layers + 2 * H
    wells, perfs = perf_cell.shape
    block = (layers, rows, columns)
    pinned = pin(*block)
    ext_block = pin(ext, rows, columns)
    z_layers = sum(count for _, count in Z_PARTS)
    z_near, z_cross = (pin(n, rows, columns) for n in (z_layers, z_layers - 1))
    entries = wells * perfs
    early, late = (pin(tiles(f(layers)), 8, columns) for f in (early_parts, late_parts))
    seams = [pin(ext, 8, columns)] * len(SEAMS)
    *fields, near, cross, part, cell, per_perf = call(
        functools.partial(prepare_kernel, gz="gz"),
        [ext_block] * 7
        + [z_near, z_cross]
        + [pin(2, LANES), pin(1, entries, dtype=jnp.int32), pin(3, entries)],
        [
            block,
            block,
            jax.ShapeDtypeStruct((perfs, wells), jnp.int32),
            (perfs, wells),
            jax.ShapeDtypeStruct((1, wells), jnp.int32),
            (1, wells),
            (perfs, LANES),
        ],
        saturation,
        sat_history,
        pressure,
        storage,
        transmiss,
        perf_cell.T,
        perf_index.T,
        control.reshape(1, wells),
        target.reshape(1, wells),
        space=HBM,
        sems=11,
    )
    cross = swap(cross, "gz", 1)
    near = swap(near, "gz", 0)
    p0e, tote, frace, stor, t0, t1, t2 = fields
    f0e, f1e, f2e, dpe, early_near, early_cross, part = call(
        functools.partial(faces_kernel, layers=layers, gx="gx"),
        [ext_block] * 4 + [early, early, pin(2, LANES)],
        [],
        *fields,
        part,
    )
    early_cross = swap(early_cross, "gx", 1)
    early_near = swap(early_near, "gx", 0)
    sums = part + near[-1, 0:2, 0:LANES]
    step = 2
    while step < lax.axis_size("gz"):
        pairs = [(i, i ^ step) for i in range(lax.axis_size("gz"))]
        sums = sums + lax.ppermute(sums, "gz", pairs)
        step *= 2
    p0e, tote, frace, stor, f0e, f1e, f2e, dpe, perf_values, hot = call(
        functools.partial(halo_kernel, layers=layers, gx="gx", gz="gz"),
        [ext_block] * 8
        + [
            pin(2, entries),
            pin((ext - 2) * rows, entries, dtype=jnp.bfloat16),
        ],
        [],
        p0e,
        tote,
        frace,
        stor,
        f0e,
        f1e,
        f2e,
        dpe,
        t0,
        cross,
        near,
        cell,
        per_perf,
        aliases={i: i for i in range(8)},
    )
    rhse, source, late_near, late_cross, hole = call(
        functools.partial(build_kernel, layers=layers, gx="gx"),
        [ext_block, pinned, late, late, pin(1, LANES)],
        [ext_block] * 6,
        p0e,
        stor,
        f0e,
        f1e,
        f2e,
        dpe,
        tote,
        sums,
        perf_values,
        hot,
        cell,
        per_perf,
    )
    late_cross = swap(late_cross, "gx", 1)
    late_near = swap(late_near, "gx", 0)
    early_near, early_cross, rhse = lax.optimization_barrier((early_near, early_cross, rhse))
    filled = call(
        functools.partial(seam_kernel, layers=layers, gx="gx"), seams, [], early_near, early_cross
    )
    field, residual, new_sat, new_hist, bottom, *_ = call(
        functools.partial(finish_kernel, gx="gx"),
        [block] * 4 + [(1, wells)] + seams,
        [(ext, rows + 8, columns)] * 4,
        saturation,
        sat_history,
        step_volume,
        storage,
        source,
        p0e,
        tote,
        frace,
        f0e,
        f1e,
        f2e,
        dpe,
        rhse,
        late_near,
        late_cross,
        *filled,
        hole,
        aliases={15 + i: 5 + i for i in range(len(SEAMS))},
    )
    return (field, residual, new_sat, new_hist, bottom.reshape(wells))


def solution(mesh):
    return jax.shard_map(
        body,
        mesh=mesh,
        in_specs=(
            P("gz", "gx", None),
            P("gz", "gx", None),
            P("gz", "gx", None),
            P("gz", "gx", None),
            P("gz", "gx", None),
            P(None, "gz", "gx", None),
            P("gx", None),
            P("gx", None),
            P("gx"),
            P("gx"),
        ),
        out_specs=(
            P("gz", "gx", None),
            P("gz", "gx", None),
            P("gz", "gx", None),
            P("gz", "gx", None),
            P("gx"),
        ),
        check_vma=False,
    )
```

```python
import functools

import jax
import jax.numpy as jnp
from jax import lax
from jax.experimental import pallas as pl
from jax.experimental.pallas import tpu as pltpu
from jax.sharding import PartitionSpec as P

SWEEPS = 4
H = SWEEPS + 1
LANES = 128
SENT = 4

Z_PARTS = (
    ("p0", H),
    ("tot", H),
    ("t0", H),
    ("stor", H - 1),
    ("t1", H - 1),
    ("t2", H - 1),
    ("frac", 1),
    ("sums", 1),
)


def early_parts(layers):
    own = (H, layers)
    inner = (H, layers - 1)
    return (
        ("t1", *own),
        ("tot", *own),
        ("p0", *own),
        ("dp", *own),
        ("f0", *inner),
        ("f2", *own),
        ("f1", *own),
        ("frac", *own),
        ("p0_d2", *own),
        ("f0_d2", *inner),
        ("f2_d2", *own),
        ("dp_d2", *own),
    )


def late_parts(layers):
    top = H + layers
    both = lambda name, n: ((name, H - n, n), (name, top, n))
    faces = lambda name, n: ((name, H - n, n), (name, top - 1, n))
    return (
        ("rhs", 2, layers + 6),
        ("p1_d2", 3, layers + 4),
        ("g2", 4, layers + 2),
        ("g3", H, layers),
        *both("t1", H - 1),
        *both("tot", H - 1),
        *both("p0", H - 1),
        *both("dp", H - 2),
        *faces("f0", H - 1),
        *both("f2", H - 2),
        *both("f1", H - 2),
        *both("p0_d2", H - 2),
        *faces("f0_d2", 2),
        *both("f2_d2", 1),
        *both("dp_d2", 1),
    )


def tiles(parts):
    return -(-sum(count for _, _, count in parts) // 8)


SEAMS = ("f0", "f1", "f2", "tot", "dp", "p0", "frac", "p1", "rhs2", "rhs3")
PLACES = {
    "t1": ("f1", None, 7),
    "f1": ("f1", 0, 6),
    "tot": ("tot", 0, 7),
    "p0": ("p0", 0, 7),
    "dp": ("dp", 0, 7),
    "dp_d2": ("dp", 1, 6),
    "f0": ("f0", 0, 7),
    "f0_d2": ("f0", 1, 6),
    "f2": ("f2", 0, 7),
    "f2_d2": ("f2", 1, 6),
    "frac": ("frac", 0, 7),
    "p0_d2": ("p0", 1, 6),
    "p1_d2": ("p1", 1, 6),
    "rhs": ("rhs2", 0, 7),
    "g2": ("rhs2", 1, 6),
    "g3": ("rhs3", 1, 6),
}


def pack(message, parts, refs, rows):
    at = 0
    for name, first, count in parts:
        for e in range(first, first + count):
            message[at // 8, at % 8 : at % 8 + 1, :] = refs[name][e, rows[name] : rows[name] + 1, :]
            at += 1


def pack_both(near, cross, parts, up, down, rows, gx):
    last = rows - 1
    outer = {name: 0 if PLACES[name][2] == 7 else 1 for name in PLACES}
    up_rows = {name: last - outer[name] for name in PLACES} | {"f1": last - 1}
    down_rows = dict(outer) | {"f1": 0}
    even = lax.axis_index(gx) % 2 == 0

    @pl.when(even)
    def _():
        pack(near, parts, up, up_rows)
        pack(cross, parts, down, down_rows)

    @pl.when(jnp.logical_not(even))
    def _():
        pack(cross, parts, up, up_rows)
        pack(near, parts, down, down_rows)


def unpack(message, parts, seams, side):
    at = 0
    for name, first, count in parts:
        seam, *places = PLACES[name]
        place = places[side]
        for e in range(first, first + count):
            if place is not None:
                seams[seam][e, place : place + 1, :] = message[at // 8, at % 8 : at % 8 + 1, :]
            at += 1


def unpack_both(near, cross, parts, seams, gx):
    even = lax.axis_index(gx) % 2 == 0

    @pl.when(even)
    def _():
        unpack(near, parts, seams, 0)
        unpack(cross, parts, seams, 1)

    @pl.when(jnp.logical_not(even))
    def _():
        unpack(cross, parts, seams, 0)
        unpack(near, parts, seams, 1)


def mobility(sat, history):
    trapped = history / (1.0 + 1.5 * history)
    excess = jnp.maximum(sat - trapped, 0.0)
    free_gas = 0.5 * (excess + jnp.sqrt(excess * excess + excess / 0.375))
    relperm = jnp.where(sat < history, free_gas * free_gas, sat * sat)
    gas = relperm / 0.5
    total = (1.0 - sat) * (1.0 - sat) + gas
    return (total, gas / total)


def roll(x, shift, axis):
    return pltpu.roll(x, shift % x.shape[axis], axis)


def loop(first, last, step, carry, unroll=4):
    groups = (last - first) // unroll

    def group(g, carry):
        for i in range(unroll):
            carry = step(first + g * unroll + i, carry)
        return carry

    carry = lax.fori_loop(0, groups, group, carry)
    for index in range(first + groups * unroll, last):
        carry = step(index, carry)
    return carry


def split(x):
    high = x.astype(jnp.bfloat16)
    return (high, (x - high.astype(jnp.float32)).astype(jnp.bfloat16))


def at_places(cell, first_layer, layers, rows, columns):
    layer = cell // (rows * columns)
    row = (cell - layer * (rows * columns)) // columns
    place = (layer - first_layer) * rows + row
    return lax.broadcasted_iota(jnp.int32, (layers * rows, cell.shape[1]), 0) == place


def at_columns(cell, columns):
    return lax.broadcasted_iota(jnp.int32, (columns, cell.shape[1]), 0) == cell % columns


def gather(field, at_place, at_column):
    high, low = split(field)
    hot = at_column.astype(jnp.bfloat16)
    by_column = jnp.dot(high, hot, preferred_element_type=jnp.float32) + jnp.dot(
        low, hot, preferred_element_type=jnp.float32
    )
    return jnp.sum(jnp.where(at_place, by_column, 0.0), axis=0, keepdims=True)


def flatten(block, spread):
    perfs, wells = block.shape
    spread[...] = jnp.zeros(spread.shape, jnp.float32)
    spread[:, 0:wells] = block
    wide = spread[...]
    shift = wells
    while shift < LANES:
        wide = wide + roll(wide, shift, 1)
        shift *= 2
    each = LANES // wells
    entry = lax.broadcasted_iota(jnp.int32, (perfs, LANES), 0)
    group = lax.broadcasted_iota(jnp.int32, (perfs, LANES), 1) // wells
    tiles = [
        jnp.sum(jnp.where(entry == first + group, wide, 0.0), axis=0, keepdims=True)
        for first in range(0, perfs, each)
    ]
    return jnp.concatenate(tiles, axis=1)


def prepare_kernel(
    sat,
    hist,
    pressure,
    storage,
    trans,
    cell_in,
    index_in,
    control_in,
    target_in,
    p0e,
    tote,
    frace,
    stor,
    t0,
    t1,
    t2,
    near,
    cross,
    sums,
    cell,
    wells,
    perfs,
    hot,
    sat_v,
    hist_v,
    cell_v,
    index_v,
    control_v,
    target_v,
    spread,
    sems,
    *,
    gz,
):
    layers, rows, columns = pressure.shape
    ext = layers + 2 * H
    own = pl.ds(H, layers)
    copies = [
        pltpu.make_async_copy(a, b, sems.at[i])
        for i, (a, b) in enumerate(
            (
                (sat, sat_v),
                (hist, hist_v),
                (cell_in, cell_v),
                (index_in, index_v),
                (control_in, control_v),
                (target_in, target_v),
                (pressure, p0e.at[own]),
                (trans.at[0], t0.at[own]),
                (storage, stor.at[own]),
                (trans.at[1], t1.at[own]),
                (trans.at[2], t2.at[own]),
            )
        )
    ]
    for copy in copies:
        copy.start()
    for copy in copies[:2]:
        copy.wait()

    def layer_step(l, carry):
        t, f = mobility(sat_v[l], hist_v[l])
        tote[l + H] = t
        frace[l + H] = f
        return carry

    loop(0, layers, layer_step, 0)
    for copy in copies[2:7]:
        copy.wait()
    count, group = cell_v.shape
    cell[...] = flatten(cell_v[...].astype(jnp.float32), spread).astype(jnp.int32)
    wells[0:1, :] = flatten(index_v[...], spread)
    wells[1:2, :] = flatten(jnp.broadcast_to(target_v[...], (count, group)), spread)
    wells[2:3, :] = flatten(
        jnp.broadcast_to(control_v[...].astype(jnp.float32), (count, group)), spread
    )
    at_place = at_places(cell[...], lax.axis_index(gz) * layers, layers, rows, columns)
    at_column = at_columns(cell[...], columns)
    hot[...] = at_place.astype(jnp.bfloat16)
    flat = (layers * rows, columns)
    weight = wells[0:1, :] * gather(tote[own].reshape(flat), at_place, at_column)
    cell_p = gather(p0e[own].reshape(flat), at_place, at_column)
    perfs[0:1, :] = weight
    perfs[1:2, :] = cell_p
    for i, value in enumerate((weight * cell_p, weight)):
        part = value[:, 0:LANES]
        for lane in range(LANES, value.shape[1], LANES):
            part = part + value[:, lane : lane + LANES]
        shift = LANES // 2
        while shift >= group:
            part = part + roll(part, shift, 1)
            shift //= 2
        sums[i : i + 1, :] = part
    for copy in copies[7:]:
        copy.wait()
    even = lax.axis_index(gz) % 2 == 0
    refs = {"p0": p0e, "tot": tote, "t0": t0, "stor": stor, "t1": t1, "t2": t2, "frac": frace}
    for message, is_top in ((near, even), (cross, jnp.logical_not(even))):
        at = 0
        for name, count in Z_PARTS:
            if name == "sums" and message is cross:
                continue
            if name == "sums":
                message[at] = jnp.zeros((rows, columns), jnp.float32)
                message[at, 0:2, 0:LANES] = sums[...]
            else:
                edge = jnp.where(is_top, H + layers - count, H)
                message[pl.ds(at, count)] = refs[name][pl.ds(edge, count)]
            at += count


def masks(rows, columns):
    row = lax.broadcasted_iota(jnp.int32, (rows, columns), 0)
    column = lax.broadcasted_iota(jnp.int32, (rows, columns), 1)
    return (row == rows - 1, column == columns - 1)


def lateral_faces(tot, t1, t2, store, last_row, last_column, top_x):
    along = jnp.where(last_row, 0.0, t1) * 0.5 * (tot + roll(tot, -1, 0))
    across = jnp.where(last_column, 0.0, t2) * 0.5 * (tot + roll(tot, -1, 1))
    part = store + along + roll(along, 1, 0) + across + roll(across, 1, 1)
    return (jnp.where(last_row, jnp.where(top_x, 0.0, t1), along), across, part)


def is_last(axis):
    return lax.axis_index(axis) == lax.axis_size(axis) - 1


def first_sweep(e, p0e, stor, f0e, f1e, f2e, dpe, last_row):
    above = f0e[e]
    below = f0e[e - 1]
    along = jnp.where(last_row, 0.0, f1e[e])
    across = f2e[e]
    diag = dpe[e] + above + below
    p = p0e[e]
    base = stor[e] * p + above * p0e[e + 1] + below * p0e[e - 1]
    base = base + along * roll(p, -1, 0) + roll(along * p, 1, 0)
    base = base + across * roll(p, -1, 1) + roll(across * p, 1, 1)
    return (base, jnp.where(diag > 0.0, 1.0 / diag, 0.0))


def faces_kernel(*refs, layers, gx):
    p0e, tote, frace, stor, t0, t1, t2, part = refs[:8]
    f0e, f1e, f2e, dpe, base, inverse, near, cross, sums = refs[8:]
    _, rows, columns = p0e.shape
    last_row, last_column = masks(rows, columns)
    top_x = is_last(gx)

    def step(e, carry):
        tot = tote[e]
        f0e[e] = t0[e] * 0.5 * (tot + tote[e + 1])
        f1e[e], f2e[e], dpe[e] = lateral_faces(
            tot, t1[e], t2[e], stor[e], last_row, last_column, top_x
        )
        return carry

    loop(H, H + layers, step, 0)
    sums[...] = part[...]
    refs = {"t1": f1e, "tot": tote, "p0": p0e, "dp": dpe, "f0": f0e, "f2": f2e, "f1": f1e}
    refs |= {"frac": frace, "p0_d2": p0e, "f0_d2": f0e, "f2_d2": f2e, "dp_d2": dpe}
    pack_both(near, cross, early_parts(layers), refs, refs, rows, gx)

    def sweep_step(e, carry):
        base[e], inverse[e] = first_sweep(e, p0e, stor, f0e, f1e, f2e, dpe, last_row)
        return carry

    loop(H + 1, H + layers - 1, sweep_step, 0)


def well_holes(sums, wells):
    repeat = lambda x: jnp.concatenate([x] * (wells.shape[1] // LANES), axis=1)
    goal = wells[1:2, :]
    return jnp.where(
        wells[2:3, :] == 0.0, (goal + repeat(sums[0:1, :])) / repeat(sums[1:2, :]), goal
    )


def join(a, b):
    return jnp.concatenate([a, b], axis=0)


def seam_faces(first, last, fields, seams, f1, inverse, p):
    p0e, tote, f0e, f1e, dpe = fields
    rows, columns = p0e.shape[1:]
    row = lax.broadcasted_iota(jnp.int32, (rows + 8, columns), 0)
    edge = (row == rows - 1) | (row == rows + 7)

    def step(e, below):
        tot = join(tote[e], seams["tot"][e])
        mixed = join(f1e[e], seams["f1"][e])
        border = jnp.where(edge, mixed * 0.5 * (tot + roll(tot, -1, 0)), 0.0)
        f1[e] = jnp.where(edge, border, mixed)
        above = join(f0e[e], seams["f0"][e])
        diag = join(dpe[e], seams["dp"][e]) + above + below + border + roll(border, 1, 0)
        inverse[e] = jnp.where(diag > 0.0, 1.0 / diag, 0.0)
        p[e] = join(p0e[e], seams["p0"][e])
        return above

    loop(first, last, step, join(f0e[first - 1], seams["f0"][first - 1]))


def seam_kernel(near, cross, *refs, layers, gx):
    fields, refs = refs[:5], refs[5:]
    seams = dict(zip(SEAMS, refs))
    for seam in seams.values():
        seam[...] = jnp.zeros(seam.shape, jnp.float32)
    unpack_both(near, cross, early_parts(layers), seams, gx)
    seam_faces(H + 1, H + layers - 1, fields, seams, *refs[len(SEAMS) :])


def halo_kernel(*refs, layers, gx, gz):
    own_t0, cross, near, cell, wells, own_perfs = refs[10:16]
    p0e, tote, frace, stor, f0e, f1e, f2e, dpe, base, inverse, perfs, hot = refs[16:]
    ext, rows, columns = p0e.shape
    even = lax.axis_index(gz) % 2 == 0
    top_z = is_last(gz)
    top_x = is_last(gx)
    last_row, last_column = masks(rows, columns)
    where = {}
    at = 0
    for name, count in Z_PARTS:
        where[name] = (at, count)
        at += count

    def halo(name, e):
        at, count = where[name]
        low = e < H
        at = at + e - (H - count if low else H + layers)
        one, two = (near[at], cross[at])
        return jnp.where(even, two, one) if low else jnp.where(even, one, two)

    for name, target in (("p0", p0e), ("tot", tote), ("frac", frace), ("stor", stor)):
        count = where[name][1]
        for e in (*range(H - count, H), *range(H + layers, H + layers + count)):
            target[e] = halo(name, e)
    f0e[H + layers - 1] = jnp.where(top_z, 0.0, own_t0[H + layers - 1]) * 0.5 * (
        tote[H + layers - 1] + tote[H + layers]
    )
    for e in (*range(0, H), *range(H + layers, ext - 1)):
        f0e[e] = halo("t0", e) * 0.5 * (tote[e] + tote[e + 1])
    for e in (*range(1, H), *range(H + layers, ext - 1)):
        f1e[e], f2e[e], dpe[e] = lateral_faces(
            tote[e], halo("t1", e), halo("t2", e), stor[e], last_row, last_column, top_x
        )
    for e in (*range(1, H + 1), *range(H + layers - 1, ext - 1)):
        base[e], inverse[e] = first_sweep(e, p0e, stor, f0e, f1e, f2e, dpe, last_row)
    width = H - 1
    first = lax.axis_index(gz) * layers
    sides = ((1, first - width), (H + layers, first + layers))
    at_place = [at_places(cell[...], layer, width, rows, columns) for _, layer in sides]
    at_place = jnp.concatenate(at_place, axis=0)
    at_column = at_columns(cell[...], columns)
    hot[...] = at_place.astype(jnp.bfloat16)
    flat = (width * rows, columns)
    both = lambda ref: join(*(ref[e : e + width].reshape(flat) for e, _ in sides))
    weight = wells[0:1, :] * gather(both(tote), at_place, at_column)
    perfs[0:1, :] = own_perfs[0:1, :] + weight
    perfs[1:2, :] = own_perfs[1:2, :] + gather(both(p0e), at_place, at_column)


def build_kernel(*refs, layers, gx):
    p0e, stor, f0e, f1e, f2e, dpe, tote, base, inverse, sums, perfs, hot, own_hot = refs[:13]
    cell, wells, rhse, source, x_near, x_cross, bottom, p1, g2u, g2d, g3u, g3d = refs[13:]
    ext, rows, columns = p0e.shape
    last_row, _ = masks(rows, columns)
    hole = well_holes(sums[...], wells[...])
    bottom[...] = hole[:, 0:LANES]
    rate = perfs[0:1, :] * (hole - perfs[1:2, :])
    pieces = split(jnp.where(at_columns(cell[...], columns), rate, 0.0))

    def scatter(mask):
        spread = [
            lax.dot_general(
                mask, piece, (((1,), (1,)), ((), ())), preferred_element_type=jnp.float32
            )
            for piece in pieces
        ]
        return (spread[0] + spread[1]).reshape(-1, rows, columns)

    width = H - 1
    inside = scatter(own_hot[...])
    outside = scatter(hot[...])
    source[...] = inside
    rhse[H : ext - H] = inside
    rhse[1:H] = outside[:width]
    rhse[ext - H : ext - 1] = outside[width:]

    def first_step(e, carry):
        wells_rate = rhse[e]
        p1[e] = (base[e] + wells_rate) * inverse[e]
        rhse[e] = stor[e] * p0e[e] + wells_rate
        return carry

    loop(1, ext - 1, first_step, 0)

    def second_step(e, carry):
        along = jnp.where(last_row, 0.0, f1e[e])
        across = f2e[e]
        p = p1[e]
        rhs = rhse[e]
        lower = roll(along * p, 1, 0)
        upper = along * roll(p, -1, 0)
        g2u[e] = rhs + lower
        g2d[e] = rhs + upper
        new = rhs + lower + upper + f0e[e] * p1[e + 1] + f0e[e - 1] * p1[e - 1]
        new = new + across * roll(p, -1, 1) + roll(across * p, 1, 1)
        p2 = new * inverse[e]
        g3u[e] = rhs + roll(along * p2, 1, 0)
        g3d[e] = rhs + along * roll(p2, -1, 0)
        return carry

    loop(H - 1, ext - H + 1, second_step, 0)

    shared = {"t1": f1e, "tot": tote, "p0": p0e, "dp": dpe, "f0": f0e, "f2": f2e, "f1": f1e}
    shared |= {"p0_d2": p0e, "f0_d2": f0e, "f2_d2": f2e, "dp_d2": dpe, "rhs": rhse, "p1_d2": p1}
    up = shared | {"g2": g2u, "g3": g3u}
    down = shared | {"g2": g2d, "g3": g3d}
    pack_both(x_near, x_cross, late_parts(layers), up, down, rows, gx)


def finish_kernel(*refs, gx):
    sat, hist, volume, storage, source = refs[:5]
    p0e, tote, frace, f0e, f1e, f2e, dpe, rhse, near, cross = refs[5:15]
    hole = refs[18 + len(SEAMS)]
    refs = refs[19 + len(SEAMS) :]
    new_p, residual, new_sat, new_hist, bottom = refs[:5]
    seams = dict(zip(SEAMS, refs[5:]))
    f1, rdiag, pa, pb, residual_v, sat_v, hist_v, sems = refs[5 + len(SEAMS) :]
    bottom[...] = hole[:, 0 : bottom.shape[1]]
    layers, rows, columns = sat.shape
    ext = layers + 2 * H
    unpack_both(near, cross, late_parts(layers), seams, gx)
    sf0, sf2, sfrac = (seams[name] for name in ("f0", "f2", "frac"))
    row = lax.broadcasted_iota(jnp.int32, (rows + 8, columns), 0)
    beyond = (row == rows + 1) | (row == rows + 6)
    blank = jnp.zeros((rows, columns), jnp.float32)
    pa[0] = join(p0e[0], seams["p0"][0])
    pa[ext - 1] = join(p0e[ext - 1], seams["p0"][ext - 1])
    for first, last in ((1, H + 1), (ext - H - 1, ext - 1)):
        seam_faces(first, last, (p0e, tote, f0e, f1e, dpe), seams, f1, rdiag, pa)

    def sweep(number, old, new):
        def step(e, below):
            p = old[e]
            above = old[e + 1]
            face = join(f0e[e], sf0[e])
            x = f1[e]
            y = join(f2e[e], sf2[e])
            side = seams["rhs2"][e]
            if number == 3:
                side = jnp.where(beyond[rows:], seams["rhs3"][e], side)
            total = join(rhse[e], side) + below + face * above
            total = total + x * roll(p, -1, 0) + roll(x * p, 1, 0)
            total = total + y * roll(p, -1, 1) + roll(y * p, 1, 1)
            value = total * rdiag[e]
            if number == 1:
                value = jnp.where(beyond, join(blank, seams["p1"][e]), value)
            new[e] = value
            return face * p

        first = join(f0e[number - 1], sf0[number - 1]) * old[number - 1]
        loop(number, ext - number, step, first)

    fields = (pa, pb)
    for number in range(1, SWEEPS + 1):
        sweep(number, fields[(number - 1) % 2], fields[number % 2])
    field = fields[SWEEPS % 2]

    copies = []

    def send(source, target):
        copies.append(pltpu.make_async_copy(source, target, sems.at[len(copies)]))
        copies[-1].start()

    send(field.at[pl.ds(H, layers), pl.ds(0, rows)], new_p)

    def flow(face, p, p_next, f, f_next):
        water = face * (p - p_next)
        return (water, water * jnp.where(water > 0, f, f_next))

    def last_step(l, carry):
        below_w, below_g = carry
        e = l + H
        p = field[e]
        f = join(frace[e], sfrac[e])
        own_p = p[:rows]
        own_f = f[:rows]
        above_w, above_g = flow(f0e[e], own_p, field[e + 1][:rows], own_f, frace[e + 1])
        xw, xg = flow(f1[e], p, roll(p, -1, 0), f, roll(f, -1, 0))
        yw, yg = flow(f2e[e], own_p, roll(own_p, -1, 1), own_f, roll(own_f, -1, 1))
        water = above_w - below_w + (xw - roll(xw, 1, 0))[:rows] + yw - roll(yw, 1, 1)
        out = above_g - below_g + (xg - roll(xg, 1, 0))[:rows] + yg - roll(yg, 1, 1)
        residual_v[l] = rhse[e] - storage[l] * own_p - water
        src = source[l]
        gas = jnp.maximum(src, 0.0) + jnp.minimum(src, 0.0) * own_f
        s = sat[l] + volume[l] * (gas - out)
        sat_v[l] = s
        hist_v[l] = jnp.maximum(hist[l], s)
        return (above_w, above_g)

    carry = flow(f0e[H - 1], field[H - 1][:rows], field[H][:rows], frace[H - 1], frace[H])
    for l in range(0, layers, SENT):
        count = min(SENT, layers - l)
        carry = loop(l, l + count, last_step, carry)
        for ref, target in ((residual_v, residual), (sat_v, new_sat), (hist_v, new_hist)):
            send(ref.at[pl.ds(l, count)], target.at[pl.ds(l, count)])
    for copy in copies:
        copy.wait()


def swap(block, axis, first):
    pairs = [(i, i + 1) for i in range(first, lax.axis_size(axis) - 1, 2)]
    return lax.ppermute(block, axis, pairs + [(b, a) for a, b in pairs])


def pin(*shape, dtype=jnp.float32):
    return pltpu.VMEM(shape, dtype)


VMEM = pl.BlockSpec(memory_space=pltpu.VMEM)
HBM = pl.BlockSpec(memory_space=pltpu.HBM)


def call(kernel, outs, scratch, *args, space=VMEM, sems=0, aliases={}, sent=0):
    as_struct = lambda s: s if hasattr(s, "dtype") else jax.ShapeDtypeStruct(s, jnp.float32)
    as_scratch = lambda s: pltpu.VMEM(as_struct(s).shape, as_struct(s).dtype)
    return pl.pallas_call(
        kernel,
        out_shape=[as_struct(s) for s in outs],
        in_specs=[space] * len(args),
        out_specs=[pl.BlockSpec(memory_space=pl.ANY)] * sent + [VMEM] * (len(outs) - sent),
        scratch_shapes=[as_scratch(s) for s in scratch]
        + ([pltpu.SemaphoreType.DMA((sems,))] if sems else []),
        input_output_aliases=aliases,
        compiler_params=pltpu.CompilerParams(vmem_limit_bytes=24 * 1024 * 1024),
    )(*(pltpu.with_memory_space_constraint(a, pltpu.HBM) if space is HBM else a for a in args))


def body(
    pressure,
    saturation,
    sat_history,
    storage,
    step_volume,
    transmiss,
    perf_cell,
    perf_index,
    control,
    target,
):
    layers, rows, columns = pressure.shape
    ext = layers + 2 * H
    wells, perfs = perf_cell.shape
    block = (layers, rows, columns)
    pinned = pin(*block)
    ext_block = pin(ext, rows, columns)
    z_layers = sum(count for _, count in Z_PARTS)
    z_near, z_cross = (pin(n, rows, columns) for n in (z_layers, z_layers - 1))
    entries = wells * perfs
    early, late = (pin(tiles(f(layers)), 8, columns) for f in (early_parts, late_parts))
    seams = [pin(ext, 8, columns)] * len(SEAMS)
    *fields, near, cross, part, cell, per_perf, perf_values, own_hot = call(
        functools.partial(prepare_kernel, gz="gz"),
        [ext_block] * 7
        + [z_near, z_cross]
        + [
            pin(2, LANES),
            pin(1, entries, dtype=jnp.int32),
            pin(3, entries),
            pin(2, entries),
            pin(layers * rows, entries, dtype=jnp.bfloat16),
        ],
        [
            block,
            block,
            jax.ShapeDtypeStruct((perfs, wells), jnp.int32),
            (perfs, wells),
            jax.ShapeDtypeStruct((1, wells), jnp.int32),
            (1, wells),
            (perfs, LANES),
        ],
        saturation,
        sat_history,
        pressure,
        storage,
        transmiss,
        perf_cell.T,
        perf_index.T,
        control.reshape(1, wells),
        target.reshape(1, wells),
        space=HBM,
        sems=11,
    )
    cross = swap(cross, "gz", 1)
    near = swap(near, "gz", 0)
    p0e, tote, frace, stor, t0, t1, t2 = fields
    f0e, f1e, f2e, dpe, base, inverse, early_near, early_cross, part = call(
        functools.partial(faces_kernel, layers=layers, gx="gx"),
        [ext_block] * 6 + [early, early, pin(2, LANES)],
        [],
        *fields,
        part,
    )
    early_cross = swap(early_cross, "gx", 1)
    early_near = swap(early_near, "gx", 0)
    sums = part + near[-1, 0:2, 0:LANES]
    step = 2
    while step < lax.axis_size("gz"):
        pairs = [(i, i ^ step) for i in range(lax.axis_size("gz"))]
        sums = sums + lax.ppermute(sums, "gz", pairs)
        step *= 2
    p0e, tote, frace, stor, f0e, f1e, f2e, dpe, base, inverse, perf_values, hot = call(
        functools.partial(halo_kernel, layers=layers, gx="gx", gz="gz"),
        [ext_block] * 10
        + [pin(2, entries), pin(2 * (H - 1) * rows, entries, dtype=jnp.bfloat16)],
        [],
        p0e,
        tote,
        frace,
        stor,
        f0e,
        f1e,
        f2e,
        dpe,
        base,
        inverse,
        t0,
        cross,
        near,
        cell,
        per_perf,
        perf_values,
        aliases={i: i for i in range(10)},
    )
    rhse, source, late_near, late_cross, hole = call(
        functools.partial(build_kernel, layers=layers, gx="gx"),
        [ext_block, pinned, late, late, pin(1, LANES)],
        [ext_block] * 5,
        p0e,
        stor,
        f0e,
        f1e,
        f2e,
        dpe,
        tote,
        base,
        inverse,
        sums,
        perf_values,
        hot,
        own_hot,
        cell,
        per_perf,
    )
    late_cross = swap(late_cross, "gx", 1)
    late_near = swap(late_near, "gx", 0)
    early_near, early_cross, rhse = lax.optimization_barrier((early_near, early_cross, rhse))
    joined = [pin(ext, rows + 8, columns)] * 3
    filled = call(
        functools.partial(seam_kernel, layers=layers, gx="gx"),
        seams + joined,
        [],
        early_near,
        early_cross,
        p0e,
        tote,
        f0e,
        f1e,
        dpe,
    )
    field, residual, new_sat, new_hist, bottom, *_ = call(
        functools.partial(finish_kernel, gx="gx"),
        [block] * 4 + [(1, wells)] + seams + joined,
        [joined[0]] + [block] * 3,
        saturation,
        sat_history,
        step_volume,
        storage,
        source,
        p0e,
        tote,
        frace,
        f0e,
        f1e,
        f2e,
        dpe,
        rhse,
        late_near,
        late_cross,
        *filled,
        hole,
        aliases={15 + i: 5 + i for i in range(len(filled))},
        sent=4,
        sems=1 + 3 * -(-layers // SENT),
    )
    return (field, residual, new_sat, new_hist, bottom.reshape(wells))


def solution(mesh):
    return jax.shard_map(
        body,
        mesh=mesh,
        in_specs=(
            P("gz", "gx", None),
            P("gz", "gx", None),
            P("gz", "gx", None),
            P("gz", "gx", None),
            P("gz", "gx", None),
            P(None, "gz", "gx", None),
            P("gx", None),
            P("gx", None),
            P("gx"),
            P("gx"),
        ),
        out_specs=(
            P("gz", "gx", None),
            P("gz", "gx", None),
            P("gz", "gx", None),
            P("gz", "gx", None),
            P("gx"),
        ),
        check_vma=False,
    )
```

```python
import functools

import jax
import jax.numpy as jnp
from jax import lax
from jax.experimental import pallas as pl
from jax.experimental.pallas import tpu as pltpu
from jax.sharding import PartitionSpec as P

SWEEPS = 4
H = SWEEPS + 1
LANES = 128

Z_PARTS = (
    ("p0", H),
    ("tot", H),
    ("t0", H),
    ("stor", H - 1),
    ("t1", H - 1),
    ("t2", H - 1),
    ("frac", 1),
    ("sums", 1),
)


def early_parts(layers):
    own = (H, layers)
    inner = (H, layers - 1)
    return (
        ("t1", *own),
        ("tot", *own),
        ("p0", *own),
        ("dp", *own),
        ("f0", *inner),
        ("f2", *own),
        ("f1", *own),
        ("frac", *own),
        ("p0_d2", *own),
        ("f0_d2", *inner),
        ("f2_d2", *own),
        ("dp_d2", *own),
    )


def late_parts(layers):
    top = H + layers
    both = lambda name, n: ((name, H - n, n), (name, top, n))
    faces = lambda name, n: ((name, H - n, n), (name, top - 1, n))
    return (
        ("rhs", 2, layers + 6),
        ("p1_d2", 3, layers + 4),
        ("g2", 4, layers + 2),
        ("g3", H, layers),
        *both("t1", H - 1),
        *both("tot", H - 1),
        *both("p0", H - 1),
        *both("dp", H - 2),
        *faces("f0", H - 1),
        *both("f2", H - 2),
        *both("f1", H - 2),
        *both("p0_d2", H - 2),
        *faces("f0_d2", 2),
        *both("f2_d2", 1),
        *both("dp_d2", 1),
    )


def tiles(parts):
    return -(-sum(count for _, _, count in parts) // 8)


SEAMS = ("f0", "f1", "f2", "tot", "dp", "p0", "frac", "p1", "rhs2", "rhs3")
PLACES = {
    "t1": ("f1", None, 7),
    "f1": ("f1", 0, 6),
    "tot": ("tot", 0, 7),
    "p0": ("p0", 0, 7),
    "dp": ("dp", 0, 7),
    "dp_d2": ("dp", 1, 6),
    "f0": ("f0", 0, 7),
    "f0_d2": ("f0", 1, 6),
    "f2": ("f2", 0, 7),
    "f2_d2": ("f2", 1, 6),
    "frac": ("frac", 0, 7),
    "p0_d2": ("p0", 1, 6),
    "p1_d2": ("p1", 1, 6),
    "rhs": ("rhs2", 0, 7),
    "g2": ("rhs2", 1, 6),
    "g3": ("rhs3", 1, 6),
}


def pack(message, parts, refs, rows):
    at = 0
    for name, first, count in parts:
        for e in range(first, first + count):
            message[at // 8, at % 8 : at % 8 + 1, :] = refs[name][e, rows[name] : rows[name] + 1, :]
            at += 1


def pack_both(near, cross, parts, up, down, rows, gx):
    last = rows - 1
    outer = {name: 0 if PLACES[name][2] == 7 else 1 for name in PLACES}
    up_rows = {name: last - outer[name] for name in PLACES} | {"f1": last - 1}
    down_rows = dict(outer) | {"f1": 0}
    even = lax.axis_index(gx) % 2 == 0

    @pl.when(even)
    def _():
        pack(near, parts, up, up_rows)
        pack(cross, parts, down, down_rows)

    @pl.when(jnp.logical_not(even))
    def _():
        pack(cross, parts, up, up_rows)
        pack(near, parts, down, down_rows)


def unpack(message, parts, seams, side):
    at = 0
    for name, first, count in parts:
        seam, *places = PLACES[name]
        place = places[side]
        for e in range(first, first + count):
            if place is not None:
                seams[seam][e, place : place + 1, :] = message[at // 8, at % 8 : at % 8 + 1, :]
            at += 1


def unpack_both(near, cross, parts, seams, gx):
    even = lax.axis_index(gx) % 2 == 0

    @pl.when(even)
    def _():
        unpack(near, parts, seams, 0)
        unpack(cross, parts, seams, 1)

    @pl.when(jnp.logical_not(even))
    def _():
        unpack(cross, parts, seams, 0)
        unpack(near, parts, seams, 1)


def mobility(sat, history):
    trapped = history / (1.0 + 1.5 * history)
    excess = jnp.maximum(sat - trapped, 0.0)
    free_gas = 0.5 * (excess + jnp.sqrt(excess * excess + excess / 0.375))
    relperm = jnp.where(sat < history, free_gas * free_gas, sat * sat)
    gas = relperm / 0.5
    total = (1.0 - sat) * (1.0 - sat) + gas
    return (total, gas / total)


def roll(x, shift, axis):
    return pltpu.roll(x, shift % x.shape[axis], axis)


def loop(first, last, step, carry, unroll=4):
    groups = (last - first) // unroll

    def group(g, carry):
        for i in range(unroll):
            carry = step(first + g * unroll + i, carry)
        return carry

    carry = lax.fori_loop(0, groups, group, carry)
    for index in range(first + groups * unroll, last):
        carry = step(index, carry)
    return carry


def split(x):
    high = x.astype(jnp.bfloat16)
    return (high, (x - high.astype(jnp.float32)).astype(jnp.bfloat16))


def at_places(cell, first_layer, layers, rows, columns):
    layer = cell // (rows * columns)
    row = (cell - layer * (rows * columns)) // columns
    place = (layer - first_layer) * rows + row
    return lax.broadcasted_iota(jnp.int32, (layers * rows, cell.shape[1]), 0) == place


def at_columns(cell, columns):
    return lax.broadcasted_iota(jnp.int32, (columns, cell.shape[1]), 0) == cell % columns


def gather(field, at_place, at_column):
    high, low = split(field)
    hot = at_column.astype(jnp.bfloat16)
    by_column = jnp.dot(high, hot, preferred_element_type=jnp.float32) + jnp.dot(
        low, hot, preferred_element_type=jnp.float32
    )
    return jnp.sum(jnp.where(at_place, by_column, 0.0), axis=0, keepdims=True)


def flatten(block, spread):
    perfs, wells = block.shape
    spread[...] = jnp.zeros(spread.shape, jnp.float32)
    spread[:, 0:wells] = block
    wide = spread[...]
    shift = wells
    while shift < LANES:
        wide = wide + roll(wide, shift, 1)
        shift *= 2
    each = LANES // wells
    entry = lax.broadcasted_iota(jnp.int32, (perfs, LANES), 0)
    group = lax.broadcasted_iota(jnp.int32, (perfs, LANES), 1) // wells
    tiles = [
        jnp.sum(jnp.where(entry == first + group, wide, 0.0), axis=0, keepdims=True)
        for first in range(0, perfs, each)
    ]
    return jnp.concatenate(tiles, axis=1)


def prepare_kernel(
    sat,
    hist,
    pressure,
    storage,
    trans,
    cell_in,
    index_in,
    control_in,
    target_in,
    p0e,
    tote,
    frace,
    stor,
    t0,
    t1,
    t2,
    near,
    cross,
    sums,
    cell,
    wells,
    perfs,
    hot,
    sat_v,
    hist_v,
    cell_v,
    index_v,
    control_v,
    target_v,
    spread,
    sems,
    *,
    gz,
):
    layers, rows, columns = pressure.shape
    ext = layers + 2 * H
    own = pl.ds(H, layers)
    copies = [
        pltpu.make_async_copy(a, b, sems.at[i])
        for i, (a, b) in enumerate(
            (
                (sat, sat_v),
                (hist, hist_v),
                (cell_in, cell_v),
                (index_in, index_v),
                (control_in, control_v),
                (target_in, target_v),
                (pressure, p0e.at[own]),
                (trans.at[0], t0.at[own]),
                (storage, stor.at[own]),
                (trans.at[1], t1.at[own]),
                (trans.at[2], t2.at[own]),
            )
        )
    ]
    for copy in copies:
        copy.start()
    for copy in copies[:2]:
        copy.wait()

    def layer_step(l, carry):
        t, f = mobility(sat_v[l], hist_v[l])
        tote[l + H] = t
        frace[l + H] = f
        return carry

    loop(0, layers, layer_step, 0)
    for copy in copies[2:7]:
        copy.wait()
    count, group = cell_v.shape
    cell[...] = flatten(cell_v[...].astype(jnp.float32), spread).astype(jnp.int32)
    wells[0:1, :] = flatten(index_v[...], spread)
    wells[1:2, :] = flatten(jnp.broadcast_to(target_v[...], (count, group)), spread)
    wells[2:3, :] = flatten(
        jnp.broadcast_to(control_v[...].astype(jnp.float32), (count, group)), spread
    )
    at_place = at_places(cell[...], lax.axis_index(gz) * layers, layers, rows, columns)
    at_column = at_columns(cell[...], columns)
    hot[...] = at_place.astype(jnp.bfloat16)
    flat = (layers * rows, columns)
    weight = wells[0:1, :] * gather(tote[own].reshape(flat), at_place, at_column)
    cell_p = gather(p0e[own].reshape(flat), at_place, at_column)
    perfs[0:1, :] = weight
    perfs[1:2, :] = cell_p
    for i, value in enumerate((weight * cell_p, weight)):
        part = value[:, 0:LANES]
        for lane in range(LANES, value.shape[1], LANES):
            part = part + value[:, lane : lane + LANES]
        shift = LANES // 2
        while shift >= group:
            part = part + roll(part, shift, 1)
            shift //= 2
        sums[i : i + 1, :] = part
    for copy in copies[7:]:
        copy.wait()
    even = lax.axis_index(gz) % 2 == 0
    refs = {"p0": p0e, "tot": tote, "t0": t0, "stor": stor, "t1": t1, "t2": t2, "frac": frace}
    for message, is_top in ((near, even), (cross, jnp.logical_not(even))):
        at = 0
        for name, count in Z_PARTS:
            if name == "sums" and message is cross:
                continue
            if name == "sums":
                message[at] = jnp.zeros((rows, columns), jnp.float32)
                message[at, 0:2, 0:LANES] = sums[...]
            else:
                edge = jnp.where(is_top, H + layers - count, H)
                message[pl.ds(at, count)] = refs[name][pl.ds(edge, count)]
            at += count


def masks(rows, columns):
    row = lax.broadcasted_iota(jnp.int32, (rows, columns), 0)
    column = lax.broadcasted_iota(jnp.int32, (rows, columns), 1)
    return (row == rows - 1, column == columns - 1)


def lateral_faces(tot, t1, t2, store, last_row, last_column, top_x):
    along = jnp.where(last_row, 0.0, t1) * 0.5 * (tot + roll(tot, -1, 0))
    across = jnp.where(last_column, 0.0, t2) * 0.5 * (tot + roll(tot, -1, 1))
    part = store + along + roll(along, 1, 0) + across + roll(across, 1, 1)
    return (jnp.where(last_row, jnp.where(top_x, 0.0, t1), along), across, part)


def is_last(axis):
    return lax.axis_index(axis) == lax.axis_size(axis) - 1


def first_sweep(e, p0e, stor, f0e, f1e, f2e, dpe, last_row):
    above = f0e[e]
    below = f0e[e - 1]
    along = jnp.where(last_row, 0.0, f1e[e])
    across = f2e[e]
    diag = dpe[e] + above + below
    p = p0e[e]
    base = stor[e] * p + above * p0e[e + 1] + below * p0e[e - 1]
    base = base + along * roll(p, -1, 0) + roll(along * p, 1, 0)
    base = base + across * roll(p, -1, 1) + roll(across * p, 1, 1)
    return (base, jnp.where(diag > 0.0, 1.0 / diag, 0.0))


def faces_kernel(*refs, layers, gx):
    p0e, tote, frace, stor, t0, t1, t2, part = refs[:8]
    f0e, f1e, f2e, dpe, base, inverse, near, cross, sums = refs[8:]
    _, rows, columns = p0e.shape
    last_row, last_column = masks(rows, columns)
    top_x = is_last(gx)

    def step(e, carry):
        tot = tote[e]
        f0e[e] = t0[e] * 0.5 * (tot + tote[e + 1])
        f1e[e], f2e[e], dpe[e] = lateral_faces(
            tot, t1[e], t2[e], stor[e], last_row, last_column, top_x
        )
        return carry

    loop(H, H + layers, step, 0)
    sums[...] = part[...]
    refs = {"t1": f1e, "tot": tote, "p0": p0e, "dp": dpe, "f0": f0e, "f2": f2e, "f1": f1e}
    refs |= {"frac": frace, "p0_d2": p0e, "f0_d2": f0e, "f2_d2": f2e, "dp_d2": dpe}
    pack_both(near, cross, early_parts(layers), refs, refs, rows, gx)

    def sweep_step(e, carry):
        base[e], inverse[e] = first_sweep(e, p0e, stor, f0e, f1e, f2e, dpe, last_row)
        return carry

    loop(H + 1, H + layers - 1, sweep_step, 0)


def well_holes(sums, wells):
    repeat = lambda x: jnp.concatenate([x] * (wells.shape[1] // LANES), axis=1)
    goal = wells[1:2, :]
    return jnp.where(
        wells[2:3, :] == 0.0, (goal + repeat(sums[0:1, :])) / repeat(sums[1:2, :]), goal
    )


def join(a, b):
    return jnp.concatenate([a, b], axis=0)


def seam_faces(first, last, fields, seams, f1, inverse, p):
    p0e, tote, f0e, f1e, dpe = fields
    rows, columns = p0e.shape[1:]
    row = lax.broadcasted_iota(jnp.int32, (rows + 8, columns), 0)
    edge = (row == rows - 1) | (row == rows + 7)

    def step(e, below):
        tot = join(tote[e], seams["tot"][e])
        mixed = join(f1e[e], seams["f1"][e])
        border = jnp.where(edge, mixed * 0.5 * (tot + roll(tot, -1, 0)), 0.0)
        f1[e] = jnp.where(edge, border, mixed)
        above = join(f0e[e], seams["f0"][e])
        diag = join(dpe[e], seams["dp"][e]) + above + below + border + roll(border, 1, 0)
        inverse[e] = jnp.where(diag > 0.0, 1.0 / diag, 0.0)
        p[e] = join(p0e[e], seams["p0"][e])
        return above

    loop(first, last, step, join(f0e[first - 1], seams["f0"][first - 1]))


def seam_kernel(near, cross, *refs, layers, gx):
    fields, refs = refs[:5], refs[5:]
    seams = dict(zip(SEAMS, refs))
    for seam in seams.values():
        seam[...] = jnp.zeros(seam.shape, jnp.float32)
    unpack_both(near, cross, early_parts(layers), seams, gx)
    seam_faces(H + 1, H + layers - 1, fields, seams, *refs[len(SEAMS) :])


def halo_kernel(*refs, layers, gx, gz):
    own_t0, cross, near, cell, wells, own_perfs = refs[10:16]
    p0e, tote, frace, stor, f0e, f1e, f2e, dpe, base, inverse, perfs, hot = refs[16:]
    ext, rows, columns = p0e.shape
    even = lax.axis_index(gz) % 2 == 0
    top_z = is_last(gz)
    top_x = is_last(gx)
    last_row, last_column = masks(rows, columns)
    where = {}
    at = 0
    for name, count in Z_PARTS:
        where[name] = (at, count)
        at += count

    def halo(name, e):
        at, count = where[name]
        low = e < H
        at = at + e - (H - count if low else H + layers)
        one, two = (near[at], cross[at])
        return jnp.where(even, two, one) if low else jnp.where(even, one, two)

    for name, target in (("p0", p0e), ("tot", tote), ("frac", frace), ("stor", stor)):
        count = where[name][1]
        for e in (*range(H - count, H), *range(H + layers, H + layers + count)):
            target[e] = halo(name, e)
    f0e[H + layers - 1] = jnp.where(top_z, 0.0, own_t0[H + layers - 1]) * 0.5 * (
        tote[H + layers - 1] + tote[H + layers]
    )
    for e in (*range(0, H), *range(H + layers, ext - 1)):
        f0e[e] = halo("t0", e) * 0.5 * (tote[e] + tote[e + 1])
    for e in (*range(1, H), *range(H + layers, ext - 1)):
        f1e[e], f2e[e], dpe[e] = lateral_faces(
            tote[e], halo("t1", e), halo("t2", e), stor[e], last_row, last_column, top_x
        )
    for e in (*range(1, H + 1), *range(H + layers - 1, ext - 1)):
        base[e], inverse[e] = first_sweep(e, p0e, stor, f0e, f1e, f2e, dpe, last_row)
    width = H - 1
    first = lax.axis_index(gz) * layers
    sides = ((1, first - width), (H + layers, first + layers))
    at_place = [at_places(cell[...], layer, width, rows, columns) for _, layer in sides]
    at_place = jnp.concatenate(at_place, axis=0)
    at_column = at_columns(cell[...], columns)
    hot[...] = at_place.astype(jnp.bfloat16)
    flat = (width * rows, columns)
    both = lambda ref: join(*(ref[e : e + width].reshape(flat) for e, _ in sides))
    weight = wells[0:1, :] * gather(both(tote), at_place, at_column)
    perfs[0:1, :] = own_perfs[0:1, :] + weight
    perfs[1:2, :] = own_perfs[1:2, :] + gather(both(p0e), at_place, at_column)


def build_kernel(*refs, layers, gx):
    p0e, stor, f0e, f1e, f2e, dpe, tote, base, inverse, sums, perfs, hot, own_hot = refs[:13]
    cell, wells, rhse, source, x_near, x_cross, bottom, p1, g2u, g2d, g3u, g3d = refs[13:]
    ext, rows, columns = p0e.shape
    last_row, _ = masks(rows, columns)
    hole = well_holes(sums[...], wells[...])
    bottom[...] = hole[:, 0:LANES]
    rate = perfs[0:1, :] * (hole - perfs[1:2, :])
    pieces = split(jnp.where(at_columns(cell[...], columns), rate, 0.0))

    def scatter(mask):
        spread = [
            lax.dot_general(
                mask, piece, (((1,), (1,)), ((), ())), preferred_element_type=jnp.float32
            )
            for piece in pieces
        ]
        return (spread[0] + spread[1]).reshape(-1, rows, columns)

    width = H - 1
    inside = scatter(own_hot[...])
    outside = scatter(hot[...])
    source[...] = inside
    rhse[H : ext - H] = inside
    rhse[1:H] = outside[:width]
    rhse[ext - H : ext - 1] = outside[width:]

    def first_step(e, carry):
        wells_rate = rhse[e]
        p1[e] = (base[e] + wells_rate) * inverse[e]
        rhse[e] = stor[e] * p0e[e] + wells_rate
        return carry

    loop(1, ext - 1, first_step, 0)

    def second_step(e, carry):
        along = jnp.where(last_row, 0.0, f1e[e])
        across = f2e[e]
        p = p1[e]
        rhs = rhse[e]
        lower = roll(along * p, 1, 0)
        upper = along * roll(p, -1, 0)
        g2u[e] = rhs + lower
        g2d[e] = rhs + upper
        new = rhs + lower + upper + f0e[e] * p1[e + 1] + f0e[e - 1] * p1[e - 1]
        new = new + across * roll(p, -1, 1) + roll(across * p, 1, 1)
        p2 = new * inverse[e]
        g3u[e] = rhs + roll(along * p2, 1, 0)
        g3d[e] = rhs + along * roll(p2, -1, 0)
        return carry

    loop(H - 1, ext - H + 1, second_step, 0)

    shared = {"t1": f1e, "tot": tote, "p0": p0e, "dp": dpe, "f0": f0e, "f2": f2e, "f1": f1e}
    shared |= {"p0_d2": p0e, "f0_d2": f0e, "f2_d2": f2e, "dp_d2": dpe, "rhs": rhse, "p1_d2": p1}
    up = shared | {"g2": g2u, "g3": g3u}
    down = shared | {"g2": g2d, "g3": g3d}
    pack_both(x_near, x_cross, late_parts(layers), up, down, rows, gx)


def finish_kernel(*refs, gx):
    sat, hist, volume, storage, source = refs[:5]
    p0e, tote, frace, f0e, f1e, f2e, dpe, rhse, near, cross = refs[5:15]
    hole = refs[18 + len(SEAMS)]
    refs = refs[19 + len(SEAMS) :]
    new_p, residual, new_sat, new_hist, bottom = refs[:5]
    seams = dict(zip(SEAMS, refs[5:]))
    f1, rdiag, pa, pb = refs[5 + len(SEAMS) :]
    bottom[...] = hole[:, 0 : bottom.shape[1]]
    layers, rows, columns = sat.shape
    ext = layers + 2 * H
    unpack_both(near, cross, late_parts(layers), seams, gx)
    sf0, sf2, sfrac = (seams[name] for name in ("f0", "f2", "frac"))
    row = lax.broadcasted_iota(jnp.int32, (rows + 8, columns), 0)
    beyond = (row == rows + 1) | (row == rows + 6)
    blank = jnp.zeros((rows, columns), jnp.float32)
    pa[0] = join(p0e[0], seams["p0"][0])
    pa[ext - 1] = join(p0e[ext - 1], seams["p0"][ext - 1])
    for first, last in ((1, H + 1), (ext - H - 1, ext - 1)):
        seam_faces(first, last, (p0e, tote, f0e, f1e, dpe), seams, f1, rdiag, pa)

    def sweep(number, old, new):
        def step(e, below):
            p = old[e]
            above = old[e + 1]
            face = join(f0e[e], sf0[e])
            x = f1[e]
            y = join(f2e[e], sf2[e])
            side = seams["rhs2"][e]
            if number == 3:
                side = jnp.where(beyond[rows:], seams["rhs3"][e], side)
            total = join(rhse[e], side) + below + face * above
            total = total + x * roll(p, -1, 0) + roll(x * p, 1, 0)
            total = total + y * roll(p, -1, 1) + roll(y * p, 1, 1)
            value = total * rdiag[e]
            if number == 1:
                value = jnp.where(beyond, join(blank, seams["p1"][e]), value)
            new[e] = value
            return face * p

        first = join(f0e[number - 1], sf0[number - 1]) * old[number - 1]
        loop(number, ext - number, step, first)

    fields = (pa, pb)
    for number in range(1, SWEEPS + 1):
        sweep(number, fields[(number - 1) % 2], fields[number % 2])
    field = fields[SWEEPS % 2]

    def flow(face, p, p_next, f, f_next):
        water = face * (p - p_next)
        return (water, water * jnp.where(water > 0, f, f_next))

    def last_step(l, carry):
        below_w, below_g = carry
        e = l + H
        p = field[e]
        f = join(frace[e], sfrac[e])
        own_p = p[:rows]
        own_f = f[:rows]
        above_w, above_g = flow(f0e[e], own_p, field[e + 1][:rows], own_f, frace[e + 1])
        xw, xg = flow(f1[e], p, roll(p, -1, 0), f, roll(f, -1, 0))
        yw, yg = flow(f2e[e], own_p, roll(own_p, -1, 1), own_f, roll(own_f, -1, 1))
        water = above_w - below_w + (xw - roll(xw, 1, 0))[:rows] + yw - roll(yw, 1, 1)
        out = above_g - below_g + (xg - roll(xg, 1, 0))[:rows] + yg - roll(yg, 1, 1)
        new_p[l] = own_p
        residual[l] = rhse[e] - storage[l] * own_p - water
        src = source[l]
        gas = jnp.maximum(src, 0.0) + jnp.minimum(src, 0.0) * own_f
        s = sat[l] + volume[l] * (gas - out)
        new_sat[l] = s
        new_hist[l] = jnp.maximum(hist[l], s)
        return (above_w, above_g)

    first = flow(f0e[H - 1], field[H - 1][:rows], field[H][:rows], frace[H - 1], frace[H])
    loop(0, layers, last_step, first)


def swap(block, axis, first):
    pairs = [(i, i + 1) for i in range(first, lax.axis_size(axis) - 1, 2)]
    return lax.ppermute(block, axis, pairs + [(b, a) for a, b in pairs])


def pin(*shape, dtype=jnp.float32):
    return pltpu.VMEM(shape, dtype)


VMEM = pl.BlockSpec(memory_space=pltpu.VMEM)
HBM = pl.BlockSpec(memory_space=pltpu.HBM)


def call(kernel, outs, scratch, *args, space=VMEM, sems=0, aliases={}):
    as_struct = lambda s: s if hasattr(s, "dtype") else jax.ShapeDtypeStruct(s, jnp.float32)
    as_scratch = lambda s: pltpu.VMEM(as_struct(s).shape, as_struct(s).dtype)
    return pl.pallas_call(
        kernel,
        out_shape=[as_struct(s) for s in outs],
        in_specs=[space] * len(args),
        out_specs=[VMEM] * len(outs),
        scratch_shapes=[as_scratch(s) for s in scratch]
        + ([pltpu.SemaphoreType.DMA((sems,))] if sems else []),
        input_output_aliases=aliases,
        compiler_params=pltpu.CompilerParams(vmem_limit_bytes=24 * 1024 * 1024),
    )(*(pltpu.with_memory_space_constraint(a, pltpu.HBM) if space is HBM else a for a in args))


def body(
    pressure,
    saturation,
    sat_history,
    storage,
    step_volume,
    transmiss,
    perf_cell,
    perf_index,
    control,
    target,
):
    layers, rows, columns = pressure.shape
    ext = layers + 2 * H
    wells, perfs = perf_cell.shape
    block = (layers, rows, columns)
    pinned = pin(*block)
    ext_block = pin(ext, rows, columns)
    z_layers = sum(count for _, count in Z_PARTS)
    z_near, z_cross = (pin(n, rows, columns) for n in (z_layers, z_layers - 1))
    entries = wells * perfs
    early, late = (pin(tiles(f(layers)), 8, columns) for f in (early_parts, late_parts))
    seams = [pin(ext, 8, columns)] * len(SEAMS)
    *fields, near, cross, part, cell, per_perf, perf_values, own_hot = call(
        functools.partial(prepare_kernel, gz="gz"),
        [ext_block] * 7
        + [z_near, z_cross]
        + [
            pin(2, LANES),
            pin(1, entries, dtype=jnp.int32),
            pin(3, entries),
            pin(2, entries),
            pin(layers * rows, entries, dtype=jnp.bfloat16),
        ],
        [
            block,
            block,
            jax.ShapeDtypeStruct((perfs, wells), jnp.int32),
            (perfs, wells),
            jax.ShapeDtypeStruct((1, wells), jnp.int32),
            (1, wells),
            (perfs, LANES),
        ],
        saturation,
        sat_history,
        pressure,
        storage,
        transmiss,
        perf_cell.T,
        perf_index.T,
        control.reshape(1, wells),
        target.reshape(1, wells),
        space=HBM,
        sems=11,
    )
    cross = swap(cross, "gz", 1)
    near = swap(near, "gz", 0)
    p0e, tote, frace, stor, t0, t1, t2 = fields
    f0e, f1e, f2e, dpe, base, inverse, early_near, early_cross, part = call(
        functools.partial(faces_kernel, layers=layers, gx="gx"),
        [ext_block] * 6 + [early, early, pin(2, LANES)],
        [],
        *fields,
        part,
    )
    early_cross = swap(early_cross, "gx", 1)
    early_near = swap(early_near, "gx", 0)
    sums = part + near[-1, 0:2, 0:LANES]
    step = 2
    while step < lax.axis_size("gz"):
        pairs = [(i, i ^ step) for i in range(lax.axis_size("gz"))]
        tile = jnp.pad(sums, ((0, 8 - sums.shape[0]), (0, 0)))
        sums = sums + lax.ppermute(tile, "gz", pairs)[: sums.shape[0]]
        step *= 2
    p0e, tote, frace, stor, f0e, f1e, f2e, dpe, base, inverse, perf_values, hot = call(
        functools.partial(halo_kernel, layers=layers, gx="gx", gz="gz"),
        [ext_block] * 10
        + [pin(2, entries), pin(2 * (H - 1) * rows, entries, dtype=jnp.bfloat16)],
        [],
        p0e,
        tote,
        frace,
        stor,
        f0e,
        f1e,
        f2e,
        dpe,
        base,
        inverse,
        t0,
        cross,
        near,
        cell,
        per_perf,
        perf_values,
        aliases={i: i for i in range(10)},
    )
    rhse, source, late_near, late_cross, hole = call(
        functools.partial(build_kernel, layers=layers, gx="gx"),
        [ext_block, pinned, late, late, pin(1, LANES)],
        [ext_block] * 5,
        p0e,
        stor,
        f0e,
        f1e,
        f2e,
        dpe,
        tote,
        base,
        inverse,
        sums,
        perf_values,
        hot,
        own_hot,
        cell,
        per_perf,
    )
    late_cross = swap(late_cross, "gx", 1)
    late_near = swap(late_near, "gx", 0)
    early_near, early_cross, rhse = lax.optimization_barrier((early_near, early_cross, rhse))
    joined = [pin(ext, rows + 8, columns)] * 3
    filled = call(
        functools.partial(seam_kernel, layers=layers, gx="gx"),
        seams + joined,
        [],
        early_near,
        early_cross,
        p0e,
        tote,
        f0e,
        f1e,
        dpe,
    )
    field, residual, new_sat, new_hist, bottom, *_ = call(
        functools.partial(finish_kernel, gx="gx"),
        [block] * 4 + [(1, wells)] + seams + joined,
        [joined[0]],
        saturation,
        sat_history,
        step_volume,
        storage,
        source,
        p0e,
        tote,
        frace,
        f0e,
        f1e,
        f2e,
        dpe,
        rhse,
        late_near,
        late_cross,
        *filled,
        hole,
        aliases={15 + i: 5 + i for i in range(len(filled))},
    )
    return (field, residual, new_sat, new_hist, bottom.reshape(wells))


def solution(mesh):
    return jax.shard_map(
        body,
        mesh=mesh,
        in_specs=(
            P("gz", "gx", None),
            P("gz", "gx", None),
            P("gz", "gx", None),
            P("gz", "gx", None),
            P("gz", "gx", None),
            P(None, "gz", "gx", None),
            P("gx", None),
            P("gx", None),
            P("gx"),
            P("gx"),
        ),
        out_specs=(
            P("gz", "gx", None),
            P("gz", "gx", None),
            P("gz", "gx", None),
            P("gz", "gx", None),
            P("gx"),
        ),
        check_vma=False,
    )
```

```python
import functools

import jax
import jax.numpy as jnp
from jax import lax
from jax.experimental import pallas as pl
from jax.experimental.pallas import tpu as pltpu
from jax.sharding import PartitionSpec as P

SWEEPS = 4
H = SWEEPS + 1
LANES = 128
LOADED = 4

Z_PARTS = (
    ("p0", H),
    ("tot", H),
    ("t0", H),
    ("stor", H - 1),
    ("t1", H - 1),
    ("t2", H - 1),
    ("frac", 1),
    ("sums", 1),
)


def early_parts(layers):
    own = (H, layers)
    inner = (H, layers - 1)
    return (
        ("t1", *own),
        ("tot", *own),
        ("p0", *own),
        ("dp", *own),
        ("f0", *inner),
        ("f2", *own),
        ("f1", *own),
        ("frac", *own),
        ("p0_d2", *own),
        ("f0_d2", *inner),
        ("f2_d2", *own),
        ("dp_d2", *own),
    )


def late_parts(layers):
    top = H + layers
    both = lambda name, n: ((name, H - n, n), (name, top, n))
    faces = lambda name, n: ((name, H - n, n), (name, top - 1, n))
    return (
        ("rhs", 2, layers + 6),
        ("p1_d2", 3, layers + 4),
        ("g2", 4, layers + 2),
        ("g3", H, layers),
        *both("t1", H - 1),
        *both("tot", H - 1),
        *both("p0", H - 1),
        *both("dp", H - 2),
        *faces("f0", H - 1),
        *both("f2", H - 2),
        *both("f1", H - 2),
        *both("p0_d2", H - 2),
        *faces("f0_d2", 2),
        *both("f2_d2", 1),
        *both("dp_d2", 1),
    )


def tiles(parts):
    return -(-sum(count for _, _, count in parts) // 8)


SEAMS = ("f0", "f1", "f2", "tot", "dp", "p0", "frac", "p1", "rhs2", "rhs3")
PLACES = {
    "t1": ("f1", None, 7),
    "f1": ("f1", 0, 6),
    "tot": ("tot", 0, 7),
    "p0": ("p0", 0, 7),
    "dp": ("dp", 0, 7),
    "dp_d2": ("dp", 1, 6),
    "f0": ("f0", 0, 7),
    "f0_d2": ("f0", 1, 6),
    "f2": ("f2", 0, 7),
    "f2_d2": ("f2", 1, 6),
    "frac": ("frac", 0, 7),
    "p0_d2": ("p0", 1, 6),
    "p1_d2": ("p1", 1, 6),
    "rhs": ("rhs2", 0, 7),
    "g2": ("rhs2", 1, 6),
    "g3": ("rhs3", 1, 6),
}


def pack(message, parts, refs, rows):
    at = 0
    for name, first, count in parts:
        for e in range(first, first + count):
            message[at // 8, at % 8 : at % 8 + 1, :] = refs[name][e, rows[name] : rows[name] + 1, :]
            at += 1


def pack_both(near, cross, parts, up, down, rows, gx):
    last = rows - 1
    outer = {name: 0 if PLACES[name][2] == 7 else 1 for name in PLACES}
    up_rows = {name: last - outer[name] for name in PLACES} | {"f1": last - 1}
    down_rows = dict(outer) | {"f1": 0}
    even = lax.axis_index(gx) % 2 == 0

    @pl.when(even)
    def _():
        pack(near, parts, up, up_rows)
        pack(cross, parts, down, down_rows)

    @pl.when(jnp.logical_not(even))
    def _():
        pack(cross, parts, up, up_rows)
        pack(near, parts, down, down_rows)


def unpack(message, parts, seams, side):
    at = 0
    for name, first, count in parts:
        seam, *places = PLACES[name]
        place = places[side]
        for e in range(first, first + count):
            if place is not None:
                seams[seam][e, place : place + 1, :] = message[at // 8, at % 8 : at % 8 + 1, :]
            at += 1


def unpack_both(near, cross, parts, seams, gx):
    even = lax.axis_index(gx) % 2 == 0

    @pl.when(even)
    def _():
        unpack(near, parts, seams, 0)
        unpack(cross, parts, seams, 1)

    @pl.when(jnp.logical_not(even))
    def _():
        unpack(cross, parts, seams, 0)
        unpack(near, parts, seams, 1)


def mobility(sat, history):
    trapped = history / (1.0 + 1.5 * history)
    excess = jnp.maximum(sat - trapped, 0.0)
    free_gas = 0.5 * (excess + jnp.sqrt(excess * excess + excess / 0.375))
    relperm = jnp.where(sat < history, free_gas * free_gas, sat * sat)
    gas = relperm / 0.5
    total = (1.0 - sat) * (1.0 - sat) + gas
    return (total, gas / total)


def roll(x, shift, axis):
    return pltpu.roll(x, shift % x.shape[axis], axis)


def loop(first, last, step, carry, unroll=4):
    groups = (last - first) // unroll

    def group(g, carry):
        for i in range(unroll):
            carry = step(first + g * unroll + i, carry)
        return carry

    carry = lax.fori_loop(0, groups, group, carry)
    for index in range(first + groups * unroll, last):
        carry = step(index, carry)
    return carry


def split(x):
    high = x.astype(jnp.bfloat16)
    return (high, (x - high.astype(jnp.float32)).astype(jnp.bfloat16))


def at_places(cell, first_layer, layers, rows, columns):
    layer = cell // (rows * columns)
    row = (cell - layer * (rows * columns)) // columns
    place = (layer - first_layer) * rows + row
    return lax.broadcasted_iota(jnp.int32, (layers * rows, cell.shape[1]), 0) == place


def at_columns(cell, columns):
    return lax.broadcasted_iota(jnp.int32, (columns, cell.shape[1]), 0) == cell % columns


def gather(field, at_place, at_column):
    high, low = split(field)
    hot = at_column.astype(jnp.bfloat16)
    by_column = jnp.dot(high, hot, preferred_element_type=jnp.float32) + jnp.dot(
        low, hot, preferred_element_type=jnp.float32
    )
    return jnp.sum(jnp.where(at_place, by_column, 0.0), axis=0, keepdims=True)


def flatten(block, spread):
    perfs, wells = block.shape
    spread[...] = jnp.zeros(spread.shape, jnp.float32)
    spread[:, 0:wells] = block
    wide = spread[...]
    shift = wells
    while shift < LANES:
        wide = wide + roll(wide, shift, 1)
        shift *= 2
    each = LANES // wells
    entry = lax.broadcasted_iota(jnp.int32, (perfs, LANES), 0)
    group = lax.broadcasted_iota(jnp.int32, (perfs, LANES), 1) // wells
    tiles = [
        jnp.sum(jnp.where(entry == first + group, wide, 0.0), axis=0, keepdims=True)
        for first in range(0, perfs, each)
    ]
    return jnp.concatenate(tiles, axis=1)


def prepare_kernel(
    sat,
    hist,
    pressure,
    storage,
    trans,
    cell_in,
    index_in,
    control_in,
    target_in,
    p0e,
    tote,
    frace,
    stor,
    t0,
    t1,
    t2,
    near,
    cross,
    sums,
    cell,
    wells,
    perfs,
    hot,
    sat_v,
    hist_v,
    cell_v,
    index_v,
    control_v,
    target_v,
    spread,
    sems,
    *,
    gz,
):
    layers, rows, columns = pressure.shape
    ext = layers + 2 * H
    own = pl.ds(H, layers)
    parts = [(l, min(LOADED, layers - l)) for l in range(0, layers, LOADED)]
    in_parts = [
        (source.at[pl.ds(l, n)], target.at[pl.ds(offset + l, n)])
        for source, target, offset in ((sat, sat_v, 0), (hist, hist_v, 0), (pressure, p0e, H))
        for l, n in parts
    ]
    small = [(cell_in, cell_v), (index_in, index_v), (control_in, control_v), (target_in, target_v)]
    large = [
        (trans.at[0], t0.at[own]),
        (storage, stor.at[own]),
        (trans.at[1], t1.at[own]),
        (trans.at[2], t2.at[own]),
    ]
    copies = [
        pltpu.make_async_copy(a, b, sems.at[i])
        for i, (a, b) in enumerate(in_parts + small + large)
    ]
    for copy in copies:
        copy.start()

    def layer_step(l, carry):
        t, f = mobility(sat_v[l], hist_v[l])
        tote[l + H] = t
        frace[l + H] = f
        return carry

    for i, (l, n) in enumerate(parts):
        copies[i].wait()
        copies[len(parts) + i].wait()
        loop(l, l + n, layer_step, 0)
    for copy in copies[2 * len(parts) : -len(large)]:
        copy.wait()
    count, group = cell_v.shape
    cell[...] = flatten(cell_v[...].astype(jnp.float32), spread).astype(jnp.int32)
    wells[0:1, :] = flatten(index_v[...], spread)
    wells[1:2, :] = flatten(jnp.broadcast_to(target_v[...], (count, group)), spread)
    wells[2:3, :] = flatten(
        jnp.broadcast_to(control_v[...].astype(jnp.float32), (count, group)), spread
    )
    at_place = at_places(cell[...], lax.axis_index(gz) * layers, layers, rows, columns)
    at_column = at_columns(cell[...], columns)
    hot[...] = at_place.astype(jnp.bfloat16)
    flat = (layers * rows, columns)
    weight = wells[0:1, :] * gather(tote[own].reshape(flat), at_place, at_column)
    cell_p = gather(p0e[own].reshape(flat), at_place, at_column)
    perfs[0:1, :] = weight
    perfs[1:2, :] = cell_p
    for i, value in enumerate((weight * cell_p, weight)):
        part = value[:, 0:LANES]
        for lane in range(LANES, value.shape[1], LANES):
            part = part + value[:, lane : lane + LANES]
        shift = LANES // 2
        while shift >= group:
            part = part + roll(part, shift, 1)
            shift //= 2
        sums[i : i + 1, :] = part
    for copy in copies[-len(large) :]:
        copy.wait()
    even = lax.axis_index(gz) % 2 == 0
    refs = {"p0": p0e, "tot": tote, "t0": t0, "stor": stor, "t1": t1, "t2": t2, "frac": frace}
    for message, is_top in ((near, even), (cross, jnp.logical_not(even))):
        at = 0
        for name, count in Z_PARTS:
            if name == "sums" and message is cross:
                continue
            if name == "sums":
                message[at] = jnp.zeros((rows, columns), jnp.float32)
                message[at, 0:2, 0:LANES] = sums[...]
            else:
                edge = jnp.where(is_top, H + layers - count, H)
                message[pl.ds(at, count)] = refs[name][pl.ds(edge, count)]
            at += count


def masks(rows, columns):
    row = lax.broadcasted_iota(jnp.int32, (rows, columns), 0)
    column = lax.broadcasted_iota(jnp.int32, (rows, columns), 1)
    return (row == rows - 1, column == columns - 1)


def lateral_faces(tot, t1, t2, store, last_row, last_column, top_x):
    along = jnp.where(last_row, 0.0, t1) * 0.5 * (tot + roll(tot, -1, 0))
    across = jnp.where(last_column, 0.0, t2) * 0.5 * (tot + roll(tot, -1, 1))
    part = store + along + roll(along, 1, 0) + across + roll(across, 1, 1)
    return (jnp.where(last_row, jnp.where(top_x, 0.0, t1), along), across, part)


def is_last(axis):
    return lax.axis_index(axis) == lax.axis_size(axis) - 1


def first_sweep(e, p0e, stor, f0e, f1e, f2e, dpe, last_row):
    above = f0e[e]
    below = f0e[e - 1]
    along = jnp.where(last_row, 0.0, f1e[e])
    across = f2e[e]
    diag = dpe[e] + above + below
    p = p0e[e]
    base = stor[e] * p + above * p0e[e + 1] + below * p0e[e - 1]
    base = base + along * roll(p, -1, 0) + roll(along * p, 1, 0)
    base = base + across * roll(p, -1, 1) + roll(across * p, 1, 1)
    return (base, jnp.where(diag > 0.0, 1.0 / diag, 0.0))


def faces_kernel(*refs, layers, gx):
    p0e, tote, frace, stor, t0, t1, t2, part = refs[:8]
    f0e, f1e, f2e, dpe, base, inverse, near, cross, sums = refs[8:]
    _, rows, columns = p0e.shape
    last_row, last_column = masks(rows, columns)
    top_x = is_last(gx)

    def step(e, carry):
        tot = tote[e]
        f0e[e] = t0[e] * 0.5 * (tot + tote[e + 1])
        f1e[e], f2e[e], dpe[e] = lateral_faces(
            tot, t1[e], t2[e], stor[e], last_row, last_column, top_x
        )
        return carry

    loop(H, H + layers, step, 0)
    sums[...] = part[...]
    refs = {"t1": f1e, "tot": tote, "p0": p0e, "dp": dpe, "f0": f0e, "f2": f2e, "f1": f1e}
    refs |= {"frac": frace, "p0_d2": p0e, "f0_d2": f0e, "f2_d2": f2e, "dp_d2": dpe}
    pack_both(near, cross, early_parts(layers), refs, refs, rows, gx)

    def sweep_step(e, carry):
        base[e], inverse[e] = first_sweep(e, p0e, stor, f0e, f1e, f2e, dpe, last_row)
        return carry

    loop(H + 1, H + layers - 1, sweep_step, 0)


def well_holes(sums, wells):
    repeat = lambda x: jnp.concatenate([x] * (wells.shape[1] // LANES), axis=1)
    goal = wells[1:2, :]
    return jnp.where(
        wells[2:3, :] == 0.0, (goal + repeat(sums[0:1, :])) / repeat(sums[1:2, :]), goal
    )


def join(a, b):
    return jnp.concatenate([a, b], axis=0)


def seam_faces(first, last, fields, seams, f1, inverse, p):
    p0e, tote, f0e, f1e, dpe = fields
    rows, columns = p0e.shape[1:]
    row = lax.broadcasted_iota(jnp.int32, (rows + 8, columns), 0)
    edge = (row == rows - 1) | (row == rows + 7)

    def step(e, below):
        tot = join(tote[e], seams["tot"][e])
        mixed = join(f1e[e], seams["f1"][e])
        border = jnp.where(edge, mixed * 0.5 * (tot + roll(tot, -1, 0)), 0.0)
        f1[e] = jnp.where(edge, border, mixed)
        above = join(f0e[e], seams["f0"][e])
        diag = join(dpe[e], seams["dp"][e]) + above + below + border + roll(border, 1, 0)
        inverse[e] = jnp.where(diag > 0.0, 1.0 / diag, 0.0)
        p[e] = join(p0e[e], seams["p0"][e])
        return above

    loop(first, last, step, join(f0e[first - 1], seams["f0"][first - 1]))


def sweep_layers(number, first, last, old, new, fields, seams, f1, inverse, part):
    rhse, f0e, f2e = fields
    rows, columns = rhse.shape[1:]
    row = lax.broadcasted_iota(jnp.int32, (rows + 8, columns), 0)
    beyond = (row == rows + 1) | (row == rows + 6)
    blank = jnp.zeros((rows, columns), jnp.float32)

    def step(e, below):
        p = old[e]
        above = old[e + 1]
        face = join(f0e[e], seams["f0"][e])
        x = f1[e]
        y = join(f2e[e], seams["f2"][e])
        side = seams["rhs2"][e]
        if number == 3:
            side = jnp.where(beyond[rows:], seams["rhs3"][e], side)
        total = join(rhse[e], side) + below + face * above
        total = total + x * roll(p, -1, 0) + roll(x * p, 1, 0)
        total = total + y * roll(p, -1, 1) + roll(y * p, 1, 1)
        value = total * inverse[e]
        if number == 1:
            value = jnp.where(beyond, join(blank, seams["p1"][e]), value)
        new[e, part] = value[part]
        return face * p

    start = join(f0e[first - 1], seams["f0"][first - 1]) * old[first - 1]
    loop(first, last, step, start)


def seam_kernel(near, cross, *refs, layers, gx):
    p0e, tote, f0e, f1e, f2e, dpe, rhse = refs[:7]
    refs = refs[7:]
    seams = dict(zip(SEAMS, refs))
    f1, inverse, p, p1 = refs[len(SEAMS) :]
    for seam in seams.values():
        seam[...] = jnp.zeros(seam.shape, jnp.float32)
    unpack_both(near, cross, early_parts(layers), seams, gx)
    inner = (H + 1, H + layers - 1)
    seam_faces(*inner, (p0e, tote, f0e, f1e, dpe), seams, f1, inverse, p)
    for e in (H, H + layers - 1):
        p[e] = join(p0e[e], jnp.zeros_like(seams["p0"][e]))
    own = slice(0, p0e.shape[1])
    sweep_layers(1, *inner, p, p1, (rhse, f0e, f2e), seams, f1, inverse, own)


def halo_kernel(*refs, layers, gx, gz):
    own_t0, cross, near, cell, wells, own_perfs = refs[10:16]
    p0e, tote, frace, stor, f0e, f1e, f2e, dpe, base, inverse, perfs, hot = refs[16:]
    ext, rows, columns = p0e.shape
    even = lax.axis_index(gz) % 2 == 0
    top_z = is_last(gz)
    top_x = is_last(gx)
    last_row, last_column = masks(rows, columns)
    where = {}
    at = 0
    for name, count in Z_PARTS:
        where[name] = (at, count)
        at += count

    def halo(name, e):
        at, count = where[name]
        low = e < H
        at = at + e - (H - count if low else H + layers)
        one, two = (near[at], cross[at])
        return jnp.where(even, two, one) if low else jnp.where(even, one, two)

    for name, target in (("p0", p0e), ("tot", tote), ("frac", frace), ("stor", stor)):
        count = where[name][1]
        for e in (*range(H - count, H), *range(H + layers, H + layers + count)):
            target[e] = halo(name, e)
    f0e[H + layers - 1] = jnp.where(top_z, 0.0, own_t0[H + layers - 1]) * 0.5 * (
        tote[H + layers - 1] + tote[H + layers]
    )
    for e in (*range(0, H), *range(H + layers, ext - 1)):
        f0e[e] = halo("t0", e) * 0.5 * (tote[e] + tote[e + 1])
    for e in (*range(1, H), *range(H + layers, ext - 1)):
        f1e[e], f2e[e], dpe[e] = lateral_faces(
            tote[e], halo("t1", e), halo("t2", e), stor[e], last_row, last_column, top_x
        )
    for e in (*range(1, H + 1), *range(H + layers - 1, ext - 1)):
        base[e], inverse[e] = first_sweep(e, p0e, stor, f0e, f1e, f2e, dpe, last_row)
    width = H - 1
    first = lax.axis_index(gz) * layers
    sides = ((1, first - width), (H + layers, first + layers))
    at_place = [at_places(cell[...], layer, width, rows, columns) for _, layer in sides]
    at_place = jnp.concatenate(at_place, axis=0)
    at_column = at_columns(cell[...], columns)
    hot[...] = at_place.astype(jnp.bfloat16)
    flat = (width * rows, columns)
    both = lambda ref: join(*(ref[e : e + width].reshape(flat) for e, _ in sides))
    weight = wells[0:1, :] * gather(both(tote), at_place, at_column)
    perfs[0:1, :] = own_perfs[0:1, :] + weight
    perfs[1:2, :] = own_perfs[1:2, :] + gather(both(p0e), at_place, at_column)


def build_kernel(*refs, layers, gx):
    p0e, stor, f0e, f1e, f2e, dpe, tote, base, inverse, sums, perfs, hot, own_hot = refs[:13]
    cell, wells, rhse, source, x_near, x_cross, bottom, p1, g2u, g2d, g3u, g3d = refs[13:]
    ext, rows, columns = p0e.shape
    last_row, _ = masks(rows, columns)
    hole = well_holes(sums[...], wells[...])
    bottom[...] = hole[:, 0:LANES]
    rate = perfs[0:1, :] * (hole - perfs[1:2, :])
    pieces = split(jnp.where(at_columns(cell[...], columns), rate, 0.0))

    def scatter(mask):
        spread = [
            lax.dot_general(
                mask, piece, (((1,), (1,)), ((), ())), preferred_element_type=jnp.float32
            )
            for piece in pieces
        ]
        return (spread[0] + spread[1]).reshape(-1, rows, columns)

    width = H - 1
    inside = scatter(own_hot[...])
    outside = scatter(hot[...])
    source[...] = inside
    rhse[H : ext - H] = inside
    rhse[1:H] = outside[:width]
    rhse[ext - H : ext - 1] = outside[width:]

    def first_step(e, carry):
        wells_rate = rhse[e]
        p1[e] = (base[e] + wells_rate) * inverse[e]
        rhse[e] = stor[e] * p0e[e] + wells_rate
        return carry

    loop(1, ext - 1, first_step, 0)

    def second_step(e, carry):
        along = jnp.where(last_row, 0.0, f1e[e])
        across = f2e[e]
        p = p1[e]
        rhs = rhse[e]
        lower = roll(along * p, 1, 0)
        upper = along * roll(p, -1, 0)
        g2u[e] = rhs + lower
        g2d[e] = rhs + upper
        new = rhs + lower + upper + f0e[e] * p1[e + 1] + f0e[e - 1] * p1[e - 1]
        new = new + across * roll(p, -1, 1) + roll(across * p, 1, 1)
        p2 = new * inverse[e]
        g3u[e] = rhs + roll(along * p2, 1, 0)
        g3d[e] = rhs + along * roll(p2, -1, 0)
        return carry

    loop(H - 1, ext - H + 1, second_step, 0)

    shared = {"t1": f1e, "tot": tote, "p0": p0e, "dp": dpe, "f0": f0e, "f2": f2e, "f1": f1e}
    shared |= {"p0_d2": p0e, "f0_d2": f0e, "f2_d2": f2e, "dp_d2": dpe, "rhs": rhse, "p1_d2": p1}
    up = shared | {"g2": g2u, "g3": g3u}
    down = shared | {"g2": g2d, "g3": g3d}
    pack_both(x_near, x_cross, late_parts(layers), up, down, rows, gx)


def finish_kernel(*refs, gx):
    sat, hist, volume, storage, source = refs[:5]
    p0e, tote, frace, f0e, f1e, f2e, dpe, rhse, near, cross = refs[5:15]
    hole = refs[19 + len(SEAMS)]
    refs = refs[20 + len(SEAMS) :]
    new_p, residual, new_sat, new_hist, bottom = refs[:5]
    seams = dict(zip(SEAMS, refs[5:]))
    f1, rdiag, pa, pb = refs[5 + len(SEAMS) :]
    bottom[...] = hole[:, 0 : bottom.shape[1]]
    layers, rows, columns = sat.shape
    ext = layers + 2 * H
    unpack_both(near, cross, late_parts(layers), seams, gx)
    sfrac = seams["frac"]
    pa[0] = join(p0e[0], seams["p0"][0])
    pa[ext - 1] = join(p0e[ext - 1], seams["p0"][ext - 1])
    for first, last in ((1, H + 1), (ext - H - 1, ext - 1)):
        seam_faces(first, last, (p0e, tote, f0e, f1e, dpe), seams, f1, rdiag, pa)

    pressures = (pa, pb)
    fields = (rhse, f0e, f2e)
    inner = (H + 1, ext - H - 1)
    everywhere = slice(0, rows + 8)
    for number in range(1, SWEEPS + 1):
        old, new = pressures[(number - 1) % 2], pressures[number % 2]
        ranges = [(number, ext - number, everywhere)]
        if number == 1:
            ranges = [
                (number, inner[0], everywhere),
                (*inner, slice(rows, rows + 8)),
                (inner[1], ext - number, everywhere),
            ]
        for first, last, part in ranges:
            sweep_layers(number, first, last, old, new, fields, seams, f1, rdiag, part)
    field = pressures[SWEEPS % 2]

    def flow(face, p, p_next, f, f_next):
        water = face * (p - p_next)
        return (water, water * jnp.where(water > 0, f, f_next))

    def last_step(l, carry):
        below_w, below_g = carry
        e = l + H
        p = field[e]
        f = join(frace[e], sfrac[e])
        own_p = p[:rows]
        own_f = f[:rows]
        above_w, above_g = flow(f0e[e], own_p, field[e + 1][:rows], own_f, frace[e + 1])
        xw, xg = flow(f1[e], p, roll(p, -1, 0), f, roll(f, -1, 0))
        yw, yg = flow(f2e[e], own_p, roll(own_p, -1, 1), own_f, roll(own_f, -1, 1))
        water = above_w - below_w + (xw - roll(xw, 1, 0))[:rows] + yw - roll(yw, 1, 1)
        out = above_g - below_g + (xg - roll(xg, 1, 0))[:rows] + yg - roll(yg, 1, 1)
        new_p[l] = own_p
        residual[l] = rhse[e] - storage[l] * own_p - water
        src = source[l]
        gas = jnp.maximum(src, 0.0) + jnp.minimum(src, 0.0) * own_f
        s = sat[l] + volume[l] * (gas - out)
        new_sat[l] = s
        new_hist[l] = jnp.maximum(hist[l], s)
        return (above_w, above_g)

    first = flow(f0e[H - 1], field[H - 1][:rows], field[H][:rows], frace[H - 1], frace[H])
    loop(0, layers, last_step, first)


def swap(block, axis, first):
    pairs = [(i, i + 1) for i in range(first, lax.axis_size(axis) - 1, 2)]
    return lax.ppermute(block, axis, pairs + [(b, a) for a, b in pairs])


def pin(*shape, dtype=jnp.float32):
    return pltpu.VMEM(shape, dtype)


VMEM = pl.BlockSpec(memory_space=pltpu.VMEM)
HBM = pl.BlockSpec(memory_space=pltpu.HBM)


def call(kernel, outs, scratch, *args, space=VMEM, sems=0, aliases={}):
    as_struct = lambda s: s if hasattr(s, "dtype") else jax.ShapeDtypeStruct(s, jnp.float32)
    as_scratch = lambda s: pltpu.VMEM(as_struct(s).shape, as_struct(s).dtype)
    return pl.pallas_call(
        kernel,
        out_shape=[as_struct(s) for s in outs],
        in_specs=[space] * len(args),
        out_specs=[VMEM] * len(outs),
        scratch_shapes=[as_scratch(s) for s in scratch]
        + ([pltpu.SemaphoreType.DMA((sems,))] if sems else []),
        input_output_aliases=aliases,
        compiler_params=pltpu.CompilerParams(vmem_limit_bytes=24 * 1024 * 1024),
    )(*(pltpu.with_memory_space_constraint(a, pltpu.HBM) if space is HBM else a for a in args))


def body(
    pressure,
    saturation,
    sat_history,
    storage,
    step_volume,
    transmiss,
    perf_cell,
    perf_index,
    control,
    target,
):
    layers, rows, columns = pressure.shape
    ext = layers + 2 * H
    wells, perfs = perf_cell.shape
    block = (layers, rows, columns)
    pinned = pin(*block)
    ext_block = pin(ext, rows, columns)
    z_layers = sum(count for _, count in Z_PARTS)
    z_near, z_cross = (pin(n, rows, columns) for n in (z_layers, z_layers - 1))
    entries = wells * perfs
    early, late = (pin(tiles(f(layers)), 8, columns) for f in (early_parts, late_parts))
    seams = [pin(ext, 8, columns)] * len(SEAMS)
    *fields, near, cross, part, cell, per_perf, perf_values, own_hot = call(
        functools.partial(prepare_kernel, gz="gz"),
        [ext_block] * 7
        + [z_near, z_cross]
        + [
            pin(2, LANES),
            pin(1, entries, dtype=jnp.int32),
            pin(3, entries),
            pin(2, entries),
            pin(layers * rows, entries, dtype=jnp.bfloat16),
        ],
        [
            block,
            block,
            jax.ShapeDtypeStruct((perfs, wells), jnp.int32),
            (perfs, wells),
            jax.ShapeDtypeStruct((1, wells), jnp.int32),
            (1, wells),
            (perfs, LANES),
        ],
        saturation,
        sat_history,
        pressure,
        storage,
        transmiss,
        perf_cell.T,
        perf_index.T,
        control.reshape(1, wells),
        target.reshape(1, wells),
        space=HBM,
        sems=3 * -(-layers // LOADED) + 8,
    )
    cross = swap(cross, "gz", 1)
    near = swap(near, "gz", 0)
    p0e, tote, frace, stor, t0, t1, t2 = fields
    f0e, f1e, f2e, dpe, base, inverse, early_near, early_cross, part = call(
        functools.partial(faces_kernel, layers=layers, gx="gx"),
        [ext_block] * 6 + [early, early, pin(2, LANES)],
        [],
        *fields,
        part,
    )
    early_cross = swap(early_cross, "gx", 1)
    early_near = swap(early_near, "gx", 0)
    sums = part + near[-1, 0:2, 0:LANES]
    step = 2
    while step < lax.axis_size("gz"):
        pairs = [(i, i ^ step) for i in range(lax.axis_size("gz"))]
        tile = jnp.pad(sums, ((0, 8 - sums.shape[0]), (0, 0)))
        sums = sums + lax.ppermute(tile, "gz", pairs)[: sums.shape[0]]
        step *= 2
    p0e, tote, frace, stor, f0e, f1e, f2e, dpe, base, inverse, perf_values, hot = call(
        functools.partial(halo_kernel, layers=layers, gx="gx", gz="gz"),
        [ext_block] * 10
        + [pin(2, entries), pin(2 * (H - 1) * rows, entries, dtype=jnp.bfloat16)],
        [],
        p0e,
        tote,
        frace,
        stor,
        f0e,
        f1e,
        f2e,
        dpe,
        base,
        inverse,
        t0,
        cross,
        near,
        cell,
        per_perf,
        perf_values,
        aliases={i: i for i in range(10)},
    )
    rhse, source, late_near, late_cross, hole = call(
        functools.partial(build_kernel, layers=layers, gx="gx"),
        [ext_block, pinned, late, late, pin(1, LANES)],
        [ext_block] * 5,
        p0e,
        stor,
        f0e,
        f1e,
        f2e,
        dpe,
        tote,
        base,
        inverse,
        sums,
        perf_values,
        hot,
        own_hot,
        cell,
        per_perf,
    )
    late_cross = swap(late_cross, "gx", 1)
    late_near = swap(late_near, "gx", 0)
    early_near, early_cross, rhse = lax.optimization_barrier((early_near, early_cross, rhse))
    joined = [pin(ext, rows + 8, columns)] * 4
    filled = call(
        functools.partial(seam_kernel, layers=layers, gx="gx"),
        seams + joined,
        [],
        early_near,
        early_cross,
        p0e,
        tote,
        f0e,
        f1e,
        f2e,
        dpe,
        rhse,
    )
    field, residual, new_sat, new_hist, bottom, *_ = call(
        functools.partial(finish_kernel, gx="gx"),
        [block] * 4 + [(1, wells)] + seams + joined,
        [],
        saturation,
        sat_history,
        step_volume,
        storage,
        source,
        p0e,
        tote,
        frace,
        f0e,
        f1e,
        f2e,
        dpe,
        rhse,
        late_near,
        late_cross,
        *filled,
        hole,
        aliases={15 + i: 5 + i for i in range(len(filled))},
    )
    return (field, residual, new_sat, new_hist, bottom.reshape(wells))


def solution(mesh):
    return jax.shard_map(
        body,
        mesh=mesh,
        in_specs=(
            P("gz", "gx", None),
            P("gz", "gx", None),
            P("gz", "gx", None),
            P("gz", "gx", None),
            P("gz", "gx", None),
            P(None, "gz", "gx", None),
            P("gx", None),
            P("gx", None),
            P("gx"),
            P("gx"),
        ),
        out_specs=(
            P("gz", "gx", None),
            P("gz", "gx", None),
            P("gz", "gx", None),
            P("gz", "gx", None),
            P("gx"),
        ),
        check_vma=False,
    )
```

```python
import functools

import jax
import jax.numpy as jnp
from jax import lax
from jax.experimental import pallas as pl
from jax.experimental.pallas import tpu as pltpu
from jax.sharding import PartitionSpec as P

SWEEPS = 4
H = SWEEPS + 1
LANES = 128
LOADED = 4

Z_PARTS = (
    ("p0", H),
    ("tot", H),
    ("t0", H),
    ("stor", H - 1),
    ("t1", H - 1),
    ("t2", H - 1),
    ("frac", 1),
    ("sums", 1),
)


def early_parts(layers):
    own = (H, layers)
    inner = (H, layers - 1)
    return (
        ("t1", *own),
        ("tot", *own),
        ("p0", *own),
        ("dp", *own),
        ("f0", *inner),
        ("f2", *own),
        ("f1", *own),
        ("frac", *own),
        ("p0_d2", *own),
        ("f0_d2", *inner),
        ("f2_d2", *own),
        ("dp_d2", *own),
    )


def late_parts(layers):
    top = H + layers
    both = lambda name, n: ((name, H - n, n), (name, top, n))
    faces = lambda name, n: ((name, H - n, n), (name, top - 1, n))
    return (
        ("rhs", 2, layers + 6),
        ("p1_d2", 3, layers + 4),
        ("g2", 4, layers + 2),
        ("g3", H, layers),
        *both("t1", H - 1),
        *both("tot", H - 1),
        *both("p0", H - 1),
        *both("dp", H - 2),
        *faces("f0", H - 1),
        *both("f2", H - 2),
        *both("f1", H - 2),
        *both("p0_d2", H - 2),
        *faces("f0_d2", 2),
        *both("f2_d2", 1),
        *both("dp_d2", 1),
    )


def tiles(parts):
    return -(-sum(count for _, _, count in parts) // 8)


SEAMS = ("f0", "f1", "f2", "tot", "dp", "p0", "frac", "p1", "rhs2", "rhs3")
PLACES = {
    "t1": ("f1", None, 7),
    "f1": ("f1", 0, 6),
    "tot": ("tot", 0, 7),
    "p0": ("p0", 0, 7),
    "dp": ("dp", 0, 7),
    "dp_d2": ("dp", 1, 6),
    "f0": ("f0", 0, 7),
    "f0_d2": ("f0", 1, 6),
    "f2": ("f2", 0, 7),
    "f2_d2": ("f2", 1, 6),
    "frac": ("frac", 0, 7),
    "p0_d2": ("p0", 1, 6),
    "p1_d2": ("p1", 1, 6),
    "rhs": ("rhs2", 0, 7),
    "g2": ("rhs2", 1, 6),
    "g3": ("rhs3", 1, 6),
}


def pack(message, parts, refs, rows):
    at = 0
    for name, first, count in parts:
        for e in range(first, first + count):
            message[at // 8, at % 8 : at % 8 + 1, :] = refs[name][e, rows[name] : rows[name] + 1, :]
            at += 1


def pack_both(near, cross, parts, up, down, rows, gx):
    last = rows - 1
    outer = {name: 0 if PLACES[name][2] == 7 else 1 for name in PLACES}
    up_rows = {name: last - outer[name] for name in PLACES} | {"f1": last - 1}
    down_rows = dict(outer) | {"f1": 0}
    even = lax.axis_index(gx) % 2 == 0

    @pl.when(even)
    def _():
        pack(near, parts, up, up_rows)
        pack(cross, parts, down, down_rows)

    @pl.when(jnp.logical_not(even))
    def _():
        pack(cross, parts, up, up_rows)
        pack(near, parts, down, down_rows)


def unpack(message, parts, seams, side):
    at = 0
    for name, first, count in parts:
        seam, *places = PLACES[name]
        place = places[side]
        for e in range(first, first + count):
            if place is not None:
                seams[seam][e, place : place + 1, :] = message[at // 8, at % 8 : at % 8 + 1, :]
            at += 1


def unpack_both(near, cross, parts, seams, gx):
    even = lax.axis_index(gx) % 2 == 0

    @pl.when(even)
    def _():
        unpack(near, parts, seams, 0)
        unpack(cross, parts, seams, 1)

    @pl.when(jnp.logical_not(even))
    def _():
        unpack(cross, parts, seams, 0)
        unpack(near, parts, seams, 1)


def mobility(sat, history):
    trapped = history / (1.0 + 1.5 * history)
    excess = jnp.maximum(sat - trapped, 0.0)
    free_gas = 0.5 * (excess + jnp.sqrt(excess * excess + excess / 0.375))
    relperm = jnp.where(sat < history, free_gas * free_gas, sat * sat)
    gas = relperm / 0.5
    total = (1.0 - sat) * (1.0 - sat) + gas
    return (total, gas / total)


def roll(x, shift, axis):
    return pltpu.roll(x, shift % x.shape[axis], axis)


def loop(first, last, step, carry):
    count = last - first
    unroll = -(-count // -(-count // 10))
    groups = count // unroll

    def group(g, carry):
        for i in range(unroll):
            carry = step(first + g * unroll + i, carry)
        return carry

    carry = lax.fori_loop(0, groups, group, carry) if groups > 1 else group(0, carry)
    for index in range(first + groups * unroll, last):
        carry = step(index, carry)
    return carry


def split(x):
    high = x.astype(jnp.bfloat16)
    return (high, (x - high.astype(jnp.float32)).astype(jnp.bfloat16))


def at_places(cell, first_layer, layers, rows, columns):
    layer = cell // (rows * columns)
    row = (cell - layer * (rows * columns)) // columns
    place = (layer - first_layer) * rows + row
    return lax.broadcasted_iota(jnp.int32, (layers * rows, cell.shape[1]), 0) == place


def at_columns(cell, columns):
    return lax.broadcasted_iota(jnp.int32, (columns, cell.shape[1]), 0) == cell % columns


def gather(field, at_place, at_column):
    high, low = split(field)
    hot = at_column.astype(jnp.bfloat16)
    by_column = jnp.dot(high, hot, preferred_element_type=jnp.float32) + jnp.dot(
        low, hot, preferred_element_type=jnp.float32
    )
    return jnp.sum(jnp.where(at_place, by_column, 0.0), axis=0, keepdims=True)


def flatten(block, spread):
    perfs, wells = block.shape
    spread[...] = jnp.zeros(spread.shape, jnp.float32)
    spread[:, 0:wells] = block
    wide = spread[...]
    shift = wells
    while shift < LANES:
        wide = wide + roll(wide, shift, 1)
        shift *= 2
    each = LANES // wells
    entry = lax.broadcasted_iota(jnp.int32, (perfs, LANES), 0)
    group = lax.broadcasted_iota(jnp.int32, (perfs, LANES), 1) // wells
    tiles = [
        jnp.sum(jnp.where(entry == first + group, wide, 0.0), axis=0, keepdims=True)
        for first in range(0, perfs, each)
    ]
    return jnp.concatenate(tiles, axis=1)


def prepare_kernel(
    sat,
    hist,
    pressure,
    storage,
    trans,
    cell_in,
    index_in,
    control_in,
    target_in,
    p0e,
    tote,
    frace,
    stor,
    t0,
    t1,
    t2,
    near,
    cross,
    sums,
    cell,
    wells,
    perfs,
    hot,
    sat_v,
    hist_v,
    cell_v,
    index_v,
    control_v,
    target_v,
    spread,
    sems,
    *,
    gz,
):
    layers, rows, columns = pressure.shape
    ext = layers + 2 * H
    own = pl.ds(H, layers)
    parts = [(l, min(LOADED, layers - l)) for l in range(0, layers, LOADED)]
    in_parts = [
        (source.at[pl.ds(l, n)], target.at[pl.ds(offset + l, n)])
        for source, target, offset in ((sat, sat_v, 0), (hist, hist_v, 0), (pressure, p0e, H))
        for l, n in parts
    ]
    small = [(cell_in, cell_v), (index_in, index_v), (control_in, control_v), (target_in, target_v)]
    large = [
        (trans.at[0], t0.at[own]),
        (storage, stor.at[own]),
        (trans.at[1], t1.at[own]),
        (trans.at[2], t2.at[own]),
    ]
    copies = [
        pltpu.make_async_copy(a, b, sems.at[i])
        for i, (a, b) in enumerate(in_parts + small + large)
    ]
    for copy in copies:
        copy.start()

    def layer_step(l, carry):
        t, f = mobility(sat_v[l], hist_v[l])
        tote[l + H] = t
        frace[l + H] = f
        return carry

    for i, (l, n) in enumerate(parts):
        copies[i].wait()
        copies[len(parts) + i].wait()
        loop(l, l + n, layer_step, 0)
    for copy in copies[2 * len(parts) : -len(large)]:
        copy.wait()
    count, group = cell_v.shape
    cell[...] = flatten(cell_v[...].astype(jnp.float32), spread).astype(jnp.int32)
    wells[0:1, :] = flatten(index_v[...], spread)
    wells[1:2, :] = flatten(jnp.broadcast_to(target_v[...], (count, group)), spread)
    wells[2:3, :] = flatten(
        jnp.broadcast_to(control_v[...].astype(jnp.float32), (count, group)), spread
    )
    at_place = at_places(cell[...], lax.axis_index(gz) * layers, layers, rows, columns)
    at_column = at_columns(cell[...], columns)
    hot[...] = at_place.astype(jnp.bfloat16)
    flat = (layers * rows, columns)
    weight = wells[0:1, :] * gather(tote[own].reshape(flat), at_place, at_column)
    cell_p = gather(p0e[own].reshape(flat), at_place, at_column)
    perfs[0:1, :] = weight
    perfs[1:2, :] = cell_p
    for i, value in enumerate((weight * cell_p, weight)):
        part = value[:, 0:LANES]
        for lane in range(LANES, value.shape[1], LANES):
            part = part + value[:, lane : lane + LANES]
        shift = LANES // 2
        while shift >= group:
            part = part + roll(part, shift, 1)
            shift //= 2
        sums[i : i + 1, :] = part
    for copy in copies[-len(large) :]:
        copy.wait()
    even = lax.axis_index(gz) % 2 == 0
    refs = {"p0": p0e, "tot": tote, "t0": t0, "stor": stor, "t1": t1, "t2": t2, "frac": frace}
    for message, is_top in ((near, even), (cross, jnp.logical_not(even))):
        at = 0
        for name, count in Z_PARTS:
            if name == "sums" and message is cross:
                continue
            if name == "sums":
                message[at] = jnp.zeros((rows, columns), jnp.float32)
                message[at, 0:2, 0:LANES] = sums[...]
            else:
                edge = jnp.where(is_top, H + layers - count, H)
                message[pl.ds(at, count)] = refs[name][pl.ds(edge, count)]
            at += count


def masks(rows, columns):
    row = lax.broadcasted_iota(jnp.int32, (rows, columns), 0)
    column = lax.broadcasted_iota(jnp.int32, (rows, columns), 1)
    return (row == rows - 1, column == columns - 1)


def lateral_faces(tot, t1, t2, store, last_row, last_column, top_x):
    along = jnp.where(last_row, 0.0, t1) * 0.5 * (tot + roll(tot, -1, 0))
    across = jnp.where(last_column, 0.0, t2) * 0.5 * (tot + roll(tot, -1, 1))
    part = store + along + roll(along, 1, 0) + across + roll(across, 1, 1)
    return (jnp.where(last_row, jnp.where(top_x, 0.0, t1), along), across, part)


def is_last(axis):
    return lax.axis_index(axis) == lax.axis_size(axis) - 1


def first_sweep(e, p0e, stor, f0e, f1e, f2e, dpe, last_row):
    above = f0e[e]
    below = f0e[e - 1]
    along = jnp.where(last_row, 0.0, f1e[e])
    across = f2e[e]
    diag = dpe[e] + above + below
    p = p0e[e]
    base = stor[e] * p + above * p0e[e + 1] + below * p0e[e - 1]
    base = base + along * roll(p, -1, 0) + roll(along * p, 1, 0)
    base = base + across * roll(p, -1, 1) + roll(across * p, 1, 1)
    return (base, jnp.where(diag > 0.0, 1.0 / diag, 0.0))


def faces_kernel(*refs, layers, gx):
    p0e, tote, frace, stor, t0, t1, t2, part = refs[:8]
    f0e, f1e, f2e, dpe, base, inverse, near, cross, sums = refs[8:]
    _, rows, columns = p0e.shape
    last_row, last_column = masks(rows, columns)
    top_x = is_last(gx)

    def step(e, carry):
        tot = tote[e]
        f0e[e] = t0[e] * 0.5 * (tot + tote[e + 1])
        f1e[e], f2e[e], dpe[e] = lateral_faces(
            tot, t1[e], t2[e], stor[e], last_row, last_column, top_x
        )
        return carry

    loop(H, H + layers, step, 0)
    sums[...] = part[...]
    refs = {"t1": f1e, "tot": tote, "p0": p0e, "dp": dpe, "f0": f0e, "f2": f2e, "f1": f1e}
    refs |= {"frac": frace, "p0_d2": p0e, "f0_d2": f0e, "f2_d2": f2e, "dp_d2": dpe}
    pack_both(near, cross, early_parts(layers), refs, refs, rows, gx)

    def sweep_step(e, carry):
        base[e], inverse[e] = first_sweep(e, p0e, stor, f0e, f1e, f2e, dpe, last_row)
        return carry

    loop(H + 1, H + layers - 1, sweep_step, 0)


def well_holes(sums, wells):
    repeat = lambda x: jnp.concatenate([x] * (wells.shape[1] // LANES), axis=1)
    goal = wells[1:2, :]
    return jnp.where(
        wells[2:3, :] == 0.0, (goal + repeat(sums[0:1, :])) / repeat(sums[1:2, :]), goal
    )


def join(a, b):
    return jnp.concatenate([a, b], axis=0)


def seam_faces(first, last, fields, seams, f1, inverse, p):
    p0e, tote, f0e, f1e, dpe = fields
    rows, columns = p0e.shape[1:]
    row = lax.broadcasted_iota(jnp.int32, (rows + 8, columns), 0)
    edge = (row == rows - 1) | (row == rows + 7)

    def step(e, below):
        tot = join(tote[e], seams["tot"][e])
        mixed = join(f1e[e], seams["f1"][e])
        border = jnp.where(edge, mixed * 0.5 * (tot + roll(tot, -1, 0)), 0.0)
        f1[e] = jnp.where(edge, border, mixed)
        above = join(f0e[e], seams["f0"][e])
        diag = join(dpe[e], seams["dp"][e]) + above + below + border + roll(border, 1, 0)
        inverse[e] = jnp.where(diag > 0.0, 1.0 / diag, 0.0)
        p[e] = join(p0e[e], seams["p0"][e])
        return above

    loop(first, last, step, join(f0e[first - 1], seams["f0"][first - 1]))


def sweep_layers(number, first, last, old, new, fields, seams, f1, inverse, part):
    rhse, f0e, f2e = fields
    rows, columns = rhse.shape[1:]
    row = lax.broadcasted_iota(jnp.int32, (rows + 8, columns), 0)
    beyond = (row == rows + 1) | (row == rows + 6)
    blank = jnp.zeros((rows, columns), jnp.float32)

    def step(e, carry):
        below, p = carry
        above = old[e + 1]
        face = join(f0e[e], seams["f0"][e])
        x = f1[e]
        y = join(f2e[e], seams["f2"][e])
        side = seams["rhs2"][e]
        if number == 3:
            side = jnp.where(beyond[rows:], seams["rhs3"][e], side)
        total = join(rhse[e], side) + below + face * above
        total = total + x * roll(p, -1, 0) + roll(x * p, 1, 0)
        total = total + y * roll(p, -1, 1) + roll(y * p, 1, 1)
        value = total * inverse[e]
        if number == 1:
            value = jnp.where(beyond, join(blank, seams["p1"][e]), value)
        new[e, part] = value[part]
        return (face * p, above)

    start = join(f0e[first - 1], seams["f0"][first - 1]) * old[first - 1]
    loop(first, last, step, (start, old[first]))


def seam_kernel(near, cross, *refs, layers, gx):
    p0e, tote, f0e, f1e, f2e, dpe, rhse = refs[:7]
    refs = refs[7:]
    seams = dict(zip(SEAMS, refs))
    f1, inverse, p, p1 = refs[len(SEAMS) :]
    for seam in seams.values():
        seam[...] = jnp.zeros(seam.shape, jnp.float32)
    unpack_both(near, cross, early_parts(layers), seams, gx)
    inner = (H + 1, H + layers - 1)
    seam_faces(*inner, (p0e, tote, f0e, f1e, dpe), seams, f1, inverse, p)
    for e in (H, H + layers - 1):
        p[e] = join(p0e[e], jnp.zeros_like(seams["p0"][e]))
    own = slice(0, p0e.shape[1])
    sweep_layers(1, *inner, p, p1, (rhse, f0e, f2e), seams, f1, inverse, own)


def halo_kernel(*refs, layers, gx, gz):
    own_t0, cross, near, cell, wells, own_perfs = refs[10:16]
    p0e, tote, frace, stor, f0e, f1e, f2e, dpe, base, inverse, perfs, hot = refs[16:]
    ext, rows, columns = p0e.shape
    even = lax.axis_index(gz) % 2 == 0
    top_z = is_last(gz)
    top_x = is_last(gx)
    last_row, last_column = masks(rows, columns)
    where = {}
    at = 0
    for name, count in Z_PARTS:
        where[name] = (at, count)
        at += count

    def halo(name, e):
        at, count = where[name]
        low = e < H
        at = at + e - (H - count if low else H + layers)
        one, two = (near[at], cross[at])
        return jnp.where(even, two, one) if low else jnp.where(even, one, two)

    for name, target in (("p0", p0e), ("tot", tote), ("frac", frace), ("stor", stor)):
        count = where[name][1]
        for e in (*range(H - count, H), *range(H + layers, H + layers + count)):
            target[e] = halo(name, e)
    f0e[H + layers - 1] = jnp.where(top_z, 0.0, own_t0[H + layers - 1]) * 0.5 * (
        tote[H + layers - 1] + tote[H + layers]
    )
    for e in (*range(0, H), *range(H + layers, ext - 1)):
        f0e[e] = halo("t0", e) * 0.5 * (tote[e] + tote[e + 1])
    for e in (*range(1, H), *range(H + layers, ext - 1)):
        f1e[e], f2e[e], dpe[e] = lateral_faces(
            tote[e], halo("t1", e), halo("t2", e), stor[e], last_row, last_column, top_x
        )
    for e in (*range(1, H + 1), *range(H + layers - 1, ext - 1)):
        base[e], inverse[e] = first_sweep(e, p0e, stor, f0e, f1e, f2e, dpe, last_row)
    width = H - 1
    first = lax.axis_index(gz) * layers
    sides = ((1, first - width), (H + layers, first + layers))
    at_place = [at_places(cell[...], layer, width, rows, columns) for _, layer in sides]
    at_place = jnp.concatenate(at_place, axis=0)
    at_column = at_columns(cell[...], columns)
    hot[...] = at_place.astype(jnp.bfloat16)
    flat = (width * rows, columns)
    both = lambda ref: join(*(ref[e : e + width].reshape(flat) for e, _ in sides))
    weight = wells[0:1, :] * gather(both(tote), at_place, at_column)
    perfs[0:1, :] = own_perfs[0:1, :] + weight
    perfs[1:2, :] = own_perfs[1:2, :] + gather(both(p0e), at_place, at_column)


def build_kernel(*refs, layers, gx):
    p0e, stor, f0e, f1e, f2e, dpe, tote, base, inverse, sums, perfs, hot, own_hot = refs[:13]
    cell, wells, rhse, source, x_near, x_cross, bottom, p1, g2u, g2d, g3u, g3d = refs[13:]
    ext, rows, columns = p0e.shape
    last_row, _ = masks(rows, columns)
    hole = well_holes(sums[...], wells[...])
    bottom[...] = hole[:, 0:LANES]
    rate = perfs[0:1, :] * (hole - perfs[1:2, :])
    pieces = split(jnp.where(at_columns(cell[...], columns), rate, 0.0))

    def scatter(mask):
        spread = [
            lax.dot_general(
                mask, piece, (((1,), (1,)), ((), ())), preferred_element_type=jnp.float32
            )
            for piece in pieces
        ]
        return (spread[0] + spread[1]).reshape(-1, rows, columns)

    width = H - 1
    inside = scatter(own_hot[...])
    outside = scatter(hot[...])
    source[...] = inside
    rhse[H : ext - H] = inside
    rhse[1:H] = outside[:width]
    rhse[ext - H : ext - 1] = outside[width:]

    def first_step(e, carry):
        wells_rate = rhse[e]
        p1[e] = (base[e] + wells_rate) * inverse[e]
        rhse[e] = stor[e] * p0e[e] + wells_rate
        return carry

    loop(1, ext - 1, first_step, 0)

    def second_step(e, carry):
        along = jnp.where(last_row, 0.0, f1e[e])
        across = f2e[e]
        p = p1[e]
        rhs = rhse[e]
        lower = roll(along * p, 1, 0)
        upper = along * roll(p, -1, 0)
        g2u[e] = rhs + lower
        g2d[e] = rhs + upper
        new = rhs + lower + upper + f0e[e] * p1[e + 1] + f0e[e - 1] * p1[e - 1]
        new = new + across * roll(p, -1, 1) + roll(across * p, 1, 1)
        p2 = new * inverse[e]
        g3u[e] = rhs + roll(along * p2, 1, 0)
        g3d[e] = rhs + along * roll(p2, -1, 0)
        return carry

    loop(H - 1, ext - H + 1, second_step, 0)

    shared = {"t1": f1e, "tot": tote, "p0": p0e, "dp": dpe, "f0": f0e, "f2": f2e, "f1": f1e}
    shared |= {"p0_d2": p0e, "f0_d2": f0e, "f2_d2": f2e, "dp_d2": dpe, "rhs": rhse, "p1_d2": p1}
    up = shared | {"g2": g2u, "g3": g3u}
    down = shared | {"g2": g2d, "g3": g3d}
    pack_both(x_near, x_cross, late_parts(layers), up, down, rows, gx)


def finish_kernel(*refs, gx):
    sat, hist, volume, storage, source = refs[:5]
    p0e, tote, frace, f0e, f1e, f2e, dpe, rhse, near, cross = refs[5:15]
    hole = refs[19 + len(SEAMS)]
    refs = refs[20 + len(SEAMS) :]
    new_p, residual, new_sat, new_hist, bottom = refs[:5]
    seams = dict(zip(SEAMS, refs[5:]))
    f1, rdiag, pa, pb = refs[5 + len(SEAMS) :]
    bottom[...] = hole[:, 0 : bottom.shape[1]]
    layers, rows, columns = sat.shape
    ext = layers + 2 * H
    unpack_both(near, cross, late_parts(layers), seams, gx)
    sfrac = seams["frac"]
    pa[0] = join(p0e[0], seams["p0"][0])
    pa[ext - 1] = join(p0e[ext - 1], seams["p0"][ext - 1])
    for first, last in ((1, H + 1), (ext - H - 1, ext - 1)):
        seam_faces(first, last, (p0e, tote, f0e, f1e, dpe), seams, f1, rdiag, pa)

    pressures = (pa, pb)
    fields = (rhse, f0e, f2e)
    inner = (H + 1, ext - H - 1)
    everywhere = slice(0, rows + 8)
    for number in range(1, SWEEPS + 1):
        old, new = pressures[(number - 1) % 2], pressures[number % 2]
        ranges = [(number, ext - number, everywhere)]
        if number == 1:
            ranges = [
                (number, inner[0], everywhere),
                (*inner, slice(rows, rows + 8)),
                (inner[1], ext - number, everywhere),
            ]
        for first, last, part in ranges:
            sweep_layers(number, first, last, old, new, fields, seams, f1, rdiag, part)
    field = pressures[SWEEPS % 2]

    def flow(face, p, p_next, f, f_next):
        water = face * (p - p_next)
        return (water, water * jnp.where(water > 0, f, f_next))

    def last_step(l, carry):
        below_w, below_g = carry
        e = l + H
        p = field[e]
        f = join(frace[e], sfrac[e])
        own_p = p[:rows]
        own_f = f[:rows]
        above_w, above_g = flow(f0e[e], own_p, field[e + 1][:rows], own_f, frace[e + 1])
        xw, xg = flow(f1[e], p, roll(p, -1, 0), f, roll(f, -1, 0))
        yw, yg = flow(f2e[e], own_p, roll(own_p, -1, 1), own_f, roll(own_f, -1, 1))
        water = above_w - below_w + (xw - roll(xw, 1, 0))[:rows] + yw - roll(yw, 1, 1)
        out = above_g - below_g + (xg - roll(xg, 1, 0))[:rows] + yg - roll(yg, 1, 1)
        new_p[l] = own_p
        residual[l] = rhse[e] - storage[l] * own_p - water
        src = source[l]
        gas = jnp.maximum(src, 0.0) + jnp.minimum(src, 0.0) * own_f
        s = sat[l] + volume[l] * (gas - out)
        new_sat[l] = s
        new_hist[l] = jnp.maximum(hist[l], s)
        return (above_w, above_g)

    first = flow(f0e[H - 1], field[H - 1][:rows], field[H][:rows], frace[H - 1], frace[H])
    loop(0, layers, last_step, first)


def swap(block, axis, first):
    pairs = [(i, i + 1) for i in range(first, lax.axis_size(axis) - 1, 2)]
    return lax.ppermute(block, axis, pairs + [(b, a) for a, b in pairs])


def pin(*shape, dtype=jnp.float32):
    return pltpu.VMEM(shape, dtype)


VMEM = pl.BlockSpec(memory_space=pltpu.VMEM)
HBM = pl.BlockSpec(memory_space=pltpu.HBM)


def call(kernel, outs, scratch, *args, space=VMEM, sems=0, aliases={}):
    as_struct = lambda s: s if hasattr(s, "dtype") else jax.ShapeDtypeStruct(s, jnp.float32)
    as_scratch = lambda s: pltpu.VMEM(as_struct(s).shape, as_struct(s).dtype)
    return pl.pallas_call(
        kernel,
        out_shape=[as_struct(s) for s in outs],
        in_specs=[space] * len(args),
        out_specs=[VMEM] * len(outs),
        scratch_shapes=[as_scratch(s) for s in scratch]
        + ([pltpu.SemaphoreType.DMA((sems,))] if sems else []),
        input_output_aliases=aliases,
        compiler_params=pltpu.CompilerParams(vmem_limit_bytes=24 * 1024 * 1024),
    )(*(pltpu.with_memory_space_constraint(a, pltpu.HBM) if space is HBM else a for a in args))


def body(
    pressure,
    saturation,
    sat_history,
    storage,
    step_volume,
    transmiss,
    perf_cell,
    perf_index,
    control,
    target,
):
    layers, rows, columns = pressure.shape
    ext = layers + 2 * H
    wells, perfs = perf_cell.shape
    block = (layers, rows, columns)
    pinned = pin(*block)
    ext_block = pin(ext, rows, columns)
    z_layers = sum(count for _, count in Z_PARTS)
    z_near, z_cross = (pin(n, rows, columns) for n in (z_layers, z_layers - 1))
    entries = wells * perfs
    early, late = (pin(tiles(f(layers)), 8, columns) for f in (early_parts, late_parts))
    seams = [pin(ext, 8, columns)] * len(SEAMS)
    *fields, near, cross, part, cell, per_perf, perf_values, own_hot = call(
        functools.partial(prepare_kernel, gz="gz"),
        [ext_block] * 7
        + [z_near, z_cross]
        + [
            pin(2, LANES),
            pin(1, entries, dtype=jnp.int32),
            pin(3, entries),
            pin(2, entries),
            pin(layers * rows, entries, dtype=jnp.bfloat16),
        ],
        [
            block,
            block,
            jax.ShapeDtypeStruct((perfs, wells), jnp.int32),
            (perfs, wells),
            jax.ShapeDtypeStruct((1, wells), jnp.int32),
            (1, wells),
            (perfs, LANES),
        ],
        saturation,
        sat_history,
        pressure,
        storage,
        transmiss,
        perf_cell.T,
        perf_index.T,
        control.reshape(1, wells),
        target.reshape(1, wells),
        space=HBM,
        sems=3 * -(-layers // LOADED) + 8,
    )
    cross = swap(cross, "gz", 1)
    near = swap(near, "gz", 0)
    p0e, tote, frace, stor, t0, t1, t2 = fields
    f0e, f1e, f2e, dpe, base, inverse, early_near, early_cross, part = call(
        functools.partial(faces_kernel, layers=layers, gx="gx"),
        [ext_block] * 6 + [early, early, pin(2, LANES)],
        [],
        *fields,
        part,
    )
    early_cross = swap(early_cross, "gx", 1)
    early_near = swap(early_near, "gx", 0)
    sums = part + near[-1, 0:2, 0:LANES]
    step = 2
    while step < lax.axis_size("gz"):
        pairs = [(i, i ^ step) for i in range(lax.axis_size("gz"))]
        tile = jnp.pad(sums, ((0, 8 - sums.shape[0]), (0, 0)))
        sums = sums + lax.ppermute(tile, "gz", pairs)[: sums.shape[0]]
        step *= 2
    p0e, tote, frace, stor, f0e, f1e, f2e, dpe, base, inverse, perf_values, hot = call(
        functools.partial(halo_kernel, layers=layers, gx="gx", gz="gz"),
        [ext_block] * 10
        + [pin(2, entries), pin(2 * (H - 1) * rows, entries, dtype=jnp.bfloat16)],
        [],
        p0e,
        tote,
        frace,
        stor,
        f0e,
        f1e,
        f2e,
        dpe,
        base,
        inverse,
        t0,
        cross,
        near,
        cell,
        per_perf,
        perf_values,
        aliases={i: i for i in range(10)},
    )
    rhse, source, late_near, late_cross, hole = call(
        functools.partial(build_kernel, layers=layers, gx="gx"),
        [ext_block, pinned, late, late, pin(1, LANES)],
        [ext_block] * 5,
        p0e,
        stor,
        f0e,
        f1e,
        f2e,
        dpe,
        tote,
        base,
        inverse,
        sums,
        perf_values,
        hot,
        own_hot,
        cell,
        per_perf,
    )
    late_cross = swap(late_cross, "gx", 1)
    late_near = swap(late_near, "gx", 0)
    early_near, early_cross, rhse = lax.optimization_barrier((early_near, early_cross, rhse))
    joined = [pin(ext, rows + 8, columns)] * 4
    filled = call(
        functools.partial(seam_kernel, layers=layers, gx="gx"),
        seams + joined,
        [],
        early_near,
        early_cross,
        p0e,
        tote,
        f0e,
        f1e,
        f2e,
        dpe,
        rhse,
    )
    field, residual, new_sat, new_hist, bottom, *_ = call(
        functools.partial(finish_kernel, gx="gx"),
        [block] * 4 + [(1, wells)] + seams + joined,
        [],
        saturation,
        sat_history,
        step_volume,
        storage,
        source,
        p0e,
        tote,
        frace,
        f0e,
        f1e,
        f2e,
        dpe,
        rhse,
        late_near,
        late_cross,
        *filled,
        hole,
        aliases={15 + i: 5 + i for i in range(len(filled))},
    )
    return (field, residual, new_sat, new_hist, bottom.reshape(wells))


def solution(mesh):
    return jax.shard_map(
        body,
        mesh=mesh,
        in_specs=(
            P("gz", "gx", None),
            P("gz", "gx", None),
            P("gz", "gx", None),
            P("gz", "gx", None),
            P("gz", "gx", None),
            P(None, "gz", "gx", None),
            P("gx", None),
            P("gx", None),
            P("gx"),
            P("gx"),
        ),
        out_specs=(
            P("gz", "gx", None),
            P("gz", "gx", None),
            P("gz", "gx", None),
            P("gz", "gx", None),
            P("gx"),
        ),
        check_vma=False,
    )
```

```python
import functools

import jax
import jax.numpy as jnp
from jax import lax
from jax.experimental import pallas as pl
from jax.experimental.pallas import tpu as pltpu
from jax.sharding import PartitionSpec as P

SWEEPS = 4
H = SWEEPS + 1
LANES = 128
LOADED = 4

Z_PARTS = (
    ("p0", H),
    ("tot", H),
    ("t0", H),
    ("stor", H - 1),
    ("t1", H - 1),
    ("t2", H - 1),
    ("frac", 1),
    ("sums", 1),
)


def early_parts(layers):
    own = (H, layers)
    inner = (H, layers - 1)
    return (
        ("t1", *own),
        ("tot", *own),
        ("p0", *own),
        ("dp", *own),
        ("f0", *inner),
        ("f2", *own),
        ("f1", *own),
        ("frac", *own),
        ("p0_d2", *own),
        ("f0_d2", *inner),
        ("f2_d2", *own),
        ("dp_d2", *own),
    )


def late_parts(layers):
    top = H + layers
    both = lambda name, n: ((name, H - n, n), (name, top, n))
    faces = lambda name, n: ((name, H - n, n), (name, top - 1, n))
    ends = lambda name: ((name, 2, 1), (name, top + 2, 1))
    return (
        ("rhs", 3, layers + 4),
        *ends("rhs_x"),
        ("p1_d2", 3, layers + 4),
        ("g2", 4, layers + 2),
        ("g3", H, layers),
        *both("t1", H - 1),
        *both("tot", H - 1),
        *both("p0", H - 1),
        *both("dp", H - 3),
        *ends("dp_x"),
        *faces("f0", H - 2),
        *both("f2", H - 3),
        *both("f1", H - 3),
        *both("p0_d2", H - 3),
        *faces("f0_d2", 2),
        *both("f2_d2", 1),
        *both("dp_d2", 1),
    )


def tiles(parts):
    return -(-sum(count for _, _, count in parts) // 8)


SEAMS = ("f0", "f1", "f2", "tot", "dp", "p0", "frac", "p1", "rhs2", "rhs3")
PLACES = {
    "t1": ("f1", None, 7),
    "f1": ("f1", 0, 6),
    "tot": ("tot", 0, 7),
    "p0": ("p0", 0, 7),
    "dp": ("dp", 0, 7),
    "dp_d2": ("dp", 1, 6),
    "f0": ("f0", 0, 7),
    "f0_d2": ("f0", 1, 6),
    "f2": ("f2", 0, 7),
    "f2_d2": ("f2", 1, 6),
    "frac": ("frac", 0, 7),
    "p0_d2": ("p0", 1, 6),
    "p1_d2": ("p1", 1, 6),
    "rhs": ("rhs2", 0, 7),
    "rhs_x": ("rhs2", 0, 7),
    "dp_x": ("dp", 0, 7),
    "g2": ("rhs2", 1, 6),
    "g3": ("rhs3", 1, 6),
}


def pack(message, parts, refs, rows):
    at = 0
    for name, first, count in parts:
        for e in range(first, first + count):
            message[at // 8, at % 8 : at % 8 + 1, :] = refs[name][e, rows[name] : rows[name] + 1, :]
            at += 1


def pack_both(near, cross, parts, up, down, rows, gx):
    last = rows - 1
    outer = {name: 0 if PLACES[name][2] == 7 else 1 for name in PLACES}
    up_rows = {name: last - outer[name] for name in PLACES} | {"f1": last - 1}
    down_rows = dict(outer) | {"f1": 0}
    even = lax.axis_index(gx) % 2 == 0

    @pl.when(even)
    def _():
        pack(near, parts, up, up_rows)
        pack(cross, parts, down, down_rows)

    @pl.when(jnp.logical_not(even))
    def _():
        pack(cross, parts, up, up_rows)
        pack(near, parts, down, down_rows)


def unpack(message, parts, seams, side):
    at = 0
    for name, first, count in parts:
        seam, *places = PLACES[name]
        place = places[side]
        for e in range(first, first + count):
            if place is not None:
                seams[seam][e, place : place + 1, :] = message[at // 8, at % 8 : at % 8 + 1, :]
            at += 1


def unpack_both(near, cross, parts, seams, gx):
    even = lax.axis_index(gx) % 2 == 0

    @pl.when(even)
    def _():
        unpack(near, parts, seams, 0)
        unpack(cross, parts, seams, 1)

    @pl.when(jnp.logical_not(even))
    def _():
        unpack(cross, parts, seams, 0)
        unpack(near, parts, seams, 1)


def mobility(sat, history):
    trapped = history / (1.0 + 1.5 * history)
    excess = jnp.maximum(sat - trapped, 0.0)
    free_gas = 0.5 * (excess + jnp.sqrt(excess * excess + excess / 0.375))
    relperm = jnp.where(sat < history, free_gas * free_gas, sat * sat)
    gas = relperm / 0.5
    total = (1.0 - sat) * (1.0 - sat) + gas
    return (total, gas / total)


def roll(x, shift, axis):
    return pltpu.roll(x, shift % x.shape[axis], axis)


def loop(first, last, step, carry):
    count = last - first
    unroll = -(-count // -(-count // 10))
    groups = count // unroll

    def group(g, carry):
        for i in range(unroll):
            carry = step(first + g * unroll + i, carry)
        return carry

    carry = lax.fori_loop(0, groups, group, carry) if groups > 1 else group(0, carry)
    for index in range(first + groups * unroll, last):
        carry = step(index, carry)
    return carry


def split(x):
    high = x.astype(jnp.bfloat16)
    return (high, (x - high.astype(jnp.float32)).astype(jnp.bfloat16))


def at_places(cell, first_layer, layers, rows, columns):
    layer = cell // (rows * columns)
    row = (cell - layer * (rows * columns)) // columns
    place = (layer - first_layer) * rows + row
    return lax.broadcasted_iota(jnp.int32, (layers * rows, cell.shape[1]), 0) == place


def at_columns(cell, columns):
    return lax.broadcasted_iota(jnp.int32, (columns, cell.shape[1]), 0) == cell % columns


def gather(field, at_place, at_column):
    high, low = split(field)
    hot = at_column.astype(jnp.bfloat16)
    by_column = jnp.dot(high, hot, preferred_element_type=jnp.float32) + jnp.dot(
        low, hot, preferred_element_type=jnp.float32
    )
    return jnp.sum(jnp.where(at_place, by_column, 0.0), axis=0, keepdims=True)


def flatten(block, spread):
    perfs, wells = block.shape
    spread[...] = jnp.zeros(spread.shape, jnp.float32)
    spread[:, 0:wells] = block
    wide = spread[...]
    shift = wells
    while shift < LANES:
        wide = wide + roll(wide, shift, 1)
        shift *= 2
    each = LANES // wells
    entry = lax.broadcasted_iota(jnp.int32, (perfs, LANES), 0)
    group = lax.broadcasted_iota(jnp.int32, (perfs, LANES), 1) // wells
    tiles = [
        jnp.sum(jnp.where(entry == first + group, wide, 0.0), axis=0, keepdims=True)
        for first in range(0, perfs, each)
    ]
    return jnp.concatenate(tiles, axis=1)


def prepare_kernel(
    sat,
    hist,
    pressure,
    storage,
    trans,
    cell_in,
    index_in,
    control_in,
    target_in,
    p0e,
    tote,
    frace,
    stor,
    t0,
    t1,
    t2,
    near,
    cross,
    sums,
    cell,
    wells,
    perfs,
    hot,
    sat_v,
    hist_v,
    cell_v,
    index_v,
    control_v,
    target_v,
    spread,
    sems,
    *,
    gz,
):
    layers, rows, columns = pressure.shape
    ext = layers + 2 * H
    own = pl.ds(H, layers)
    parts = [(l, min(LOADED, layers - l)) for l in range(0, layers, LOADED)]
    in_parts = [
        (source.at[pl.ds(l, n)], target.at[pl.ds(offset + l, n)])
        for source, target, offset in ((sat, sat_v, 0), (hist, hist_v, 0), (pressure, p0e, H))
        for l, n in parts
    ]
    small = [(cell_in, cell_v), (index_in, index_v), (control_in, control_v), (target_in, target_v)]
    large = [
        (trans.at[0], t0.at[own]),
        (storage, stor.at[own]),
        (trans.at[1], t1.at[own]),
        (trans.at[2], t2.at[own]),
    ]
    copies = [
        pltpu.make_async_copy(a, b, sems.at[i])
        for i, (a, b) in enumerate(in_parts + small + large)
    ]
    for copy in copies:
        copy.start()

    def layer_step(l, carry):
        t, f = mobility(sat_v[l], hist_v[l])
        tote[l + H] = t
        frace[l + H] = f
        return carry

    for i, (l, n) in enumerate(parts):
        copies[i].wait()
        copies[len(parts) + i].wait()
        loop(l, l + n, layer_step, 0)
    for copy in copies[2 * len(parts) : -len(large)]:
        copy.wait()
    count, group = cell_v.shape
    cell[...] = flatten(cell_v[...].astype(jnp.float32), spread).astype(jnp.int32)
    wells[0:1, :] = flatten(index_v[...], spread)
    wells[1:2, :] = flatten(jnp.broadcast_to(target_v[...], (count, group)), spread)
    wells[2:3, :] = flatten(
        jnp.broadcast_to(control_v[...].astype(jnp.float32), (count, group)), spread
    )
    at_place = at_places(cell[...], lax.axis_index(gz) * layers, layers, rows, columns)
    at_column = at_columns(cell[...], columns)
    hot[...] = at_place.astype(jnp.bfloat16)
    flat = (layers * rows, columns)
    weight = wells[0:1, :] * gather(tote[own].reshape(flat), at_place, at_column)
    cell_p = gather(p0e[own].reshape(flat), at_place, at_column)
    perfs[0:1, :] = weight
    perfs[1:2, :] = cell_p
    for i, value in enumerate((weight * cell_p, weight)):
        part = value[:, 0:LANES]
        for lane in range(LANES, value.shape[1], LANES):
            part = part + value[:, lane : lane + LANES]
        shift = LANES // 2
        while shift >= group:
            part = part + roll(part, shift, 1)
            shift //= 2
        sums[i : i + 1, :] = part
    for copy in copies[-len(large) :]:
        copy.wait()
    even = lax.axis_index(gz) % 2 == 0
    refs = {"p0": p0e, "tot": tote, "t0": t0, "stor": stor, "t1": t1, "t2": t2, "frac": frace}
    for message, is_top in ((near, even), (cross, jnp.logical_not(even))):
        at = 0
        for name, count in Z_PARTS:
            if name == "sums" and message is cross:
                continue
            if name == "sums":
                message[at] = jnp.zeros((rows, columns), jnp.float32)
                message[at, 0:2, 0:LANES] = sums[...]
            else:
                edge = jnp.where(is_top, H + layers - count, H)
                message[pl.ds(at, count)] = refs[name][pl.ds(edge, count)]
            at += count


def masks(rows, columns):
    row = lax.broadcasted_iota(jnp.int32, (rows, columns), 0)
    column = lax.broadcasted_iota(jnp.int32, (rows, columns), 1)
    return (row == rows - 1, column == columns - 1)


def lateral_faces(tot, t1, t2, store, last_row, last_column, top_x):
    along = jnp.where(last_row, 0.0, t1) * 0.5 * (tot + roll(tot, -1, 0))
    across = jnp.where(last_column, 0.0, t2) * 0.5 * (tot + roll(tot, -1, 1))
    part = store + along + roll(along, 1, 0) + across + roll(across, 1, 1)
    return (jnp.where(last_row, jnp.where(top_x, 0.0, t1), along), across, part)


def is_last(axis):
    return lax.axis_index(axis) == lax.axis_size(axis) - 1


def first_sweep(e, p0e, stor, f0e, f1e, f2e, dpe, last_row):
    above = f0e[e]
    below = f0e[e - 1]
    along = jnp.where(last_row, 0.0, f1e[e])
    across = f2e[e]
    diag = dpe[e] + above + below
    p = p0e[e]
    base = stor[e] * p + above * p0e[e + 1] + below * p0e[e - 1]
    base = base + along * roll(p, -1, 0) + roll(along * p, 1, 0)
    base = base + across * roll(p, -1, 1) + roll(across * p, 1, 1)
    return (base, jnp.where(diag > 0.0, 1.0 / diag, 0.0))


def faces_kernel(*refs, layers, gx):
    p0e, tote, frace, stor, t0, t1, t2, part = refs[:8]
    f0e, f1e, f2e, dpe, base, inverse, near, cross, sums = refs[8:]
    _, rows, columns = p0e.shape
    last_row, last_column = masks(rows, columns)
    top_x = is_last(gx)

    def step(e, carry):
        tot = tote[e]
        f0e[e] = t0[e] * 0.5 * (tot + tote[e + 1])
        f1e[e], f2e[e], dpe[e] = lateral_faces(
            tot, t1[e], t2[e], stor[e], last_row, last_column, top_x
        )
        return carry

    loop(H, H + layers, step, 0)
    sums[...] = part[...]
    refs = {"t1": f1e, "tot": tote, "p0": p0e, "dp": dpe, "f0": f0e, "f2": f2e, "f1": f1e}
    refs |= {"frac": frace, "p0_d2": p0e, "f0_d2": f0e, "f2_d2": f2e, "dp_d2": dpe}
    pack_both(near, cross, early_parts(layers), refs, refs, rows, gx)

    def sweep_step(e, carry):
        base[e], inverse[e] = first_sweep(e, p0e, stor, f0e, f1e, f2e, dpe, last_row)
        return carry

    loop(H + 1, H + layers - 1, sweep_step, 0)


def well_holes(sums, wells):
    repeat = lambda x: jnp.concatenate([x] * (wells.shape[1] // LANES), axis=1)
    goal = wells[1:2, :]
    return jnp.where(
        wells[2:3, :] == 0.0, (goal + repeat(sums[0:1, :])) / repeat(sums[1:2, :]), goal
    )


def join(a, b):
    return jnp.concatenate([a, b], axis=0)


def seam_faces(first, last, fields, seams, f1, inverse, p):
    p0e, tote, f0e, f1e, dpe = fields
    rows, columns = p0e.shape[1:]
    row = lax.broadcasted_iota(jnp.int32, (rows + 8, columns), 0)
    edge = (row == rows - 1) | (row == rows + 7)

    def step(e, below):
        tot = join(tote[e], seams["tot"][e])
        mixed = join(f1e[e], seams["f1"][e])
        border = jnp.where(edge, mixed * 0.5 * (tot + roll(tot, -1, 0)), 0.0)
        f1[e] = jnp.where(edge, border, mixed)
        above = join(f0e[e], seams["f0"][e])
        diag = join(dpe[e], seams["dp"][e]) + above + below + border + roll(border, 1, 0)
        inverse[e] = jnp.where(diag > 0.0, 1.0 / diag, 0.0)
        p[e] = join(p0e[e], seams["p0"][e])
        return above

    loop(first, last, step, join(f0e[first - 1], seams["f0"][first - 1]))


def sweep_layers(number, first, last, old, new, fields, seams, f1, inverse, part):
    rhse, f0e, f2e = fields
    rows, columns = rhse.shape[1:]
    row = lax.broadcasted_iota(jnp.int32, (rows + 8, columns), 0)
    beyond = (row == rows + 1) | (row == rows + 6)
    blank = jnp.zeros((rows, columns), jnp.float32)

    def step(e, carry):
        below, p = carry
        above = old[e + 1]
        face = join(f0e[e], seams["f0"][e])
        x = f1[e]
        y = join(f2e[e], seams["f2"][e])
        side = seams["rhs2"][e]
        if number == 3:
            side = jnp.where(beyond[rows:], seams["rhs3"][e], side)
        total = join(rhse[e], side) + below + face * above
        total = total + x * roll(p, -1, 0) + roll(x * p, 1, 0)
        total = total + y * roll(p, -1, 1) + roll(y * p, 1, 1)
        value = total * inverse[e]
        if number == 1:
            value = jnp.where(beyond, join(blank, seams["p1"][e]), value)
        new[e, part] = value[part]
        return (face * p, above)

    start = join(f0e[first - 1], seams["f0"][first - 1]) * old[first - 1]
    loop(first, last, step, (start, old[first]))


def seam_kernel(near, cross, *refs, layers, gx):
    p0e, tote, f0e, f1e, f2e, dpe, rhse = refs[:7]
    refs = refs[7:]
    seams = dict(zip(SEAMS, refs))
    f1, inverse, p, p1 = refs[len(SEAMS) :]
    for seam in seams.values():
        seam[...] = jnp.zeros(seam.shape, jnp.float32)
    unpack_both(near, cross, early_parts(layers), seams, gx)
    inner = (H + 1, H + layers - 1)
    seam_faces(*inner, (p0e, tote, f0e, f1e, dpe), seams, f1, inverse, p)
    for e in (H, H + layers - 1):
        p[e] = join(p0e[e], jnp.zeros_like(seams["p0"][e]))
    own = slice(0, p0e.shape[1])
    sweep_layers(1, *inner, p, p1, (rhse, f0e, f2e), seams, f1, inverse, own)


def halo_kernel(*refs, layers, gx, gz):
    own_t0, cross, near, cell, wells, own_perfs = refs[10:16]
    p0e, tote, frace, stor, f0e, f1e, f2e, dpe, base, inverse, perfs, hot = refs[16:]
    ext, rows, columns = p0e.shape
    even = lax.axis_index(gz) % 2 == 0
    top_z = is_last(gz)
    top_x = is_last(gx)
    last_row, last_column = masks(rows, columns)
    where = {}
    at = 0
    for name, count in Z_PARTS:
        where[name] = (at, count)
        at += count

    def halo(name, e):
        at, count = where[name]
        low = e < H
        at = at + e - (H - count if low else H + layers)
        one, two = (near[at], cross[at])
        return jnp.where(even, two, one) if low else jnp.where(even, one, two)

    for name, target in (("p0", p0e), ("tot", tote), ("frac", frace), ("stor", stor)):
        count = where[name][1]
        for e in (*range(H - count, H), *range(H + layers, H + layers + count)):
            target[e] = halo(name, e)
    f0e[H + layers - 1] = jnp.where(top_z, 0.0, own_t0[H + layers - 1]) * 0.5 * (
        tote[H + layers - 1] + tote[H + layers]
    )
    for e in (*range(0, H), *range(H + layers, ext - 1)):
        f0e[e] = halo("t0", e) * 0.5 * (tote[e] + tote[e + 1])
    for e in (*range(1, H), *range(H + layers, ext - 1)):
        f1e[e], f2e[e], dpe[e] = lateral_faces(
            tote[e], halo("t1", e), halo("t2", e), stor[e], last_row, last_column, top_x
        )
    for e in (*range(1, H + 1), *range(H + layers - 1, ext - 1)):
        base[e], inverse[e] = first_sweep(e, p0e, stor, f0e, f1e, f2e, dpe, last_row)
    width = H - 1
    first = lax.axis_index(gz) * layers
    sides = ((1, first - width), (H + layers, first + layers))
    at_place = [at_places(cell[...], layer, width, rows, columns) for _, layer in sides]
    at_place = jnp.concatenate(at_place, axis=0)
    at_column = at_columns(cell[...], columns)
    hot[...] = at_place.astype(jnp.bfloat16)
    flat = (width * rows, columns)
    both = lambda ref: join(*(ref[e : e + width].reshape(flat) for e, _ in sides))
    weight = wells[0:1, :] * gather(both(tote), at_place, at_column)
    perfs[0:1, :] = own_perfs[0:1, :] + weight
    perfs[1:2, :] = own_perfs[1:2, :] + gather(both(p0e), at_place, at_column)


def build_kernel(*refs, layers, gx):
    p0e, stor, f0e, f1e, f2e, dpe, tote, base, inverse, sums, perfs, hot, own_hot = refs[:13]
    cell, wells, rhse, source, x_near, x_cross, bottom = refs[13:20]
    p1, g2u, g2d, g3u, g3d, rxu, rxd, dpx = refs[20:]
    ext, rows, columns = p0e.shape
    last_row, _ = masks(rows, columns)
    hole = well_holes(sums[...], wells[...])
    bottom[...] = hole[:, 0:LANES]
    rate = perfs[0:1, :] * (hole - perfs[1:2, :])
    pieces = split(jnp.where(at_columns(cell[...], columns), rate, 0.0))

    def scatter(mask):
        spread = [
            lax.dot_general(
                mask, piece, (((1,), (1,)), ((), ())), preferred_element_type=jnp.float32
            )
            for piece in pieces
        ]
        return (spread[0] + spread[1]).reshape(-1, rows, columns)

    width = H - 1
    inside = scatter(own_hot[...])
    outside = scatter(hot[...])
    source[...] = inside
    rhse[H : ext - H] = inside
    rhse[1:H] = outside[:width]
    rhse[ext - H : ext - 1] = outside[width:]

    def first_step(e, carry):
        wells_rate = rhse[e]
        p1[e] = (base[e] + wells_rate) * inverse[e]
        rhse[e] = stor[e] * p0e[e] + wells_rate
        return carry

    loop(1, ext - 1, first_step, 0)

    def second_step(e, carry):
        along = jnp.where(last_row, 0.0, f1e[e])
        across = f2e[e]
        p = p1[e]
        rhs = rhse[e]
        lower = roll(along * p, 1, 0)
        upper = along * roll(p, -1, 0)
        g2u[e] = rhs + lower
        g2d[e] = rhs + upper
        new = rhs + lower + upper + f0e[e] * p1[e + 1] + f0e[e - 1] * p1[e - 1]
        new = new + across * roll(p, -1, 1) + roll(across * p, 1, 1)
        p2 = new * inverse[e]
        g3u[e] = rhs + roll(along * p2, 1, 0)
        g3d[e] = rhs + along * roll(p2, -1, 0)
        return carry

    loop(H - 1, ext - H + 1, second_step, 0)

    for e, beside, face in ((2, 1, 1), (ext - 3, ext - 2, ext - 3)):
        along = jnp.where(last_row, 0.0, f1e[e])
        across = f2e[e]
        p = p0e[e]
        rhs = rhse[e] + f0e[face] * p0e[beside]
        rhs = rhs + across * roll(p, -1, 1) + roll(across * p, 1, 1)
        rxu[e] = rhs + roll(along * p, 1, 0)
        rxd[e] = rhs + along * roll(p, -1, 0)
        dpx[e] = dpe[e] + f0e[face]

    shared = {"t1": f1e, "tot": tote, "p0": p0e, "dp": dpe, "f0": f0e, "f2": f2e, "f1": f1e}
    shared |= {"p0_d2": p0e, "f0_d2": f0e, "f2_d2": f2e, "dp_d2": dpe, "rhs": rhse, "p1_d2": p1}
    shared["dp_x"] = dpx
    up = shared | {"g2": g2u, "g3": g3u, "rhs_x": rxu}
    down = shared | {"g2": g2d, "g3": g3d, "rhs_x": rxd}
    pack_both(x_near, x_cross, late_parts(layers), up, down, rows, gx)


def finish_kernel(*refs, gx):
    sat, hist, volume, storage, source = refs[:5]
    p0e, tote, frace, f0e, f1e, f2e, dpe, rhse, near, cross = refs[5:15]
    hole = refs[19 + len(SEAMS)]
    refs = refs[20 + len(SEAMS) :]
    new_p, residual, new_sat, new_hist, bottom = refs[:5]
    seams = dict(zip(SEAMS, refs[5:]))
    f1, rdiag, pa, pb = refs[5 + len(SEAMS) :]
    bottom[...] = hole[:, 0 : bottom.shape[1]]
    layers, rows, columns = sat.shape
    ext = layers + 2 * H
    unpack_both(near, cross, late_parts(layers), seams, gx)
    sfrac = seams["frac"]
    pa[0] = join(p0e[0], seams["p0"][0])
    pa[ext - 1] = join(p0e[ext - 1], seams["p0"][ext - 1])
    for first, last in ((1, H + 1), (ext - H - 1, ext - 1)):
        seam_faces(first, last, (p0e, tote, f0e, f1e, dpe), seams, f1, rdiag, pa)

    pressures = (pa, pb)
    fields = (rhse, f0e, f2e)
    inner = (H + 1, ext - H - 1)
    everywhere = slice(0, rows + 8)
    for number in range(1, SWEEPS + 1):
        old, new = pressures[(number - 1) % 2], pressures[number % 2]
        ranges = [(number, ext - number, everywhere)]
        if number == 1:
            ranges = [
                (number, inner[0], everywhere),
                (*inner, slice(rows, rows + 8)),
                (inner[1], ext - number, everywhere),
            ]
        for first, last, part in ranges:
            sweep_layers(number, first, last, old, new, fields, seams, f1, rdiag, part)
    field = pressures[SWEEPS % 2]

    def flow(face, p, p_next, f, f_next):
        water = face * (p - p_next)
        return (water, water * jnp.where(water > 0, f, f_next))

    def last_step(l, carry):
        below_w, below_g = carry
        e = l + H
        p = field[e]
        f = join(frace[e], sfrac[e])
        own_p = p[:rows]
        own_f = f[:rows]
        above_w, above_g = flow(f0e[e], own_p, field[e + 1][:rows], own_f, frace[e + 1])
        xw, xg = flow(f1[e], p, roll(p, -1, 0), f, roll(f, -1, 0))
        yw, yg = flow(f2e[e], own_p, roll(own_p, -1, 1), own_f, roll(own_f, -1, 1))
        water = above_w - below_w + (xw - roll(xw, 1, 0))[:rows] + yw - roll(yw, 1, 1)
        out = above_g - below_g + (xg - roll(xg, 1, 0))[:rows] + yg - roll(yg, 1, 1)
        new_p[l] = own_p
        residual[l] = rhse[e] - storage[l] * own_p - water
        src = source[l]
        gas = jnp.maximum(src, 0.0) + jnp.minimum(src, 0.0) * own_f
        s = sat[l] + volume[l] * (gas - out)
        new_sat[l] = s
        new_hist[l] = jnp.maximum(hist[l], s)
        return (above_w, above_g)

    first = flow(f0e[H - 1], field[H - 1][:rows], field[H][:rows], frace[H - 1], frace[H])
    loop(0, layers, last_step, first)


def swap(block, axis, first):
    pairs = [(i, i + 1) for i in range(first, lax.axis_size(axis) - 1, 2)]
    return lax.ppermute(block, axis, pairs + [(b, a) for a, b in pairs])


def pin(*shape, dtype=jnp.float32):
    return pltpu.VMEM(shape, dtype)


VMEM = pl.BlockSpec(memory_space=pltpu.VMEM)
HBM = pl.BlockSpec(memory_space=pltpu.HBM)


def call(kernel, outs, scratch, *args, space=VMEM, sems=0, aliases={}):
    as_struct = lambda s: s if hasattr(s, "dtype") else jax.ShapeDtypeStruct(s, jnp.float32)
    as_scratch = lambda s: pltpu.VMEM(as_struct(s).shape, as_struct(s).dtype)
    return pl.pallas_call(
        kernel,
        out_shape=[as_struct(s) for s in outs],
        in_specs=[space] * len(args),
        out_specs=[VMEM] * len(outs),
        scratch_shapes=[as_scratch(s) for s in scratch]
        + ([pltpu.SemaphoreType.DMA((sems,))] if sems else []),
        input_output_aliases=aliases,
        compiler_params=pltpu.CompilerParams(vmem_limit_bytes=24 * 1024 * 1024),
    )(*(pltpu.with_memory_space_constraint(a, pltpu.HBM) if space is HBM else a for a in args))


def body(
    pressure,
    saturation,
    sat_history,
    storage,
    step_volume,
    transmiss,
    perf_cell,
    perf_index,
    control,
    target,
):
    layers, rows, columns = pressure.shape
    ext = layers + 2 * H
    wells, perfs = perf_cell.shape
    block = (layers, rows, columns)
    pinned = pin(*block)
    ext_block = pin(ext, rows, columns)
    z_layers = sum(count for _, count in Z_PARTS)
    z_near, z_cross = (pin(n, rows, columns) for n in (z_layers, z_layers - 1))
    entries = wells * perfs
    early, late = (pin(tiles(f(layers)), 8, columns) for f in (early_parts, late_parts))
    seams = [pin(ext, 8, columns)] * len(SEAMS)
    *fields, near, cross, part, cell, per_perf, perf_values, own_hot = call(
        functools.partial(prepare_kernel, gz="gz"),
        [ext_block] * 7
        + [z_near, z_cross]
        + [
            pin(2, LANES),
            pin(1, entries, dtype=jnp.int32),
            pin(3, entries),
            pin(2, entries),
            pin(layers * rows, entries, dtype=jnp.bfloat16),
        ],
        [
            block,
            block,
            jax.ShapeDtypeStruct((perfs, wells), jnp.int32),
            (perfs, wells),
            jax.ShapeDtypeStruct((1, wells), jnp.int32),
            (1, wells),
            (perfs, LANES),
        ],
        saturation,
        sat_history,
        pressure,
        storage,
        transmiss,
        perf_cell.T,
        perf_index.T,
        control.reshape(1, wells),
        target.reshape(1, wells),
        space=HBM,
        sems=3 * -(-layers // LOADED) + 8,
    )
    cross = swap(cross, "gz", 1)
    near = swap(near, "gz", 0)
    p0e, tote, frace, stor, t0, t1, t2 = fields
    f0e, f1e, f2e, dpe, base, inverse, early_near, early_cross, part = call(
        functools.partial(faces_kernel, layers=layers, gx="gx"),
        [ext_block] * 6 + [early, early, pin(2, LANES)],
        [],
        *fields,
        part,
    )
    early_cross = swap(early_cross, "gx", 1)
    early_near = swap(early_near, "gx", 0)
    sums = part + near[-1, 0:2, 0:LANES]
    step = 2
    while step < lax.axis_size("gz"):
        pairs = [(i, i ^ step) for i in range(lax.axis_size("gz"))]
        tile = jnp.pad(sums, ((0, 8 - sums.shape[0]), (0, 0)))
        sums = sums + lax.ppermute(tile, "gz", pairs)[: sums.shape[0]]
        step *= 2
    p0e, tote, frace, stor, f0e, f1e, f2e, dpe, base, inverse, perf_values, hot = call(
        functools.partial(halo_kernel, layers=layers, gx="gx", gz="gz"),
        [ext_block] * 10
        + [pin(2, entries), pin(2 * (H - 1) * rows, entries, dtype=jnp.bfloat16)],
        [],
        p0e,
        tote,
        frace,
        stor,
        f0e,
        f1e,
        f2e,
        dpe,
        base,
        inverse,
        t0,
        cross,
        near,
        cell,
        per_perf,
        perf_values,
        aliases={i: i for i in range(10)},
    )
    rhse, source, late_near, late_cross, hole = call(
        functools.partial(build_kernel, layers=layers, gx="gx"),
        [ext_block, pinned, late, late, pin(1, LANES)],
        [ext_block] * 8,
        p0e,
        stor,
        f0e,
        f1e,
        f2e,
        dpe,
        tote,
        base,
        inverse,
        sums,
        perf_values,
        hot,
        own_hot,
        cell,
        per_perf,
    )
    late_cross = swap(late_cross, "gx", 1)
    late_near = swap(late_near, "gx", 0)
    early_near, early_cross, rhse = lax.optimization_barrier((early_near, early_cross, rhse))
    joined = [pin(ext, rows + 8, columns)] * 4
    filled = call(
        functools.partial(seam_kernel, layers=layers, gx="gx"),
        seams + joined,
        [],
        early_near,
        early_cross,
        p0e,
        tote,
        f0e,
        f1e,
        f2e,
        dpe,
        rhse,
    )
    field, residual, new_sat, new_hist, bottom, *_ = call(
        functools.partial(finish_kernel, gx="gx"),
        [block] * 4 + [(1, wells)] + seams + joined,
        [],
        saturation,
        sat_history,
        step_volume,
        storage,
        source,
        p0e,
        tote,
        frace,
        f0e,
        f1e,
        f2e,
        dpe,
        rhse,
        late_near,
        late_cross,
        *filled,
        hole,
        aliases={15 + i: 5 + i for i in range(len(filled))},
    )
    return (field, residual, new_sat, new_hist, bottom.reshape(wells))


def solution(mesh):
    return jax.shard_map(
        body,
        mesh=mesh,
        in_specs=(
            P("gz", "gx", None),
            P("gz", "gx", None),
            P("gz", "gx", None),
            P("gz", "gx", None),
            P("gz", "gx", None),
            P(None, "gz", "gx", None),
            P("gx", None),
            P("gx", None),
            P("gx"),
            P("gx"),
        ),
        out_specs=(
            P("gz", "gx", None),
            P("gz", "gx", None),
            P("gz", "gx", None),
            P("gz", "gx", None),
            P("gx"),
        ),
        check_vma=False,
    )
```

```python
import functools

import jax
import jax.numpy as jnp
from jax import lax
from jax.experimental import pallas as pl
from jax.experimental.pallas import tpu as pltpu
from jax.sharding import PartitionSpec as P

SWEEPS = 4
H = SWEEPS + 1
LANES = 128
LOADED = 4

Z_PARTS = (
    ("p0", H),
    ("tot", H),
    ("t0", H),
    ("stor", H - 1),
    ("t1", H - 1),
    ("t2", H - 1),
    ("frac", 1),
    ("sums", 1),
)


def early_parts(layers):
    own = (H, layers)
    inner = (H, layers - 1)
    return (
        ("t1", *own),
        ("tot", *own),
        ("p0", *own),
        ("dp", *own),
        ("f0", *inner),
        ("f2", *own),
        ("f1", *own),
        ("frac", *own),
        ("p0_d2", *own),
        ("f0_d2", *inner),
        ("f2_d2", *own),
        ("dp_d2", *own),
    )


def late_parts(layers):
    top = H + layers
    both = lambda name, n: ((name, H - n, n), (name, top, n))
    faces = lambda name, n: ((name, H - n, n), (name, top - 1, n))
    ends = lambda name: ((name, 2, 1), (name, top + 2, 1))
    return (
        ("rhs", 3, layers + 4),
        *ends("rhs_x"),
        ("p1_d2", 3, layers + 4),
        ("g2", 4, layers + 2),
        ("g3", H, layers),
        *both("t1", H - 1),
        *both("tot", H - 1),
        *both("p0", H - 1),
        *both("dp", H - 3),
        *ends("dp_x"),
        *faces("f0", H - 2),
        *both("f2", H - 3),
        *both("f1", H - 3),
        *both("p0_d2", H - 3),
        *faces("f0_d2", 2),
        *both("f2_d2", 1),
        *both("dp_d2", 1),
    )


def tiles(parts):
    return -(-sum(count for _, _, count in parts) // 8)


SEAMS = ("f0", "f1", "f2", "tot", "dp", "p0", "frac", "p1", "rhs2", "rhs3")
PLACES = {
    "t1": ("f1", None, 7),
    "f1": ("f1", 0, 6),
    "tot": ("tot", 0, 7),
    "p0": ("p0", 0, 7),
    "dp": ("dp", 0, 7),
    "dp_d2": ("dp", 1, 6),
    "f0": ("f0", 0, 7),
    "f0_d2": ("f0", 1, 6),
    "f2": ("f2", 0, 7),
    "f2_d2": ("f2", 1, 6),
    "frac": ("frac", 0, 7),
    "p0_d2": ("p0", 1, 6),
    "p1_d2": ("p1", 1, 6),
    "rhs": ("rhs2", 0, 7),
    "rhs_x": ("rhs2", 0, 7),
    "dp_x": ("dp", 0, 7),
    "g2": ("rhs2", 1, 6),
    "g3": ("rhs3", 1, 6),
}


def pack(message, parts, refs, rows):
    at = 0
    for name, first, count in parts:
        for e in range(first, first + count):
            message[at // 8, at % 8 : at % 8 + 1, :] = refs[name][e, rows[name] : rows[name] + 1, :]
            at += 1


def pack_both(near, cross, parts, up, down, rows, gx):
    last = rows - 1
    outer = {name: 0 if PLACES[name][2] == 7 else 1 for name in PLACES}
    up_rows = {name: last - outer[name] for name in PLACES} | {"f1": last - 1}
    down_rows = dict(outer) | {"f1": 0}
    even = lax.axis_index(gx) % 2 == 0

    @pl.when(even)
    def _():
        pack(near, parts, up, up_rows)
        pack(cross, parts, down, down_rows)

    @pl.when(jnp.logical_not(even))
    def _():
        pack(cross, parts, up, up_rows)
        pack(near, parts, down, down_rows)


def unpack(message, parts, seams, side):
    at = 0
    for name, first, count in parts:
        seam, *places = PLACES[name]
        place = places[side]
        for e in range(first, first + count):
            if place is not None:
                seams[seam][e, place : place + 1, :] = message[at // 8, at % 8 : at % 8 + 1, :]
            at += 1


def unpack_both(near, cross, parts, seams, gx):
    even = lax.axis_index(gx) % 2 == 0

    @pl.when(even)
    def _():
        unpack(near, parts, seams, 0)
        unpack(cross, parts, seams, 1)

    @pl.when(jnp.logical_not(even))
    def _():
        unpack(cross, parts, seams, 0)
        unpack(near, parts, seams, 1)


def mobility(sat, history):
    trapped = history / (1.0 + 1.5 * history)
    excess = jnp.maximum(sat - trapped, 0.0)
    free_gas = 0.5 * (excess + jnp.sqrt(excess * excess + excess / 0.375))
    relperm = jnp.where(sat < history, free_gas * free_gas, sat * sat)
    gas = relperm / 0.5
    total = (1.0 - sat) * (1.0 - sat) + gas
    return (total, gas / total)


def roll(x, shift, axis):
    return pltpu.roll(x, shift % x.shape[axis], axis)


def loop(first, last, step, carry):
    count = last - first
    unroll = -(-count // -(-count // 10))
    groups = count // unroll

    def group(g, carry):
        for i in range(unroll):
            carry = step(first + g * unroll + i, carry)
        return carry

    carry = lax.fori_loop(0, groups, group, carry) if groups > 1 else group(0, carry)
    for index in range(first + groups * unroll, last):
        carry = step(index, carry)
    return carry


def split(x):
    high = x.astype(jnp.bfloat16)
    return (high, (x - high.astype(jnp.float32)).astype(jnp.bfloat16))


def at_places(cell, first_layer, layers, rows, columns):
    layer = cell // (rows * columns)
    row = (cell - layer * (rows * columns)) // columns
    place = (layer - first_layer) * rows + row
    return lax.broadcasted_iota(jnp.int32, (layers * rows, cell.shape[1]), 0) == place


def at_columns(cell, columns):
    return lax.broadcasted_iota(jnp.int32, (columns, cell.shape[1]), 0) == cell % columns


def gather(field, at_place, at_column):
    high, low = split(field)
    hot = at_column.astype(jnp.bfloat16)
    by_column = jnp.dot(high, hot, preferred_element_type=jnp.float32) + jnp.dot(
        low, hot, preferred_element_type=jnp.float32
    )
    return jnp.sum(jnp.where(at_place, by_column, 0.0), axis=0, keepdims=True)


def flatten(block, spread):
    perfs, wells = block.shape
    spread[...] = jnp.zeros(spread.shape, jnp.float32)
    spread[:, 0:wells] = block
    wide = spread[...]
    shift = wells
    while shift < LANES:
        wide = wide + roll(wide, shift, 1)
        shift *= 2
    each = LANES // wells
    entry = lax.broadcasted_iota(jnp.int32, (perfs, LANES), 0)
    group = lax.broadcasted_iota(jnp.int32, (perfs, LANES), 1) // wells
    tiles = [
        jnp.sum(jnp.where(entry == first + group, wide, 0.0), axis=0, keepdims=True)
        for first in range(0, perfs, each)
    ]
    return jnp.concatenate(tiles, axis=1)


def prepare_kernel(
    sat,
    hist,
    pressure,
    storage,
    trans,
    cell_in,
    index_in,
    control_in,
    target_in,
    p0e,
    tote,
    frace,
    stor,
    t0,
    t1,
    t2,
    near,
    cross,
    sums,
    cell,
    wells,
    perfs,
    hot,
    sat_v,
    hist_v,
    cell_v,
    index_v,
    control_v,
    target_v,
    spread,
    sems,
    *,
    gz,
):
    layers, rows, columns = pressure.shape
    ext = layers + 2 * H
    own = pl.ds(H, layers)
    parts = [(l, min(LOADED, layers - l)) for l in range(0, layers, LOADED)]
    in_parts = [
        (source.at[pl.ds(l, n)], target.at[pl.ds(offset + l, n)])
        for source, target, offset in ((sat, sat_v, 0), (hist, hist_v, 0), (pressure, p0e, H))
        for l, n in parts
    ]
    small = [(cell_in, cell_v), (index_in, index_v), (control_in, control_v), (target_in, target_v)]
    large = [
        (trans.at[0], t0.at[own]),
        (storage, stor.at[own]),
        (trans.at[1], t1.at[own]),
        (trans.at[2], t2.at[own]),
    ]
    copies = [
        pltpu.make_async_copy(a, b, sems.at[i])
        for i, (a, b) in enumerate(in_parts + small + large)
    ]
    for copy in copies:
        copy.start()

    def layer_step(l, carry):
        t, f = mobility(sat_v[l], hist_v[l])
        tote[l + H] = t
        frace[l + H] = f
        return carry

    for i, (l, n) in enumerate(parts):
        copies[i].wait()
        copies[len(parts) + i].wait()
        loop(l, l + n, layer_step, 0)
    for copy in copies[2 * len(parts) : -len(large)]:
        copy.wait()
    count, group = cell_v.shape
    cell[...] = flatten(cell_v[...].astype(jnp.float32), spread).astype(jnp.int32)
    wells[0:1, :] = flatten(index_v[...], spread)
    wells[1:2, :] = flatten(jnp.broadcast_to(target_v[...], (count, group)), spread)
    wells[2:3, :] = flatten(
        jnp.broadcast_to(control_v[...].astype(jnp.float32), (count, group)), spread
    )
    at_place = at_places(cell[...], lax.axis_index(gz) * layers, layers, rows, columns)
    at_column = at_columns(cell[...], columns)
    hot[...] = at_place.astype(jnp.bfloat16)
    flat = (layers * rows, columns)
    weight = wells[0:1, :] * gather(tote[own].reshape(flat), at_place, at_column)
    cell_p = gather(p0e[own].reshape(flat), at_place, at_column)
    perfs[0:1, :] = weight
    perfs[1:2, :] = cell_p
    for i, value in enumerate((weight * cell_p, weight)):
        part = value[:, 0:LANES]
        for lane in range(LANES, value.shape[1], LANES):
            part = part + value[:, lane : lane + LANES]
        shift = LANES // 2
        while shift >= group:
            part = part + roll(part, shift, 1)
            shift //= 2
        sums[i : i + 1, :] = part
    for copy in copies[-len(large) :]:
        copy.wait()
    even = lax.axis_index(gz) % 2 == 0
    refs = {"p0": p0e, "tot": tote, "t0": t0, "stor": stor, "t1": t1, "t2": t2, "frac": frace}
    for message, is_top in ((near, even), (cross, jnp.logical_not(even))):
        at = 0
        for name, count in Z_PARTS:
            if name == "sums" and message is cross:
                continue
            if name == "sums":
                message[at] = jnp.zeros((rows, columns), jnp.float32)
                message[at, 0:2, 0:LANES] = sums[...]
            else:
                edge = jnp.where(is_top, H + layers - count, H)
                message[pl.ds(at, count)] = refs[name][pl.ds(edge, count)]
            at += count


def masks(rows, columns):
    row = lax.broadcasted_iota(jnp.int32, (rows, columns), 0)
    column = lax.broadcasted_iota(jnp.int32, (rows, columns), 1)
    return (row == rows - 1, column == columns - 1)


def lateral_faces(tot, t1, t2, store, last_row, last_column, top_x):
    along = jnp.where(last_row, 0.0, t1) * 0.5 * (tot + roll(tot, -1, 0))
    across = jnp.where(last_column, 0.0, t2) * 0.5 * (tot + roll(tot, -1, 1))
    part = store + along + roll(along, 1, 0) + across + roll(across, 1, 1)
    return (jnp.where(last_row, jnp.where(top_x, 0.0, t1), along), across, part)


def is_last(axis):
    return lax.axis_index(axis) == lax.axis_size(axis) - 1


def first_sweep(e, p0e, stor, f0e, f1e, f2e, dpe, last_row):
    above = f0e[e]
    below = f0e[e - 1]
    along = jnp.where(last_row, 0.0, f1e[e])
    across = f2e[e]
    diag = dpe[e] + above + below
    p = p0e[e]
    base = stor[e] * p + above * p0e[e + 1] + below * p0e[e - 1]
    base = base + along * roll(p, -1, 0) + roll(along * p, 1, 0)
    base = base + across * roll(p, -1, 1) + roll(across * p, 1, 1)
    return (base, jnp.where(diag > 0.0, 1.0 / diag, 0.0))


def faces_kernel(*refs, layers, gx):
    p0e, tote, frace, stor, t0, t1, t2, part = refs[:8]
    f0e, f1e, f2e, dpe, base, inverse, near, cross, sums = refs[8:]
    _, rows, columns = p0e.shape
    last_row, last_column = masks(rows, columns)
    top_x = is_last(gx)

    def step(e, carry):
        tot = tote[e]
        f0e[e] = t0[e] * 0.5 * (tot + tote[e + 1])
        f1e[e], f2e[e], dpe[e] = lateral_faces(
            tot, t1[e], t2[e], stor[e], last_row, last_column, top_x
        )
        return carry

    loop(H, H + layers, step, 0)
    sums[...] = part[...]
    refs = {"t1": f1e, "tot": tote, "p0": p0e, "dp": dpe, "f0": f0e, "f2": f2e, "f1": f1e}
    refs |= {"frac": frace, "p0_d2": p0e, "f0_d2": f0e, "f2_d2": f2e, "dp_d2": dpe}
    pack_both(near, cross, early_parts(layers), refs, refs, rows, gx)

    def sweep_step(e, carry):
        base[e], inverse[e] = first_sweep(e, p0e, stor, f0e, f1e, f2e, dpe, last_row)
        return carry

    loop(H + 1, H + layers - 1, sweep_step, 0)


def well_holes(sums, wells):
    repeat = lambda x: jnp.concatenate([x] * (wells.shape[1] // LANES), axis=1)
    goal = wells[1:2, :]
    return jnp.where(
        wells[2:3, :] == 0.0, (goal + repeat(sums[0:1, :])) / repeat(sums[1:2, :]), goal
    )


def join(a, b):
    return jnp.concatenate([a, b], axis=0)


def seam_faces(first, last, fields, seams, f1, inverse, p):
    p0e, tote, f0e, f1e, dpe = fields
    rows, columns = p0e.shape[1:]
    row = lax.broadcasted_iota(jnp.int32, (rows + 8, columns), 0)
    edge = (row == rows - 1) | (row == rows + 7)

    def step(e, below):
        tot = join(tote[e], seams["tot"][e])
        mixed = join(f1e[e], seams["f1"][e])
        border = jnp.where(edge, mixed * 0.5 * (tot + roll(tot, -1, 0)), 0.0)
        f1[e] = jnp.where(edge, border, mixed)
        above = join(f0e[e], seams["f0"][e])
        diag = join(dpe[e], seams["dp"][e]) + above + below + border + roll(border, 1, 0)
        inverse[e] = jnp.where(diag > 0.0, 1.0 / diag, 0.0)
        p[e] = join(p0e[e], seams["p0"][e])
        return above

    loop(first, last, step, join(f0e[first - 1], seams["f0"][first - 1]))


def sweep_layers(number, first, last, old, new, fields, seams, f1, inverse, part):
    rhse, f0e, f2e = fields
    rows, columns = rhse.shape[1:]
    row = lax.broadcasted_iota(jnp.int32, (rows + 8, columns), 0)
    beyond = (row == rows + 1) | (row == rows + 6)
    blank = jnp.zeros((rows, columns), jnp.float32)

    def step(e, carry):
        below, p = carry
        above = old[e + 1]
        face = join(f0e[e], seams["f0"][e])
        x = f1[e]
        y = join(f2e[e], seams["f2"][e])
        side = seams["rhs2"][e]
        if number == 3:
            side = jnp.where(beyond[rows:], seams["rhs3"][e], side)
        total = join(rhse[e], side) + below + face * above
        total = total + x * roll(p, -1, 0) + roll(x * p, 1, 0)
        total = total + y * roll(p, -1, 1) + roll(y * p, 1, 1)
        value = total * inverse[e]
        if number == 1:
            value = jnp.where(beyond, join(blank, seams["p1"][e]), value)
        new[e, part] = value[part]
        return (face * p, above)

    start = join(f0e[first - 1], seams["f0"][first - 1]) * old[first - 1]
    loop(first, last, step, (start, old[first]))


def seam_kernel(near, cross, *refs, layers, gx):
    p0e, tote, f0e, f1e, f2e, dpe, rhse = refs[:7]
    refs = refs[7:]
    seams = dict(zip(SEAMS, refs))
    f1, inverse, p, p1 = refs[len(SEAMS) :]
    for seam in seams.values():
        seam[...] = jnp.zeros(seam.shape, jnp.float32)
    unpack_both(near, cross, early_parts(layers), seams, gx)
    inner = (H + 1, H + layers - 1)
    seam_faces(*inner, (p0e, tote, f0e, f1e, dpe), seams, f1, inverse, p)
    for e in (H, H + layers - 1):
        p[e] = join(p0e[e], jnp.zeros_like(seams["p0"][e]))
    own = slice(0, p0e.shape[1])
    sweep_layers(1, *inner, p, p1, (rhse, f0e, f2e), seams, f1, inverse, own)


def halo_kernel(*refs, layers, gx, gz):
    own_t0, cross, near, cell, wells, own_perfs = refs[10:16]
    p0e, tote, frace, stor, f0e, f1e, f2e, dpe, base, inverse, perfs, hot = refs[16:]
    ext, rows, columns = p0e.shape
    even = lax.axis_index(gz) % 2 == 0
    top_z = is_last(gz)
    top_x = is_last(gx)
    last_row, last_column = masks(rows, columns)
    where = {}
    at = 0
    for name, count in Z_PARTS:
        where[name] = (at, count)
        at += count

    def halo(name, e):
        at, count = where[name]
        low = e < H
        at = at + e - (H - count if low else H + layers)
        one, two = (near[at], cross[at])
        return jnp.where(even, two, one) if low else jnp.where(even, one, two)

    for name, target in (("p0", p0e), ("tot", tote), ("frac", frace), ("stor", stor)):
        count = where[name][1]
        for e in (*range(H - count, H), *range(H + layers, H + layers + count)):
            target[e] = halo(name, e)
    f0e[H + layers - 1] = jnp.where(top_z, 0.0, own_t0[H + layers - 1]) * 0.5 * (
        tote[H + layers - 1] + tote[H + layers]
    )
    for e in (*range(0, H), *range(H + layers, ext - 1)):
        f0e[e] = halo("t0", e) * 0.5 * (tote[e] + tote[e + 1])
    for e in (*range(1, H), *range(H + layers, ext - 1)):
        f1e[e], f2e[e], dpe[e] = lateral_faces(
            tote[e], halo("t1", e), halo("t2", e), stor[e], last_row, last_column, top_x
        )
    for e in (*range(1, H + 1), *range(H + layers - 1, ext - 1)):
        base[e], inverse[e] = first_sweep(e, p0e, stor, f0e, f1e, f2e, dpe, last_row)
    width = H - 1
    first = lax.axis_index(gz) * layers
    sides = ((1, first - width), (H + layers, first + layers))
    at_place = [at_places(cell[...], layer, width, rows, columns) for _, layer in sides]
    at_place = jnp.concatenate(at_place, axis=0)
    at_column = at_columns(cell[...], columns)
    hot[...] = at_place.astype(jnp.bfloat16)
    flat = (width * rows, columns)
    both = lambda ref: join(*(ref[e : e + width].reshape(flat) for e, _ in sides))
    weight = wells[0:1, :] * gather(both(tote), at_place, at_column)
    perfs[0:1, :] = own_perfs[0:1, :] + weight
    perfs[1:2, :] = own_perfs[1:2, :] + gather(both(p0e), at_place, at_column)


def build_kernel(*refs, layers, gx):
    p0e, stor, f0e, f1e, f2e, dpe, tote, base, inverse, sums, perfs, hot, own_hot = refs[:13]
    cell, wells, rhse, source, x_near, x_cross, bottom = refs[13:20]
    p1, g2u, g2d, g3u, g3d, rxu, rxd, dpx = refs[20:]
    ext, rows, columns = p0e.shape
    last_row, _ = masks(rows, columns)
    hole = well_holes(sums[...], wells[...])
    bottom[...] = hole[:, 0:LANES]
    rate = perfs[0:1, :] * (hole - perfs[1:2, :])
    pieces = split(jnp.where(at_columns(cell[...], columns), rate, 0.0))

    def scatter(mask):
        spread = [
            lax.dot_general(
                mask, piece, (((1,), (1,)), ((), ())), preferred_element_type=jnp.float32
            )
            for piece in pieces
        ]
        return (spread[0] + spread[1]).reshape(-1, rows, columns)

    width = H - 1
    inside = scatter(own_hot[...])
    outside = scatter(hot[...])
    source[...] = inside
    rhse[H : ext - H] = inside
    rhse[1:H] = outside[:width]
    rhse[ext - H : ext - 1] = outside[width:]

    def first_step(e, carry):
        wells_rate = rhse[e]
        p1[e] = (base[e] + wells_rate) * inverse[e]
        rhse[e] = stor[e] * p0e[e] + wells_rate
        return carry

    loop(1, ext - 1, first_step, 0)

    def second_step(e, carry):
        along = jnp.where(last_row, 0.0, f1e[e])
        across = f2e[e]
        p = p1[e]
        rhs = rhse[e]
        lower = roll(along * p, 1, 0)
        upper = along * roll(p, -1, 0)
        g2u[e] = rhs + lower
        g2d[e] = rhs + upper
        new = rhs + lower + upper + f0e[e] * p1[e + 1] + f0e[e - 1] * p1[e - 1]
        new = new + across * roll(p, -1, 1) + roll(across * p, 1, 1)
        p2 = new * inverse[e]
        g3u[e] = rhs + roll(along * p2, 1, 0)
        g3d[e] = rhs + along * roll(p2, -1, 0)
        return carry

    loop(H - 1, ext - H + 1, second_step, 0)

    for e, beside, face in ((2, 1, 1), (ext - 3, ext - 2, ext - 3)):
        along = jnp.where(last_row, 0.0, f1e[e])
        across = f2e[e]
        p = p0e[e]
        rhs = rhse[e] + f0e[face] * p0e[beside]
        rhs = rhs + across * roll(p, -1, 1) + roll(across * p, 1, 1)
        rxu[e] = rhs + roll(along * p, 1, 0)
        rxd[e] = rhs + along * roll(p, -1, 0)
        dpx[e] = dpe[e] + f0e[face]

    shared = {"t1": f1e, "tot": tote, "p0": p0e, "dp": dpe, "f0": f0e, "f2": f2e, "f1": f1e}
    shared |= {"p0_d2": p0e, "f0_d2": f0e, "f2_d2": f2e, "dp_d2": dpe, "rhs": rhse, "p1_d2": p1}
    shared["dp_x"] = dpx
    up = shared | {"g2": g2u, "g3": g3u, "rhs_x": rxu}
    down = shared | {"g2": g2d, "g3": g3d, "rhs_x": rxd}
    pack_both(x_near, x_cross, late_parts(layers), up, down, rows, gx)


def finish_kernel(*refs, gx):
    sat, hist, volume, storage, source = refs[:5]
    p0e, tote, frace, f0e, f1e, f2e, dpe, rhse, near, cross = refs[5:15]
    hole = refs[19 + len(SEAMS)]
    refs = refs[20 + len(SEAMS) :]
    new_p, residual, new_sat, new_hist, bottom = refs[:5]
    seams = dict(zip(SEAMS, refs[5:]))
    f1, rdiag, pa, pb = refs[5 + len(SEAMS) :]
    bottom[...] = hole[:, 0 : bottom.shape[1]]
    layers, rows, columns = sat.shape
    ext = layers + 2 * H
    unpack_both(near, cross, late_parts(layers), seams, gx)
    sfrac = seams["frac"]
    pa[0] = join(p0e[0], seams["p0"][0])
    pa[ext - 1] = join(p0e[ext - 1], seams["p0"][ext - 1])
    for first, last in ((1, H + 1), (ext - H - 1, ext - 1)):
        seam_faces(first, last, (p0e, tote, f0e, f1e, dpe), seams, f1, rdiag, pa)

    pressures = (pa, pb)
    fields = (rhse, f0e, f2e)
    inner = (H + 1, ext - H - 1)
    everywhere = slice(0, rows + 8)
    for number in range(1, SWEEPS + 1):
        old, new = pressures[(number - 1) % 2], pressures[number % 2]
        ranges = [(number, ext - number, everywhere)]
        if number == 1:
            ranges = [
                (number, inner[0], everywhere),
                (*inner, slice(rows, rows + 8)),
                (inner[1], ext - number, everywhere),
            ]
        for first, last, part in ranges:
            sweep_layers(number, first, last, old, new, fields, seams, f1, rdiag, part)
    field = pressures[SWEEPS % 2]

    def flow(face, p, p_next, f, f_next):
        water = face * (p - p_next)
        return (water, water * jnp.where(water > 0, f, f_next))

    def last_step(l, carry):
        below_w, below_g = carry
        e = l + H
        p = field[e]
        f = join(frace[e], sfrac[e])
        own_p = p[:rows]
        own_f = f[:rows]
        above_w, above_g = flow(f0e[e], own_p, field[e + 1][:rows], own_f, frace[e + 1])
        xw, xg = flow(f1[e], p, roll(p, -1, 0), f, roll(f, -1, 0))
        yw, yg = flow(f2e[e], own_p, roll(own_p, -1, 1), own_f, roll(own_f, -1, 1))
        water = above_w - below_w + (xw - roll(xw, 1, 0))[:rows] + yw - roll(yw, 1, 1)
        out = above_g - below_g + (xg - roll(xg, 1, 0))[:rows] + yg - roll(yg, 1, 1)
        new_p[l] = own_p
        residual[l] = rhse[e] - storage[l] * own_p - water
        src = source[l]
        gas = jnp.maximum(src, 0.0) + jnp.minimum(src, 0.0) * own_f
        s = sat[l] + volume[l] * (gas - out)
        new_sat[l] = s
        new_hist[l] = jnp.maximum(hist[l], s)
        return (above_w, above_g)

    first = flow(f0e[H - 1], field[H - 1][:rows], field[H][:rows], frace[H - 1], frace[H])
    loop(0, layers, last_step, first)


def swap(block, axis, first):
    pairs = [(i, i + 1) for i in range(first, lax.axis_size(axis) - 1, 2)]
    return lax.ppermute(block, axis, pairs + [(b, a) for a, b in pairs])


def pin(*shape, dtype=jnp.float32):
    return pltpu.VMEM(shape, dtype)


VMEM = pl.BlockSpec(memory_space=pltpu.VMEM)
HBM = pl.BlockSpec(memory_space=pltpu.HBM)


def call(kernel, outs, scratch, *args, space=VMEM, sems=0, aliases={}):
    as_struct = lambda s: s if hasattr(s, "dtype") else jax.ShapeDtypeStruct(s, jnp.float32)
    as_scratch = lambda s: pltpu.VMEM(as_struct(s).shape, as_struct(s).dtype)
    return pl.pallas_call(
        kernel,
        out_shape=[as_struct(s) for s in outs],
        in_specs=[space] * len(args),
        out_specs=[VMEM] * len(outs),
        scratch_shapes=[as_scratch(s) for s in scratch]
        + ([pltpu.SemaphoreType.DMA((sems,))] if sems else []),
        input_output_aliases=aliases,
        compiler_params=pltpu.CompilerParams(vmem_limit_bytes=24 * 1024 * 1024),
    )(*(pltpu.with_memory_space_constraint(a, pltpu.HBM) if space is HBM else a for a in args))


def body(
    pressure,
    saturation,
    sat_history,
    storage,
    step_volume,
    transmiss,
    perf_cell,
    perf_index,
    control,
    target,
):
    layers, rows, columns = pressure.shape
    ext = layers + 2 * H
    wells, perfs = perf_cell.shape
    block = (layers, rows, columns)
    pinned = pin(*block)
    ext_block = pin(ext, rows, columns)
    z_layers = sum(count for _, count in Z_PARTS)
    z_near, z_cross = (pin(n, rows, columns) for n in (z_layers, z_layers - 1))
    entries = wells * perfs
    early, late = (pin(tiles(f(layers)), 8, columns) for f in (early_parts, late_parts))
    seams = [pin(ext, 8, columns)] * len(SEAMS)
    *fields, near, cross, part, cell, per_perf, perf_values, own_hot = call(
        functools.partial(prepare_kernel, gz="gz"),
        [ext_block] * 7
        + [z_near, z_cross]
        + [
            pin(2, LANES),
            pin(1, entries, dtype=jnp.int32),
            pin(3, entries),
            pin(2, entries),
            pin(layers * rows, entries, dtype=jnp.bfloat16),
        ],
        [
            block,
            block,
            jax.ShapeDtypeStruct((perfs, wells), jnp.int32),
            (perfs, wells),
            jax.ShapeDtypeStruct((1, wells), jnp.int32),
            (1, wells),
            (perfs, LANES),
        ],
        saturation,
        sat_history,
        pressure,
        storage,
        transmiss,
        perf_cell.T,
        perf_index.T,
        control.reshape(1, wells),
        target.reshape(1, wells),
        space=HBM,
        sems=3 * -(-layers // LOADED) + 8,
    )
    cross = swap(cross, "gz", 1)
    near = swap(near, "gz", 0)
    p0e, tote, frace, stor, t0, t1, t2 = fields
    f0e, f1e, f2e, dpe, base, inverse, early_near, early_cross, part = call(
        functools.partial(faces_kernel, layers=layers, gx="gx"),
        [ext_block] * 6 + [early, early, pin(2, LANES)],
        [],
        *fields,
        part,
    )
    early_cross = swap(early_cross, "gx", 1)
    early_near = swap(early_near, "gx", 0)
    sums = part + near[-1, 0:2, 0:LANES]
    step = 2
    while step < lax.axis_size("gz"):
        pairs = [(i, i ^ step) for i in range(lax.axis_size("gz"))]
        tile = jnp.pad(sums, ((0, 8 - sums.shape[0]), (0, 0)))
        sums = sums + lax.ppermute(tile, "gz", pairs)[: sums.shape[0]]
        step *= 2
    early_near, near = lax.optimization_barrier((early_near, near))
    p0e, tote, frace, stor, f0e, f1e, f2e, dpe, base, inverse, perf_values, hot = call(
        functools.partial(halo_kernel, layers=layers, gx="gx", gz="gz"),
        [ext_block] * 10
        + [pin(2, entries), pin(2 * (H - 1) * rows, entries, dtype=jnp.bfloat16)],
        [],
        p0e,
        tote,
        frace,
        stor,
        f0e,
        f1e,
        f2e,
        dpe,
        base,
        inverse,
        t0,
        cross,
        near,
        cell,
        per_perf,
        perf_values,
        aliases={i: i for i in range(10)},
    )
    rhse, source, late_near, late_cross, hole = call(
        functools.partial(build_kernel, layers=layers, gx="gx"),
        [ext_block, pinned, late, late, pin(1, LANES)],
        [ext_block] * 8,
        p0e,
        stor,
        f0e,
        f1e,
        f2e,
        dpe,
        tote,
        base,
        inverse,
        sums,
        perf_values,
        hot,
        own_hot,
        cell,
        per_perf,
    )
    late_cross = swap(late_cross, "gx", 1)
    late_near = swap(late_near, "gx", 0)
    early_near, early_cross, rhse = lax.optimization_barrier((early_near, early_cross, rhse))
    joined = [pin(ext, rows + 8, columns)] * 4
    filled = call(
        functools.partial(seam_kernel, layers=layers, gx="gx"),
        seams + joined,
        [],
        early_near,
        early_cross,
        p0e,
        tote,
        f0e,
        f1e,
        f2e,
        dpe,
        rhse,
    )
    field, residual, new_sat, new_hist, bottom, *_ = call(
        functools.partial(finish_kernel, gx="gx"),
        [block] * 4 + [(1, wells)] + seams + joined,
        [],
        saturation,
        sat_history,
        step_volume,
        storage,
        source,
        p0e,
        tote,
        frace,
        f0e,
        f1e,
        f2e,
        dpe,
        rhse,
        late_near,
        late_cross,
        *filled,
        hole,
        aliases={15 + i: 5 + i for i in range(len(filled))},
    )
    return (field, residual, new_sat, new_hist, bottom.reshape(wells))


def solution(mesh):
    return jax.shard_map(
        body,
        mesh=mesh,
        in_specs=(
            P("gz", "gx", None),
            P("gz", "gx", None),
            P("gz", "gx", None),
            P("gz", "gx", None),
            P("gz", "gx", None),
            P(None, "gz", "gx", None),
            P("gx", None),
            P("gx", None),
            P("gx"),
            P("gx"),
        ),
        out_specs=(
            P("gz", "gx", None),
            P("gz", "gx", None),
            P("gz", "gx", None),
            P("gz", "gx", None),
            P("gx"),
        ),
        check_vma=False,
    )
```

```python
import functools

import jax
import jax.numpy as jnp
from jax import lax
from jax.experimental import pallas as pl
from jax.experimental.pallas import tpu as pltpu
from jax.sharding import PartitionSpec as P

SWEEPS = 4
H = SWEEPS + 1
LANES = 128
LOADED = 4

Z_PARTS = (
    ("p0", H),
    ("tot", H),
    ("t0", H),
    ("stor", H - 1),
    ("t1", H - 1),
    ("t2", H - 1),
    ("frac", 1),
    ("sums", 1),
)


def early_parts(layers):
    own = (H, layers)
    inner = (H, layers - 1)
    return (
        ("t1", *own),
        ("tot", *own),
        ("p0", *own),
        ("dp", *own),
        ("f0", *inner),
        ("f2", *own),
        ("f1", *own),
        ("frac", *own),
        ("p0_d2", *own),
        ("f0_d2", *inner),
        ("f2_d2", *own),
        ("dp_d2", *own),
    )


def late_parts(layers):
    top = H + layers
    both = lambda name, n: ((name, H - n, n), (name, top, n))
    faces = lambda name, n: ((name, H - n, n), (name, top - 1, n))
    ends = lambda name: ((name, 2, 1), (name, top + 2, 1))
    return (
        ("rhs", 3, layers + 4),
        *ends("rhs_x"),
        ("p1_d2", 3, layers + 4),
        ("g2", 4, layers + 2),
        ("g3", H, layers),
        *both("t1", H - 1),
        *both("tot", H - 1),
        *both("p0", H - 1),
        *both("dp", H - 3),
        *ends("dp_x"),
        *faces("f0", H - 2),
        *both("f2", H - 3),
        *both("f1", H - 3),
        *both("p0_d2", H - 3),
        *faces("f0_d2", 2),
        *both("f2_d2", 1),
        *both("dp_d2", 1),
    )


def tiles(parts):
    return -(-sum(count for _, _, count in parts) // 8)


SEAMS = ("f0", "f1", "f2", "tot", "dp", "p0", "frac", "p1", "rhs2", "rhs3")
PLACES = {
    "t1": ("f1", None, 7),
    "f1": ("f1", 0, 6),
    "tot": ("tot", 0, 7),
    "p0": ("p0", 0, 7),
    "dp": ("dp", 0, 7),
    "dp_d2": ("dp", 1, 6),
    "f0": ("f0", 0, 7),
    "f0_d2": ("f0", 1, 6),
    "f2": ("f2", 0, 7),
    "f2_d2": ("f2", 1, 6),
    "frac": ("frac", 0, 7),
    "p0_d2": ("p0", 1, 6),
    "p1_d2": ("p1", 1, 6),
    "rhs": ("rhs2", 0, 7),
    "rhs_x": ("rhs2", 0, 7),
    "dp_x": ("dp", 0, 7),
    "g2": ("rhs2", 1, 6),
    "g3": ("rhs3", 1, 6),
}


def pack(message, parts, refs, rows):
    at = 0
    for name, first, count in parts:
        for e in range(first, first + count):
            message[at // 8, at % 8 : at % 8 + 1, :] = refs[name][e, rows[name] : rows[name] + 1, :]
            at += 1


def pack_both(near, cross, parts, up, down, rows, gx):
    last = rows - 1
    outer = {name: 0 if PLACES[name][2] == 7 else 1 for name in PLACES}
    up_rows = {name: last - outer[name] for name in PLACES} | {"f1": last - 1}
    down_rows = dict(outer) | {"f1": 0}
    even = lax.axis_index(gx) % 2 == 0

    @pl.when(even)
    def _():
        pack(near, parts, up, up_rows)
        pack(cross, parts, down, down_rows)

    @pl.when(jnp.logical_not(even))
    def _():
        pack(cross, parts, up, up_rows)
        pack(near, parts, down, down_rows)


def unpack(message, parts, seams, side):
    at = 0
    for name, first, count in parts:
        seam, *places = PLACES[name]
        place = places[side]
        for e in range(first, first + count):
            if place is not None:
                seams[seam][e, place : place + 1, :] = message[at // 8, at % 8 : at % 8 + 1, :]
            at += 1


def unpack_both(near, cross, parts, seams, gx):
    even = lax.axis_index(gx) % 2 == 0

    @pl.when(even)
    def _():
        unpack(near, parts, seams, 0)
        unpack(cross, parts, seams, 1)

    @pl.when(jnp.logical_not(even))
    def _():
        unpack(cross, parts, seams, 0)
        unpack(near, parts, seams, 1)


def mobility(sat, history):
    trapped = history / (1.0 + 1.5 * history)
    excess = jnp.maximum(sat - trapped, 0.0)
    free_gas = 0.5 * (excess + jnp.sqrt(excess * excess + excess / 0.375))
    relperm = jnp.where(sat < history, free_gas * free_gas, sat * sat)
    gas = relperm / 0.5
    total = (1.0 - sat) * (1.0 - sat) + gas
    return (total, gas / total)


def roll(x, shift, axis):
    return pltpu.roll(x, shift % x.shape[axis], axis)


def loop(first, last, step, carry):
    count = last - first
    unroll = -(-count // -(-count // 10))
    groups = count // unroll

    def group(g, carry):
        for i in range(unroll):
            carry = step(first + g * unroll + i, carry)
        return carry

    carry = lax.fori_loop(0, groups, group, carry) if groups > 1 else group(0, carry)
    for index in range(first + groups * unroll, last):
        carry = step(index, carry)
    return carry


def split(x):
    high = x.astype(jnp.bfloat16)
    return (high, (x - high.astype(jnp.float32)).astype(jnp.bfloat16))


def at_places(cell, first_layer, layers, rows, columns):
    layer = cell // (rows * columns)
    row = (cell - layer * (rows * columns)) // columns
    place = (layer - first_layer) * rows + row
    return lax.broadcasted_iota(jnp.int32, (layers * rows, cell.shape[1]), 0) == place


def at_columns(cell, columns):
    return lax.broadcasted_iota(jnp.int32, (columns, cell.shape[1]), 0) == cell % columns


def gather(field, at_place, at_column):
    high, low = split(field)
    hot = at_column.astype(jnp.bfloat16)
    by_column = jnp.dot(high, hot, preferred_element_type=jnp.float32) + jnp.dot(
        low, hot, preferred_element_type=jnp.float32
    )
    return jnp.sum(jnp.where(at_place, by_column, 0.0), axis=0, keepdims=True)


def flatten(block, spread):
    perfs, wells = block.shape
    spread[...] = jnp.zeros(spread.shape, jnp.float32)
    spread[:, 0:wells] = block
    wide = spread[...]
    shift = wells
    while shift < LANES:
        wide = wide + roll(wide, shift, 1)
        shift *= 2
    each = LANES // wells
    entry = lax.broadcasted_iota(jnp.int32, (perfs, LANES), 0)
    group = lax.broadcasted_iota(jnp.int32, (perfs, LANES), 1) // wells
    tiles = [
        jnp.sum(jnp.where(entry == first + group, wide, 0.0), axis=0, keepdims=True)
        for first in range(0, perfs, each)
    ]
    return jnp.concatenate(tiles, axis=1)


def prepare_kernel(
    sat,
    hist,
    pressure,
    storage,
    trans,
    cell_in,
    index_in,
    control_in,
    target_in,
    p0e,
    tote,
    frace,
    stor,
    t0,
    t1,
    t2,
    near,
    cross,
    sums,
    cell,
    wells,
    perfs,
    hot,
    sat_v,
    hist_v,
    cell_v,
    index_v,
    control_v,
    target_v,
    spread,
    sems,
    *,
    gz,
):
    layers, rows, columns = pressure.shape
    ext = layers + 2 * H
    own = pl.ds(H, layers)
    parts = [(l, min(LOADED, layers - l)) for l in range(0, layers, LOADED)]
    in_parts = [
        (source.at[pl.ds(l, n)], target.at[pl.ds(offset + l, n)])
        for source, target, offset in ((sat, sat_v, 0), (hist, hist_v, 0), (pressure, p0e, H))
        for l, n in parts
    ]
    small = [(cell_in, cell_v), (index_in, index_v), (control_in, control_v), (target_in, target_v)]
    large = [
        (trans.at[0], t0.at[own]),
        (storage, stor.at[own]),
        (trans.at[1], t1.at[own]),
        (trans.at[2], t2.at[own]),
    ]
    copies = [
        pltpu.make_async_copy(a, b, sems.at[i])
        for i, (a, b) in enumerate(in_parts + small + large)
    ]
    for copy in copies:
        copy.start()

    def layer_step(l, carry):
        t, f = mobility(sat_v[l], hist_v[l])
        tote[l + H] = t
        frace[l + H] = f
        return carry

    for i, (l, n) in enumerate(parts):
        copies[i].wait()
        copies[len(parts) + i].wait()
        loop(l, l + n, layer_step, 0)
    for copy in copies[2 * len(parts) : -len(large)]:
        copy.wait()
    count, group = cell_v.shape
    cell[...] = flatten(cell_v[...].astype(jnp.float32), spread).astype(jnp.int32)
    wells[0:1, :] = flatten(index_v[...], spread)
    wells[1:2, :] = flatten(jnp.broadcast_to(target_v[...], (count, group)), spread)
    wells[2:3, :] = flatten(
        jnp.broadcast_to(control_v[...].astype(jnp.float32), (count, group)), spread
    )
    at_place = at_places(cell[...], lax.axis_index(gz) * layers, layers, rows, columns)
    at_column = at_columns(cell[...], columns)
    hot[...] = at_place.astype(jnp.bfloat16)
    flat = (layers * rows, columns)
    weight = wells[0:1, :] * gather(tote[own].reshape(flat), at_place, at_column)
    cell_p = gather(p0e[own].reshape(flat), at_place, at_column)
    perfs[0:1, :] = weight
    perfs[1:2, :] = cell_p
    for i, value in enumerate((weight * cell_p, weight)):
        part = value[:, 0:LANES]
        for lane in range(LANES, value.shape[1], LANES):
            part = part + value[:, lane : lane + LANES]
        shift = LANES // 2
        while shift >= group:
            part = part + roll(part, shift, 1)
            shift //= 2
        sums[i : i + 1, :] = part
    for copy in copies[-len(large) :]:
        copy.wait()
    even = lax.axis_index(gz) % 2 == 0
    refs = {"p0": p0e, "tot": tote, "t0": t0, "stor": stor, "t1": t1, "t2": t2, "frac": frace}
    for message, is_top in ((near, even), (cross, jnp.logical_not(even))):
        at = 0
        for name, count in Z_PARTS:
            if name == "sums" and message is cross:
                continue
            if name == "sums":
                message[at] = jnp.zeros((rows, columns), jnp.float32)
                message[at, 0:2, 0:LANES] = sums[...]
            else:
                edge = jnp.where(is_top, H + layers - count, H)
                message[pl.ds(at, count)] = refs[name][pl.ds(edge, count)]
            at += count


def masks(rows, columns):
    row = lax.broadcasted_iota(jnp.int32, (rows, columns), 0)
    column = lax.broadcasted_iota(jnp.int32, (rows, columns), 1)
    return (row == rows - 1, column == columns - 1)


def lateral_faces(tot, t1, t2, store, last_row, last_column, top_x):
    along = jnp.where(last_row, 0.0, t1) * 0.5 * (tot + roll(tot, -1, 0))
    across = jnp.where(last_column, 0.0, t2) * 0.5 * (tot + roll(tot, -1, 1))
    part = store + along + roll(along, 1, 0) + across + roll(across, 1, 1)
    return (jnp.where(last_row, jnp.where(top_x, 0.0, t1), along), across, part)


def is_last(axis):
    return lax.axis_index(axis) == lax.axis_size(axis) - 1


def first_sweep(e, p0e, stor, f0e, f1e, f2e, dpe, last_row):
    above = f0e[e]
    below = f0e[e - 1]
    along = jnp.where(last_row, 0.0, f1e[e])
    across = f2e[e]
    diag = dpe[e] + above + below
    p = p0e[e]
    base = stor[e] * p + above * p0e[e + 1] + below * p0e[e - 1]
    base = base + along * roll(p, -1, 0) + roll(along * p, 1, 0)
    base = base + across * roll(p, -1, 1) + roll(across * p, 1, 1)
    return (base, jnp.where(diag > 0.0, 1.0 / diag, 0.0))


def faces_kernel(*refs, layers, gx):
    p0e, tote, frace, stor, t0, t1, t2, part = refs[:8]
    f0e, f1e, f2e, dpe, base, inverse, near, cross, sums = refs[8:]
    _, rows, columns = p0e.shape
    last_row, last_column = masks(rows, columns)
    top_x = is_last(gx)

    def step(e, carry):
        tot = tote[e]
        f0e[e] = t0[e] * 0.5 * (tot + tote[e + 1])
        f1e[e], f2e[e], dpe[e] = lateral_faces(
            tot, t1[e], t2[e], stor[e], last_row, last_column, top_x
        )
        return carry

    loop(H, H + layers, step, 0)
    sums[...] = part[...]
    refs = {"t1": f1e, "tot": tote, "p0": p0e, "dp": dpe, "f0": f0e, "f2": f2e, "f1": f1e}
    refs |= {"frac": frace, "p0_d2": p0e, "f0_d2": f0e, "f2_d2": f2e, "dp_d2": dpe}
    pack_both(near, cross, early_parts(layers), refs, refs, rows, gx)

    def sweep_step(e, carry):
        base[e], inverse[e] = first_sweep(e, p0e, stor, f0e, f1e, f2e, dpe, last_row)
        return carry

    loop(H + 1, H + layers - 1, sweep_step, 0)


def well_holes(sums, wells):
    repeat = lambda x: jnp.concatenate([x] * (wells.shape[1] // LANES), axis=1)
    goal = wells[1:2, :]
    return jnp.where(
        wells[2:3, :] == 0.0, (goal + repeat(sums[0:1, :])) / repeat(sums[1:2, :]), goal
    )


def join(a, b):
    return jnp.concatenate([a, b], axis=0)


def seam_faces(first, last, fields, seams, f1, inverse, p):
    p0e, tote, f0e, f1e, dpe = fields
    rows, columns = p0e.shape[1:]
    row = lax.broadcasted_iota(jnp.int32, (rows + 8, columns), 0)
    edge = (row == rows - 1) | (row == rows + 7)

    def step(e, below):
        tot = join(tote[e], seams["tot"][e])
        mixed = join(f1e[e], seams["f1"][e])
        border = jnp.where(edge, mixed * 0.5 * (tot + roll(tot, -1, 0)), 0.0)
        f1[e] = jnp.where(edge, border, mixed)
        above = join(f0e[e], seams["f0"][e])
        diag = join(dpe[e], seams["dp"][e]) + above + below + border + roll(border, 1, 0)
        inverse[e] = jnp.where(diag > 0.0, 1.0 / diag, 0.0)
        p[e] = join(p0e[e], seams["p0"][e])
        return above

    loop(first, last, step, join(f0e[first - 1], seams["f0"][first - 1]))


def sweep_layers(number, first, last, old, new, fields, seams, f1, inverse, part):
    rhse, f0e, f2e = fields
    rows, columns = rhse.shape[1:]
    row = lax.broadcasted_iota(jnp.int32, (rows + 8, columns), 0)
    beyond = (row == rows + 1) | (row == rows + 6)
    blank = jnp.zeros((rows, columns), jnp.float32)

    def step(e, carry):
        below, p = carry
        above = old[e + 1]
        face = join(f0e[e], seams["f0"][e])
        x = f1[e]
        y = join(f2e[e], seams["f2"][e])
        side = seams["rhs2"][e]
        if number == 3:
            side = jnp.where(beyond[rows:], seams["rhs3"][e], side)
        total = join(rhse[e], side) + below + face * above
        total = total + x * roll(p, -1, 0) + roll(x * p, 1, 0)
        total = total + y * roll(p, -1, 1) + roll(y * p, 1, 1)
        value = total * inverse[e]
        if number == 1:
            value = jnp.where(beyond, join(blank, seams["p1"][e]), value)
        new[e, part] = value[part]
        return (face * p, above)

    start = join(f0e[first - 1], seams["f0"][first - 1]) * old[first - 1]
    loop(first, last, step, (start, old[first]))


def seam_kernel(near, cross, *refs, layers, gx):
    p0e, tote, f0e, f1e, f2e, dpe, rhse = refs[:7]
    refs = refs[7:]
    seams = dict(zip(SEAMS, refs))
    f1, inverse, p, p1 = refs[len(SEAMS) :]
    for seam in seams.values():
        seam[...] = jnp.zeros(seam.shape, jnp.float32)
    unpack_both(near, cross, early_parts(layers), seams, gx)
    inner = (H + 1, H + layers - 1)
    seam_faces(*inner, (p0e, tote, f0e, f1e, dpe), seams, f1, inverse, p)
    for e in (H, H + layers - 1):
        p[e] = join(p0e[e], jnp.zeros_like(seams["p0"][e]))
    own = slice(0, p0e.shape[1])
    sweep_layers(1, *inner, p, p1, (rhse, f0e, f2e), seams, f1, inverse, own)


def halo_kernel(*refs, layers, gx, gz):
    own_t0, cross, near, cell, wells, own_perfs = refs[10:16]
    p0e, tote, frace, stor, f0e, f1e, f2e, dpe, base, inverse, perfs, hot = refs[16:]
    ext, rows, columns = p0e.shape
    even = lax.axis_index(gz) % 2 == 0
    top_z = is_last(gz)
    top_x = is_last(gx)
    last_row, last_column = masks(rows, columns)
    where = {}
    at = 0
    for name, count in Z_PARTS:
        where[name] = (at, count)
        at += count

    def halo(name, e):
        at, count = where[name]
        low = e < H
        at = at + e - (H - count if low else H + layers)
        one, two = (near[at], cross[at])
        return jnp.where(even, two, one) if low else jnp.where(even, one, two)

    for name, target in (("p0", p0e), ("tot", tote), ("frac", frace), ("stor", stor)):
        count = where[name][1]
        for e in (*range(H - count, H), *range(H + layers, H + layers + count)):
            target[e] = halo(name, e)
    f0e[H + layers - 1] = jnp.where(top_z, 0.0, own_t0[H + layers - 1]) * 0.5 * (
        tote[H + layers - 1] + tote[H + layers]
    )
    for e in (*range(0, H), *range(H + layers, ext - 1)):
        f0e[e] = halo("t0", e) * 0.5 * (tote[e] + tote[e + 1])
    for e in (*range(1, H), *range(H + layers, ext - 1)):
        f1e[e], f2e[e], dpe[e] = lateral_faces(
            tote[e], halo("t1", e), halo("t2", e), stor[e], last_row, last_column, top_x
        )
    for e in (*range(1, H + 1), *range(H + layers - 1, ext - 1)):
        base[e], inverse[e] = first_sweep(e, p0e, stor, f0e, f1e, f2e, dpe, last_row)
    width = H - 1
    first = lax.axis_index(gz) * layers
    sides = ((1, first - width), (H + layers, first + layers))
    at_place = [at_places(cell[...], layer, width, rows, columns) for _, layer in sides]
    at_place = jnp.concatenate(at_place, axis=0)
    at_column = at_columns(cell[...], columns)
    hot[...] = at_place.astype(jnp.bfloat16)
    flat = (width * rows, columns)
    both = lambda ref: join(*(ref[e : e + width].reshape(flat) for e, _ in sides))
    weight = wells[0:1, :] * gather(both(tote), at_place, at_column)
    perfs[0:1, :] = own_perfs[0:1, :] + weight
    perfs[1:2, :] = own_perfs[1:2, :] + gather(both(p0e), at_place, at_column)


def build_kernel(*refs, layers, gx):
    p0e, stor, f0e, f1e, f2e, dpe, tote, base, inverse, sums, perfs, hot, own_hot = refs[:13]
    cell, wells, rhse, source, x_near, x_cross, bottom = refs[13:20]
    p1, g2u, g2d, g3u, g3d, rxu, rxd, dpx = refs[20:]
    ext, rows, columns = p0e.shape
    last_row, _ = masks(rows, columns)
    hole = well_holes(sums[...], wells[...])
    bottom[...] = hole[:, 0:LANES]
    rate = perfs[0:1, :] * (hole - perfs[1:2, :])
    pieces = split(jnp.where(at_columns(cell[...], columns), rate, 0.0))

    def scatter(mask):
        spread = [
            lax.dot_general(
                mask, piece, (((1,), (1,)), ((), ())), preferred_element_type=jnp.float32
            )
            for piece in pieces
        ]
        return (spread[0] + spread[1]).reshape(-1, rows, columns)

    width = H - 1
    inside = scatter(own_hot[...])
    outside = scatter(hot[...])
    source[...] = inside
    rhse[H : ext - H] = inside
    rhse[1:H] = outside[:width]
    rhse[ext - H : ext - 1] = outside[width:]

    def first_step(e, carry):
        wells_rate = rhse[e]
        p1[e] = (base[e] + wells_rate) * inverse[e]
        rhse[e] = stor[e] * p0e[e] + wells_rate
        return carry

    loop(1, ext - 1, first_step, 0)

    def second_step(e, carry):
        along = jnp.where(last_row, 0.0, f1e[e])
        across = f2e[e]
        p = p1[e]
        rhs = rhse[e]
        lower = roll(along * p, 1, 0)
        upper = along * roll(p, -1, 0)
        g2u[e] = rhs + lower
        g2d[e] = rhs + upper
        new = rhs + lower + upper + f0e[e] * p1[e + 1] + f0e[e - 1] * p1[e - 1]
        new = new + across * roll(p, -1, 1) + roll(across * p, 1, 1)
        p2 = new * inverse[e]
        g3u[e] = rhs + roll(along * p2, 1, 0)
        g3d[e] = rhs + along * roll(p2, -1, 0)
        return carry

    loop(H - 1, ext - H + 1, second_step, 0)

    for e, beside, face in ((2, 1, 1), (ext - 3, ext - 2, ext - 3)):
        along = jnp.where(last_row, 0.0, f1e[e])
        across = f2e[e]
        p = p0e[e]
        rhs = rhse[e] + f0e[face] * p0e[beside]
        rhs = rhs + across * roll(p, -1, 1) + roll(across * p, 1, 1)
        rxu[e] = rhs + roll(along * p, 1, 0)
        rxd[e] = rhs + along * roll(p, -1, 0)
        dpx[e] = dpe[e] + f0e[face]

    shared = {"t1": f1e, "tot": tote, "p0": p0e, "dp": dpe, "f0": f0e, "f2": f2e, "f1": f1e}
    shared |= {"p0_d2": p0e, "f0_d2": f0e, "f2_d2": f2e, "dp_d2": dpe, "rhs": rhse, "p1_d2": p1}
    shared["dp_x"] = dpx
    up = shared | {"g2": g2u, "g3": g3u, "rhs_x": rxu}
    down = shared | {"g2": g2d, "g3": g3d, "rhs_x": rxd}
    pack_both(x_near, x_cross, late_parts(layers), up, down, rows, gx)


def finish_kernel(*refs, gx):
    sat, hist, volume, storage, source = refs[:5]
    p0e, tote, frace, f0e, f1e, f2e, dpe, rhse, cross, near = refs[5:15]
    hole = refs[19 + len(SEAMS)]
    refs = refs[20 + len(SEAMS) :]
    new_p, residual, new_sat, new_hist, bottom = refs[:5]
    seams = dict(zip(SEAMS, refs[5:]))
    f1, rdiag, pa, pb = refs[5 + len(SEAMS) :]
    bottom[...] = hole[:, 0 : bottom.shape[1]]
    layers, rows, columns = sat.shape
    ext = layers + 2 * H
    unpack_both(near, cross, late_parts(layers), seams, gx)
    sfrac = seams["frac"]
    pa[0] = join(p0e[0], seams["p0"][0])
    pa[ext - 1] = join(p0e[ext - 1], seams["p0"][ext - 1])
    for first, last in ((1, H + 1), (ext - H - 1, ext - 1)):
        seam_faces(first, last, (p0e, tote, f0e, f1e, dpe), seams, f1, rdiag, pa)

    pressures = (pa, pb)
    fields = (rhse, f0e, f2e)
    inner = (H + 1, ext - H - 1)
    everywhere = slice(0, rows + 8)
    for number in range(1, SWEEPS + 1):
        old, new = pressures[(number - 1) % 2], pressures[number % 2]
        ranges = [(number, ext - number, everywhere)]
        if number == 1:
            ranges = [
                (number, inner[0], everywhere),
                (*inner, slice(rows, rows + 8)),
                (inner[1], ext - number, everywhere),
            ]
        for first, last, part in ranges:
            sweep_layers(number, first, last, old, new, fields, seams, f1, rdiag, part)
    field = pressures[SWEEPS % 2]

    def flow(face, p, p_next, f, f_next):
        water = face * (p - p_next)
        return (water, water * jnp.where(water > 0, f, f_next))

    def last_step(l, carry):
        below_w, below_g = carry
        e = l + H
        p = field[e]
        f = join(frace[e], sfrac[e])
        own_p = p[:rows]
        own_f = f[:rows]
        above_w, above_g = flow(f0e[e], own_p, field[e + 1][:rows], own_f, frace[e + 1])
        xw, xg = flow(f1[e], p, roll(p, -1, 0), f, roll(f, -1, 0))
        yw, yg = flow(f2e[e], own_p, roll(own_p, -1, 1), own_f, roll(own_f, -1, 1))
        water = above_w - below_w + (xw - roll(xw, 1, 0))[:rows] + yw - roll(yw, 1, 1)
        out = above_g - below_g + (xg - roll(xg, 1, 0))[:rows] + yg - roll(yg, 1, 1)
        new_p[l] = own_p
        residual[l] = rhse[e] - storage[l] * own_p - water
        src = source[l]
        gas = jnp.maximum(src, 0.0) + jnp.minimum(src, 0.0) * own_f
        s = sat[l] + volume[l] * (gas - out)
        new_sat[l] = s
        new_hist[l] = jnp.maximum(hist[l], s)
        return (above_w, above_g)

    first = flow(f0e[H - 1], field[H - 1][:rows], field[H][:rows], frace[H - 1], frace[H])
    loop(0, layers, last_step, first)


def swap(block, axis, first):
    pairs = [(i, i + 1) for i in range(first, lax.axis_size(axis) - 1, 2)]
    return lax.ppermute(block, axis, pairs + [(b, a) for a, b in pairs])


def pin(*shape, dtype=jnp.float32):
    return pltpu.VMEM(shape, dtype)


VMEM = pl.BlockSpec(memory_space=pltpu.VMEM)
HBM = pl.BlockSpec(memory_space=pltpu.HBM)


def call(kernel, outs, scratch, *args, space=VMEM, sems=0, aliases={}):
    as_struct = lambda s: s if hasattr(s, "dtype") else jax.ShapeDtypeStruct(s, jnp.float32)
    as_scratch = lambda s: pltpu.VMEM(as_struct(s).shape, as_struct(s).dtype)
    return pl.pallas_call(
        kernel,
        out_shape=[as_struct(s) for s in outs],
        in_specs=[space] * len(args),
        out_specs=[VMEM] * len(outs),
        scratch_shapes=[as_scratch(s) for s in scratch]
        + ([pltpu.SemaphoreType.DMA((sems,))] if sems else []),
        input_output_aliases=aliases,
        compiler_params=pltpu.CompilerParams(vmem_limit_bytes=24 * 1024 * 1024),
    )(*(pltpu.with_memory_space_constraint(a, pltpu.HBM) if space is HBM else a for a in args))


def body(
    pressure,
    saturation,
    sat_history,
    storage,
    step_volume,
    transmiss,
    perf_cell,
    perf_index,
    control,
    target,
):
    layers, rows, columns = pressure.shape
    ext = layers + 2 * H
    wells, perfs = perf_cell.shape
    block = (layers, rows, columns)
    pinned = pin(*block)
    ext_block = pin(ext, rows, columns)
    z_layers = sum(count for _, count in Z_PARTS)
    z_near, z_cross = (pin(n, rows, columns) for n in (z_layers, z_layers - 1))
    entries = wells * perfs
    early, late = (pin(tiles(f(layers)), 8, columns) for f in (early_parts, late_parts))
    seams = [pin(ext, 8, columns)] * len(SEAMS)
    *fields, near, cross, part, cell, per_perf, perf_values, own_hot = call(
        functools.partial(prepare_kernel, gz="gz"),
        [ext_block] * 7
        + [z_near, z_cross]
        + [
            pin(2, LANES),
            pin(1, entries, dtype=jnp.int32),
            pin(3, entries),
            pin(2, entries),
            pin(layers * rows, entries, dtype=jnp.bfloat16),
        ],
        [
            block,
            block,
            jax.ShapeDtypeStruct((perfs, wells), jnp.int32),
            (perfs, wells),
            jax.ShapeDtypeStruct((1, wells), jnp.int32),
            (1, wells),
            (perfs, LANES),
        ],
        saturation,
        sat_history,
        pressure,
        storage,
        transmiss,
        perf_cell.T,
        perf_index.T,
        control.reshape(1, wells),
        target.reshape(1, wells),
        space=HBM,
        sems=3 * -(-layers // LOADED) + 8,
    )
    cross = swap(cross, "gz", 1)
    near = swap(near, "gz", 0)
    p0e, tote, frace, stor, t0, t1, t2 = fields
    f0e, f1e, f2e, dpe, base, inverse, early_near, early_cross, part = call(
        functools.partial(faces_kernel, layers=layers, gx="gx"),
        [ext_block] * 6 + [early, early, pin(2, LANES)],
        [],
        *fields,
        part,
    )
    early_cross = swap(early_cross, "gx", 1)
    early_near = swap(early_near, "gx", 0)
    sums = part + near[-1, 0:2, 0:LANES]
    step = 2
    while step < lax.axis_size("gz"):
        pairs = [(i, i ^ step) for i in range(lax.axis_size("gz"))]
        tile = jnp.pad(sums, ((0, 8 - sums.shape[0]), (0, 0)))
        sums = sums + lax.ppermute(tile, "gz", pairs)[: sums.shape[0]]
        step *= 2
    early_near, near = lax.optimization_barrier((early_near, near))
    p0e, tote, frace, stor, f0e, f1e, f2e, dpe, base, inverse, perf_values, hot = call(
        functools.partial(halo_kernel, layers=layers, gx="gx", gz="gz"),
        [ext_block] * 10
        + [pin(2, entries), pin(2 * (H - 1) * rows, entries, dtype=jnp.bfloat16)],
        [],
        p0e,
        tote,
        frace,
        stor,
        f0e,
        f1e,
        f2e,
        dpe,
        base,
        inverse,
        t0,
        cross,
        near,
        cell,
        per_perf,
        perf_values,
        aliases={i: i for i in range(10)},
    )
    rhse, source, late_near, late_cross, hole = call(
        functools.partial(build_kernel, layers=layers, gx="gx"),
        [ext_block, pinned, late, late, pin(1, LANES)],
        [ext_block] * 8,
        p0e,
        stor,
        f0e,
        f1e,
        f2e,
        dpe,
        tote,
        base,
        inverse,
        sums,
        perf_values,
        hot,
        own_hot,
        cell,
        per_perf,
    )
    late_cross = swap(late_cross, "gx", 1)
    late_near = swap(late_near, "gx", 0)
    early_near, early_cross, rhse = lax.optimization_barrier((early_near, early_cross, rhse))
    joined = [pin(ext, rows + 8, columns)] * 4
    filled = call(
        functools.partial(seam_kernel, layers=layers, gx="gx"),
        seams + joined,
        [],
        early_near,
        early_cross,
        p0e,
        tote,
        f0e,
        f1e,
        f2e,
        dpe,
        rhse,
    )
    field, residual, new_sat, new_hist, bottom, *_ = call(
        functools.partial(finish_kernel, gx="gx"),
        [block] * 4 + [(1, wells)] + seams + joined,
        [],
        saturation,
        sat_history,
        step_volume,
        storage,
        source,
        p0e,
        tote,
        frace,
        f0e,
        f1e,
        f2e,
        dpe,
        rhse,
        late_cross,
        late_near,
        *filled,
        hole,
        aliases={15 + i: 5 + i for i in range(len(filled))},
    )
    return (field, residual, new_sat, new_hist, bottom.reshape(wells))


def solution(mesh):
    return jax.shard_map(
        body,
        mesh=mesh,
        in_specs=(
            P("gz", "gx", None),
            P("gz", "gx", None),
            P("gz", "gx", None),
            P("gz", "gx", None),
            P("gz", "gx", None),
            P(None, "gz", "gx", None),
            P("gx", None),
            P("gx", None),
            P("gx"),
            P("gx"),
        ),
        out_specs=(
            P("gz", "gx", None),
            P("gz", "gx", None),
            P("gz", "gx", None),
            P("gz", "gx", None),
            P("gx"),
        ),
        check_vma=False,
    )
```

```python
import functools

import jax
import jax.numpy as jnp
from jax import lax
from jax.experimental import pallas as pl
from jax.experimental.pallas import tpu as pltpu
from jax.sharding import PartitionSpec as P

SWEEPS = 4
H = SWEEPS + 1
LANES = 128
LOADED = 4

Z_PARTS = (
    ("p0", H),
    ("tot", H),
    ("t0", H),
    ("stor", H - 1),
    ("t1", H - 1),
    ("t2", H - 1),
    ("frac", 1),
    ("sums", 1),
)


def early_parts(layers):
    own = (H, layers)
    inner = (H, layers - 1)
    return (
        ("t1", *own),
        ("tot", *own),
        ("p0", *own),
        ("dp", *own),
        ("f0", *inner),
        ("f2", *own),
        ("f1", *own),
        ("frac", *own),
        ("p0_d2", *own),
        ("f0_d2", *inner),
        ("f2_d2", *own),
        ("dp_d2", *own),
    )


def late_parts(layers):
    top = H + layers
    both = lambda name, n: ((name, H - n, n), (name, top, n))
    faces = lambda name, n: ((name, H - n, n), (name, top - 1, n))
    ends = lambda name: ((name, 2, 1), (name, top + 2, 1))
    return (
        ("rhs", 3, layers + 4),
        *ends("rhs_x"),
        ("p1_d2", 3, layers + 4),
        ("g2", 4, layers + 2),
        ("g3", H, layers),
        *both("t1", H - 1),
        *both("tot", H - 1),
        *both("p0", H - 1),
        *both("dp", H - 3),
        *ends("dp_x"),
        *faces("f0", H - 2),
        *both("f2", H - 3),
        *both("f1", H - 3),
        *both("p0_d2", H - 3),
        *faces("f0_d2", 1),
        *both("dp2_x", 1),
    )


def tiles(parts):
    return -(-sum(count for _, _, count in parts) // 8)


SEAMS = ("f0", "f1", "f2", "tot", "dp", "p0", "frac", "p1", "rhs2", "rhs3")
PLACES = {
    "t1": ("f1", None, 7),
    "f1": ("f1", 0, 6),
    "tot": ("tot", 0, 7),
    "p0": ("p0", 0, 7),
    "dp": ("dp", 0, 7),
    "dp_d2": ("dp", 1, 6),
    "f0": ("f0", 0, 7),
    "f0_d2": ("f0", 1, 6),
    "f2": ("f2", 0, 7),
    "f2_d2": ("f2", 1, 6),
    "frac": ("frac", 0, 7),
    "p0_d2": ("p0", 1, 6),
    "p1_d2": ("p1", 1, 6),
    "rhs": ("rhs2", 0, 7),
    "rhs_x": ("rhs2", 0, 7),
    "dp_x": ("dp", 0, 7),
    "dp2_x": ("dp", 1, 6),
    "g2": ("rhs2", 1, 6),
    "g3": ("rhs3", 1, 6),
}


def pack(message, parts, refs, rows):
    at = 0
    for name, first, count in parts:
        for e in range(first, first + count):
            message[at // 8, at % 8 : at % 8 + 1, :] = refs[name][e, rows[name] : rows[name] + 1, :]
            at += 1


def pack_both(near, cross, parts, up, down, rows, gx):
    last = rows - 1
    outer = {name: 0 if PLACES[name][2] == 7 else 1 for name in PLACES}
    up_rows = {name: last - outer[name] for name in PLACES} | {"f1": last - 1}
    down_rows = dict(outer) | {"f1": 0}
    even = lax.axis_index(gx) % 2 == 0

    @pl.when(even)
    def _():
        pack(near, parts, up, up_rows)
        pack(cross, parts, down, down_rows)

    @pl.when(jnp.logical_not(even))
    def _():
        pack(cross, parts, up, up_rows)
        pack(near, parts, down, down_rows)


def unpack(message, parts, seams, side):
    at = 0
    for name, first, count in parts:
        seam, *places = PLACES[name]
        place = places[side]
        for e in range(first, first + count):
            if place is not None:
                seams[seam][e, place : place + 1, :] = message[at // 8, at % 8 : at % 8 + 1, :]
            at += 1


def unpack_both(near, cross, parts, seams, gx):
    even = lax.axis_index(gx) % 2 == 0

    @pl.when(even)
    def _():
        unpack(near, parts, seams, 0)
        unpack(cross, parts, seams, 1)

    @pl.when(jnp.logical_not(even))
    def _():
        unpack(cross, parts, seams, 0)
        unpack(near, parts, seams, 1)


def mobility(sat, history):
    trapped = history / (1.0 + 1.5 * history)
    excess = jnp.maximum(sat - trapped, 0.0)
    free_gas = 0.5 * (excess + jnp.sqrt(excess * excess + excess / 0.375))
    relperm = jnp.where(sat < history, free_gas * free_gas, sat * sat)
    gas = relperm / 0.5
    total = (1.0 - sat) * (1.0 - sat) + gas
    return (total, gas / total)


def roll(x, shift, axis):
    return pltpu.roll(x, shift % x.shape[axis], axis)


def loop(first, last, step, carry):
    count = last - first
    unroll = -(-count // -(-count // 10))
    groups = count // unroll

    def group(g, carry):
        for i in range(unroll):
            carry = step(first + g * unroll + i, carry)
        return carry

    carry = lax.fori_loop(0, groups, group, carry) if groups > 1 else group(0, carry)
    for index in range(first + groups * unroll, last):
        carry = step(index, carry)
    return carry


def split(x):
    high = x.astype(jnp.bfloat16)
    return (high, (x - high.astype(jnp.float32)).astype(jnp.bfloat16))


def at_places(cell, first_layer, layers, rows, columns):
    layer = cell // (rows * columns)
    row = (cell - layer * (rows * columns)) // columns
    place = (layer - first_layer) * rows + row
    return lax.broadcasted_iota(jnp.int32, (layers * rows, cell.shape[1]), 0) == place


def at_columns(cell, columns):
    return lax.broadcasted_iota(jnp.int32, (columns, cell.shape[1]), 0) == cell % columns


def gather(field, at_place, at_column):
    high, low = split(field)
    hot = at_column.astype(jnp.bfloat16)
    by_column = jnp.dot(high, hot, preferred_element_type=jnp.float32) + jnp.dot(
        low, hot, preferred_element_type=jnp.float32
    )
    return jnp.sum(jnp.where(at_place, by_column, 0.0), axis=0, keepdims=True)


def flatten(block, spread):
    perfs, wells = block.shape
    spread[...] = jnp.zeros(spread.shape, jnp.float32)
    spread[:, 0:wells] = block
    wide = spread[...]
    shift = wells
    while shift < LANES:
        wide = wide + roll(wide, shift, 1)
        shift *= 2
    each = LANES // wells
    entry = lax.broadcasted_iota(jnp.int32, (perfs, LANES), 0)
    group = lax.broadcasted_iota(jnp.int32, (perfs, LANES), 1) // wells
    tiles = [
        jnp.sum(jnp.where(entry == first + group, wide, 0.0), axis=0, keepdims=True)
        for first in range(0, perfs, each)
    ]
    return jnp.concatenate(tiles, axis=1)


def prepare_kernel(
    sat,
    hist,
    pressure,
    storage,
    trans,
    cell_in,
    index_in,
    control_in,
    target_in,
    p0e,
    tote,
    frace,
    stor,
    t0,
    t1,
    t2,
    near,
    cross,
    sums,
    cell,
    wells,
    perfs,
    hot,
    sat_v,
    hist_v,
    cell_v,
    index_v,
    control_v,
    target_v,
    spread,
    sems,
    *,
    gz,
):
    layers, rows, columns = pressure.shape
    ext = layers + 2 * H
    own = pl.ds(H, layers)
    parts = [(l, min(LOADED, layers - l)) for l in range(0, layers, LOADED)]
    in_parts = [
        (source.at[pl.ds(l, n)], target.at[pl.ds(offset + l, n)])
        for source, target, offset in ((sat, sat_v, 0), (hist, hist_v, 0), (pressure, p0e, H))
        for l, n in parts
    ]
    small = [(cell_in, cell_v), (index_in, index_v), (control_in, control_v), (target_in, target_v)]
    large = [
        (trans.at[0], t0.at[own]),
        (storage, stor.at[own]),
        (trans.at[1], t1.at[own]),
        (trans.at[2], t2.at[own]),
    ]
    copies = [
        pltpu.make_async_copy(a, b, sems.at[i])
        for i, (a, b) in enumerate(in_parts + small + large)
    ]
    for copy in copies:
        copy.start()

    def layer_step(l, carry):
        t, f = mobility(sat_v[l], hist_v[l])
        tote[l + H] = t
        frace[l + H] = f
        return carry

    for i, (l, n) in enumerate(parts):
        copies[i].wait()
        copies[len(parts) + i].wait()
        loop(l, l + n, layer_step, 0)
    for copy in copies[2 * len(parts) : -len(large)]:
        copy.wait()
    count, group = cell_v.shape
    cell[...] = flatten(cell_v[...].astype(jnp.float32), spread).astype(jnp.int32)
    wells[0:1, :] = flatten(index_v[...], spread)
    wells[1:2, :] = flatten(jnp.broadcast_to(target_v[...], (count, group)), spread)
    wells[2:3, :] = flatten(
        jnp.broadcast_to(control_v[...].astype(jnp.float32), (count, group)), spread
    )
    at_place = at_places(cell[...], lax.axis_index(gz) * layers, layers, rows, columns)
    at_column = at_columns(cell[...], columns)
    hot[...] = at_place.astype(jnp.bfloat16)
    flat = (layers * rows, columns)
    weight = wells[0:1, :] * gather(tote[own].reshape(flat), at_place, at_column)
    cell_p = gather(p0e[own].reshape(flat), at_place, at_column)
    perfs[0:1, :] = weight
    perfs[1:2, :] = cell_p
    for i, value in enumerate((weight * cell_p, weight)):
        part = value[:, 0:LANES]
        for lane in range(LANES, value.shape[1], LANES):
            part = part + value[:, lane : lane + LANES]
        shift = LANES // 2
        while shift >= group:
            part = part + roll(part, shift, 1)
            shift //= 2
        sums[i : i + 1, :] = part
    for copy in copies[-len(large) :]:
        copy.wait()
    even = lax.axis_index(gz) % 2 == 0
    refs = {"p0": p0e, "tot": tote, "t0": t0, "stor": stor, "t1": t1, "t2": t2, "frac": frace}
    for message, is_top in ((near, even), (cross, jnp.logical_not(even))):
        at = 0
        for name, count in Z_PARTS:
            if name == "sums" and message is cross:
                continue
            if name == "sums":
                message[at] = jnp.zeros((rows, columns), jnp.float32)
                message[at, 0:2, 0:LANES] = sums[...]
            else:
                edge = jnp.where(is_top, H + layers - count, H)
                message[pl.ds(at, count)] = refs[name][pl.ds(edge, count)]
            at += count


def masks(rows, columns):
    row = lax.broadcasted_iota(jnp.int32, (rows, columns), 0)
    column = lax.broadcasted_iota(jnp.int32, (rows, columns), 1)
    return (row == rows - 1, column == columns - 1)


def lateral_faces(tot, t1, t2, store, last_row, last_column, top_x):
    along = jnp.where(last_row, 0.0, t1) * 0.5 * (tot + roll(tot, -1, 0))
    across = jnp.where(last_column, 0.0, t2) * 0.5 * (tot + roll(tot, -1, 1))
    part = store + along + roll(along, 1, 0) + across + roll(across, 1, 1)
    return (jnp.where(last_row, jnp.where(top_x, 0.0, t1), along), across, part)


def is_last(axis):
    return lax.axis_index(axis) == lax.axis_size(axis) - 1


def first_sweep(e, p0e, stor, f0e, f1e, f2e, dpe, last_row):
    above = f0e[e]
    below = f0e[e - 1]
    along = jnp.where(last_row, 0.0, f1e[e])
    across = f2e[e]
    diag = dpe[e] + above + below
    p = p0e[e]
    base = stor[e] * p + above * p0e[e + 1] + below * p0e[e - 1]
    base = base + along * roll(p, -1, 0) + roll(along * p, 1, 0)
    base = base + across * roll(p, -1, 1) + roll(across * p, 1, 1)
    return (base, jnp.where(diag > 0.0, 1.0 / diag, 0.0))


def faces_kernel(*refs, layers, gx):
    p0e, tote, frace, stor, t0, t1, t2, part = refs[:8]
    f0e, f1e, f2e, dpe, base, inverse, near, cross, sums = refs[8:]
    _, rows, columns = p0e.shape
    last_row, last_column = masks(rows, columns)
    top_x = is_last(gx)

    def step(e, carry):
        tot = tote[e]
        f0e[e] = t0[e] * 0.5 * (tot + tote[e + 1])
        f1e[e], f2e[e], dpe[e] = lateral_faces(
            tot, t1[e], t2[e], stor[e], last_row, last_column, top_x
        )
        return carry

    loop(H, H + layers, step, 0)
    sums[...] = part[...]
    refs = {"t1": f1e, "tot": tote, "p0": p0e, "dp": dpe, "f0": f0e, "f2": f2e, "f1": f1e}
    refs |= {"frac": frace, "p0_d2": p0e, "f0_d2": f0e, "f2_d2": f2e, "dp_d2": dpe}
    pack_both(near, cross, early_parts(layers), refs, refs, rows, gx)

    def sweep_step(e, carry):
        base[e], inverse[e] = first_sweep(e, p0e, stor, f0e, f1e, f2e, dpe, last_row)
        return carry

    loop(H + 1, H + layers - 1, sweep_step, 0)


def well_holes(sums, wells):
    repeat = lambda x: jnp.concatenate([x] * (wells.shape[1] // LANES), axis=1)
    goal = wells[1:2, :]
    return jnp.where(
        wells[2:3, :] == 0.0, (goal + repeat(sums[0:1, :])) / repeat(sums[1:2, :]), goal
    )


def join(a, b):
    return jnp.concatenate([a, b], axis=0)


def seam_faces(first, last, fields, seams, f1, inverse, p):
    p0e, tote, f0e, f1e, dpe = fields
    rows, columns = p0e.shape[1:]
    row = lax.broadcasted_iota(jnp.int32, (rows + 8, columns), 0)
    edge = (row == rows - 1) | (row == rows + 7)

    def step(e, below):
        tot = join(tote[e], seams["tot"][e])
        mixed = join(f1e[e], seams["f1"][e])
        border = jnp.where(edge, mixed * 0.5 * (tot + roll(tot, -1, 0)), 0.0)
        f1[e] = jnp.where(edge, border, mixed)
        above = join(f0e[e], seams["f0"][e])
        diag = join(dpe[e], seams["dp"][e]) + above + below + border + roll(border, 1, 0)
        inverse[e] = jnp.where(diag > 0.0, 1.0 / diag, 0.0)
        p[e] = join(p0e[e], seams["p0"][e])
        return above

    loop(first, last, step, join(f0e[first - 1], seams["f0"][first - 1]))


def sweep_layers(number, first, last, old, new, fields, seams, f1, inverse, part):
    rhse, f0e, f2e = fields
    rows, columns = rhse.shape[1:]
    row = lax.broadcasted_iota(jnp.int32, (rows + 8, columns), 0)
    beyond = (row == rows + 1) | (row == rows + 6)
    blank = jnp.zeros((rows, columns), jnp.float32)

    def step(e, carry):
        below, p = carry
        above = old[e + 1]
        face = join(f0e[e], seams["f0"][e])
        x = f1[e]
        y = join(f2e[e], seams["f2"][e])
        side = seams["rhs2"][e]
        if number == 3:
            side = jnp.where(beyond[rows:], seams["rhs3"][e], side)
        total = join(rhse[e], side) + below + face * above
        total = total + x * roll(p, -1, 0) + roll(x * p, 1, 0)
        total = total + y * roll(p, -1, 1) + roll(y * p, 1, 1)
        value = total * inverse[e]
        if number == 1:
            value = jnp.where(beyond, join(blank, seams["p1"][e]), value)
        new[e, part] = value[part]
        return (face * p, above)

    start = join(f0e[first - 1], seams["f0"][first - 1]) * old[first - 1]
    loop(first, last, step, (start, old[first]))


def seam_kernel(near, cross, *refs, layers, gx):
    p0e, tote, f0e, f1e, f2e, dpe, rhse = refs[:7]
    refs = refs[7:]
    seams = dict(zip(SEAMS, refs))
    f1, inverse, p, p1 = refs[len(SEAMS) :]
    for seam in seams.values():
        seam[...] = jnp.zeros(seam.shape, jnp.float32)
    unpack_both(near, cross, early_parts(layers), seams, gx)
    inner = (H + 1, H + layers - 1)
    seam_faces(*inner, (p0e, tote, f0e, f1e, dpe), seams, f1, inverse, p)
    for e in (H, H + layers - 1):
        p[e] = join(p0e[e], jnp.zeros_like(seams["p0"][e]))
    own = slice(0, p0e.shape[1])
    sweep_layers(1, *inner, p, p1, (rhse, f0e, f2e), seams, f1, inverse, own)


def halo_kernel(*refs, layers, gx, gz):
    own_t0, cross, near, cell, wells, own_perfs = refs[10:16]
    p0e, tote, frace, stor, f0e, f1e, f2e, dpe, base, inverse, perfs, hot = refs[16:]
    ext, rows, columns = p0e.shape
    even = lax.axis_index(gz) % 2 == 0
    top_z = is_last(gz)
    top_x = is_last(gx)
    last_row, last_column = masks(rows, columns)
    where = {}
    at = 0
    for name, count in Z_PARTS:
        where[name] = (at, count)
        at += count

    def halo(name, e):
        at, count = where[name]
        low = e < H
        at = at + e - (H - count if low else H + layers)
        one, two = (near[at], cross[at])
        return jnp.where(even, two, one) if low else jnp.where(even, one, two)

    for name, target in (("p0", p0e), ("tot", tote), ("frac", frace), ("stor", stor)):
        count = where[name][1]
        for e in (*range(H - count, H), *range(H + layers, H + layers + count)):
            target[e] = halo(name, e)
    f0e[H + layers - 1] = jnp.where(top_z, 0.0, own_t0[H + layers - 1]) * 0.5 * (
        tote[H + layers - 1] + tote[H + layers]
    )
    for e in (*range(0, H), *range(H + layers, ext - 1)):
        f0e[e] = halo("t0", e) * 0.5 * (tote[e] + tote[e + 1])
    for e in (*range(1, H), *range(H + layers, ext - 1)):
        f1e[e], f2e[e], dpe[e] = lateral_faces(
            tote[e], halo("t1", e), halo("t2", e), stor[e], last_row, last_column, top_x
        )
    for e in (*range(1, H + 1), *range(H + layers - 1, ext - 1)):
        base[e], inverse[e] = first_sweep(e, p0e, stor, f0e, f1e, f2e, dpe, last_row)
    width = H - 1
    first = lax.axis_index(gz) * layers
    sides = ((1, first - width), (H + layers, first + layers))
    at_place = [at_places(cell[...], layer, width, rows, columns) for _, layer in sides]
    at_place = jnp.concatenate(at_place, axis=0)
    at_column = at_columns(cell[...], columns)
    hot[...] = at_place.astype(jnp.bfloat16)
    flat = (width * rows, columns)
    both = lambda ref: join(*(ref[e : e + width].reshape(flat) for e, _ in sides))
    weight = wells[0:1, :] * gather(both(tote), at_place, at_column)
    perfs[0:1, :] = own_perfs[0:1, :] + weight
    perfs[1:2, :] = own_perfs[1:2, :] + gather(both(p0e), at_place, at_column)


def build_kernel(*refs, layers, gx):
    p0e, stor, f0e, f1e, f2e, dpe, tote, base, inverse, sums, perfs, hot, own_hot = refs[:13]
    cell, wells, rhse, source, x_near, x_cross, bottom = refs[13:20]
    p1, g2u, g2d, g3u, g3d, rxu, rxd, dpx = refs[20:]
    ext, rows, columns = p0e.shape
    last_row, _ = masks(rows, columns)
    hole = well_holes(sums[...], wells[...])
    bottom[...] = hole[:, 0:LANES]
    rate = perfs[0:1, :] * (hole - perfs[1:2, :])
    pieces = split(jnp.where(at_columns(cell[...], columns), rate, 0.0))

    def scatter(mask):
        spread = [
            lax.dot_general(
                mask, piece, (((1,), (1,)), ((), ())), preferred_element_type=jnp.float32
            )
            for piece in pieces
        ]
        return (spread[0] + spread[1]).reshape(-1, rows, columns)

    width = H - 1
    inside = scatter(own_hot[...])
    outside = scatter(hot[...])
    source[...] = inside
    rhse[H : ext - H] = inside
    rhse[1:H] = outside[:width]
    rhse[ext - H : ext - 1] = outside[width:]

    def first_step(e, carry):
        wells_rate = rhse[e]
        p1[e] = (base[e] + wells_rate) * inverse[e]
        rhse[e] = stor[e] * p0e[e] + wells_rate
        return carry

    loop(1, ext - 1, first_step, 0)

    def second_step(e, carry):
        along = jnp.where(last_row, 0.0, f1e[e])
        across = f2e[e]
        p = p1[e]
        rhs = rhse[e]
        lower = roll(along * p, 1, 0)
        upper = along * roll(p, -1, 0)
        g2u[e] = rhs + lower
        g2d[e] = rhs + upper
        new = rhs + lower + upper + f0e[e] * p1[e + 1] + f0e[e - 1] * p1[e - 1]
        new = new + across * roll(p, -1, 1) + roll(across * p, 1, 1)
        p2 = new * inverse[e]
        g3u[e] = rhs + roll(along * p2, 1, 0)
        g3d[e] = rhs + along * roll(p2, -1, 0)
        return carry

    loop(H - 1, ext - H + 1, second_step, 0)

    for e, beside, face in ((2, 1, 1), (ext - 3, ext - 2, ext - 3)):
        along = jnp.where(last_row, 0.0, f1e[e])
        across = f2e[e]
        p = p0e[e]
        rhs = rhse[e] + f0e[face] * p0e[beside]
        rhs = rhs + across * roll(p, -1, 1) + roll(across * p, 1, 1)
        rxu[e] = rhs + roll(along * p, 1, 0)
        rxd[e] = rhs + along * roll(p, -1, 0)
        dpx[e] = dpe[e] + f0e[face]

    shared = {"t1": f1e, "tot": tote, "p0": p0e, "dp": dpe, "f0": f0e, "f2": f2e, "f1": f1e}
    shared |= {"p0_d2": p0e, "f0_d2": f0e, "f2_d2": f2e, "dp_d2": dpe, "rhs": rhse, "p1_d2": p1}
    for e, beside, face in ((H - 1, H - 2, H - 2), (ext - H, ext - H + 1, ext - H)):
        across = f2e[e]
        p = p1[e]
        beyond = f0e[face] * p1[beside] + across * roll(p, -1, 1) + roll(across * p, 1, 1)
        g2u[e] = g2u[e] + beyond
        g2d[e] = g2d[e] + beyond
        dpx[e] = dpe[e] + f0e[face]
    shared["dp_x"] = shared["dp2_x"] = dpx
    up = shared | {"g2": g2u, "g3": g3u, "rhs_x": rxu}
    down = shared | {"g2": g2d, "g3": g3d, "rhs_x": rxd}
    pack_both(x_near, x_cross, late_parts(layers), up, down, rows, gx)


def finish_kernel(*refs, gx):
    sat, hist, volume, storage, source = refs[:5]
    p0e, tote, frace, f0e, f1e, f2e, dpe, rhse, near, cross = refs[5:15]
    hole = refs[19 + len(SEAMS)]
    refs = refs[20 + len(SEAMS) :]
    new_p, residual, new_sat, new_hist, bottom = refs[:5]
    seams = dict(zip(SEAMS, refs[5:]))
    f1, rdiag, pa, pb = refs[5 + len(SEAMS) :]
    bottom[...] = hole[:, 0 : bottom.shape[1]]
    layers, rows, columns = sat.shape
    ext = layers + 2 * H
    unpack_both(near, cross, late_parts(layers), seams, gx)
    sfrac = seams["frac"]
    pa[0] = join(p0e[0], seams["p0"][0])
    pa[ext - 1] = join(p0e[ext - 1], seams["p0"][ext - 1])
    for first, last in ((1, H + 1), (ext - H - 1, ext - 1)):
        seam_faces(first, last, (p0e, tote, f0e, f1e, dpe), seams, f1, rdiag, pa)

    pressures = (pa, pb)
    fields = (rhse, f0e, f2e)
    inner = (H + 1, ext - H - 1)
    everywhere = slice(0, rows + 8)
    for number in range(1, SWEEPS + 1):
        old, new = pressures[(number - 1) % 2], pressures[number % 2]
        ranges = [(number, ext - number, everywhere)]
        if number == 1:
            ranges = [
                (number, inner[0], everywhere),
                (*inner, slice(rows, rows + 8)),
                (inner[1], ext - number, everywhere),
            ]
        for first, last, part in ranges:
            sweep_layers(number, first, last, old, new, fields, seams, f1, rdiag, part)
    field = pressures[SWEEPS % 2]

    def flow(face, p, p_next, f, f_next):
        water = face * (p - p_next)
        return (water, water * jnp.where(water > 0, f, f_next))

    def last_step(l, carry):
        below_w, below_g = carry
        e = l + H
        p = field[e]
        f = join(frace[e], sfrac[e])
        own_p = p[:rows]
        own_f = f[:rows]
        above_w, above_g = flow(f0e[e], own_p, field[e + 1][:rows], own_f, frace[e + 1])
        xw, xg = flow(f1[e], p, roll(p, -1, 0), f, roll(f, -1, 0))
        yw, yg = flow(f2e[e], own_p, roll(own_p, -1, 1), own_f, roll(own_f, -1, 1))
        water = above_w - below_w + (xw - roll(xw, 1, 0))[:rows] + yw - roll(yw, 1, 1)
        out = above_g - below_g + (xg - roll(xg, 1, 0))[:rows] + yg - roll(yg, 1, 1)
        new_p[l] = own_p
        residual[l] = rhse[e] - storage[l] * own_p - water
        src = source[l]
        gas = jnp.maximum(src, 0.0) + jnp.minimum(src, 0.0) * own_f
        s = sat[l] + volume[l] * (gas - out)
        new_sat[l] = s
        new_hist[l] = jnp.maximum(hist[l], s)
        return (above_w, above_g)

    first = flow(f0e[H - 1], field[H - 1][:rows], field[H][:rows], frace[H - 1], frace[H])
    loop(0, layers, last_step, first)


def swap(block, axis, first):
    pairs = [(i, i + 1) for i in range(first, lax.axis_size(axis) - 1, 2)]
    return lax.ppermute(block, axis, pairs + [(b, a) for a, b in pairs])


def pin(*shape, dtype=jnp.float32):
    return pltpu.VMEM(shape, dtype)


VMEM = pl.BlockSpec(memory_space=pltpu.VMEM)
HBM = pl.BlockSpec(memory_space=pltpu.HBM)


def call(kernel, outs, scratch, *args, space=VMEM, sems=0, aliases={}):
    as_struct = lambda s: s if hasattr(s, "dtype") else jax.ShapeDtypeStruct(s, jnp.float32)
    as_scratch = lambda s: pltpu.VMEM(as_struct(s).shape, as_struct(s).dtype)
    return pl.pallas_call(
        kernel,
        out_shape=[as_struct(s) for s in outs],
        in_specs=[space] * len(args),
        out_specs=[VMEM] * len(outs),
        scratch_shapes=[as_scratch(s) for s in scratch]
        + ([pltpu.SemaphoreType.DMA((sems,))] if sems else []),
        input_output_aliases=aliases,
        compiler_params=pltpu.CompilerParams(vmem_limit_bytes=24 * 1024 * 1024),
    )(*(pltpu.with_memory_space_constraint(a, pltpu.HBM) if space is HBM else a for a in args))


def body(
    pressure,
    saturation,
    sat_history,
    storage,
    step_volume,
    transmiss,
    perf_cell,
    perf_index,
    control,
    target,
):
    layers, rows, columns = pressure.shape
    ext = layers + 2 * H
    wells, perfs = perf_cell.shape
    block = (layers, rows, columns)
    pinned = pin(*block)
    ext_block = pin(ext, rows, columns)
    z_layers = sum(count for _, count in Z_PARTS)
    z_near, z_cross = (pin(n, rows, columns) for n in (z_layers, z_layers - 1))
    entries = wells * perfs
    early, late = (pin(tiles(f(layers)), 8, columns) for f in (early_parts, late_parts))
    seams = [pin(ext, 8, columns)] * len(SEAMS)
    *fields, near, cross, part, cell, per_perf, perf_values, own_hot = call(
        functools.partial(prepare_kernel, gz="gz"),
        [ext_block] * 7
        + [z_near, z_cross]
        + [
            pin(2, LANES),
            pin(1, entries, dtype=jnp.int32),
            pin(3, entries),
            pin(2, entries),
            pin(layers * rows, entries, dtype=jnp.bfloat16),
        ],
        [
            block,
            block,
            jax.ShapeDtypeStruct((perfs, wells), jnp.int32),
            (perfs, wells),
            jax.ShapeDtypeStruct((1, wells), jnp.int32),
            (1, wells),
            (perfs, LANES),
        ],
        saturation,
        sat_history,
        pressure,
        storage,
        transmiss,
        perf_cell.T,
        perf_index.T,
        control.reshape(1, wells),
        target.reshape(1, wells),
        space=HBM,
        sems=3 * -(-layers // LOADED) + 8,
    )
    cross = swap(cross, "gz", 1)
    near = swap(near, "gz", 0)
    p0e, tote, frace, stor, t0, t1, t2 = fields
    f0e, f1e, f2e, dpe, base, inverse, early_near, early_cross, part = call(
        functools.partial(faces_kernel, layers=layers, gx="gx"),
        [ext_block] * 6 + [early, early, pin(2, LANES)],
        [],
        *fields,
        part,
    )
    early_cross = swap(early_cross, "gx", 1)
    early_near = swap(early_near, "gx", 0)
    sums = part + near[-1, 0:2, 0:LANES]
    step = 2
    while step < lax.axis_size("gz"):
        pairs = [(i, i ^ step) for i in range(lax.axis_size("gz"))]
        tile = jnp.pad(sums, ((0, 8 - sums.shape[0]), (0, 0)))
        sums = sums + lax.ppermute(tile, "gz", pairs)[: sums.shape[0]]
        step *= 2
    early_near, near = lax.optimization_barrier((early_near, near))
    p0e, tote, frace, stor, f0e, f1e, f2e, dpe, base, inverse, perf_values, hot = call(
        functools.partial(halo_kernel, layers=layers, gx="gx", gz="gz"),
        [ext_block] * 10
        + [pin(2, entries), pin(2 * (H - 1) * rows, entries, dtype=jnp.bfloat16)],
        [],
        p0e,
        tote,
        frace,
        stor,
        f0e,
        f1e,
        f2e,
        dpe,
        base,
        inverse,
        t0,
        cross,
        near,
        cell,
        per_perf,
        perf_values,
        aliases={i: i for i in range(10)},
    )
    rhse, source, late_near, late_cross, hole = call(
        functools.partial(build_kernel, layers=layers, gx="gx"),
        [ext_block, pinned, late, late, pin(1, LANES)],
        [ext_block] * 8,
        p0e,
        stor,
        f0e,
        f1e,
        f2e,
        dpe,
        tote,
        base,
        inverse,
        sums,
        perf_values,
        hot,
        own_hot,
        cell,
        per_perf,
    )
    late_cross = swap(late_cross, "gx", 1)
    late_near = swap(late_near, "gx", 0)
    early_near, early_cross, rhse = lax.optimization_barrier((early_near, early_cross, rhse))
    joined = [pin(ext, rows + 8, columns)] * 4
    filled = call(
        functools.partial(seam_kernel, layers=layers, gx="gx"),
        seams + joined,
        [],
        early_near,
        early_cross,
        p0e,
        tote,
        f0e,
        f1e,
        f2e,
        dpe,
        rhse,
    )
    field, residual, new_sat, new_hist, bottom, *_ = call(
        functools.partial(finish_kernel, gx="gx"),
        [block] * 4 + [(1, wells)] + seams + joined,
        [],
        saturation,
        sat_history,
        step_volume,
        storage,
        source,
        p0e,
        tote,
        frace,
        f0e,
        f1e,
        f2e,
        dpe,
        rhse,
        late_near,
        late_cross,
        *filled,
        hole,
        aliases={15 + i: 5 + i for i in range(len(filled))},
    )
    return (field, residual, new_sat, new_hist, bottom.reshape(wells))


def solution(mesh):
    return jax.shard_map(
        body,
        mesh=mesh,
        in_specs=(
            P("gz", "gx", None),
            P("gz", "gx", None),
            P("gz", "gx", None),
            P("gz", "gx", None),
            P("gz", "gx", None),
            P(None, "gz", "gx", None),
            P("gx", None),
            P("gx", None),
            P("gx"),
            P("gx"),
        ),
        out_specs=(
            P("gz", "gx", None),
            P("gz", "gx", None),
            P("gz", "gx", None),
            P("gz", "gx", None),
            P("gx"),
        ),
        check_vma=False,
    )
```

```python
import functools

import jax
import jax.numpy as jnp
from jax import lax
from jax.experimental import pallas as pl
from jax.experimental.pallas import tpu as pltpu
from jax.sharding import PartitionSpec as P

SWEEPS = 4
H = SWEEPS + 1
LANES = 128
LOADED = 4

Z_PARTS = (
    ("p0", H),
    ("tot", H),
    ("t0", H),
    ("stor", H - 1),
    ("t1", H - 1),
    ("t2", H - 1),
    ("frac", 1),
)


def early_parts(layers):
    own = (H, layers)
    inner = (H, layers - 1)
    return (
        ("t1", *own),
        ("tot", *own),
        ("p0", *own),
        ("dp", *own),
        ("f0", *inner),
        ("f2", *own),
        ("f1", *own),
        ("frac", *own),
        ("p0_d2", *own),
        ("f0_d2", *inner),
        ("f2_d2", *own),
        ("dp_d2", *own),
    )


def late_parts(layers):
    top = H + layers
    both = lambda name, n: ((name, H - n, n), (name, top, n))
    faces = lambda name, n: ((name, H - n, n), (name, top - 1, n))
    ends = lambda name: ((name, 2, 1), (name, top + 2, 1))
    return (
        ("rhs", 3, layers + 4),
        *ends("rhs_x"),
        ("p1_d2", 3, layers + 4),
        ("g2", 4, layers + 2),
        ("g3", H, layers),
        *both("t1", H - 1),
        *both("tot", H - 1),
        *both("p0", H - 1),
        *both("dp", H - 3),
        *ends("dp_x"),
        *faces("f0", H - 2),
        *both("f2", H - 3),
        *both("f1", H - 3),
        *both("p0_d2", H - 3),
        *faces("f0_d2", 1),
        *both("dp2_x", 1),
    )


def tiles(parts):
    return -(-sum(count for _, _, count in parts) // 8)


SEAMS = ("f0", "f1", "f2", "tot", "dp", "p0", "frac", "p1", "rhs2", "rhs3")
PLACES = {
    "t1": ("f1", None, 7),
    "f1": ("f1", 0, 6),
    "tot": ("tot", 0, 7),
    "p0": ("p0", 0, 7),
    "dp": ("dp", 0, 7),
    "dp_d2": ("dp", 1, 6),
    "f0": ("f0", 0, 7),
    "f0_d2": ("f0", 1, 6),
    "f2": ("f2", 0, 7),
    "f2_d2": ("f2", 1, 6),
    "frac": ("frac", 0, 7),
    "p0_d2": ("p0", 1, 6),
    "p1_d2": ("p1", 1, 6),
    "rhs": ("rhs2", 0, 7),
    "rhs_x": ("rhs2", 0, 7),
    "dp_x": ("dp", 0, 7),
    "dp2_x": ("dp", 1, 6),
    "g2": ("rhs2", 1, 6),
    "g3": ("rhs3", 1, 6),
}


def pack(message, parts, refs, rows):
    at = 0
    for name, first, count in parts:
        for e in range(first, first + count):
            message[at // 8, at % 8 : at % 8 + 1, :] = refs[name][e, rows[name] : rows[name] + 1, :]
            at += 1


def pack_both(near, cross, parts, up, down, rows, gx):
    last = rows - 1
    outer = {name: 0 if PLACES[name][2] == 7 else 1 for name in PLACES}
    up_rows = {name: last - outer[name] for name in PLACES} | {"f1": last - 1}
    down_rows = dict(outer) | {"f1": 0}
    even = lax.axis_index(gx) % 2 == 0

    @pl.when(even)
    def _():
        pack(near, parts, up, up_rows)
        pack(cross, parts, down, down_rows)

    @pl.when(jnp.logical_not(even))
    def _():
        pack(cross, parts, up, up_rows)
        pack(near, parts, down, down_rows)


def unpack(message, parts, seams, side):
    at = 0
    for name, first, count in parts:
        seam, *places = PLACES[name]
        place = places[side]
        for e in range(first, first + count):
            if place is not None:
                seams[seam][e, place : place + 1, :] = message[at // 8, at % 8 : at % 8 + 1, :]
            at += 1


def unpack_both(near, cross, parts, seams, gx):
    even = lax.axis_index(gx) % 2 == 0

    @pl.when(even)
    def _():
        unpack(near, parts, seams, 0)
        unpack(cross, parts, seams, 1)

    @pl.when(jnp.logical_not(even))
    def _():
        unpack(cross, parts, seams, 0)
        unpack(near, parts, seams, 1)


def mobility(sat, history):
    trapped = history / (1.0 + 1.5 * history)
    excess = jnp.maximum(sat - trapped, 0.0)
    free_gas = 0.5 * (excess + jnp.sqrt(excess * excess + excess / 0.375))
    relperm = jnp.where(sat < history, free_gas * free_gas, sat * sat)
    gas = relperm / 0.5
    total = (1.0 - sat) * (1.0 - sat) + gas
    return (total, gas / total)


def roll(x, shift, axis):
    return pltpu.roll(x, shift % x.shape[axis], axis)


def loop(first, last, step, carry):
    count = last - first
    unroll = -(-count // -(-count // 10))
    groups = count // unroll

    def group(g, carry):
        for i in range(unroll):
            carry = step(first + g * unroll + i, carry)
        return carry

    carry = lax.fori_loop(0, groups, group, carry) if groups > 1 else group(0, carry)
    for index in range(first + groups * unroll, last):
        carry = step(index, carry)
    return carry


def split(x):
    high = x.astype(jnp.bfloat16)
    return (high, (x - high.astype(jnp.float32)).astype(jnp.bfloat16))


def at_places(cell, first_layer, layers, rows, columns):
    layer = cell // (rows * columns)
    row = (cell - layer * (rows * columns)) // columns
    place = (layer - first_layer) * rows + row
    return lax.broadcasted_iota(jnp.int32, (layers * rows, cell.shape[1]), 0) == place


def at_columns(cell, columns):
    return lax.broadcasted_iota(jnp.int32, (columns, cell.shape[1]), 0) == cell % columns


def gather(field, at_place, at_column):
    high, low = split(field)
    hot = at_column.astype(jnp.bfloat16)
    by_column = jnp.dot(high, hot, preferred_element_type=jnp.float32) + jnp.dot(
        low, hot, preferred_element_type=jnp.float32
    )
    return jnp.sum(jnp.where(at_place, by_column, 0.0), axis=0, keepdims=True)


def flatten(block, spread):
    perfs, wells = block.shape
    spread[...] = jnp.zeros(spread.shape, jnp.float32)
    spread[:, 0:wells] = block
    wide = spread[...]
    shift = wells
    while shift < LANES:
        wide = wide + roll(wide, shift, 1)
        shift *= 2
    each = LANES // wells
    entry = lax.broadcasted_iota(jnp.int32, (perfs, LANES), 0)
    group = lax.broadcasted_iota(jnp.int32, (perfs, LANES), 1) // wells
    tiles = [
        jnp.sum(jnp.where(entry == first + group, wide, 0.0), axis=0, keepdims=True)
        for first in range(0, perfs, each)
    ]
    return jnp.concatenate(tiles, axis=1)


def prepare_kernel(
    sat,
    hist,
    pressure,
    storage,
    trans,
    cell_in,
    index_in,
    control_in,
    target_in,
    p0e,
    tote,
    frace,
    stor,
    t0,
    t1,
    t2,
    near,
    cross,
    cell,
    wells,
    sat_v,
    hist_v,
    cell_v,
    index_v,
    control_v,
    target_v,
    spread,
    sems,
    *,
    gz,
):
    layers, rows, columns = pressure.shape
    ext = layers + 2 * H
    own = pl.ds(H, layers)
    parts = [(l, min(LOADED, layers - l)) for l in range(0, layers, LOADED)]
    in_parts = [
        (source.at[pl.ds(l, n)], target.at[pl.ds(offset + l, n)])
        for source, target, offset in ((sat, sat_v, 0), (hist, hist_v, 0), (pressure, p0e, H))
        for l, n in parts
    ]
    small = [(cell_in, cell_v), (index_in, index_v), (control_in, control_v), (target_in, target_v)]
    large = [
        (trans.at[0], t0.at[own]),
        (storage, stor.at[own]),
        (trans.at[1], t1.at[own]),
        (trans.at[2], t2.at[own]),
    ]
    copies = [
        pltpu.make_async_copy(a, b, sems.at[i])
        for i, (a, b) in enumerate(in_parts + small + large)
    ]
    for copy in copies:
        copy.start()

    def layer_step(l, carry):
        t, f = mobility(sat_v[l], hist_v[l])
        tote[l + H] = t
        frace[l + H] = f
        return carry

    for i, (l, n) in enumerate(parts):
        copies[i].wait()
        copies[len(parts) + i].wait()
        loop(l, l + n, layer_step, 0)
    for copy in copies[2 * len(parts) : -len(large)]:
        copy.wait()
    count, group = cell_v.shape
    cell[...] = flatten(cell_v[...].astype(jnp.float32), spread).astype(jnp.int32)
    wells[0:1, :] = flatten(index_v[...], spread)
    wells[1:2, :] = flatten(jnp.broadcast_to(target_v[...], (count, group)), spread)
    wells[2:3, :] = flatten(
        jnp.broadcast_to(control_v[...].astype(jnp.float32), (count, group)), spread
    )
    for copy in copies[-len(large) :]:
        copy.wait()
    even = lax.axis_index(gz) % 2 == 0
    refs = {"p0": p0e, "tot": tote, "t0": t0, "stor": stor, "t1": t1, "t2": t2, "frac": frace}
    for message, is_top in ((near, even), (cross, jnp.logical_not(even))):
        at = 0
        for name, count in Z_PARTS:
            edge = jnp.where(is_top, H + layers - count, H)
            message[pl.ds(at, count)] = refs[name][pl.ds(edge, count)]
            at += count


def masks(rows, columns):
    row = lax.broadcasted_iota(jnp.int32, (rows, columns), 0)
    column = lax.broadcasted_iota(jnp.int32, (rows, columns), 1)
    return (row == rows - 1, column == columns - 1)


def lateral_faces(tot, t1, t2, store, last_row, last_column, top_x):
    along = jnp.where(last_row, 0.0, t1) * 0.5 * (tot + roll(tot, -1, 0))
    across = jnp.where(last_column, 0.0, t2) * 0.5 * (tot + roll(tot, -1, 1))
    part = store + along + roll(along, 1, 0) + across + roll(across, 1, 1)
    return (jnp.where(last_row, jnp.where(top_x, 0.0, t1), along), across, part)


def is_last(axis):
    return lax.axis_index(axis) == lax.axis_size(axis) - 1


def first_sweep(e, p0e, stor, f0e, f1e, f2e, dpe, last_row):
    above = f0e[e]
    below = f0e[e - 1]
    along = jnp.where(last_row, 0.0, f1e[e])
    across = f2e[e]
    diag = dpe[e] + above + below
    p = p0e[e]
    base = stor[e] * p + above * p0e[e + 1] + below * p0e[e - 1]
    base = base + along * roll(p, -1, 0) + roll(along * p, 1, 0)
    base = base + across * roll(p, -1, 1) + roll(across * p, 1, 1)
    return (base, jnp.where(diag > 0.0, 1.0 / diag, 0.0))


def well_sums(p0e, tote, cell, wells, sums, perfs, hot, layers, group, gz):
    _, rows, columns = p0e.shape
    own = pl.ds(H, layers)
    at_place = at_places(cell[...], lax.axis_index(gz) * layers, layers, rows, columns)
    at_column = at_columns(cell[...], columns)
    hot[...] = at_place.astype(jnp.bfloat16)
    flat = (layers * rows, columns)
    weight = wells[0:1, :] * gather(tote[own].reshape(flat), at_place, at_column)
    cell_p = gather(p0e[own].reshape(flat), at_place, at_column)
    perfs[0:1, :] = weight
    perfs[1:2, :] = cell_p
    for i, value in enumerate((weight * cell_p, weight)):
        part = value[:, 0:LANES]
        for lane in range(LANES, value.shape[1], LANES):
            part = part + value[:, lane : lane + LANES]
        shift = LANES // 2
        while shift >= group:
            part = part + roll(part, shift, 1)
            shift //= 2
        sums[i : i + 1, :] = part


def faces_kernel(*refs, layers, gx, gz, group):
    p0e, tote, frace, stor, t0, t1, t2, cell, wells = refs[:9]
    f0e, f1e, f2e, dpe, base, inverse, near, cross, sums, perfs, hot = refs[9:]
    well_sums(p0e, tote, cell, wells, sums, perfs, hot, layers, group, gz)
    _, rows, columns = p0e.shape
    last_row, last_column = masks(rows, columns)
    top_x = is_last(gx)

    def step(e, carry):
        tot = tote[e]
        f0e[e] = t0[e] * 0.5 * (tot + tote[e + 1])
        f1e[e], f2e[e], dpe[e] = lateral_faces(
            tot, t1[e], t2[e], stor[e], last_row, last_column, top_x
        )
        return carry

    loop(H, H + layers, step, 0)
    refs = {"t1": f1e, "tot": tote, "p0": p0e, "dp": dpe, "f0": f0e, "f2": f2e, "f1": f1e}
    refs |= {"frac": frace, "p0_d2": p0e, "f0_d2": f0e, "f2_d2": f2e, "dp_d2": dpe}
    pack_both(near, cross, early_parts(layers), refs, refs, rows, gx)

    def sweep_step(e, carry):
        base[e], inverse[e] = first_sweep(e, p0e, stor, f0e, f1e, f2e, dpe, last_row)
        return carry

    loop(H + 1, H + layers - 1, sweep_step, 0)


def well_holes(sums, wells):
    repeat = lambda x: jnp.concatenate([x] * (wells.shape[1] // LANES), axis=1)
    goal = wells[1:2, :]
    return jnp.where(
        wells[2:3, :] == 0.0, (goal + repeat(sums[0:1, :])) / repeat(sums[1:2, :]), goal
    )


def join(a, b):
    return jnp.concatenate([a, b], axis=0)


def seam_faces(first, last, fields, seams, f1, inverse, p):
    p0e, tote, f0e, f1e, dpe = fields
    rows, columns = p0e.shape[1:]
    row = lax.broadcasted_iota(jnp.int32, (rows + 8, columns), 0)
    edge = (row == rows - 1) | (row == rows + 7)

    def step(e, below):
        tot = join(tote[e], seams["tot"][e])
        mixed = join(f1e[e], seams["f1"][e])
        border = jnp.where(edge, mixed * 0.5 * (tot + roll(tot, -1, 0)), 0.0)
        f1[e] = jnp.where(edge, border, mixed)
        above = join(f0e[e], seams["f0"][e])
        diag = join(dpe[e], seams["dp"][e]) + above + below + border + roll(border, 1, 0)
        inverse[e] = jnp.where(diag > 0.0, 1.0 / diag, 0.0)
        p[e] = join(p0e[e], seams["p0"][e])
        return above

    loop(first, last, step, join(f0e[first - 1], seams["f0"][first - 1]))


def sweep_layers(number, first, last, old, new, fields, seams, f1, inverse, part):
    rhse, f0e, f2e = fields
    rows, columns = rhse.shape[1:]
    row = lax.broadcasted_iota(jnp.int32, (rows + 8, columns), 0)
    beyond = (row == rows + 1) | (row == rows + 6)
    blank = jnp.zeros((rows, columns), jnp.float32)

    def step(e, carry):
        below, p = carry
        above = old[e + 1]
        face = join(f0e[e], seams["f0"][e])
        x = f1[e]
        y = join(f2e[e], seams["f2"][e])
        side = seams["rhs2"][e]
        if number == 3:
            side = jnp.where(beyond[rows:], seams["rhs3"][e], side)
        total = join(rhse[e], side) + below + face * above
        total = total + x * roll(p, -1, 0) + roll(x * p, 1, 0)
        total = total + y * roll(p, -1, 1) + roll(y * p, 1, 1)
        value = total * inverse[e]
        if number == 1:
            value = jnp.where(beyond, join(blank, seams["p1"][e]), value)
        new[e, part] = value[part]
        return (face * p, above)

    start = join(f0e[first - 1], seams["f0"][first - 1]) * old[first - 1]
    loop(first, last, step, (start, old[first]))


def seam_kernel(near, cross, *refs, layers, gx):
    p0e, tote, f0e, f1e, f2e, dpe, rhse = refs[:7]
    refs = refs[7:]
    seams = dict(zip(SEAMS, refs))
    f1, inverse, p, p1 = refs[len(SEAMS) :]
    for seam in seams.values():
        seam[...] = jnp.zeros(seam.shape, jnp.float32)
    unpack_both(near, cross, early_parts(layers), seams, gx)
    inner = (H + 1, H + layers - 1)
    seam_faces(*inner, (p0e, tote, f0e, f1e, dpe), seams, f1, inverse, p)
    for e in (H, H + layers - 1):
        p[e] = join(p0e[e], jnp.zeros_like(seams["p0"][e]))
    own = slice(0, p0e.shape[1])
    sweep_layers(1, *inner, p, p1, (rhse, f0e, f2e), seams, f1, inverse, own)


def halo_kernel(*refs, layers, gx, gz):
    own_t0, cross, near, cell, wells, own_perfs = refs[10:16]
    p0e, tote, frace, stor, f0e, f1e, f2e, dpe, base, inverse, perfs, hot = refs[16:]
    ext, rows, columns = p0e.shape
    even = lax.axis_index(gz) % 2 == 0
    top_z = is_last(gz)
    top_x = is_last(gx)
    last_row, last_column = masks(rows, columns)
    where = {}
    at = 0
    for name, count in Z_PARTS:
        where[name] = (at, count)
        at += count

    def halo(name, e):
        at, count = where[name]
        low = e < H
        at = at + e - (H - count if low else H + layers)
        one, two = (near[at], cross[at])
        return jnp.where(even, two, one) if low else jnp.where(even, one, two)

    for name, target in (("p0", p0e), ("tot", tote), ("frac", frace), ("stor", stor)):
        count = where[name][1]
        for e in (*range(H - count, H), *range(H + layers, H + layers + count)):
            target[e] = halo(name, e)
    f0e[H + layers - 1] = jnp.where(top_z, 0.0, own_t0[H + layers - 1]) * 0.5 * (
        tote[H + layers - 1] + tote[H + layers]
    )
    for e in (*range(0, H), *range(H + layers, ext - 1)):
        f0e[e] = halo("t0", e) * 0.5 * (tote[e] + tote[e + 1])
    for e in (*range(1, H), *range(H + layers, ext - 1)):
        f1e[e], f2e[e], dpe[e] = lateral_faces(
            tote[e], halo("t1", e), halo("t2", e), stor[e], last_row, last_column, top_x
        )
    for e in (*range(1, H + 1), *range(H + layers - 1, ext - 1)):
        base[e], inverse[e] = first_sweep(e, p0e, stor, f0e, f1e, f2e, dpe, last_row)
    width = H - 1
    first = lax.axis_index(gz) * layers
    sides = ((1, first - width), (H + layers, first + layers))
    at_place = [at_places(cell[...], layer, width, rows, columns) for _, layer in sides]
    at_place = jnp.concatenate(at_place, axis=0)
    at_column = at_columns(cell[...], columns)
    hot[...] = at_place.astype(jnp.bfloat16)
    flat = (width * rows, columns)
    both = lambda ref: join(*(ref[e : e + width].reshape(flat) for e, _ in sides))
    weight = wells[0:1, :] * gather(both(tote), at_place, at_column)
    perfs[0:1, :] = own_perfs[0:1, :] + weight
    perfs[1:2, :] = own_perfs[1:2, :] + gather(both(p0e), at_place, at_column)


def build_kernel(*refs, layers, gx):
    p0e, stor, f0e, f1e, f2e, dpe, tote, base, inverse, sums, perfs, hot, own_hot = refs[:13]
    cell, wells, rhse, source, x_near, x_cross, bottom = refs[13:20]
    p1, g2u, g2d, g3u, g3d, rxu, rxd, dpx = refs[20:]
    ext, rows, columns = p0e.shape
    last_row, _ = masks(rows, columns)
    hole = well_holes(sums[...], wells[...])
    bottom[...] = hole[:, 0:LANES]
    rate = perfs[0:1, :] * (hole - perfs[1:2, :])
    pieces = split(jnp.where(at_columns(cell[...], columns), rate, 0.0))

    def scatter(mask):
        spread = [
            lax.dot_general(
                mask, piece, (((1,), (1,)), ((), ())), preferred_element_type=jnp.float32
            )
            for piece in pieces
        ]
        return (spread[0] + spread[1]).reshape(-1, rows, columns)

    width = H - 1
    inside = scatter(own_hot[...])
    outside = scatter(hot[...])
    source[...] = inside
    rhse[H : ext - H] = inside
    rhse[1:H] = outside[:width]
    rhse[ext - H : ext - 1] = outside[width:]

    def first_step(e, carry):
        wells_rate = rhse[e]
        p1[e] = (base[e] + wells_rate) * inverse[e]
        rhse[e] = stor[e] * p0e[e] + wells_rate
        return carry

    loop(1, ext - 1, first_step, 0)

    def second_step(e, carry):
        along = jnp.where(last_row, 0.0, f1e[e])
        across = f2e[e]
        p = p1[e]
        rhs = rhse[e]
        lower = roll(along * p, 1, 0)
        upper = along * roll(p, -1, 0)
        g2u[e] = rhs + lower
        g2d[e] = rhs + upper
        new = rhs + lower + upper + f0e[e] * p1[e + 1] + f0e[e - 1] * p1[e - 1]
        new = new + across * roll(p, -1, 1) + roll(across * p, 1, 1)
        p2 = new * inverse[e]
        g3u[e] = rhs + roll(along * p2, 1, 0)
        g3d[e] = rhs + along * roll(p2, -1, 0)
        return carry

    loop(H - 1, ext - H + 1, second_step, 0)

    for e, beside, face in ((2, 1, 1), (ext - 3, ext - 2, ext - 3)):
        along = jnp.where(last_row, 0.0, f1e[e])
        across = f2e[e]
        p = p0e[e]
        rhs = rhse[e] + f0e[face] * p0e[beside]
        rhs = rhs + across * roll(p, -1, 1) + roll(across * p, 1, 1)
        rxu[e] = rhs + roll(along * p, 1, 0)
        rxd[e] = rhs + along * roll(p, -1, 0)
        dpx[e] = dpe[e] + f0e[face]

    shared = {"t1": f1e, "tot": tote, "p0": p0e, "dp": dpe, "f0": f0e, "f2": f2e, "f1": f1e}
    shared |= {"p0_d2": p0e, "f0_d2": f0e, "f2_d2": f2e, "dp_d2": dpe, "rhs": rhse, "p1_d2": p1}
    for e, beside, face in ((H - 1, H - 2, H - 2), (ext - H, ext - H + 1, ext - H)):
        across = f2e[e]
        p = p1[e]
        beyond = f0e[face] * p1[beside] + across * roll(p, -1, 1) + roll(across * p, 1, 1)
        g2u[e] = g2u[e] + beyond
        g2d[e] = g2d[e] + beyond
        dpx[e] = dpe[e] + f0e[face]
    shared["dp_x"] = shared["dp2_x"] = dpx
    up = shared | {"g2": g2u, "g3": g3u, "rhs_x": rxu}
    down = shared | {"g2": g2d, "g3": g3d, "rhs_x": rxd}
    pack_both(x_near, x_cross, late_parts(layers), up, down, rows, gx)


def finish_kernel(*refs, gx):
    sat, hist, volume, storage, source = refs[:5]
    p0e, tote, frace, f0e, f1e, f2e, dpe, rhse, near, cross = refs[5:15]
    hole = refs[19 + len(SEAMS)]
    refs = refs[20 + len(SEAMS) :]
    new_p, residual, new_sat, new_hist, bottom = refs[:5]
    seams = dict(zip(SEAMS, refs[5:]))
    f1, rdiag, pa, pb = refs[5 + len(SEAMS) :]
    bottom[...] = hole[:, 0 : bottom.shape[1]]
    layers, rows, columns = sat.shape
    ext = layers + 2 * H
    unpack_both(near, cross, late_parts(layers), seams, gx)
    sfrac = seams["frac"]
    pa[0] = join(p0e[0], seams["p0"][0])
    pa[ext - 1] = join(p0e[ext - 1], seams["p0"][ext - 1])
    for first, last in ((1, H + 1), (ext - H - 1, ext - 1)):
        seam_faces(first, last, (p0e, tote, f0e, f1e, dpe), seams, f1, rdiag, pa)

    pressures = (pa, pb)
    fields = (rhse, f0e, f2e)
    inner = (H + 1, ext - H - 1)
    everywhere = slice(0, rows + 8)
    for number in range(1, SWEEPS + 1):
        old, new = pressures[(number - 1) % 2], pressures[number % 2]
        ranges = [(number, ext - number, everywhere)]
        if number == 1:
            ranges = [
                (number, inner[0], everywhere),
                (*inner, slice(rows, rows + 8)),
                (inner[1], ext - number, everywhere),
            ]
        for first, last, part in ranges:
            sweep_layers(number, first, last, old, new, fields, seams, f1, rdiag, part)
    field = pressures[SWEEPS % 2]

    def flow(face, p, p_next, f, f_next):
        water = face * (p - p_next)
        return (water, water * jnp.where(water > 0, f, f_next))

    def last_step(l, carry):
        below_w, below_g = carry
        e = l + H
        p = field[e]
        f = join(frace[e], sfrac[e])
        own_p = p[:rows]
        own_f = f[:rows]
        above_w, above_g = flow(f0e[e], own_p, field[e + 1][:rows], own_f, frace[e + 1])
        xw, xg = flow(f1[e], p, roll(p, -1, 0), f, roll(f, -1, 0))
        yw, yg = flow(f2e[e], own_p, roll(own_p, -1, 1), own_f, roll(own_f, -1, 1))
        water = above_w - below_w + (xw - roll(xw, 1, 0))[:rows] + yw - roll(yw, 1, 1)
        out = above_g - below_g + (xg - roll(xg, 1, 0))[:rows] + yg - roll(yg, 1, 1)
        new_p[l] = own_p
        residual[l] = rhse[e] - storage[l] * own_p - water
        src = source[l]
        gas = jnp.maximum(src, 0.0) + jnp.minimum(src, 0.0) * own_f
        s = sat[l] + volume[l] * (gas - out)
        new_sat[l] = s
        new_hist[l] = jnp.maximum(hist[l], s)
        return (above_w, above_g)

    first = flow(f0e[H - 1], field[H - 1][:rows], field[H][:rows], frace[H - 1], frace[H])
    loop(0, layers, last_step, first)


def swap(block, axis, first):
    pairs = [(i, i + 1) for i in range(first, lax.axis_size(axis) - 1, 2)]
    return lax.ppermute(block, axis, pairs + [(b, a) for a, b in pairs])


def pin(*shape, dtype=jnp.float32):
    return pltpu.VMEM(shape, dtype)


VMEM = pl.BlockSpec(memory_space=pltpu.VMEM)
HBM = pl.BlockSpec(memory_space=pltpu.HBM)


def call(kernel, outs, scratch, *args, space=VMEM, sems=0, aliases={}):
    as_struct = lambda s: s if hasattr(s, "dtype") else jax.ShapeDtypeStruct(s, jnp.float32)
    as_scratch = lambda s: pltpu.VMEM(as_struct(s).shape, as_struct(s).dtype)
    return pl.pallas_call(
        kernel,
        out_shape=[as_struct(s) for s in outs],
        in_specs=[space] * len(args),
        out_specs=[VMEM] * len(outs),
        scratch_shapes=[as_scratch(s) for s in scratch]
        + ([pltpu.SemaphoreType.DMA((sems,))] if sems else []),
        input_output_aliases=aliases,
        compiler_params=pltpu.CompilerParams(vmem_limit_bytes=24 * 1024 * 1024),
    )(*(pltpu.with_memory_space_constraint(a, pltpu.HBM) if space is HBM else a for a in args))


def body(
    pressure,
    saturation,
    sat_history,
    storage,
    step_volume,
    transmiss,
    perf_cell,
    perf_index,
    control,
    target,
):
    layers, rows, columns = pressure.shape
    ext = layers + 2 * H
    wells, perfs = perf_cell.shape
    block = (layers, rows, columns)
    pinned = pin(*block)
    ext_block = pin(ext, rows, columns)
    z_message = pin(sum(count for _, count in Z_PARTS), rows, columns)
    entries = wells * perfs
    early, late = (pin(tiles(f(layers)), 8, columns) for f in (early_parts, late_parts))
    seams = [pin(ext, 8, columns)] * len(SEAMS)
    *fields, near, cross, cell, per_perf = call(
        functools.partial(prepare_kernel, gz="gz"),
        [ext_block] * 7
        + [z_message, z_message]
        + [pin(1, entries, dtype=jnp.int32), pin(3, entries)],
        [
            block,
            block,
            jax.ShapeDtypeStruct((perfs, wells), jnp.int32),
            (perfs, wells),
            jax.ShapeDtypeStruct((1, wells), jnp.int32),
            (1, wells),
            (perfs, LANES),
        ],
        saturation,
        sat_history,
        pressure,
        storage,
        transmiss,
        perf_cell.T,
        perf_index.T,
        control.reshape(1, wells),
        target.reshape(1, wells),
        space=HBM,
        sems=3 * -(-layers // LOADED) + 8,
    )
    cross = swap(cross, "gz", 1)
    near = swap(near, "gz", 0)
    p0e, tote, frace, stor, t0, t1, t2 = fields
    f0e, f1e, f2e, dpe, base, inverse, early_near, early_cross, part, perf_values, own_hot = call(
        functools.partial(faces_kernel, layers=layers, gx="gx", gz="gz", group=wells),
        [ext_block] * 6
        + [
            early,
            early,
            pin(2, LANES),
            pin(2, entries),
            pin(layers * rows, entries, dtype=jnp.bfloat16),
        ],
        [],
        *fields,
        cell,
        per_perf,
    )
    early_cross = swap(early_cross, "gx", 1)
    early_near = swap(early_near, "gx", 0)
    sums = part
    step = 1
    while step < lax.axis_size("gz"):
        pairs = [(i, i ^ step) for i in range(lax.axis_size("gz"))]
        tile = jnp.pad(sums, ((0, 8 - sums.shape[0]), (0, 0)))
        sums = sums + lax.ppermute(tile, "gz", pairs)[: sums.shape[0]]
        step *= 2
    early_near, near = lax.optimization_barrier((early_near, near))
    p0e, tote, frace, stor, f0e, f1e, f2e, dpe, base, inverse, perf_values, hot = call(
        functools.partial(halo_kernel, layers=layers, gx="gx", gz="gz"),
        [ext_block] * 10
        + [pin(2, entries), pin(2 * (H - 1) * rows, entries, dtype=jnp.bfloat16)],
        [],
        p0e,
        tote,
        frace,
        stor,
        f0e,
        f1e,
        f2e,
        dpe,
        base,
        inverse,
        t0,
        cross,
        near,
        cell,
        per_perf,
        perf_values,
        aliases={i: i for i in range(10)},
    )
    rhse, source, late_near, late_cross, hole = call(
        functools.partial(build_kernel, layers=layers, gx="gx"),
        [ext_block, pinned, late, late, pin(1, LANES)],
        [ext_block] * 8,
        p0e,
        stor,
        f0e,
        f1e,
        f2e,
        dpe,
        tote,
        base,
        inverse,
        sums,
        perf_values,
        hot,
        own_hot,
        cell,
        per_perf,
    )
    late_cross = swap(late_cross, "gx", 1)
    late_near = swap(late_near, "gx", 0)
    early_near, early_cross, rhse = lax.optimization_barrier((early_near, early_cross, rhse))
    joined = [pin(ext, rows + 8, columns)] * 4
    filled = call(
        functools.partial(seam_kernel, layers=layers, gx="gx"),
        seams + joined,
        [],
        early_near,
        early_cross,
        p0e,
        tote,
        f0e,
        f1e,
        f2e,
        dpe,
        rhse,
    )
    field, residual, new_sat, new_hist, bottom, *_ = call(
        functools.partial(finish_kernel, gx="gx"),
        [block] * 4 + [(1, wells)] + seams + joined,
        [],
        saturation,
        sat_history,
        step_volume,
        storage,
        source,
        p0e,
        tote,
        frace,
        f0e,
        f1e,
        f2e,
        dpe,
        rhse,
        late_near,
        late_cross,
        *filled,
        hole,
        aliases={15 + i: 5 + i for i in range(len(filled))},
    )
    return (field, residual, new_sat, new_hist, bottom.reshape(wells))


def solution(mesh):
    return jax.shard_map(
        body,
        mesh=mesh,
        in_specs=(
            P("gz", "gx", None),
            P("gz", "gx", None),
            P("gz", "gx", None),
            P("gz", "gx", None),
            P("gz", "gx", None),
            P(None, "gz", "gx", None),
            P("gx", None),
            P("gx", None),
            P("gx"),
            P("gx"),
        ),
        out_specs=(
            P("gz", "gx", None),
            P("gz", "gx", None),
            P("gz", "gx", None),
            P("gz", "gx", None),
            P("gx"),
        ),
        check_vma=False,
    )
```

```python
import functools

import jax
import jax.numpy as jnp
from jax import lax
from jax.experimental import pallas as pl
from jax.experimental.pallas import tpu as pltpu
from jax.sharding import PartitionSpec as P

SWEEPS = 4
H = SWEEPS + 1
LANES = 128
LOADED = 4

Z_PARTS = (
    ("p0", H),
    ("tot", H),
    ("t0", H),
    ("stor", H - 1),
    ("t1", H - 1),
    ("t2", H - 1),
    ("frac", 1),
    ("sums", 1),
)


def early_parts(layers):
    own = (H, layers)
    inner = (H, layers - 1)
    return (
        ("t1", *own),
        ("tot", *own),
        ("p0", *own),
        ("dp", *own),
        ("f0", *inner),
        ("f2", *own),
        ("f1", *own),
        ("frac", *own),
        ("p0_d2", *own),
        ("f0_d2", *inner),
        ("f2_d2", *own),
        ("dp_d2", *own),
    )


def late_parts(layers):
    top = H + layers
    both = lambda name, n: ((name, H - n, n), (name, top, n))
    faces = lambda name, n: ((name, H - n, n), (name, top - 1, n))
    ends = lambda name: ((name, 2, 1), (name, top + 2, 1))
    return (
        ("rhs", 3, layers + 4),
        *ends("rhs_x"),
        ("p1_d2", 3, layers + 4),
        ("g2", 4, layers + 2),
        ("g3", H, layers),
        *both("t1", H - 1),
        *both("tot", H - 1),
        *both("p0", H - 1),
        *both("dp", H - 3),
        *ends("dp_x"),
        *faces("f0", H - 2),
        *both("f2", H - 3),
        *both("f1", H - 3),
        *both("p0_d2", H - 3),
        *faces("f0_d2", 1),
        *both("dp2_x", 1),
    )


def tiles(parts):
    return -(-sum(count for _, _, count in parts) // 8)


SEAMS = ("f0", "f1", "f2", "tot", "dp", "p0", "frac", "p1", "rhs2", "rhs3")
PLACES = {
    "t1": ("f1", None, 7),
    "f1": ("f1", 0, 6),
    "tot": ("tot", 0, 7),
    "p0": ("p0", 0, 7),
    "dp": ("dp", 0, 7),
    "dp_d2": ("dp", 1, 6),
    "f0": ("f0", 0, 7),
    "f0_d2": ("f0", 1, 6),
    "f2": ("f2", 0, 7),
    "f2_d2": ("f2", 1, 6),
    "frac": ("frac", 0, 7),
    "p0_d2": ("p0", 1, 6),
    "p1_d2": ("p1", 1, 6),
    "rhs": ("rhs2", 0, 7),
    "rhs_x": ("rhs2", 0, 7),
    "dp_x": ("dp", 0, 7),
    "dp2_x": ("dp", 1, 6),
    "g2": ("rhs2", 1, 6),
    "g3": ("rhs3", 1, 6),
}


def pack(message, parts, refs, rows):
    at = 0
    for name, first, count in parts:
        for e in range(first, first + count):
            message[at // 8, at % 8 : at % 8 + 1, :] = refs[name][e, rows[name] : rows[name] + 1, :]
            at += 1


def pack_both(near, cross, parts, up, down, rows, gx):
    last = rows - 1
    outer = {name: 0 if PLACES[name][2] == 7 else 1 for name in PLACES}
    up_rows = {name: last - outer[name] for name in PLACES} | {"f1": last - 1}
    down_rows = dict(outer) | {"f1": 0}
    even = lax.axis_index(gx) % 2 == 0

    @pl.when(even)
    def _():
        pack(near, parts, up, up_rows)
        pack(cross, parts, down, down_rows)

    @pl.when(jnp.logical_not(even))
    def _():
        pack(cross, parts, up, up_rows)
        pack(near, parts, down, down_rows)


def unpack(message, parts, seams, side):
    at = 0
    for name, first, count in parts:
        seam, *places = PLACES[name]
        place = places[side]
        for e in range(first, first + count):
            if place is not None:
                seams[seam][e, place : place + 1, :] = message[at // 8, at % 8 : at % 8 + 1, :]
            at += 1


def unpack_both(near, cross, parts, seams, gx):
    even = lax.axis_index(gx) % 2 == 0

    @pl.when(even)
    def _():
        unpack(near, parts, seams, 0)
        unpack(cross, parts, seams, 1)

    @pl.when(jnp.logical_not(even))
    def _():
        unpack(cross, parts, seams, 0)
        unpack(near, parts, seams, 1)


def mobility(sat, history):
    trapped = history / (1.0 + 1.5 * history)
    excess = jnp.maximum(sat - trapped, 0.0)
    free_gas = 0.5 * (excess + jnp.sqrt(excess * excess + excess / 0.375))
    relperm = jnp.where(sat < history, free_gas * free_gas, sat * sat)
    gas = relperm / 0.5
    total = (1.0 - sat) * (1.0 - sat) + gas
    return (total, gas / total)


def roll(x, shift, axis):
    return pltpu.roll(x, shift % x.shape[axis], axis)


def loop(first, last, step, carry):
    count = last - first
    unroll = -(-count // -(-count // 16))
    groups = count // unroll

    def group(g, carry):
        for i in range(unroll):
            carry = step(first + g * unroll + i, carry)
        return carry

    carry = lax.fori_loop(0, groups, group, carry) if groups > 1 else group(0, carry)
    for index in range(first + groups * unroll, last):
        carry = step(index, carry)
    return carry


def split(x):
    high = x.astype(jnp.bfloat16)
    return (high, (x - high.astype(jnp.float32)).astype(jnp.bfloat16))


def at_places(cell, first_layer, layers, rows, columns):
    layer = cell // (rows * columns)
    row = (cell - layer * (rows * columns)) // columns
    place = (layer - first_layer) * rows + row
    return lax.broadcasted_iota(jnp.int32, (layers * rows, cell.shape[1]), 0) == place


def at_columns(cell, columns):
    return lax.broadcasted_iota(jnp.int32, (columns, cell.shape[1]), 0) == cell % columns


def gather(field, at_place, at_column):
    high, low = split(field)
    hot = at_column.astype(jnp.bfloat16)
    by_column = jnp.dot(high, hot, preferred_element_type=jnp.float32) + jnp.dot(
        low, hot, preferred_element_type=jnp.float32
    )
    return jnp.sum(jnp.where(at_place, by_column, 0.0), axis=0, keepdims=True)


def flatten(block, spread):
    perfs, wells = block.shape
    spread[...] = jnp.zeros(spread.shape, jnp.float32)
    spread[:, 0:wells] = block
    wide = spread[...]
    shift = wells
    while shift < LANES:
        wide = wide + roll(wide, shift, 1)
        shift *= 2
    each = LANES // wells
    entry = lax.broadcasted_iota(jnp.int32, (perfs, LANES), 0)
    group = lax.broadcasted_iota(jnp.int32, (perfs, LANES), 1) // wells
    tiles = [
        jnp.sum(jnp.where(entry == first + group, wide, 0.0), axis=0, keepdims=True)
        for first in range(0, perfs, each)
    ]
    return jnp.concatenate(tiles, axis=1)


def prepare_kernel(
    sat,
    hist,
    pressure,
    storage,
    trans,
    cell_in,
    index_in,
    control_in,
    target_in,
    p0e,
    tote,
    frace,
    stor,
    t0,
    t1,
    t2,
    near,
    cross,
    sums,
    cell,
    wells,
    perfs,
    hot,
    sat_v,
    hist_v,
    cell_v,
    index_v,
    control_v,
    target_v,
    spread,
    sems,
    *,
    gz,
):
    layers, rows, columns = pressure.shape
    ext = layers + 2 * H
    own = pl.ds(H, layers)
    parts = [(l, min(LOADED, layers - l)) for l in range(0, layers, LOADED)]
    in_parts = [
        (source.at[pl.ds(l, n)], target.at[pl.ds(offset + l, n)])
        for source, target, offset in ((sat, sat_v, 0), (hist, hist_v, 0), (pressure, p0e, H))
        for l, n in parts
    ]
    small = [(cell_in, cell_v), (index_in, index_v), (control_in, control_v), (target_in, target_v)]
    large = [
        (trans.at[0], t0.at[own]),
        (storage, stor.at[own]),
        (trans.at[1], t1.at[own]),
        (trans.at[2], t2.at[own]),
    ]
    copies = [
        pltpu.make_async_copy(a, b, sems.at[i])
        for i, (a, b) in enumerate(in_parts + small + large)
    ]
    for copy in copies:
        copy.start()

    def layer_step(l, carry):
        t, f = mobility(sat_v[l], hist_v[l])
        tote[l + H] = t
        frace[l + H] = f
        return carry

    for i, (l, n) in enumerate(parts):
        copies[i].wait()
        copies[len(parts) + i].wait()
        loop(l, l + n, layer_step, 0)
    for copy in copies[2 * len(parts) : -len(large)]:
        copy.wait()
    count, group = cell_v.shape
    cell[...] = flatten(cell_v[...].astype(jnp.float32), spread).astype(jnp.int32)
    wells[0:1, :] = flatten(index_v[...], spread)
    wells[1:2, :] = flatten(jnp.broadcast_to(target_v[...], (count, group)), spread)
    wells[2:3, :] = flatten(
        jnp.broadcast_to(control_v[...].astype(jnp.float32), (count, group)), spread
    )
    at_place = at_places(cell[...], lax.axis_index(gz) * layers, layers, rows, columns)
    at_column = at_columns(cell[...], columns)
    hot[...] = at_place.astype(jnp.bfloat16)
    flat = (layers * rows, columns)
    weight = wells[0:1, :] * gather(tote[own].reshape(flat), at_place, at_column)
    cell_p = gather(p0e[own].reshape(flat), at_place, at_column)
    perfs[0:1, :] = weight
    perfs[1:2, :] = cell_p
    for i, value in enumerate((weight * cell_p, weight)):
        part = value[:, 0:LANES]
        for lane in range(LANES, value.shape[1], LANES):
            part = part + value[:, lane : lane + LANES]
        shift = LANES // 2
        while shift >= group:
            part = part + roll(part, shift, 1)
            shift //= 2
        sums[i : i + 1, :] = part
    for copy in copies[-len(large) :]:
        copy.wait()
    even = lax.axis_index(gz) % 2 == 0
    refs = {"p0": p0e, "tot": tote, "t0": t0, "stor": stor, "t1": t1, "t2": t2, "frac": frace}
    for message, is_top in ((near, even), (cross, jnp.logical_not(even))):
        at = 0
        for name, count in Z_PARTS:
            if name == "sums" and message is cross:
                continue
            if name == "sums":
                message[at] = jnp.zeros((rows, columns), jnp.float32)
                message[at, 0:2, 0:LANES] = sums[...]
            else:
                edge = jnp.where(is_top, H + layers - count, H)
                message[pl.ds(at, count)] = refs[name][pl.ds(edge, count)]
            at += count


def masks(rows, columns):
    row = lax.broadcasted_iota(jnp.int32, (rows, columns), 0)
    column = lax.broadcasted_iota(jnp.int32, (rows, columns), 1)
    return (row == rows - 1, column == columns - 1)


def lateral_faces(tot, t1, t2, store, last_row, last_column, top_x):
    along = jnp.where(last_row, 0.0, t1) * 0.5 * (tot + roll(tot, -1, 0))
    across = jnp.where(last_column, 0.0, t2) * 0.5 * (tot + roll(tot, -1, 1))
    part = store + along + roll(along, 1, 0) + across + roll(across, 1, 1)
    return (jnp.where(last_row, jnp.where(top_x, 0.0, t1), along), across, part)


def is_last(axis):
    return lax.axis_index(axis) == lax.axis_size(axis) - 1


def first_sweep(e, p0e, stor, f0e, f1e, f2e, dpe, last_row):
    above = f0e[e]
    below = f0e[e - 1]
    along = jnp.where(last_row, 0.0, f1e[e])
    across = f2e[e]
    diag = dpe[e] + above + below
    p = p0e[e]
    base = stor[e] * p + above * p0e[e + 1] + below * p0e[e - 1]
    base = base + along * roll(p, -1, 0) + roll(along * p, 1, 0)
    base = base + across * roll(p, -1, 1) + roll(across * p, 1, 1)
    return (base, jnp.where(diag > 0.0, 1.0 / diag, 0.0))


def faces_kernel(*refs, layers, gx):
    p0e, tote, frace, stor, t0, t1, t2, part = refs[:8]
    f0e, f1e, f2e, dpe, base, inverse, near, cross, sums = refs[8:]
    _, rows, columns = p0e.shape
    last_row, last_column = masks(rows, columns)
    top_x = is_last(gx)

    def step(e, carry):
        tot = tote[e]
        f0e[e] = t0[e] * 0.5 * (tot + tote[e + 1])
        f1e[e], f2e[e], dpe[e] = lateral_faces(
            tot, t1[e], t2[e], stor[e], last_row, last_column, top_x
        )
        return carry

    loop(H, H + layers, step, 0)
    sums[...] = part[...]
    refs = {"t1": f1e, "tot": tote, "p0": p0e, "dp": dpe, "f0": f0e, "f2": f2e, "f1": f1e}
    refs |= {"frac": frace, "p0_d2": p0e, "f0_d2": f0e, "f2_d2": f2e, "dp_d2": dpe}
    pack_both(near, cross, early_parts(layers), refs, refs, rows, gx)

    def sweep_step(e, carry):
        base[e], inverse[e] = first_sweep(e, p0e, stor, f0e, f1e, f2e, dpe, last_row)
        return carry

    loop(H + 1, H + layers - 1, sweep_step, 0)


def well_holes(sums, wells):
    repeat = lambda x: jnp.concatenate([x] * (wells.shape[1] // LANES), axis=1)
    goal = wells[1:2, :]
    return jnp.where(
        wells[2:3, :] == 0.0, (goal + repeat(sums[0:1, :])) / repeat(sums[1:2, :]), goal
    )


def join(a, b):
    return jnp.concatenate([a, b], axis=0)


def seam_faces(first, last, fields, seams, f1, inverse, p):
    p0e, tote, f0e, f1e, dpe = fields
    rows, columns = p0e.shape[1:]
    row = lax.broadcasted_iota(jnp.int32, (rows + 8, columns), 0)
    edge = (row == rows - 1) | (row == rows + 7)

    def step(e, below):
        tot = join(tote[e], seams["tot"][e])
        mixed = join(f1e[e], seams["f1"][e])
        border = jnp.where(edge, mixed * 0.5 * (tot + roll(tot, -1, 0)), 0.0)
        f1[e] = jnp.where(edge, border, mixed)
        above = join(f0e[e], seams["f0"][e])
        diag = join(dpe[e], seams["dp"][e]) + above + below + border + roll(border, 1, 0)
        inverse[e] = jnp.where(diag > 0.0, 1.0 / diag, 0.0)
        p[e] = join(p0e[e], seams["p0"][e])
        return above

    loop(first, last, step, join(f0e[first - 1], seams["f0"][first - 1]))


def sweep_layers(number, first, last, old, new, fields, seams, f1, inverse, part):
    rhse, f0e, f2e = fields
    rows, columns = rhse.shape[1:]
    row = lax.broadcasted_iota(jnp.int32, (rows + 8, columns), 0)
    beyond = (row == rows + 1) | (row == rows + 6)
    blank = jnp.zeros((rows, columns), jnp.float32)

    def step(e, carry):
        below, p = carry
        above = old[e + 1]
        face = join(f0e[e], seams["f0"][e])
        x = f1[e]
        y = join(f2e[e], seams["f2"][e])
        side = seams["rhs2"][e]
        if number == 3:
            side = jnp.where(beyond[rows:], seams["rhs3"][e], side)
        total = join(rhse[e], side) + below + face * above
        total = total + x * roll(p, -1, 0) + roll(x * p, 1, 0)
        total = total + y * roll(p, -1, 1) + roll(y * p, 1, 1)
        value = total * inverse[e]
        if number == 1:
            value = jnp.where(beyond, join(blank, seams["p1"][e]), value)
        new[e, part] = value[part]
        return (face * p, above)

    start = join(f0e[first - 1], seams["f0"][first - 1]) * old[first - 1]
    loop(first, last, step, (start, old[first]))


def seam_kernel(near, cross, *refs, layers, gx):
    p0e, tote, f0e, f1e, f2e, dpe, rhse = refs[:7]
    refs = refs[7:]
    seams = dict(zip(SEAMS, refs))
    f1, inverse, p, p1 = refs[len(SEAMS) :]
    for seam in seams.values():
        seam[...] = jnp.zeros(seam.shape, jnp.float32)
    unpack_both(near, cross, early_parts(layers), seams, gx)
    inner = (H + 1, H + layers - 1)
    seam_faces(*inner, (p0e, tote, f0e, f1e, dpe), seams, f1, inverse, p)
    for e in (H, H + layers - 1):
        p[e] = join(p0e[e], jnp.zeros_like(seams["p0"][e]))
    own = slice(0, p0e.shape[1])
    sweep_layers(1, *inner, p, p1, (rhse, f0e, f2e), seams, f1, inverse, own)


def halo_kernel(*refs, layers, gx, gz):
    own_t0, cross, near, cell, wells, own_perfs = refs[10:16]
    p0e, tote, frace, stor, f0e, f1e, f2e, dpe, base, inverse, perfs, hot = refs[16:]
    ext, rows, columns = p0e.shape
    even = lax.axis_index(gz) % 2 == 0
    top_z = is_last(gz)
    top_x = is_last(gx)
    last_row, last_column = masks(rows, columns)
    where = {}
    at = 0
    for name, count in Z_PARTS:
        where[name] = (at, count)
        at += count

    def halo(name, e):
        at, count = where[name]
        low = e < H
        at = at + e - (H - count if low else H + layers)
        one, two = (near[at], cross[at])
        return jnp.where(even, two, one) if low else jnp.where(even, one, two)

    for name, target in (("p0", p0e), ("tot", tote), ("frac", frace), ("stor", stor)):
        count = where[name][1]
        for e in (*range(H - count, H), *range(H + layers, H + layers + count)):
            target[e] = halo(name, e)
    f0e[H + layers - 1] = jnp.where(top_z, 0.0, own_t0[H + layers - 1]) * 0.5 * (
        tote[H + layers - 1] + tote[H + layers]
    )
    for e in (*range(0, H), *range(H + layers, ext - 1)):
        f0e[e] = halo("t0", e) * 0.5 * (tote[e] + tote[e + 1])
    for e in (*range(1, H), *range(H + layers, ext - 1)):
        f1e[e], f2e[e], dpe[e] = lateral_faces(
            tote[e], halo("t1", e), halo("t2", e), stor[e], last_row, last_column, top_x
        )
    for e in (*range(1, H + 1), *range(H + layers - 1, ext - 1)):
        base[e], inverse[e] = first_sweep(e, p0e, stor, f0e, f1e, f2e, dpe, last_row)
    width = H - 1
    first = lax.axis_index(gz) * layers
    sides = ((1, first - width), (H + layers, first + layers))
    at_place = [at_places(cell[...], layer, width, rows, columns) for _, layer in sides]
    at_place = jnp.concatenate(at_place, axis=0)
    at_column = at_columns(cell[...], columns)
    hot[...] = at_place.astype(jnp.bfloat16)
    flat = (width * rows, columns)
    both = lambda ref: join(*(ref[e : e + width].reshape(flat) for e, _ in sides))
    weight = wells[0:1, :] * gather(both(tote), at_place, at_column)
    perfs[0:1, :] = own_perfs[0:1, :] + weight
    perfs[1:2, :] = own_perfs[1:2, :] + gather(both(p0e), at_place, at_column)


def build_kernel(*refs, layers, gx):
    p0e, stor, f0e, f1e, f2e, dpe, tote, base, inverse, sums, perfs, hot, own_hot = refs[:13]
    cell, wells, rhse, source, x_near, x_cross, bottom = refs[13:20]
    p1, g2u, g2d, g3u, g3d, rxu, rxd, dpx = refs[20:]
    ext, rows, columns = p0e.shape
    last_row, _ = masks(rows, columns)
    hole = well_holes(sums[...], wells[...])
    bottom[...] = hole[:, 0:LANES]
    rate = perfs[0:1, :] * (hole - perfs[1:2, :])
    pieces = split(jnp.where(at_columns(cell[...], columns), rate, 0.0))

    def scatter(mask):
        spread = [
            lax.dot_general(
                mask, piece, (((1,), (1,)), ((), ())), preferred_element_type=jnp.float32
            )
            for piece in pieces
        ]
        return (spread[0] + spread[1]).reshape(-1, rows, columns)

    width = H - 1
    inside = scatter(own_hot[...])
    outside = scatter(hot[...])
    source[...] = inside
    rhse[H : ext - H] = inside
    rhse[1:H] = outside[:width]
    rhse[ext - H : ext - 1] = outside[width:]

    def first_step(e, carry):
        wells_rate = rhse[e]
        p1[e] = (base[e] + wells_rate) * inverse[e]
        rhse[e] = stor[e] * p0e[e] + wells_rate
        return carry

    loop(1, ext - 1, first_step, 0)

    def second_step(e, carry):
        along = jnp.where(last_row, 0.0, f1e[e])
        across = f2e[e]
        p = p1[e]
        rhs = rhse[e]
        lower = roll(along * p, 1, 0)
        upper = along * roll(p, -1, 0)
        g2u[e] = rhs + lower
        g2d[e] = rhs + upper
        new = rhs + lower + upper + f0e[e] * p1[e + 1] + f0e[e - 1] * p1[e - 1]
        new = new + across * roll(p, -1, 1) + roll(across * p, 1, 1)
        p2 = new * inverse[e]
        g3u[e] = rhs + roll(along * p2, 1, 0)
        g3d[e] = rhs + along * roll(p2, -1, 0)
        return carry

    loop(H - 1, ext - H + 1, second_step, 0)

    for e, beside, face in ((2, 1, 1), (ext - 3, ext - 2, ext - 3)):
        along = jnp.where(last_row, 0.0, f1e[e])
        across = f2e[e]
        p = p0e[e]
        rhs = rhse[e] + f0e[face] * p0e[beside]
        rhs = rhs + across * roll(p, -1, 1) + roll(across * p, 1, 1)
        rxu[e] = rhs + roll(along * p, 1, 0)
        rxd[e] = rhs + along * roll(p, -1, 0)
        dpx[e] = dpe[e] + f0e[face]

    shared = {"t1": f1e, "tot": tote, "p0": p0e, "dp": dpe, "f0": f0e, "f2": f2e, "f1": f1e}
    shared |= {"p0_d2": p0e, "f0_d2": f0e, "f2_d2": f2e, "dp_d2": dpe, "rhs": rhse, "p1_d2": p1}
    for e, beside, face in ((H - 1, H - 2, H - 2), (ext - H, ext - H + 1, ext - H)):
        across = f2e[e]
        p = p1[e]
        beyond = f0e[face] * p1[beside] + across * roll(p, -1, 1) + roll(across * p, 1, 1)
        g2u[e] = g2u[e] + beyond
        g2d[e] = g2d[e] + beyond
        dpx[e] = dpe[e] + f0e[face]
    shared["dp_x"] = shared["dp2_x"] = dpx
    up = shared | {"g2": g2u, "g3": g3u, "rhs_x": rxu}
    down = shared | {"g2": g2d, "g3": g3d, "rhs_x": rxd}
    pack_both(x_near, x_cross, late_parts(layers), up, down, rows, gx)


def finish_kernel(*refs, gx):
    sat, hist, volume, storage, source = refs[:5]
    p0e, tote, frace, f0e, f1e, f2e, dpe, rhse, near, cross = refs[5:15]
    hole = refs[19 + len(SEAMS)]
    refs = refs[20 + len(SEAMS) :]
    new_p, residual, new_sat, new_hist, bottom = refs[:5]
    seams = dict(zip(SEAMS, refs[5:]))
    f1, rdiag, pa, pb = refs[5 + len(SEAMS) :]
    bottom[...] = hole[:, 0 : bottom.shape[1]]
    layers, rows, columns = sat.shape
    ext = layers + 2 * H
    unpack_both(near, cross, late_parts(layers), seams, gx)
    sfrac = seams["frac"]
    pa[0] = join(p0e[0], seams["p0"][0])
    pa[ext - 1] = join(p0e[ext - 1], seams["p0"][ext - 1])
    for first, last in ((1, H + 1), (ext - H - 1, ext - 1)):
        seam_faces(first, last, (p0e, tote, f0e, f1e, dpe), seams, f1, rdiag, pa)

    pressures = (pa, pb)
    fields = (rhse, f0e, f2e)
    inner = (H + 1, ext - H - 1)
    everywhere = slice(0, rows + 8)
    for number in range(1, SWEEPS + 1):
        old, new = pressures[(number - 1) % 2], pressures[number % 2]
        ranges = [(number, ext - number, everywhere)]
        if number == 1:
            ranges = [
                (number, inner[0], everywhere),
                (*inner, slice(rows, rows + 8)),
                (inner[1], ext - number, everywhere),
            ]
        for first, last, part in ranges:
            sweep_layers(number, first, last, old, new, fields, seams, f1, rdiag, part)
    field = pressures[SWEEPS % 2]

    def flow(face, p, p_next, f, f_next):
        water = face * (p - p_next)
        return (water, water * jnp.where(water > 0, f, f_next))

    def last_step(l, carry):
        below_w, below_g = carry
        e = l + H
        p = field[e]
        f = join(frace[e], sfrac[e])
        own_p = p[:rows]
        own_f = f[:rows]
        above_w, above_g = flow(f0e[e], own_p, field[e + 1][:rows], own_f, frace[e + 1])
        xw, xg = flow(f1[e], p, roll(p, -1, 0), f, roll(f, -1, 0))
        yw, yg = flow(f2e[e], own_p, roll(own_p, -1, 1), own_f, roll(own_f, -1, 1))
        water = above_w - below_w + (xw - roll(xw, 1, 0))[:rows] + yw - roll(yw, 1, 1)
        out = above_g - below_g + (xg - roll(xg, 1, 0))[:rows] + yg - roll(yg, 1, 1)
        new_p[l] = own_p
        residual[l] = rhse[e] - storage[l] * own_p - water
        src = source[l]
        gas = jnp.maximum(src, 0.0) + jnp.minimum(src, 0.0) * own_f
        s = sat[l] + volume[l] * (gas - out)
        new_sat[l] = s
        new_hist[l] = jnp.maximum(hist[l], s)
        return (above_w, above_g)

    first = flow(f0e[H - 1], field[H - 1][:rows], field[H][:rows], frace[H - 1], frace[H])
    loop(0, layers, last_step, first)


def swap(block, axis, first):
    pairs = [(i, i + 1) for i in range(first, lax.axis_size(axis) - 1, 2)]
    return lax.ppermute(block, axis, pairs + [(b, a) for a, b in pairs])


def pin(*shape, dtype=jnp.float32):
    return pltpu.VMEM(shape, dtype)


VMEM = pl.BlockSpec(memory_space=pltpu.VMEM)
HBM = pl.BlockSpec(memory_space=pltpu.HBM)


def call(kernel, outs, scratch, *args, space=VMEM, sems=0, aliases={}):
    as_struct = lambda s: s if hasattr(s, "dtype") else jax.ShapeDtypeStruct(s, jnp.float32)
    as_scratch = lambda s: pltpu.VMEM(as_struct(s).shape, as_struct(s).dtype)
    return pl.pallas_call(
        kernel,
        out_shape=[as_struct(s) for s in outs],
        in_specs=[space] * len(args),
        out_specs=[VMEM] * len(outs),
        scratch_shapes=[as_scratch(s) for s in scratch]
        + ([pltpu.SemaphoreType.DMA((sems,))] if sems else []),
        input_output_aliases=aliases,
        compiler_params=pltpu.CompilerParams(vmem_limit_bytes=24 * 1024 * 1024),
    )(*(pltpu.with_memory_space_constraint(a, pltpu.HBM) if space is HBM else a for a in args))


def body(
    pressure,
    saturation,
    sat_history,
    storage,
    step_volume,
    transmiss,
    perf_cell,
    perf_index,
    control,
    target,
):
    layers, rows, columns = pressure.shape
    ext = layers + 2 * H
    wells, perfs = perf_cell.shape
    block = (layers, rows, columns)
    pinned = pin(*block)
    ext_block = pin(ext, rows, columns)
    z_layers = sum(count for _, count in Z_PARTS)
    z_near, z_cross = (pin(n, rows, columns) for n in (z_layers, z_layers - 1))
    entries = wells * perfs
    early, late = (pin(tiles(f(layers)), 8, columns) for f in (early_parts, late_parts))
    seams = [pin(ext, 8, columns)] * len(SEAMS)
    *fields, near, cross, part, cell, per_perf, perf_values, own_hot = call(
        functools.partial(prepare_kernel, gz="gz"),
        [ext_block] * 7
        + [z_near, z_cross]
        + [
            pin(2, LANES),
            pin(1, entries, dtype=jnp.int32),
            pin(3, entries),
            pin(2, entries),
            pin(layers * rows, entries, dtype=jnp.bfloat16),
        ],
        [
            block,
            block,
            jax.ShapeDtypeStruct((perfs, wells), jnp.int32),
            (perfs, wells),
            jax.ShapeDtypeStruct((1, wells), jnp.int32),
            (1, wells),
            (perfs, LANES),
        ],
        saturation,
        sat_history,
        pressure,
        storage,
        transmiss,
        perf_cell.T,
        perf_index.T,
        control.reshape(1, wells),
        target.reshape(1, wells),
        space=HBM,
        sems=3 * -(-layers // LOADED) + 8,
    )
    cross = swap(cross, "gz", 1)
    near = swap(near, "gz", 0)
    p0e, tote, frace, stor, t0, t1, t2 = fields
    f0e, f1e, f2e, dpe, base, inverse, early_near, early_cross, part = call(
        functools.partial(faces_kernel, layers=layers, gx="gx"),
        [ext_block] * 6 + [early, early, pin(2, LANES)],
        [],
        *fields,
        part,
    )
    early_cross = swap(early_cross, "gx", 1)
    early_near = swap(early_near, "gx", 0)
    sums = part + near[-1, 0:2, 0:LANES]
    step = 2
    while step < lax.axis_size("gz"):
        pairs = [(i, i ^ step) for i in range(lax.axis_size("gz"))]
        tile = jnp.pad(sums, ((0, 8 - sums.shape[0]), (0, 0)))
        sums = sums + lax.ppermute(tile, "gz", pairs)[: sums.shape[0]]
        step *= 2
    early_near, near = lax.optimization_barrier((early_near, near))
    p0e, tote, frace, stor, f0e, f1e, f2e, dpe, base, inverse, perf_values, hot = call(
        functools.partial(halo_kernel, layers=layers, gx="gx", gz="gz"),
        [ext_block] * 10
        + [pin(2, entries), pin(2 * (H - 1) * rows, entries, dtype=jnp.bfloat16)],
        [],
        p0e,
        tote,
        frace,
        stor,
        f0e,
        f1e,
        f2e,
        dpe,
        base,
        inverse,
        t0,
        cross,
        near,
        cell,
        per_perf,
        perf_values,
        aliases={i: i for i in range(10)},
    )
    rhse, source, late_near, late_cross, hole = call(
        functools.partial(build_kernel, layers=layers, gx="gx"),
        [ext_block, pinned, late, late, pin(1, LANES)],
        [ext_block] * 8,
        p0e,
        stor,
        f0e,
        f1e,
        f2e,
        dpe,
        tote,
        base,
        inverse,
        sums,
        perf_values,
        hot,
        own_hot,
        cell,
        per_perf,
    )
    late_cross = swap(late_cross, "gx", 1)
    late_near = swap(late_near, "gx", 0)
    early_near, early_cross, rhse = lax.optimization_barrier((early_near, early_cross, rhse))
    joined = [pin(ext, rows + 8, columns)] * 4
    filled = call(
        functools.partial(seam_kernel, layers=layers, gx="gx"),
        seams + joined,
        [],
        early_near,
        early_cross,
        p0e,
        tote,
        f0e,
        f1e,
        f2e,
        dpe,
        rhse,
    )
    field, residual, new_sat, new_hist, bottom, *_ = call(
        functools.partial(finish_kernel, gx="gx"),
        [block] * 4 + [(1, wells)] + seams + joined,
        [],
        saturation,
        sat_history,
        step_volume,
        storage,
        source,
        p0e,
        tote,
        frace,
        f0e,
        f1e,
        f2e,
        dpe,
        rhse,
        late_near,
        late_cross,
        *filled,
        hole,
        aliases={15 + i: 5 + i for i in range(len(filled))},
    )
    return (field, residual, new_sat, new_hist, bottom.reshape(wells))


def solution(mesh):
    return jax.shard_map(
        body,
        mesh=mesh,
        in_specs=(
            P("gz", "gx", None),
            P("gz", "gx", None),
            P("gz", "gx", None),
            P("gz", "gx", None),
            P("gz", "gx", None),
            P(None, "gz", "gx", None),
            P("gx", None),
            P("gx", None),
            P("gx"),
            P("gx"),
        ),
        out_specs=(
            P("gz", "gx", None),
            P("gz", "gx", None),
            P("gz", "gx", None),
            P("gz", "gx", None),
            P("gx"),
        ),
        check_vma=False,
    )
```

```python
import functools

import jax
import jax.numpy as jnp
from jax import lax
from jax.experimental import pallas as pl
from jax.experimental.pallas import tpu as pltpu
from jax.sharding import PartitionSpec as P

SWEEPS = 4
H = SWEEPS + 1
LANES = 128
LOADED = 4

Z_PARTS = (
    ("p0", H),
    ("tot", H),
    ("t0", H),
    ("stor", H - 1),
    ("t1", H - 1),
    ("t2", H - 1),
    ("frac", 1),
    ("sums", 1),
)


def early_parts(layers):
    own = (H, layers)
    inner = (H, layers - 1)
    return (
        ("t1", *own),
        ("tot", *own),
        ("p0", *own),
        ("dp", *own),
        ("f0", *inner),
        ("f2", *own),
        ("f1", *own),
        ("frac", *own),
        ("p0_d2", *own),
        ("f0_d2", *inner),
        ("f2_d2", *own),
        ("dp_d2", *own),
    )


def late_parts(layers):
    top = H + layers
    both = lambda name, n: ((name, H - n, n), (name, top, n))
    faces = lambda name, n: ((name, H - n, n), (name, top - 1, n))
    ends = lambda name: ((name, 2, 1), (name, top + 2, 1))
    return (
        ("rhs", 3, layers + 4),
        *ends("rhs_x"),
        ("p1_d2", 3, layers + 4),
        ("g2", 4, layers + 2),
        ("g3", H, layers),
        *both("t1", H - 1),
        *both("tot", H - 1),
        *both("p0", H - 1),
        *both("dp", H - 3),
        *ends("dp_x"),
        *faces("f0", H - 2),
        *both("f2", H - 3),
        *both("f1", H - 3),
        *both("p0_d2", H - 3),
        *faces("f0_d2", 1),
        *both("dp2_x", 1),
    )


def tiles(parts):
    return -(-sum(count for _, _, count in parts) // 8)


SEAMS = ("f0", "f1", "f2", "tot", "dp", "p0", "frac", "p1", "rhs2", "rhs3")
PLACES = {
    "t1": ("f1", None, 7),
    "f1": ("f1", 0, 6),
    "tot": ("tot", 0, 7),
    "p0": ("p0", 0, 7),
    "dp": ("dp", 0, 7),
    "dp_d2": ("dp", 1, 6),
    "f0": ("f0", 0, 7),
    "f0_d2": ("f0", 1, 6),
    "f2": ("f2", 0, 7),
    "f2_d2": ("f2", 1, 6),
    "frac": ("frac", 0, 7),
    "p0_d2": ("p0", 1, 6),
    "p1_d2": ("p1", 1, 6),
    "rhs": ("rhs2", 0, 7),
    "rhs_x": ("rhs2", 0, 7),
    "dp_x": ("dp", 0, 7),
    "dp2_x": ("dp", 1, 6),
    "g2": ("rhs2", 1, 6),
    "g3": ("rhs3", 1, 6),
}


def pack(message, parts, refs, rows):
    at = 0
    for name, first, count in parts:
        for e in range(first, first + count):
            message[at // 8, at % 8 : at % 8 + 1, :] = refs[name][e, rows[name] : rows[name] + 1, :]
            at += 1


def pack_both(near, cross, parts, up, down, rows, gx):
    last = rows - 1
    outer = {name: 0 if PLACES[name][2] == 7 else 1 for name in PLACES}
    up_rows = {name: last - outer[name] for name in PLACES} | {"f1": last - 1}
    down_rows = dict(outer) | {"f1": 0}
    even = lax.axis_index(gx) % 2 == 0

    @pl.when(even)
    def _():
        pack(near, parts, up, up_rows)
        pack(cross, parts, down, down_rows)

    @pl.when(jnp.logical_not(even))
    def _():
        pack(cross, parts, up, up_rows)
        pack(near, parts, down, down_rows)


def unpack(message, parts, seams, side):
    at = 0
    for name, first, count in parts:
        seam, *places = PLACES[name]
        place = places[side]
        for e in range(first, first + count):
            if place is not None:
                seams[seam][e, place : place + 1, :] = message[at // 8, at % 8 : at % 8 + 1, :]
            at += 1


def unpack_one(message, parts, seams, axis, first):
    is_lower = lax.axis_index(axis) % 2 == first

    @pl.when(is_lower)
    def _():
        unpack(message, parts, seams, 0)

    @pl.when(jnp.logical_not(is_lower))
    def _():
        unpack(message, parts, seams, 1)


def unpack_both(near, cross, parts, seams, gx):
    even = lax.axis_index(gx) % 2 == 0

    @pl.when(even)
    def _():
        unpack(near, parts, seams, 0)
        unpack(cross, parts, seams, 1)

    @pl.when(jnp.logical_not(even))
    def _():
        unpack(cross, parts, seams, 0)
        unpack(near, parts, seams, 1)


def mobility(sat, history):
    trapped = history / (1.0 + 1.5 * history)
    excess = jnp.maximum(sat - trapped, 0.0)
    free_gas = 0.5 * (excess + jnp.sqrt(excess * excess + excess / 0.375))
    relperm = jnp.where(sat < history, free_gas * free_gas, sat * sat)
    gas = relperm / 0.5
    total = (1.0 - sat) * (1.0 - sat) + gas
    return (total, gas / total)


def roll(x, shift, axis):
    return pltpu.roll(x, shift % x.shape[axis], axis)


def loop(first, last, step, carry):
    count = last - first
    unroll = -(-count // -(-count // 16))
    groups = count // unroll

    def group(g, carry):
        for i in range(unroll):
            carry = step(first + g * unroll + i, carry)
        return carry

    carry = lax.fori_loop(0, groups, group, carry) if groups > 1 else group(0, carry)
    for index in range(first + groups * unroll, last):
        carry = step(index, carry)
    return carry


def split(x):
    high = x.astype(jnp.bfloat16)
    return (high, (x - high.astype(jnp.float32)).astype(jnp.bfloat16))


def at_places(cell, first_layer, layers, rows, columns):
    layer = cell // (rows * columns)
    row = (cell - layer * (rows * columns)) // columns
    place = (layer - first_layer) * rows + row
    return lax.broadcasted_iota(jnp.int32, (layers * rows, cell.shape[1]), 0) == place


def at_columns(cell, columns):
    return lax.broadcasted_iota(jnp.int32, (columns, cell.shape[1]), 0) == cell % columns


def gather(field, at_place, at_column):
    high, low = split(field)
    hot = at_column.astype(jnp.bfloat16)
    by_column = jnp.dot(high, hot, preferred_element_type=jnp.float32) + jnp.dot(
        low, hot, preferred_element_type=jnp.float32
    )
    return jnp.sum(jnp.where(at_place, by_column, 0.0), axis=0, keepdims=True)


def flatten(block, spread):
    perfs, wells = block.shape
    spread[...] = jnp.zeros(spread.shape, jnp.float32)
    spread[:, 0:wells] = block
    wide = spread[...]
    shift = wells
    while shift < LANES:
        wide = wide + roll(wide, shift, 1)
        shift *= 2
    each = LANES // wells
    entry = lax.broadcasted_iota(jnp.int32, (perfs, LANES), 0)
    group = lax.broadcasted_iota(jnp.int32, (perfs, LANES), 1) // wells
    tiles = [
        jnp.sum(jnp.where(entry == first + group, wide, 0.0), axis=0, keepdims=True)
        for first in range(0, perfs, each)
    ]
    return jnp.concatenate(tiles, axis=1)


def prepare_kernel(
    sat,
    hist,
    pressure,
    storage,
    trans,
    cell_in,
    index_in,
    control_in,
    target_in,
    p0e,
    tote,
    frace,
    stor,
    t0,
    t1,
    t2,
    near,
    cross,
    sums,
    cell,
    wells,
    perfs,
    hot,
    sat_v,
    hist_v,
    cell_v,
    index_v,
    control_v,
    target_v,
    spread,
    sems,
    *,
    gz,
):
    layers, rows, columns = pressure.shape
    ext = layers + 2 * H
    own = pl.ds(H, layers)
    parts = [(l, min(LOADED, layers - l)) for l in range(0, layers, LOADED)]
    in_parts = [
        (source.at[pl.ds(l, n)], target.at[pl.ds(offset + l, n)])
        for source, target, offset in ((sat, sat_v, 0), (hist, hist_v, 0), (pressure, p0e, H))
        for l, n in parts
    ]
    small = [(cell_in, cell_v), (index_in, index_v), (control_in, control_v), (target_in, target_v)]
    large = [
        (trans.at[0], t0.at[own]),
        (storage, stor.at[own]),
        (trans.at[1], t1.at[own]),
        (trans.at[2], t2.at[own]),
    ]
    copies = [
        pltpu.make_async_copy(a, b, sems.at[i])
        for i, (a, b) in enumerate(in_parts + small + large)
    ]
    for copy in copies:
        copy.start()

    def layer_step(l, carry):
        t, f = mobility(sat_v[l], hist_v[l])
        tote[l + H] = t
        frace[l + H] = f
        return carry

    for i, (l, n) in enumerate(parts):
        copies[i].wait()
        copies[len(parts) + i].wait()
        loop(l, l + n, layer_step, 0)
    for copy in copies[2 * len(parts) : -len(large)]:
        copy.wait()
    count, group = cell_v.shape
    cell[...] = flatten(cell_v[...].astype(jnp.float32), spread).astype(jnp.int32)
    wells[0:1, :] = flatten(index_v[...], spread)
    wells[1:2, :] = flatten(jnp.broadcast_to(target_v[...], (count, group)), spread)
    wells[2:3, :] = flatten(
        jnp.broadcast_to(control_v[...].astype(jnp.float32), (count, group)), spread
    )
    at_place = at_places(cell[...], lax.axis_index(gz) * layers, layers, rows, columns)
    at_column = at_columns(cell[...], columns)
    hot[...] = at_place.astype(jnp.bfloat16)
    flat = (layers * rows, columns)
    weight = wells[0:1, :] * gather(tote[own].reshape(flat), at_place, at_column)
    cell_p = gather(p0e[own].reshape(flat), at_place, at_column)
    perfs[0:1, :] = weight
    perfs[1:2, :] = cell_p
    for i, value in enumerate((weight * cell_p, weight)):
        part = value[:, 0:LANES]
        for lane in range(LANES, value.shape[1], LANES):
            part = part + value[:, lane : lane + LANES]
        shift = LANES // 2
        while shift >= group:
            part = part + roll(part, shift, 1)
            shift //= 2
        sums[i : i + 1, :] = part
    for copy in copies[-len(large) :]:
        copy.wait()
    even = lax.axis_index(gz) % 2 == 0
    refs = {"p0": p0e, "tot": tote, "t0": t0, "stor": stor, "t1": t1, "t2": t2, "frac": frace}
    for message, is_top in ((near, even), (cross, jnp.logical_not(even))):
        at = 0
        for name, count in Z_PARTS:
            if name == "sums" and message is cross:
                continue
            if name == "sums":
                message[at] = jnp.zeros((rows, columns), jnp.float32)
                message[at, 0:2, 0:LANES] = sums[...]
            else:
                edge = jnp.where(is_top, H + layers - count, H)
                message[pl.ds(at, count)] = refs[name][pl.ds(edge, count)]
            at += count


def masks(rows, columns):
    row = lax.broadcasted_iota(jnp.int32, (rows, columns), 0)
    column = lax.broadcasted_iota(jnp.int32, (rows, columns), 1)
    return (row == rows - 1, column == columns - 1)


def lateral_faces(tot, t1, t2, store, last_row, last_column, top_x):
    along = jnp.where(last_row, 0.0, t1) * 0.5 * (tot + roll(tot, -1, 0))
    across = jnp.where(last_column, 0.0, t2) * 0.5 * (tot + roll(tot, -1, 1))
    part = store + along + roll(along, 1, 0) + across + roll(across, 1, 1)
    return (jnp.where(last_row, jnp.where(top_x, 0.0, t1), along), across, part)


def is_last(axis):
    return lax.axis_index(axis) == lax.axis_size(axis) - 1


def first_sweep(e, p0e, stor, f0e, f1e, f2e, dpe, last_row):
    above = f0e[e]
    below = f0e[e - 1]
    along = jnp.where(last_row, 0.0, f1e[e])
    across = f2e[e]
    diag = dpe[e] + above + below
    p = p0e[e]
    base = stor[e] * p + above * p0e[e + 1] + below * p0e[e - 1]
    base = base + along * roll(p, -1, 0) + roll(along * p, 1, 0)
    base = base + across * roll(p, -1, 1) + roll(across * p, 1, 1)
    return (base, jnp.where(diag > 0.0, 1.0 / diag, 0.0))


def faces_kernel(*refs, layers, gx):
    p0e, tote, frace, stor, t0, t1, t2, part = refs[:8]
    f0e, f1e, f2e, dpe, base, inverse, near, cross, sums = refs[8:]
    _, rows, columns = p0e.shape
    last_row, last_column = masks(rows, columns)
    top_x = is_last(gx)

    def step(e, carry):
        tot = tote[e]
        f0e[e] = t0[e] * 0.5 * (tot + tote[e + 1])
        f1e[e], f2e[e], dpe[e] = lateral_faces(
            tot, t1[e], t2[e], stor[e], last_row, last_column, top_x
        )
        return carry

    loop(H, H + layers, step, 0)
    sums[...] = part[...]
    refs = {"t1": f1e, "tot": tote, "p0": p0e, "dp": dpe, "f0": f0e, "f2": f2e, "f1": f1e}
    refs |= {"frac": frace, "p0_d2": p0e, "f0_d2": f0e, "f2_d2": f2e, "dp_d2": dpe}
    pack_both(near, cross, early_parts(layers), refs, refs, rows, gx)

    def sweep_step(e, carry):
        base[e], inverse[e] = first_sweep(e, p0e, stor, f0e, f1e, f2e, dpe, last_row)
        return carry

    loop(H + 1, H + layers - 1, sweep_step, 0)


def well_holes(sums, wells):
    repeat = lambda x: jnp.concatenate([x] * (wells.shape[1] // LANES), axis=1)
    goal = wells[1:2, :]
    return jnp.where(
        wells[2:3, :] == 0.0, (goal + repeat(sums[0:1, :])) / repeat(sums[1:2, :]), goal
    )


def join(a, b):
    return jnp.concatenate([a, b], axis=0)


def seam_faces(first, last, fields, seams, f1, inverse, p):
    p0e, tote, f0e, f1e, dpe = fields
    rows, columns = p0e.shape[1:]
    row = lax.broadcasted_iota(jnp.int32, (rows + 8, columns), 0)
    edge = (row == rows - 1) | (row == rows + 7)

    def step(e, below):
        tot = join(tote[e], seams["tot"][e])
        mixed = join(f1e[e], seams["f1"][e])
        border = jnp.where(edge, mixed * 0.5 * (tot + roll(tot, -1, 0)), 0.0)
        f1[e] = jnp.where(edge, border, mixed)
        above = join(f0e[e], seams["f0"][e])
        diag = join(dpe[e], seams["dp"][e]) + above + below + border + roll(border, 1, 0)
        inverse[e] = jnp.where(diag > 0.0, 1.0 / diag, 0.0)
        p[e] = join(p0e[e], seams["p0"][e])
        return above

    loop(first, last, step, join(f0e[first - 1], seams["f0"][first - 1]))


def sweep_layers(number, first, last, old, new, fields, seams, f1, inverse, part):
    rhse, f0e, f2e = fields
    rows, columns = rhse.shape[1:]
    row = lax.broadcasted_iota(jnp.int32, (rows + 8, columns), 0)
    beyond = (row == rows + 1) | (row == rows + 6)
    blank = jnp.zeros((rows, columns), jnp.float32)

    def step(e, carry):
        below, p = carry
        above = old[e + 1]
        face = join(f0e[e], seams["f0"][e])
        x = f1[e]
        y = join(f2e[e], seams["f2"][e])
        side = seams["rhs2"][e]
        if number == 3:
            side = jnp.where(beyond[rows:], seams["rhs3"][e], side)
        total = join(rhse[e], side) + below + face * above
        total = total + x * roll(p, -1, 0) + roll(x * p, 1, 0)
        total = total + y * roll(p, -1, 1) + roll(y * p, 1, 1)
        value = total * inverse[e]
        if number == 1:
            value = jnp.where(beyond, join(blank, seams["p1"][e]), value)
        new[e, part] = value[part]
        return (face * p, above)

    start = join(f0e[first - 1], seams["f0"][first - 1]) * old[first - 1]
    loop(first, last, step, (start, old[first]))


def seam_kernel(near, cross, *refs, layers, gx):
    p0e, tote, f0e, f1e, f2e, dpe, rhse = refs[:7]
    refs = refs[7:]
    seams = dict(zip(SEAMS, refs))
    f1, inverse, p, p1 = refs[len(SEAMS) :]
    for seam in seams.values():
        seam[...] = jnp.zeros(seam.shape, jnp.float32)
    unpack_both(near, cross, early_parts(layers), seams, gx)
    inner = (H + 1, H + layers - 1)
    seam_faces(*inner, (p0e, tote, f0e, f1e, dpe), seams, f1, inverse, p)
    for e in (H, H + layers - 1):
        p[e] = join(p0e[e], jnp.zeros_like(seams["p0"][e]))
    own = slice(0, p0e.shape[1])
    sweep_layers(1, *inner, p, p1, (rhse, f0e, f2e), seams, f1, inverse, own)


def halo_kernel(*refs, layers, gx, gz):
    own_t0, cross, near, cell, wells, own_perfs = refs[10:16]
    p0e, tote, frace, stor, f0e, f1e, f2e, dpe, base, inverse, perfs, hot = refs[16:]
    ext, rows, columns = p0e.shape
    even = lax.axis_index(gz) % 2 == 0
    top_z = is_last(gz)
    top_x = is_last(gx)
    last_row, last_column = masks(rows, columns)
    where = {}
    at = 0
    for name, count in Z_PARTS:
        where[name] = (at, count)
        at += count

    def halo(name, e):
        at, count = where[name]
        low = e < H
        at = at + e - (H - count if low else H + layers)
        one, two = (near[at], cross[at])
        return jnp.where(even, two, one) if low else jnp.where(even, one, two)

    for name, target in (("p0", p0e), ("tot", tote), ("frac", frace), ("stor", stor)):
        count = where[name][1]
        for e in (*range(H - count, H), *range(H + layers, H + layers + count)):
            target[e] = halo(name, e)
    f0e[H + layers - 1] = jnp.where(top_z, 0.0, own_t0[H + layers - 1]) * 0.5 * (
        tote[H + layers - 1] + tote[H + layers]
    )
    for e in (*range(0, H), *range(H + layers, ext - 1)):
        f0e[e] = halo("t0", e) * 0.5 * (tote[e] + tote[e + 1])
    for e in (*range(1, H), *range(H + layers, ext - 1)):
        f1e[e], f2e[e], dpe[e] = lateral_faces(
            tote[e], halo("t1", e), halo("t2", e), stor[e], last_row, last_column, top_x
        )
    for e in (*range(1, H + 1), *range(H + layers - 1, ext - 1)):
        base[e], inverse[e] = first_sweep(e, p0e, stor, f0e, f1e, f2e, dpe, last_row)
    width = H - 1
    first = lax.axis_index(gz) * layers
    sides = ((1, first - width), (H + layers, first + layers))
    at_place = [at_places(cell[...], layer, width, rows, columns) for _, layer in sides]
    at_place = jnp.concatenate(at_place, axis=0)
    at_column = at_columns(cell[...], columns)
    hot[...] = at_place.astype(jnp.bfloat16)
    flat = (width * rows, columns)
    both = lambda ref: join(*(ref[e : e + width].reshape(flat) for e, _ in sides))
    weight = wells[0:1, :] * gather(both(tote), at_place, at_column)
    perfs[0:1, :] = own_perfs[0:1, :] + weight
    perfs[1:2, :] = own_perfs[1:2, :] + gather(both(p0e), at_place, at_column)


def build_kernel(*refs, layers, gx):
    p0e, stor, f0e, f1e, f2e, dpe, tote, base, inverse, sums, perfs, hot, own_hot = refs[:13]
    cell, wells, rhse, source, x_near, x_cross, bottom = refs[13:20]
    p1, g2u, g2d, g3u, g3d, rxu, rxd, dpx = refs[20:]
    ext, rows, columns = p0e.shape
    last_row, _ = masks(rows, columns)
    hole = well_holes(sums[...], wells[...])
    bottom[...] = hole[:, 0:LANES]
    rate = perfs[0:1, :] * (hole - perfs[1:2, :])
    pieces = split(jnp.where(at_columns(cell[...], columns), rate, 0.0))

    def scatter(mask):
        spread = [
            lax.dot_general(
                mask, piece, (((1,), (1,)), ((), ())), preferred_element_type=jnp.float32
            )
            for piece in pieces
        ]
        return (spread[0] + spread[1]).reshape(-1, rows, columns)

    width = H - 1
    inside = scatter(own_hot[...])
    outside = scatter(hot[...])
    source[...] = inside
    rhse[H : ext - H] = inside
    rhse[1:H] = outside[:width]
    rhse[ext - H : ext - 1] = outside[width:]

    def first_step(e, carry):
        wells_rate = rhse[e]
        p1[e] = (base[e] + wells_rate) * inverse[e]
        rhse[e] = stor[e] * p0e[e] + wells_rate
        return carry

    loop(1, ext - 1, first_step, 0)

    def second_step(e, carry):
        along = jnp.where(last_row, 0.0, f1e[e])
        across = f2e[e]
        p = p1[e]
        rhs = rhse[e]
        lower = roll(along * p, 1, 0)
        upper = along * roll(p, -1, 0)
        g2u[e] = rhs + lower
        g2d[e] = rhs + upper
        new = rhs + lower + upper + f0e[e] * p1[e + 1] + f0e[e - 1] * p1[e - 1]
        new = new + across * roll(p, -1, 1) + roll(across * p, 1, 1)
        p2 = new * inverse[e]
        g3u[e] = rhs + roll(along * p2, 1, 0)
        g3d[e] = rhs + along * roll(p2, -1, 0)
        return carry

    loop(H - 1, ext - H + 1, second_step, 0)

    for e, beside, face in ((2, 1, 1), (ext - 3, ext - 2, ext - 3)):
        along = jnp.where(last_row, 0.0, f1e[e])
        across = f2e[e]
        p = p0e[e]
        rhs = rhse[e] + f0e[face] * p0e[beside]
        rhs = rhs + across * roll(p, -1, 1) + roll(across * p, 1, 1)
        rxu[e] = rhs + roll(along * p, 1, 0)
        rxd[e] = rhs + along * roll(p, -1, 0)
        dpx[e] = dpe[e] + f0e[face]

    shared = {"t1": f1e, "tot": tote, "p0": p0e, "dp": dpe, "f0": f0e, "f2": f2e, "f1": f1e}
    shared |= {"p0_d2": p0e, "f0_d2": f0e, "f2_d2": f2e, "dp_d2": dpe, "rhs": rhse, "p1_d2": p1}
    for e, beside, face in ((H - 1, H - 2, H - 2), (ext - H, ext - H + 1, ext - H)):
        across = f2e[e]
        p = p1[e]
        beyond = f0e[face] * p1[beside] + across * roll(p, -1, 1) + roll(across * p, 1, 1)
        g2u[e] = g2u[e] + beyond
        g2d[e] = g2d[e] + beyond
        dpx[e] = dpe[e] + f0e[face]
    shared["dp_x"] = shared["dp2_x"] = dpx
    up = shared | {"g2": g2u, "g3": g3u, "rhs_x": rxu}
    down = shared | {"g2": g2d, "g3": g3d, "rhs_x": rxd}
    pack_both(x_near, x_cross, late_parts(layers), up, down, rows, gx)


def near_kernel(near, *refs, layers, gx):
    unpack_one(near, late_parts(layers), dict(zip(SEAMS, refs[len(SEAMS) :])), gx, 0)


def finish_kernel(*refs, gx):
    sat, hist, volume, storage, source = refs[:5]
    p0e, tote, frace, f0e, f1e, f2e, dpe, rhse, cross = refs[5:14]
    hole = refs[18 + len(SEAMS)]
    refs = refs[19 + len(SEAMS) :]
    new_p, residual, new_sat, new_hist, bottom = refs[:5]
    seams = dict(zip(SEAMS, refs[5:]))
    f1, rdiag, pa, pb = refs[5 + len(SEAMS) :]
    bottom[...] = hole[:, 0 : bottom.shape[1]]
    layers, rows, columns = sat.shape
    ext = layers + 2 * H
    unpack_one(cross, late_parts(layers), seams, gx, 1)
    sfrac = seams["frac"]
    pa[0] = join(p0e[0], seams["p0"][0])
    pa[ext - 1] = join(p0e[ext - 1], seams["p0"][ext - 1])
    for first, last in ((1, H + 1), (ext - H - 1, ext - 1)):
        seam_faces(first, last, (p0e, tote, f0e, f1e, dpe), seams, f1, rdiag, pa)

    pressures = (pa, pb)
    fields = (rhse, f0e, f2e)
    inner = (H + 1, ext - H - 1)
    everywhere = slice(0, rows + 8)
    for number in range(1, SWEEPS + 1):
        old, new = pressures[(number - 1) % 2], pressures[number % 2]
        ranges = [(number, ext - number, everywhere)]
        if number == 1:
            ranges = [
                (number, inner[0], everywhere),
                (*inner, slice(rows, rows + 8)),
                (inner[1], ext - number, everywhere),
            ]
        for first, last, part in ranges:
            sweep_layers(number, first, last, old, new, fields, seams, f1, rdiag, part)
    field = pressures[SWEEPS % 2]

    def flow(face, p, p_next, f, f_next):
        water = face * (p - p_next)
        return (water, water * jnp.where(water > 0, f, f_next))

    def last_step(l, carry):
        below_w, below_g = carry
        e = l + H
        p = field[e]
        f = join(frace[e], sfrac[e])
        own_p = p[:rows]
        own_f = f[:rows]
        above_w, above_g = flow(f0e[e], own_p, field[e + 1][:rows], own_f, frace[e + 1])
        xw, xg = flow(f1[e], p, roll(p, -1, 0), f, roll(f, -1, 0))
        yw, yg = flow(f2e[e], own_p, roll(own_p, -1, 1), own_f, roll(own_f, -1, 1))
        water = above_w - below_w + (xw - roll(xw, 1, 0))[:rows] + yw - roll(yw, 1, 1)
        out = above_g - below_g + (xg - roll(xg, 1, 0))[:rows] + yg - roll(yg, 1, 1)
        new_p[l] = own_p
        residual[l] = rhse[e] - storage[l] * own_p - water
        src = source[l]
        gas = jnp.maximum(src, 0.0) + jnp.minimum(src, 0.0) * own_f
        s = sat[l] + volume[l] * (gas - out)
        new_sat[l] = s
        new_hist[l] = jnp.maximum(hist[l], s)
        return (above_w, above_g)

    first = flow(f0e[H - 1], field[H - 1][:rows], field[H][:rows], frace[H - 1], frace[H])
    loop(0, layers, last_step, first)


def swap(block, axis, first):
    pairs = [(i, i + 1) for i in range(first, lax.axis_size(axis) - 1, 2)]
    return lax.ppermute(block, axis, pairs + [(b, a) for a, b in pairs])


def pin(*shape, dtype=jnp.float32):
    return pltpu.VMEM(shape, dtype)


VMEM = pl.BlockSpec(memory_space=pltpu.VMEM)
HBM = pl.BlockSpec(memory_space=pltpu.HBM)


def call(kernel, outs, scratch, *args, space=VMEM, sems=0, aliases={}):
    as_struct = lambda s: s if hasattr(s, "dtype") else jax.ShapeDtypeStruct(s, jnp.float32)
    as_scratch = lambda s: pltpu.VMEM(as_struct(s).shape, as_struct(s).dtype)
    return pl.pallas_call(
        kernel,
        out_shape=[as_struct(s) for s in outs],
        in_specs=[space] * len(args),
        out_specs=[VMEM] * len(outs),
        scratch_shapes=[as_scratch(s) for s in scratch]
        + ([pltpu.SemaphoreType.DMA((sems,))] if sems else []),
        input_output_aliases=aliases,
        compiler_params=pltpu.CompilerParams(vmem_limit_bytes=24 * 1024 * 1024),
    )(*(pltpu.with_memory_space_constraint(a, pltpu.HBM) if space is HBM else a for a in args))


def body(
    pressure,
    saturation,
    sat_history,
    storage,
    step_volume,
    transmiss,
    perf_cell,
    perf_index,
    control,
    target,
):
    layers, rows, columns = pressure.shape
    ext = layers + 2 * H
    wells, perfs = perf_cell.shape
    block = (layers, rows, columns)
    pinned = pin(*block)
    ext_block = pin(ext, rows, columns)
    z_layers = sum(count for _, count in Z_PARTS)
    z_near, z_cross = (pin(n, rows, columns) for n in (z_layers, z_layers - 1))
    entries = wells * perfs
    early, late = (pin(tiles(f(layers)), 8, columns) for f in (early_parts, late_parts))
    seams = [pin(ext, 8, columns)] * len(SEAMS)
    *fields, near, cross, part, cell, per_perf, perf_values, own_hot = call(
        functools.partial(prepare_kernel, gz="gz"),
        [ext_block] * 7
        + [z_near, z_cross]
        + [
            pin(2, LANES),
            pin(1, entries, dtype=jnp.int32),
            pin(3, entries),
            pin(2, entries),
            pin(layers * rows, entries, dtype=jnp.bfloat16),
        ],
        [
            block,
            block,
            jax.ShapeDtypeStruct((perfs, wells), jnp.int32),
            (perfs, wells),
            jax.ShapeDtypeStruct((1, wells), jnp.int32),
            (1, wells),
            (perfs, LANES),
        ],
        saturation,
        sat_history,
        pressure,
        storage,
        transmiss,
        perf_cell.T,
        perf_index.T,
        control.reshape(1, wells),
        target.reshape(1, wells),
        space=HBM,
        sems=3 * -(-layers // LOADED) + 8,
    )
    cross = swap(cross, "gz", 1)
    near = swap(near, "gz", 0)
    p0e, tote, frace, stor, t0, t1, t2 = fields
    f0e, f1e, f2e, dpe, base, inverse, early_near, early_cross, part = call(
        functools.partial(faces_kernel, layers=layers, gx="gx"),
        [ext_block] * 6 + [early, early, pin(2, LANES)],
        [],
        *fields,
        part,
    )
    early_cross = swap(early_cross, "gx", 1)
    early_near = swap(early_near, "gx", 0)
    sums = part + near[-1, 0:2, 0:LANES]
    step = 2
    while step < lax.axis_size("gz"):
        pairs = [(i, i ^ step) for i in range(lax.axis_size("gz"))]
        tile = jnp.pad(sums, ((0, 8 - sums.shape[0]), (0, 0)))
        sums = sums + lax.ppermute(tile, "gz", pairs)[: sums.shape[0]]
        step *= 2
    early_near, near = lax.optimization_barrier((early_near, near))
    p0e, tote, frace, stor, f0e, f1e, f2e, dpe, base, inverse, perf_values, hot = call(
        functools.partial(halo_kernel, layers=layers, gx="gx", gz="gz"),
        [ext_block] * 10
        + [pin(2, entries), pin(2 * (H - 1) * rows, entries, dtype=jnp.bfloat16)],
        [],
        p0e,
        tote,
        frace,
        stor,
        f0e,
        f1e,
        f2e,
        dpe,
        base,
        inverse,
        t0,
        cross,
        near,
        cell,
        per_perf,
        perf_values,
        aliases={i: i for i in range(10)},
    )
    rhse, source, late_near, late_cross, hole = call(
        functools.partial(build_kernel, layers=layers, gx="gx"),
        [ext_block, pinned, late, late, pin(1, LANES)],
        [ext_block] * 8,
        p0e,
        stor,
        f0e,
        f1e,
        f2e,
        dpe,
        tote,
        base,
        inverse,
        sums,
        perf_values,
        hot,
        own_hot,
        cell,
        per_perf,
    )
    late_cross = swap(late_cross, "gx", 1)
    late_near = swap(late_near, "gx", 0)
    early_near, early_cross, rhse = lax.optimization_barrier((early_near, early_cross, rhse))
    joined = [pin(ext, rows + 8, columns)] * 4
    filled = call(
        functools.partial(seam_kernel, layers=layers, gx="gx"),
        seams + joined,
        [],
        early_near,
        early_cross,
        p0e,
        tote,
        f0e,
        f1e,
        f2e,
        dpe,
        rhse,
    )
    filled = list(filled)
    count = len(SEAMS)
    filled[:count] = call(
        functools.partial(near_kernel, layers=layers, gx="gx"),
        seams,
        [],
        late_near,
        *filled[:count],
        aliases={1 + i: i for i in range(count)},
    )
    field, residual, new_sat, new_hist, bottom, *_ = call(
        functools.partial(finish_kernel, gx="gx"),
        [block] * 4 + [(1, wells)] + seams + joined,
        [],
        saturation,
        sat_history,
        step_volume,
        storage,
        source,
        p0e,
        tote,
        frace,
        f0e,
        f1e,
        f2e,
        dpe,
        rhse,
        late_cross,
        *filled,
        hole,
        aliases={14 + i: 5 + i for i in range(len(filled))},
    )
    return (field, residual, new_sat, new_hist, bottom.reshape(wells))


def solution(mesh):
    return jax.shard_map(
        body,
        mesh=mesh,
        in_specs=(
            P("gz", "gx", None),
            P("gz", "gx", None),
            P("gz", "gx", None),
            P("gz", "gx", None),
            P("gz", "gx", None),
            P(None, "gz", "gx", None),
            P("gx", None),
            P("gx", None),
            P("gx"),
            P("gx"),
        ),
        out_specs=(
            P("gz", "gx", None),
            P("gz", "gx", None),
            P("gz", "gx", None),
            P("gz", "gx", None),
            P("gx"),
        ),
        check_vma=False,
    )
```

```python
import functools

import jax
import jax.numpy as jnp
from jax import lax
from jax.experimental import pallas as pl
from jax.experimental.pallas import tpu as pltpu
from jax.sharding import PartitionSpec as P

SWEEPS = 4
H = SWEEPS + 1
LANES = 128
LOADED = 4

Z_PARTS = (
    ("p0", H),
    ("tot", H),
    ("t0", H),
    ("stor", H - 1),
    ("t1", H - 1),
    ("t2", H - 1),
    ("frac", 1),
    ("sums", 1),
)


def early_parts(layers):
    own = (H, layers)
    inner = (H, layers - 1)
    return (
        ("t1", *own),
        ("tot", *own),
        ("p0", *own),
        ("dp", *own),
        ("f0", *inner),
        ("f2", *own),
        ("f1", *own),
        ("frac", *own),
        ("p0_d2", *own),
        ("f0_d2", *inner),
        ("f2_d2", *own),
        ("dp_d2", *own),
    )


def late_parts(layers):
    top = H + layers
    both = lambda name, n: ((name, H - n, n), (name, top, n))
    faces = lambda name, n: ((name, H - n, n), (name, top - 1, n))
    ends = lambda name: ((name, 2, 1), (name, top + 2, 1))
    return (
        ("rhs", 3, layers + 4),
        *ends("rhs_x"),
        ("p1_d2", 3, layers + 4),
        ("g2", 4, layers + 2),
        ("g3", H, layers),
        *both("t1", H - 1),
        *both("tot", H - 1),
        *both("p0", H - 1),
        *both("dp", H - 3),
        *ends("dp_x"),
        *faces("f0", H - 2),
        *both("f2", H - 3),
        *both("f1", H - 3),
        *both("p0_d2", H - 3),
        *faces("f0_d2", 1),
        *both("dp2_x", 1),
    )


def tiles(parts):
    return -(-sum(count for _, _, count in parts) // 8)


SEAMS = ("f0", "f1", "f2", "tot", "dp", "p0", "frac", "p1", "rhs2", "rhs3")
PLACES = {
    "t1": ("f1", None, 7),
    "f1": ("f1", 0, 6),
    "tot": ("tot", 0, 7),
    "p0": ("p0", 0, 7),
    "dp": ("dp", 0, 7),
    "dp_d2": ("dp", 1, 6),
    "f0": ("f0", 0, 7),
    "f0_d2": ("f0", 1, 6),
    "f2": ("f2", 0, 7),
    "f2_d2": ("f2", 1, 6),
    "frac": ("frac", 0, 7),
    "p0_d2": ("p0", 1, 6),
    "p1_d2": ("p1", 1, 6),
    "rhs": ("rhs2", 0, 7),
    "rhs_x": ("rhs2", 0, 7),
    "dp_x": ("dp", 0, 7),
    "dp2_x": ("dp", 1, 6),
    "g2": ("rhs2", 1, 6),
    "g3": ("rhs3", 1, 6),
}


def pack(message, parts, refs, rows):
    at = 0
    for name, first, count in parts:
        for e in range(first, first + count):
            message[at // 8, at % 8 : at % 8 + 1, :] = refs[name][e, rows[name] : rows[name] + 1, :]
            at += 1


def pack_both(near, cross, parts, up, down, rows, gx):
    last = rows - 1
    outer = {name: 0 if PLACES[name][2] == 7 else 1 for name in PLACES}
    up_rows = {name: last - outer[name] for name in PLACES} | {"f1": last - 1}
    down_rows = dict(outer) | {"f1": 0}
    even = lax.axis_index(gx) % 2 == 0

    @pl.when(even)
    def _():
        pack(near, parts, up, up_rows)
        pack(cross, parts, down, down_rows)

    @pl.when(jnp.logical_not(even))
    def _():
        pack(cross, parts, up, up_rows)
        pack(near, parts, down, down_rows)


def unpack(message, parts, seams, side):
    at = 0
    for name, first, count in parts:
        seam, *places = PLACES[name]
        place = places[side]
        for e in range(first, first + count):
            if place is not None:
                seams[seam][e, place : place + 1, :] = message[at // 8, at % 8 : at % 8 + 1, :]
            at += 1


def unpack_both(near, cross, parts, seams, gx):
    even = lax.axis_index(gx) % 2 == 0

    @pl.when(even)
    def _():
        unpack(near, parts, seams, 0)
        unpack(cross, parts, seams, 1)

    @pl.when(jnp.logical_not(even))
    def _():
        unpack(cross, parts, seams, 0)
        unpack(near, parts, seams, 1)


def mobility(sat, history):
    trapped = history / (1.0 + 1.5 * history)
    excess = jnp.maximum(sat - trapped, 0.0)
    free_gas = 0.5 * (excess + jnp.sqrt(excess * excess + excess / 0.375))
    relperm = jnp.where(sat < history, free_gas * free_gas, sat * sat)
    gas = relperm / 0.5
    total = (1.0 - sat) * (1.0 - sat) + gas
    return (total, gas / total)


def roll(x, shift, axis):
    return pltpu.roll(x, shift % x.shape[axis], axis)


def loop(first, last, step, carry):
    count = last - first
    unroll = -(-count // -(-count // 26))
    groups = count // unroll

    def group(g, carry):
        for i in range(unroll):
            carry = step(first + g * unroll + i, carry)
        return carry

    carry = lax.fori_loop(0, groups, group, carry) if groups > 1 else group(0, carry)
    for index in range(first + groups * unroll, last):
        carry = step(index, carry)
    return carry


def split(x):
    high = x.astype(jnp.bfloat16)
    return (high, (x - high.astype(jnp.float32)).astype(jnp.bfloat16))


def at_places(cell, first_layer, layers, rows, columns):
    layer = cell // (rows * columns)
    row = (cell - layer * (rows * columns)) // columns
    place = (layer - first_layer) * rows + row
    return lax.broadcasted_iota(jnp.int32, (layers * rows, cell.shape[1]), 0) == place


def at_columns(cell, columns):
    return lax.broadcasted_iota(jnp.int32, (columns, cell.shape[1]), 0) == cell % columns


def gather(field, at_place, at_column):
    high, low = split(field)
    hot = at_column.astype(jnp.bfloat16)
    by_column = jnp.dot(high, hot, preferred_element_type=jnp.float32) + jnp.dot(
        low, hot, preferred_element_type=jnp.float32
    )
    return jnp.sum(jnp.where(at_place, by_column, 0.0), axis=0, keepdims=True)


def flatten(block, spread):
    perfs, wells = block.shape
    spread[...] = jnp.zeros(spread.shape, jnp.float32)
    spread[:, 0:wells] = block
    wide = spread[...]
    shift = wells
    while shift < LANES:
        wide = wide + roll(wide, shift, 1)
        shift *= 2
    each = LANES // wells
    entry = lax.broadcasted_iota(jnp.int32, (perfs, LANES), 0)
    group = lax.broadcasted_iota(jnp.int32, (perfs, LANES), 1) // wells
    tiles = [
        jnp.sum(jnp.where(entry == first + group, wide, 0.0), axis=0, keepdims=True)
        for first in range(0, perfs, each)
    ]
    return jnp.concatenate(tiles, axis=1)


def prepare_kernel(
    sat,
    hist,
    pressure,
    storage,
    trans,
    cell_in,
    index_in,
    control_in,
    target_in,
    p0e,
    tote,
    frace,
    stor,
    t0,
    t1,
    t2,
    near,
    cross,
    sums,
    cell,
    wells,
    perfs,
    hot,
    sat_v,
    hist_v,
    cell_v,
    index_v,
    control_v,
    target_v,
    spread,
    sems,
    *,
    gz,
):
    layers, rows, columns = pressure.shape
    ext = layers + 2 * H
    own = pl.ds(H, layers)
    parts = [(l, min(LOADED, layers - l)) for l in range(0, layers, LOADED)]
    in_parts = [
        (source.at[pl.ds(l, n)], target.at[pl.ds(offset + l, n)])
        for source, target, offset in ((sat, sat_v, 0), (hist, hist_v, 0), (pressure, p0e, H))
        for l, n in parts
    ]
    small = [(cell_in, cell_v), (index_in, index_v), (control_in, control_v), (target_in, target_v)]
    large = [
        (trans.at[0], t0.at[own]),
        (storage, stor.at[own]),
        (trans.at[1], t1.at[own]),
        (trans.at[2], t2.at[own]),
    ]
    copies = [
        pltpu.make_async_copy(a, b, sems.at[i])
        for i, (a, b) in enumerate(in_parts + small + large)
    ]
    for copy in copies:
        copy.start()

    def layer_step(l, carry):
        t, f = mobility(sat_v[l], hist_v[l])
        tote[l + H] = t
        frace[l + H] = f
        return carry

    for i, (l, n) in enumerate(parts):
        copies[i].wait()
        copies[len(parts) + i].wait()
        loop(l, l + n, layer_step, 0)
    for copy in copies[2 * len(parts) : -len(large)]:
        copy.wait()
    count, group = cell_v.shape
    cell[...] = flatten(cell_v[...].astype(jnp.float32), spread).astype(jnp.int32)
    wells[0:1, :] = flatten(index_v[...], spread)
    wells[1:2, :] = flatten(jnp.broadcast_to(target_v[...], (count, group)), spread)
    wells[2:3, :] = flatten(
        jnp.broadcast_to(control_v[...].astype(jnp.float32), (count, group)), spread
    )
    at_place = at_places(cell[...], lax.axis_index(gz) * layers, layers, rows, columns)
    at_column = at_columns(cell[...], columns)
    hot[...] = at_place.astype(jnp.bfloat16)
    flat = (layers * rows, columns)
    weight = wells[0:1, :] * gather(tote[own].reshape(flat), at_place, at_column)
    cell_p = gather(p0e[own].reshape(flat), at_place, at_column)
    perfs[0:1, :] = weight
    perfs[1:2, :] = cell_p
    for i, value in enumerate((weight * cell_p, weight)):
        part = value[:, 0:LANES]
        for lane in range(LANES, value.shape[1], LANES):
            part = part + value[:, lane : lane + LANES]
        shift = LANES // 2
        while shift >= group:
            part = part + roll(part, shift, 1)
            shift //= 2
        sums[i : i + 1, :] = part
    for copy in copies[-len(large) :]:
        copy.wait()
    even = lax.axis_index(gz) % 2 == 0
    refs = {"p0": p0e, "tot": tote, "t0": t0, "stor": stor, "t1": t1, "t2": t2, "frac": frace}
    for message, is_top in ((near, even), (cross, jnp.logical_not(even))):
        at = 0
        for name, count in Z_PARTS:
            if name == "sums" and message is cross:
                continue
            if name == "sums":
                message[at] = jnp.zeros((rows, columns), jnp.float32)
                message[at, 0:2, 0:LANES] = sums[...]
            else:
                edge = jnp.where(is_top, H + layers - count, H)
                message[pl.ds(at, count)] = refs[name][pl.ds(edge, count)]
            at += count


def masks(rows, columns):
    row = lax.broadcasted_iota(jnp.int32, (rows, columns), 0)
    column = lax.broadcasted_iota(jnp.int32, (rows, columns), 1)
    return (row == rows - 1, column == columns - 1)


def lateral_faces(tot, t1, t2, store, last_row, last_column, top_x):
    along = jnp.where(last_row, 0.0, t1) * 0.5 * (tot + roll(tot, -1, 0))
    across = jnp.where(last_column, 0.0, t2) * 0.5 * (tot + roll(tot, -1, 1))
    part = store + along + roll(along, 1, 0) + across + roll(across, 1, 1)
    return (jnp.where(last_row, jnp.where(top_x, 0.0, t1), along), across, part)


def is_last(axis):
    return lax.axis_index(axis) == lax.axis_size(axis) - 1


def first_sweep(e, p0e, stor, f0e, f1e, f2e, dpe, last_row):
    above = f0e[e]
    below = f0e[e - 1]
    along = jnp.where(last_row, 0.0, f1e[e])
    across = f2e[e]
    diag = dpe[e] + above + below
    p = p0e[e]
    base = stor[e] * p + above * p0e[e + 1] + below * p0e[e - 1]
    base = base + along * roll(p, -1, 0) + roll(along * p, 1, 0)
    base = base + across * roll(p, -1, 1) + roll(across * p, 1, 1)
    return (base, jnp.where(diag > 0.0, 1.0 / diag, 0.0))


def faces_kernel(*refs, layers, gx):
    p0e, tote, frace, stor, t0, t1, t2, part = refs[:8]
    f0e, f1e, f2e, dpe, base, inverse, near, cross, sums = refs[8:]
    _, rows, columns = p0e.shape
    last_row, last_column = masks(rows, columns)
    top_x = is_last(gx)

    def step(e, carry):
        tot = tote[e]
        f0e[e] = t0[e] * 0.5 * (tot + tote[e + 1])
        f1e[e], f2e[e], dpe[e] = lateral_faces(
            tot, t1[e], t2[e], stor[e], last_row, last_column, top_x
        )
        return carry

    loop(H, H + layers, step, 0)
    sums[...] = part[...]
    refs = {"t1": f1e, "tot": tote, "p0": p0e, "dp": dpe, "f0": f0e, "f2": f2e, "f1": f1e}
    refs |= {"frac": frace, "p0_d2": p0e, "f0_d2": f0e, "f2_d2": f2e, "dp_d2": dpe}
    pack_both(near, cross, early_parts(layers), refs, refs, rows, gx)

    def sweep_step(e, carry):
        base[e], inverse[e] = first_sweep(e, p0e, stor, f0e, f1e, f2e, dpe, last_row)
        return carry

    loop(H + 1, H + layers - 1, sweep_step, 0)


def well_holes(sums, wells):
    repeat = lambda x: jnp.concatenate([x] * (wells.shape[1] // LANES), axis=1)
    goal = wells[1:2, :]
    return jnp.where(
        wells[2:3, :] == 0.0, (goal + repeat(sums[0:1, :])) / repeat(sums[1:2, :]), goal
    )


def join(a, b):
    return jnp.concatenate([a, b], axis=0)


def seam_faces(first, last, fields, seams, f1, inverse, p):
    p0e, tote, f0e, f1e, dpe = fields
    rows, columns = p0e.shape[1:]
    row = lax.broadcasted_iota(jnp.int32, (rows + 8, columns), 0)
    edge = (row == rows - 1) | (row == rows + 7)

    def step(e, below):
        tot = join(tote[e], seams["tot"][e])
        mixed = join(f1e[e], seams["f1"][e])
        border = jnp.where(edge, mixed * 0.5 * (tot + roll(tot, -1, 0)), 0.0)
        f1[e] = jnp.where(edge, border, mixed)
        above = join(f0e[e], seams["f0"][e])
        diag = join(dpe[e], seams["dp"][e]) + above + below + border + roll(border, 1, 0)
        inverse[e] = jnp.where(diag > 0.0, 1.0 / diag, 0.0)
        p[e] = join(p0e[e], seams["p0"][e])
        return above

    loop(first, last, step, join(f0e[first - 1], seams["f0"][first - 1]))


def sweep_layers(number, first, last, old, new, fields, seams, f1, inverse, part):
    rhse, f0e, f2e = fields
    rows, columns = rhse.shape[1:]
    row = lax.broadcasted_iota(jnp.int32, (rows + 8, columns), 0)
    beyond = (row == rows + 1) | (row == rows + 6)
    blank = jnp.zeros((rows, columns), jnp.float32)

    def step(e, carry):
        below, p = carry
        above = old[e + 1]
        face = join(f0e[e], seams["f0"][e])
        x = f1[e]
        y = join(f2e[e], seams["f2"][e])
        side = seams["rhs2"][e]
        if number == 3:
            side = jnp.where(beyond[rows:], seams["rhs3"][e], side)
        total = join(rhse[e], side) + below + face * above
        total = total + x * roll(p, -1, 0) + roll(x * p, 1, 0)
        total = total + y * roll(p, -1, 1) + roll(y * p, 1, 1)
        value = total * inverse[e]
        if number == 1:
            value = jnp.where(beyond, join(blank, seams["p1"][e]), value)
        new[e, part] = value[part]
        return (face * p, above)

    start = join(f0e[first - 1], seams["f0"][first - 1]) * old[first - 1]
    loop(first, last, step, (start, old[first]))


def seam_kernel(near, cross, *refs, layers, gx):
    p0e, tote, f0e, f1e, f2e, dpe, rhse = refs[:7]
    refs = refs[7:]
    seams = dict(zip(SEAMS, refs))
    f1, inverse, p, p1 = refs[len(SEAMS) :]
    for seam in seams.values():
        seam[...] = jnp.zeros(seam.shape, jnp.float32)
    unpack_both(near, cross, early_parts(layers), seams, gx)
    inner = (H + 1, H + layers - 1)
    seam_faces(*inner, (p0e, tote, f0e, f1e, dpe), seams, f1, inverse, p)
    for e in (H, H + layers - 1):
        p[e] = join(p0e[e], jnp.zeros_like(seams["p0"][e]))
    own = slice(0, p0e.shape[1])
    sweep_layers(1, *inner, p, p1, (rhse, f0e, f2e), seams, f1, inverse, own)


def halo_kernel(*refs, layers, gx, gz):
    own_t0, cross, near, cell, wells, own_perfs = refs[10:16]
    p0e, tote, frace, stor, f0e, f1e, f2e, dpe, base, inverse, perfs, hot = refs[16:]
    ext, rows, columns = p0e.shape
    even = lax.axis_index(gz) % 2 == 0
    top_z = is_last(gz)
    top_x = is_last(gx)
    last_row, last_column = masks(rows, columns)
    where = {}
    at = 0
    for name, count in Z_PARTS:
        where[name] = (at, count)
        at += count

    def halo(name, e):
        at, count = where[name]
        low = e < H
        at = at + e - (H - count if low else H + layers)
        one, two = (near[at], cross[at])
        return jnp.where(even, two, one) if low else jnp.where(even, one, two)

    for name, target in (("p0", p0e), ("tot", tote), ("frac", frace), ("stor", stor)):
        count = where[name][1]
        for e in (*range(H - count, H), *range(H + layers, H + layers + count)):
            target[e] = halo(name, e)
    f0e[H + layers - 1] = jnp.where(top_z, 0.0, own_t0[H + layers - 1]) * 0.5 * (
        tote[H + layers - 1] + tote[H + layers]
    )
    for e in (*range(0, H), *range(H + layers, ext - 1)):
        f0e[e] = halo("t0", e) * 0.5 * (tote[e] + tote[e + 1])
    for e in (*range(1, H), *range(H + layers, ext - 1)):
        f1e[e], f2e[e], dpe[e] = lateral_faces(
            tote[e], halo("t1", e), halo("t2", e), stor[e], last_row, last_column, top_x
        )
    for e in (*range(1, H + 1), *range(H + layers - 1, ext - 1)):
        base[e], inverse[e] = first_sweep(e, p0e, stor, f0e, f1e, f2e, dpe, last_row)
    width = H - 1
    first = lax.axis_index(gz) * layers
    sides = ((1, first - width), (H + layers, first + layers))
    at_place = [at_places(cell[...], layer, width, rows, columns) for _, layer in sides]
    at_place = jnp.concatenate(at_place, axis=0)
    at_column = at_columns(cell[...], columns)
    hot[...] = at_place.astype(jnp.bfloat16)
    flat = (width * rows, columns)
    both = lambda ref: join(*(ref[e : e + width].reshape(flat) for e, _ in sides))
    weight = wells[0:1, :] * gather(both(tote), at_place, at_column)
    perfs[0:1, :] = own_perfs[0:1, :] + weight
    perfs[1:2, :] = own_perfs[1:2, :] + gather(both(p0e), at_place, at_column)


def build_kernel(*refs, layers, gx):
    p0e, stor, f0e, f1e, f2e, dpe, tote, base, inverse, sums, perfs, hot, own_hot = refs[:13]
    cell, wells, rhse, source, x_near, x_cross, bottom = refs[13:20]
    p1, g2u, g2d, g3u, g3d, rxu, rxd, dpx = refs[20:]
    ext, rows, columns = p0e.shape
    last_row, _ = masks(rows, columns)
    hole = well_holes(sums[...], wells[...])
    bottom[...] = hole[:, 0:LANES]
    rate = perfs[0:1, :] * (hole - perfs[1:2, :])
    pieces = split(jnp.where(at_columns(cell[...], columns), rate, 0.0))

    def scatter(mask):
        spread = [
            lax.dot_general(
                mask, piece, (((1,), (1,)), ((), ())), preferred_element_type=jnp.float32
            )
            for piece in pieces
        ]
        return (spread[0] + spread[1]).reshape(-1, rows, columns)

    width = H - 1
    inside = scatter(own_hot[...])
    outside = scatter(hot[...])
    source[...] = inside
    rhse[H : ext - H] = inside
    rhse[1:H] = outside[:width]
    rhse[ext - H : ext - 1] = outside[width:]

    def first_step(e, carry):
        wells_rate = rhse[e]
        p1[e] = (base[e] + wells_rate) * inverse[e]
        rhse[e] = stor[e] * p0e[e] + wells_rate
        return carry

    loop(1, ext - 1, first_step, 0)

    def second_step(e, carry):
        along = jnp.where(last_row, 0.0, f1e[e])
        across = f2e[e]
        p = p1[e]
        rhs = rhse[e]
        lower = roll(along * p, 1, 0)
        upper = along * roll(p, -1, 0)
        g2u[e] = rhs + lower
        g2d[e] = rhs + upper
        new = rhs + lower + upper + f0e[e] * p1[e + 1] + f0e[e - 1] * p1[e - 1]
        new = new + across * roll(p, -1, 1) + roll(across * p, 1, 1)
        p2 = new * inverse[e]
        g3u[e] = rhs + roll(along * p2, 1, 0)
        g3d[e] = rhs + along * roll(p2, -1, 0)
        return carry

    loop(H - 1, ext - H + 1, second_step, 0)

    for e, beside, face in ((2, 1, 1), (ext - 3, ext - 2, ext - 3)):
        along = jnp.where(last_row, 0.0, f1e[e])
        across = f2e[e]
        p = p0e[e]
        rhs = rhse[e] + f0e[face] * p0e[beside]
        rhs = rhs + across * roll(p, -1, 1) + roll(across * p, 1, 1)
        rxu[e] = rhs + roll(along * p, 1, 0)
        rxd[e] = rhs + along * roll(p, -1, 0)
        dpx[e] = dpe[e] + f0e[face]

    shared = {"t1": f1e, "tot": tote, "p0": p0e, "dp": dpe, "f0": f0e, "f2": f2e, "f1": f1e}
    shared |= {"p0_d2": p0e, "f0_d2": f0e, "f2_d2": f2e, "dp_d2": dpe, "rhs": rhse, "p1_d2": p1}
    for e, beside, face in ((H - 1, H - 2, H - 2), (ext - H, ext - H + 1, ext - H)):
        across = f2e[e]
        p = p1[e]
        beyond = f0e[face] * p1[beside] + across * roll(p, -1, 1) + roll(across * p, 1, 1)
        g2u[e] = g2u[e] + beyond
        g2d[e] = g2d[e] + beyond
        dpx[e] = dpe[e] + f0e[face]
    shared["dp_x"] = shared["dp2_x"] = dpx
    up = shared | {"g2": g2u, "g3": g3u, "rhs_x": rxu}
    down = shared | {"g2": g2d, "g3": g3d, "rhs_x": rxd}
    pack_both(x_near, x_cross, late_parts(layers), up, down, rows, gx)


def finish_kernel(*refs, gx):
    sat, hist, volume, storage, source = refs[:5]
    p0e, tote, frace, f0e, f1e, f2e, dpe, rhse, near, cross = refs[5:15]
    hole = refs[19 + len(SEAMS)]
    refs = refs[20 + len(SEAMS) :]
    new_p, residual, new_sat, new_hist, bottom = refs[:5]
    seams = dict(zip(SEAMS, refs[5:]))
    f1, rdiag, pa, pb = refs[5 + len(SEAMS) :]
    bottom[...] = hole[:, 0 : bottom.shape[1]]
    layers, rows, columns = sat.shape
    ext = layers + 2 * H
    unpack_both(near, cross, late_parts(layers), seams, gx)
    sfrac = seams["frac"]
    pa[0] = join(p0e[0], seams["p0"][0])
    pa[ext - 1] = join(p0e[ext - 1], seams["p0"][ext - 1])
    for first, last in ((1, H + 1), (ext - H - 1, ext - 1)):
        seam_faces(first, last, (p0e, tote, f0e, f1e, dpe), seams, f1, rdiag, pa)

    pressures = (pa, pb)
    fields = (rhse, f0e, f2e)
    inner = (H + 1, ext - H - 1)
    everywhere = slice(0, rows + 8)
    for number in range(1, SWEEPS + 1):
        old, new = pressures[(number - 1) % 2], pressures[number % 2]
        ranges = [(number, ext - number, everywhere)]
        if number == 1:
            ranges = [
                (number, inner[0], everywhere),
                (*inner, slice(rows, rows + 8)),
                (inner[1], ext - number, everywhere),
            ]
        for first, last, part in ranges:
            sweep_layers(number, first, last, old, new, fields, seams, f1, rdiag, part)
    field = pressures[SWEEPS % 2]

    def flow(face, p, p_next, f, f_next):
        water = face * (p - p_next)
        return (water, water * jnp.where(water > 0, f, f_next))

    def last_step(l, carry):
        below_w, below_g = carry
        e = l + H
        p = field[e]
        f = join(frace[e], sfrac[e])
        own_p = p[:rows]
        own_f = f[:rows]
        above_w, above_g = flow(f0e[e], own_p, field[e + 1][:rows], own_f, frace[e + 1])
        xw, xg = flow(f1[e], p, roll(p, -1, 0), f, roll(f, -1, 0))
        yw, yg = flow(f2e[e], own_p, roll(own_p, -1, 1), own_f, roll(own_f, -1, 1))
        water = above_w - below_w + (xw - roll(xw, 1, 0))[:rows] + yw - roll(yw, 1, 1)
        out = above_g - below_g + (xg - roll(xg, 1, 0))[:rows] + yg - roll(yg, 1, 1)
        new_p[l] = own_p
        residual[l] = rhse[e] - storage[l] * own_p - water
        src = source[l]
        gas = jnp.maximum(src, 0.0) + jnp.minimum(src, 0.0) * own_f
        s = sat[l] + volume[l] * (gas - out)
        new_sat[l] = s
        new_hist[l] = jnp.maximum(hist[l], s)
        return (above_w, above_g)

    first = flow(f0e[H - 1], field[H - 1][:rows], field[H][:rows], frace[H - 1], frace[H])
    loop(0, layers, last_step, first)


def swap(block, axis, first):
    pairs = [(i, i + 1) for i in range(first, lax.axis_size(axis) - 1, 2)]
    return lax.ppermute(block, axis, pairs + [(b, a) for a, b in pairs])


def pin(*shape, dtype=jnp.float32):
    return pltpu.VMEM(shape, dtype)


VMEM = pl.BlockSpec(memory_space=pltpu.VMEM)
HBM = pl.BlockSpec(memory_space=pltpu.HBM)


def call(kernel, outs, scratch, *args, space=VMEM, sems=0, aliases={}):
    as_struct = lambda s: s if hasattr(s, "dtype") else jax.ShapeDtypeStruct(s, jnp.float32)
    as_scratch = lambda s: pltpu.VMEM(as_struct(s).shape, as_struct(s).dtype)
    return pl.pallas_call(
        kernel,
        out_shape=[as_struct(s) for s in outs],
        in_specs=[space] * len(args),
        out_specs=[VMEM] * len(outs),
        scratch_shapes=[as_scratch(s) for s in scratch]
        + ([pltpu.SemaphoreType.DMA((sems,))] if sems else []),
        input_output_aliases=aliases,
        compiler_params=pltpu.CompilerParams(vmem_limit_bytes=24 * 1024 * 1024),
    )(*(pltpu.with_memory_space_constraint(a, pltpu.HBM) if space is HBM else a for a in args))


def body(
    pressure,
    saturation,
    sat_history,
    storage,
    step_volume,
    transmiss,
    perf_cell,
    perf_index,
    control,
    target,
):
    layers, rows, columns = pressure.shape
    ext = layers + 2 * H
    wells, perfs = perf_cell.shape
    block = (layers, rows, columns)
    pinned = pin(*block)
    ext_block = pin(ext, rows, columns)
    z_layers = sum(count for _, count in Z_PARTS)
    z_near, z_cross = (pin(n, rows, columns) for n in (z_layers, z_layers - 1))
    entries = wells * perfs
    early, late = (pin(tiles(f(layers)), 8, columns) for f in (early_parts, late_parts))
    seams = [pin(ext, 8, columns)] * len(SEAMS)
    *fields, near, cross, part, cell, per_perf, perf_values, own_hot = call(
        functools.partial(prepare_kernel, gz="gz"),
        [ext_block] * 7
        + [z_near, z_cross]
        + [
            pin(2, LANES),
            pin(1, entries, dtype=jnp.int32),
            pin(3, entries),
            pin(2, entries),
            pin(layers * rows, entries, dtype=jnp.bfloat16),
        ],
        [
            block,
            block,
            jax.ShapeDtypeStruct((perfs, wells), jnp.int32),
            (perfs, wells),
            jax.ShapeDtypeStruct((1, wells), jnp.int32),
            (1, wells),
            (perfs, LANES),
        ],
        saturation,
        sat_history,
        pressure,
        storage,
        transmiss,
        perf_cell.T,
        perf_index.T,
        control.reshape(1, wells),
        target.reshape(1, wells),
        space=HBM,
        sems=3 * -(-layers // LOADED) + 8,
    )
    cross = swap(cross, "gz", 1)
    near = swap(near, "gz", 0)
    p0e, tote, frace, stor, t0, t1, t2 = fields
    f0e, f1e, f2e, dpe, base, inverse, early_near, early_cross, part = call(
        functools.partial(faces_kernel, layers=layers, gx="gx"),
        [ext_block] * 6 + [early, early, pin(2, LANES)],
        [],
        *fields,
        part,
    )
    early_cross = swap(early_cross, "gx", 1)
    early_near = swap(early_near, "gx", 0)
    sums = part + near[-1, 0:2, 0:LANES]
    step = 2
    while step < lax.axis_size("gz"):
        pairs = [(i, i ^ step) for i in range(lax.axis_size("gz"))]
        tile = jnp.pad(sums, ((0, 8 - sums.shape[0]), (0, 0)))
        sums = sums + lax.ppermute(tile, "gz", pairs)[: sums.shape[0]]
        step *= 2
    early_near, near = lax.optimization_barrier((early_near, near))
    p0e, tote, frace, stor, f0e, f1e, f2e, dpe, base, inverse, perf_values, hot = call(
        functools.partial(halo_kernel, layers=layers, gx="gx", gz="gz"),
        [ext_block] * 10
        + [pin(2, entries), pin(2 * (H - 1) * rows, entries, dtype=jnp.bfloat16)],
        [],
        p0e,
        tote,
        frace,
        stor,
        f0e,
        f1e,
        f2e,
        dpe,
        base,
        inverse,
        t0,
        cross,
        near,
        cell,
        per_perf,
        perf_values,
        aliases={i: i for i in range(10)},
    )
    rhse, source, late_near, late_cross, hole = call(
        functools.partial(build_kernel, layers=layers, gx="gx"),
        [ext_block, pinned, late, late, pin(1, LANES)],
        [ext_block] * 8,
        p0e,
        stor,
        f0e,
        f1e,
        f2e,
        dpe,
        tote,
        base,
        inverse,
        sums,
        perf_values,
        hot,
        own_hot,
        cell,
        per_perf,
    )
    late_cross = swap(late_cross, "gx", 1)
    late_near = swap(late_near, "gx", 0)
    early_near, early_cross, rhse = lax.optimization_barrier((early_near, early_cross, rhse))
    joined = [pin(ext, rows + 8, columns)] * 4
    filled = call(
        functools.partial(seam_kernel, layers=layers, gx="gx"),
        seams + joined,
        [],
        early_near,
        early_cross,
        p0e,
        tote,
        f0e,
        f1e,
        f2e,
        dpe,
        rhse,
    )
    field, residual, new_sat, new_hist, bottom, *_ = call(
        functools.partial(finish_kernel, gx="gx"),
        [block] * 4 + [(1, wells)] + seams + joined,
        [],
        saturation,
        sat_history,
        step_volume,
        storage,
        source,
        p0e,
        tote,
        frace,
        f0e,
        f1e,
        f2e,
        dpe,
        rhse,
        late_near,
        late_cross,
        *filled,
        hole,
        aliases={15 + i: 5 + i for i in range(len(filled))},
    )
    return (field, residual, new_sat, new_hist, bottom.reshape(wells))


def solution(mesh):
    return jax.shard_map(
        body,
        mesh=mesh,
        in_specs=(
            P("gz", "gx", None),
            P("gz", "gx", None),
            P("gz", "gx", None),
            P("gz", "gx", None),
            P("gz", "gx", None),
            P(None, "gz", "gx", None),
            P("gx", None),
            P("gx", None),
            P("gx"),
            P("gx"),
        ),
        out_specs=(
            P("gz", "gx", None),
            P("gz", "gx", None),
            P("gz", "gx", None),
            P("gz", "gx", None),
            P("gx"),
        ),
        check_vma=False,
    )
```
